32 devices in a mesh: seq: 8 (over y, x, core), head: 4 (over z).
Axes of the slice: x: 2, y: 2, z: 4, core: 2. Of those that a mesh axis runs over, the one named last changes fastest.
Arguments:
- byte_ids: int32 [8, 2048], P('seq', 'head'), may hold values from 0 to 255
- next_bytes: int32 [8, 2048], P('seq', 'head'), may hold values from 0 to 255
- loss_mask: int32 [8, 2048], P('seq', 'head'), may hold values from 0 to 1
- pool_slots: int32 [8, 2048], P('seq', 'head'), may hold values from 0 to 255, as said below
- qkv_weight: float32 [3, 512, 1536], P(None, 'seq'), may hold values from -0.25 to 0.25
- proj_weight: float32 [4, 512, 512], P(None, 'seq'), may hold values from -0.5 to 0.5
- upward_weight: float32 [3, 512, 2048], P(None, 'seq'), may hold values from -0.25 to 0.25
- downward_weight: float32 [3, 2048, 512], P(None, 'seq'), may hold values from -0.125 to 0.125
- table_weight: float32 [2, 256, 512], P(None, 'seq')
- gain_weight: float32 [9, 512], P(None, 'seq')
- qkv_first: float32 [3, 512, 1536], P(None, 'seq'), may hold values from -1.9073486e-06 to 1.9073486e-06
- qkv_second: float32 [3, 512, 1536], P(None, 'seq'), may hold values from 5.2779027e-13 to 2.1071474e-12
- proj_first: float32 [4, 512, 512], P(None, 'seq'), may hold values from -1.9073486e-06 to 1.9073486e-06
- proj_second: float32 [4, 512, 512], P(None, 'seq'), may hold values from 5.2779027e-13 to 2.1071474e-12
- upward_first: float32 [3, 512, 2048], P(None, 'seq'), may hold values from -1.9073486e-06 to 1.9073486e-06
- upward_second: float32 [3, 512, 2048], P(None, 'seq'), may hold values from 5.2779027e-13 to 2.1071474e-12
- downward_first: float32 [3, 2048, 512], P(None, 'seq'), may hold values from -1.9073486e-06 to 1.9073486e-06
- downward_second: float32 [3, 2048, 512], P(None, 'seq'), may hold values from 5.2779027e-13 to 2.1071474e-12
- table_first: float32 [2, 256, 512], P(None, 'seq'), may hold values from -1.9073486e-06 to 1.9073486e-06
- table_second: float32 [2, 256, 512], P(None, 'seq'), may hold values from 5.2779027e-13 to 2.1071474e-12
- gain_first: float32 [9, 512], P(None, 'seq'), may hold values from -9.536743e-06 to 9.536743e-06
- gain_second: float32 [9, 512], P(None, 'seq'), may hold values from 1.3144586e-11 to 5.2779028e-11
Outputs:
- qkv_master: float32 [3, 512, 1536], P(None, 'seq')
- qkv_mean: float32 [3, 512, 1536], P(None, 'seq')
- qkv_meansq: float32 [3, 512, 1536], P(None, 'seq')
- proj_master: float32 [4, 512, 512], P(None, 'seq')
- proj_mean: float32 [4, 512, 512], P(None, 'seq')
- proj_meansq: float32 [4, 512, 512], P(None, 'seq')
- upward_master: float32 [3, 512, 2048], P(None, 'seq')
- upward_mean: float32 [3, 512, 2048], P(None, 'seq')
- upward_meansq: float32 [3, 512, 2048], P(None, 'seq')
- downward_master: float32 [3, 2048, 512], P(None, 'seq')
- downward_mean: float32 [3, 2048, 512], P(None, 'seq')
- downward_meansq: float32 [3, 2048, 512], P(None, 'seq')
- table_master: float32 [2, 256, 512], P(None, 'seq')
- table_mean: float32 [2, 256, 512], P(None, 'seq')
- table_meansq: float32 [2, 256, 512], P(None, 'seq')
- gain_master: float32 [9, 512], P(None, 'seq')
- gain_mean: float32 [9, 512], P(None, 'seq')
- gain_meansq: float32 [9, 512], P(None, 'seq')
- qkv_copy: bfloat16 [3, 512, 1536], P(None, 'seq')
- proj_copy: bfloat16 [4, 512, 512], P(None, 'seq')
- upward_copy: bfloat16 [3, 512, 2048], P(None, 'seq')
- downward_copy: bfloat16 [3, 2048, 512], P(None, 'seq')
- table_copy: bfloat16 [2, 256, 512], P(None, 'seq')
- loss_sums: float32 [2], replicated
- valid_count: float32 [], replicated
- grad_norm: float32 [], replicated
- residual_rms: float32 [3], replicated
The draws below stay inside these ranges and needn't reach their ends.
Inputs may be any that keep to these rules, and one draw needn't show every extreme that they name: `pool_slots`: within each block of 512 positions of a sequence on one index of head, slots start at 0 and rise by 0 or 1 from a position to the next; a block has at most 256 slots, and one block of each sequence has exactly 256.
All inputs are finite; a program needn't handle non-finite values.
Results may differ from the reference program's by a relative error of at most 0.019.
Values may be sent and summed in bfloat16 or wider, within the bound.
No kernel may reach another device: no remote copies, remote signals or barrier semaphores. Data moves between devices by JAX's collectives and lax.ppermute only.
A program may use at most 256 MiB of HBM per device.

```python
import math
import jax
import jax.numpy as jnp
from jax import lax

D = 512
HEADS = 8
FF = 2048
VOCAB = 256
HEAD_DIM = 64
LOC = 512
CAP = 256
STEP = 10
SEQS = 8
LENGTH = 2048
NPARAM = 9966080
N_HEAD = 4


def draw_loss_mask(key, part):
    key = jax.random.fold_in(key, 21)
    key_rows, key_cols = jax.random.split(key)
    seq_limit = 1024 * (SEQS + 2 * jnp.arange(SEQS)) // (3 * SEQS)
    pos_limit = 1024 * (LENGTH + 2 * jnp.arange(LENGTH)) // (3 * LENGTH)
    keep_rows = jax.random.randint(key_rows, (SEQS, LENGTH), 0, 1024) < seq_limit[:, None]
    keep_cols = jax.random.randint(key_cols, (SEQS, LENGTH), 0, 1024) < pos_limit[None, :]
    return (keep_rows & keep_cols).astype(jnp.int32)


def draw_pool_slots(key, part):
    key = jax.random.fold_in(key, 22)
    key_count, key_full, key_order = jax.random.split(key, 3)
    block_total = SEQS * N_HEAD
    counts = jax.random.randint(key_count, (SEQS, N_HEAD), CAP // 3 + 1, CAP + 1)
    full_block = jax.random.randint(key_full, (SEQS, 1), 0, N_HEAD)
    counts = jnp.where(jnp.arange(N_HEAD)[None, :] == full_block, CAP, counts).reshape(block_total, 1)
    noise = jax.random.randint(key_order, (block_total, LOC - 1), 0, 1 << 18) * LOC + jnp.arange(LOC - 1)[None, :]
    order = jnp.argsort(noise, axis=1)
    ranking = jnp.argsort(order, axis=1)
    cuts = (ranking < counts - 1).astype(jnp.int32)
    slots = jnp.concatenate([jnp.zeros((block_total, 1), jnp.int32), jnp.cumsum(cuts, axis=1).astype(jnp.int32)], axis=1)
    return slots.reshape(SEQS, LENGTH).astype(jnp.int32)


def draw_table_weight(key, part):
    key = jax.random.fold_in(key, 23)
    entries = jax.random.normal(key, (2, VOCAB, D), jnp.float32)
    scales = jnp.array([1.0, 2.0 / D ** 0.5], jnp.float32)
    return entries * scales[:, None, None]


def draw_gain_weight(key, part):
    key = jax.random.fold_in(key, 24)
    key_factor, key_sign = jax.random.split(key)
    ramp = jnp.arange(D, dtype=jnp.float32)[None, :] / D
    base = 0.5 + ramp
    factor = jax.random.uniform(key_factor, (9, D), jnp.float32, 0.8, 1.2)
    signs = jnp.where(jax.random.bernoulli(key_sign, 0.5, (9, D)), 1.0, -1.0)
    signs = jnp.where(jnp.arange(9)[:, None] == 8, signs, 1.0)
    return base * factor * signs


def plant(drawn, key, low, high):
    longest = drawn.shape.index(max(drawn.shape))
    spots = []
    for shift in (0, 1):
        where = [jax.random.randint(jax.random.fold_in(key, axis), (), 0, length) for axis, length in enumerate(drawn.shape)]
        where[longest] = (where[longest] + shift) % drawn.shape[longest]
        spots.append(tuple(where))
    return drawn.at[spots[0]].set(low).at[spots[1]].set(high)


def level_of(stream_key, extent, pieces, low, high):
    def one(axis_at, blocks):
        draws = jax.random.uniform(jax.random.fold_in(jax.random.fold_in(stream_key, 6), axis_at), (blocks,), jnp.float32, low / len(pieces), high / len(pieces))
        return jnp.repeat(jnp.exp(draws), extent[axis_at] // blocks).reshape((-1,) + (1,) * (len(extent) - axis_at - 1))

    factor_of = one(*pieces[0])
    for cut in pieces[1:]:
        factor_of = factor_of * one(*cut)
    return factor_of


def bell_draw(key, extent, width, reach, shards=(), kind=jnp.bfloat16):
    level = level_of(key, extent, shards, -0.22, 0.18) if shards else 1.0
    drawn = jax.random.normal(key, extent, jnp.float32) * width * level
    return jnp.minimum(jnp.maximum(drawn, -reach), reach).astype(kind)


def setup_inputs(seed: int = 0) -> dict:
    keys = jax.random.split(jax.random.key(seed), 23)
    return {
        "byte_ids": plant(jax.random.randint(keys[0], (SEQS, LENGTH), 0, VOCAB), jax.random.fold_in(keys[0], 1), 0, VOCAB - 1).astype(jnp.int32),
        "next_bytes": plant(jax.random.randint(keys[1], (SEQS, LENGTH), 0, VOCAB), jax.random.fold_in(keys[1], 1), 0, VOCAB - 1).astype(jnp.int32),
        "loss_mask": draw_loss_mask(jax.random.fold_in(keys[22], 71), 0),
        "pool_slots": draw_pool_slots(jax.random.fold_in(keys[22], 71), 0),
        "qkv_weight": bell_draw(keys[4], (3, D, 3 * D), D ** -0.5, 0.25, ((1, 8),), jnp.float32),
        "proj_weight": bell_draw(keys[5], (4, D, D), (D // 4) ** -0.5, 0.5, ((1, 8),), jnp.float32),
        "upward_weight": bell_draw(keys[6], (3, D, FF), D ** -0.5, 0.25, ((1, 8),), jnp.float32),
        "downward_weight": bell_draw(keys[7], (3, FF, D), FF ** -0.5, 0.125, ((1, 8),), jnp.float32),
        "table_weight": draw_table_weight(jax.random.fold_in(keys[22], 71), 0),
        "gain_weight": draw_gain_weight(jax.random.fold_in(keys[22], 71), 0),
        "qkv_first": bell_draw(keys[10], (3, D, 3 * D), (0.0011 / NPARAM ** 0.5), 1.9073486328125e-06, ((1, 8),), jnp.float32),
        "qkv_second": jnp.clip(jnp.exp(math.log(2.107147355906447e-12) - 1.38439136 * jax.random.uniform(keys[11], (3, D, 3 * D), jnp.float32) ** level_of(keys[11], (3, D, 3 * D), ((1, 8),), -0.2, 0.2)), 5.27790268087247e-13, 2.107147355906447e-12),
        "proj_first": bell_draw(keys[12], (4, D, D), (0.0011 / NPARAM ** 0.5), 1.9073486328125e-06, ((1, 8),), jnp.float32),
        "proj_second": jnp.clip(jnp.exp(math.log(2.107147355906447e-12) - 1.38439136 * jax.random.uniform(keys[13], (4, D, D), jnp.float32) ** level_of(keys[13], (4, D, D), ((1, 8),), -0.2, 0.2)), 5.27790268087247e-13, 2.107147355906447e-12),
        "upward_first": bell_draw(keys[14], (3, D, FF), (0.0011 / NPARAM ** 0.5), 1.9073486328125e-06, ((1, 8),), jnp.float32),
        "upward_second": jnp.clip(jnp.exp(math.log(2.107147355906447e-12) - 1.38439136 * jax.random.uniform(keys[15], (3, D, FF), jnp.float32) ** level_of(keys[15], (3, D, FF), ((1, 8),), -0.2, 0.2)), 5.27790268087247e-13, 2.107147355906447e-12),
        "downward_first": bell_draw(keys[16], (3, FF, D), (0.0011 / NPARAM ** 0.5), 1.9073486328125e-06, ((1, 8),), jnp.float32),
        "downward_second": jnp.clip(jnp.exp(math.log(2.107147355906447e-12) - 1.38439136 * jax.random.uniform(keys[17], (3, FF, D), jnp.float32) ** level_of(keys[17], (3, FF, D), ((1, 8),), -0.2, 0.2)), 5.27790268087247e-13, 2.107147355906447e-12),
        "table_first": bell_draw(keys[18], (2, VOCAB, D), (0.0011 / NPARAM ** 0.5), 1.9073486328125e-06, ((1, 8),), jnp.float32),
        "table_second": jnp.clip(jnp.exp(math.log(2.107147355906447e-12) - 1.38439136 * jax.random.uniform(keys[19], (2, VOCAB, D), jnp.float32) ** level_of(keys[19], (2, VOCAB, D), ((1, 8),), -0.2, 0.2)), 5.27790268087247e-13, 2.107147355906447e-12),
        "gain_first": bell_draw(keys[20], (9, D), (0.0055 / NPARAM ** 0.5), 9.5367431640625e-06, ((1, 8),), jnp.float32),
        "gain_second": jnp.clip(jnp.exp(math.log(5.277902767608644e-11) - 1.3901039 * jax.random.uniform(keys[21], (9, D), jnp.float32) ** level_of(keys[21], (9, D), ((1, 8),), -0.2, 0.2)), 1.3144586114011148e-11, 5.277902767608644e-11),
    }


EXACT = lax.Precision.HIGHEST
NORM_EPS = 1e-06
BETA_FIRST = 0.9
BETA_SECOND = 0.95
ADAM_EPS = 1e-08
DECAY_RATE = 0.1
RATE_MATRIX = 0.05
RATE_VECTOR = 0.5
CLIP_NORM = 0.01

@jax.custom_vjp
def low(v):
    return lax.optimization_barrier(v.astype(jnp.bfloat16)).astype(jnp.float32)

@jax.custom_vjp
def low_back(v):
    return v

def low_keep(v):
    return (low(v), None)

def low_pass(kept, grad):
    return (grad,)

def back_keep(v):
    return (v, None)

def back_low(kept, grad):
    return (low(grad),)
low.defvjp(low_keep, low_pass)
low_back.defvjp(back_keep, back_low)

def norm_rows(stream, gain):
    return stream * lax.rsqrt(lax.optimization_barrier(jnp.mean(stream * stream, axis=-1, keepdims=True)) + NORM_EPS) * gain

def rotate(rows, positions):
    half = rows.shape[-1] // 2
    frequency = 10000.0 ** (-jnp.arange(half, dtype=jnp.float32) / half)
    angles = positions.astype(jnp.float32)[:, None, None] * frequency
    cosine = jnp.cos(angles)
    sine_part = jnp.sin(angles)
    first_half = rows[..., :half]
    second_half = rows[..., half:]
    return jnp.concatenate([first_half * cosine - second_half * sine_part, second_half * cosine + first_half * sine_part], axis=-1)

def transformer(stream, w_qkv, w_proj, w_up, w_down, gain_attn, gain_ffn, positions, allowed):
    count_rows = stream.shape[0]
    normed = low(norm_rows(stream, gain_attn))
    mixed = low_back(jnp.dot(normed, w_qkv, precision=EXACT)).reshape(count_rows, 3, HEADS, HEAD_DIM)
    queries = low(rotate(mixed[:, 0], positions))
    key_rows = low(rotate(mixed[:, 1], positions))
    value_rows = low(mixed[:, 2])
    scores = jnp.einsum('qhe,khe->hqk', queries, key_rows, precision=EXACT) * HEAD_DIM ** (-0.5)
    scores = low_back(jnp.where(allowed[None], scores, -1000000000.0))
    attn_probs = low(jax.nn.softmax(scores, axis=-1))
    context = jnp.einsum('hqk,khe->qhe', attn_probs, value_rows, precision=EXACT)
    context = low(low_back(context)).reshape(count_rows, D)
    middle = stream + low_back(jnp.dot(context, w_proj, precision=EXACT))
    hidden = low_back(jnp.dot(low(norm_rows(middle, gain_ffn)), w_up, precision=EXACT))
    return middle + low_back(jnp.dot(low(jax.nn.gelu(hidden)), w_down, precision=EXACT))

def sequence_terms(copies, tokens, targets, valid, slots):
    qkv_all, proj_all, upward_all, downward_all, table_all, gain_all = copies
    onehot_ids = (tokens[:, None] == jnp.arange(VOCAB)[None, :]).astype(jnp.float32)
    stream0 = low_back(jnp.dot(onehot_ids, table_all[0], precision=EXACT))
    positions = jnp.arange(LENGTH)
    causal = positions[:, None] >= positions[None, :]
    stream1 = transformer(stream0, qkv_all[0], proj_all[0], upward_all[0], downward_all[0], gain_all[0], gain_all[1], positions, causal)
    blocks = slots.reshape(N_HEAD, LOC)
    previous = jnp.concatenate([blocks[:, :1], blocks[:, :-1]], axis=1)
    opening = (jnp.arange(LOC) == 0)[None, :]
    bound_target = jnp.where(opening | (blocks != previous), 1.0, 0.0).reshape(LENGTH)
    bound_normed = low(norm_rows(stream1, gain_all[7]))
    bound_hidden = low_back(jnp.dot(bound_normed, proj_all[3], precision=EXACT))
    bound_logit = lax.optimization_barrier(jnp.sum(jax.nn.gelu(bound_hidden) * gain_all[8], axis=-1)) * D ** (-0.5)
    bce_sum = jnp.sum(valid * (jax.nn.softplus(bound_logit) - bound_target * bound_logit))
    member = (blocks[:, :, None] == jnp.arange(CAP)[None, None, :]).astype(jnp.float32)
    counts = lax.optimization_barrier(jnp.sum(member, axis=1))
    pooled = jnp.einsum('jpc,jpd->jcd', member, stream1.reshape(N_HEAD, LOC, D), precision=EXACT)
    pooled = (pooled / jnp.maximum(counts, 1.0)[:, :, None]).reshape(N_HEAD * CAP, D)
    slot_pos = jnp.arange(N_HEAD * CAP)
    live = (counts > 0).reshape(N_HEAD * CAP)
    slot_allowed = (slot_pos[:, None] >= slot_pos[None, :]) & live[None, :]
    middle_out = transformer(pooled, qkv_all[1], proj_all[1], upward_all[1], downward_all[1], gain_all[2], gain_all[3], slot_pos, slot_allowed)
    spread = jnp.einsum('jpc,jcd->jpd', member, middle_out.reshape(N_HEAD, CAP, D), precision=EXACT)
    stream2 = stream1 + spread.reshape(LENGTH, D)
    stream3 = transformer(stream2, qkv_all[2], proj_all[2], upward_all[2], downward_all[2], gain_all[4], gain_all[5], positions, causal)
    final_rows = low(norm_rows(stream3, gain_all[6]))
    logits = low_back(jnp.dot(final_rows, table_all[1].T, precision=EXACT))
    onehot_next = (targets[:, None] == jnp.arange(VOCAB)[None, :]).astype(jnp.float32)
    picked = lax.optimization_barrier(jnp.sum(logits * onehot_next, axis=-1))
    ce_sum = jnp.sum(valid * (jax.nn.logsumexp(logits, axis=-1) - picked))
    squares = jnp.stack([jnp.sum(valid[:, None] * section * section) for section in (stream1, stream2, stream3)])
    return (ce_sum, bce_sum, squares)

def adam_update(weight, first, second, grad, rate):
    mean = BETA_FIRST * first + (1.0 - BETA_FIRST) * grad
    meansq = BETA_SECOND * second + (1.0 - BETA_SECOND) * grad * grad
    mean_hat = mean / (1.0 - BETA_FIRST ** STEP)
    meansq_hat = meansq / (1.0 - BETA_SECOND ** STEP)
    master = weight - rate * (mean_hat / (jnp.sqrt(meansq_hat) + ADAM_EPS) + DECAY_RATE * weight)
    return (master, mean, meansq)

def reference(byte_ids, next_bytes, loss_mask, pool_slots, qkv_weight, proj_weight, upward_weight, downward_weight, table_weight, gain_weight, qkv_first, qkv_second, proj_first, proj_second, upward_first, upward_second, downward_first, downward_second, table_first, table_second, gain_first, gain_second):
    masters = (qkv_weight, proj_weight, upward_weight, downward_weight, table_weight, gain_weight)
    valid = loss_mask.astype(jnp.float32)
    valid_count = jnp.sum(valid)

    def total_loss(weights):
        copies = tuple((low(weight) for weight in weights))

        def one_sequence(totals, items):
            ce_part, bce_part, square_part = jax.checkpoint(sequence_terms)(copies, items[0], items[1], items[2], items[3])
            return ((totals[0] + ce_part, totals[1] + bce_part, totals[2] + square_part), None)
        start_totals = (jnp.zeros((), jnp.float32), jnp.zeros((), jnp.float32), jnp.zeros((3,), jnp.float32))
        totals, _ = lax.scan(one_sequence, start_totals, (byte_ids, next_bytes, valid, pool_slots))
        return ((totals[0] + totals[1]) / valid_count, totals)
    _, pullback, totals = jax.vjp(total_loss, masters, has_aux=True)
    grads, = pullback(jnp.ones((), jnp.float32))
    grad_norm = jnp.sqrt(sum((jnp.sum(grad * grad) for grad in grads)))
    clip = jnp.minimum(1.0, CLIP_NORM / (grad_norm + 1e-06))
    qkv_out = adam_update(qkv_weight, qkv_first, qkv_second, grads[0] * clip, RATE_MATRIX)
    proj_out = adam_update(proj_weight, proj_first, proj_second, grads[1] * clip, RATE_MATRIX)
    upward_out = adam_update(upward_weight, upward_first, upward_second, grads[2] * clip, RATE_MATRIX)
    downward_out = adam_update(downward_weight, downward_first, downward_second, grads[3] * clip, RATE_MATRIX)
    table_out = adam_update(table_weight, table_first, table_second, grads[4] * clip, RATE_VECTOR)
    gain_out = adam_update(gain_weight, gain_first, gain_second, grads[5] * clip, RATE_VECTOR)
    loss_sums = jnp.stack([totals[0], totals[1]])
    residual_rms = jnp.sqrt(totals[2] / (valid_count * D))
    return (qkv_out[0], qkv_out[1], qkv_out[2], proj_out[0], proj_out[1], proj_out[2], upward_out[0], upward_out[1], upward_out[2], downward_out[0], downward_out[1], downward_out[2], table_out[0], table_out[1], table_out[2], gain_out[0], gain_out[1], gain_out[2], qkv_out[0].astype(jnp.bfloat16), proj_out[0].astype(jnp.bfloat16), upward_out[0].astype(jnp.bfloat16), downward_out[0].astype(jnp.bfloat16), table_out[0].astype(jnp.bfloat16), loss_sums, valid_count, grad_norm, residual_rms)
```

```python
import functools
import math

import jax
import jax.numpy as jnp
import numpy as np
from jax import lax
from jax.experimental import pallas as pl
from jax.experimental.pallas import tpu as pltpu
from jax.sharding import PartitionSpec as P

D = 512
HEADS = 8
FF = 2048
VOCAB = 256
HEAD_DIM = 64
CAP = 256
STEP = 10
CHUNK = 512
HALF = HEAD_DIM // 2

NORM_EPS = 1e-06
BETA_FIRST = 0.9
BETA_SECOND = 0.95
ADAM_EPS = 1e-08
DECAY_RATE = 0.1
RATE_MATRIX = 0.05
RATE_VECTOR = 0.5
CLIP_NORM = 0.01
MASKED = -1000000000.0
SCALE = HEAD_DIM ** (-0.5)
GELU_A = math.sqrt(2.0 / math.pi)
GELU_B = 0.044715

BF = jnp.bfloat16
F32 = jnp.float32
NN = (((1,), (0,)), ((), ()))
NT = (((1,), (1,)), ((), ()))
AXES = ("seq", "head")
VM = pl.BlockSpec(memory_space=pltpu.VMEM)
SM = pl.BlockSpec(memory_space=pltpu.SMEM)


def dot(a, b, dims=NN):
    return lax.dot_general(a, b, dims, preferred_element_type=F32)


def split3(v):
    high = v.astype(BF)
    rest = v - high.astype(F32)
    mid = rest.astype(BF)
    low = (rest - mid.astype(F32)).astype(BF)
    return (high, mid, low)


def exact_dot(ones, v):
    high, mid, low = split3(v)
    return dot(ones, high) + (dot(ones, mid) + dot(ones, low))


def root_of(v):
    return lax.rsqrt(jnp.mean(v * v, axis=-1, keepdims=True) + NORM_EPS)


def norm_back(unit, root, gain, grad):
    turned = grad * gain
    dx = root * (turned - unit * jnp.mean(turned * unit, axis=-1, keepdims=True))
    return dx, jnp.sum(grad * unit, axis=0, keepdims=True)


def gelu_parts(h):
    square = h * h
    t = jnp.tanh(GELU_A * h * (1.0 + GELU_B * square))
    half = 0.5 * (1.0 + t)
    value = h * half
    slope = half + 0.5 * h * (1.0 - t * t) * (GELU_A * (1.0 + 3.0 * GELU_B * square))
    return value, slope


def gelu_value(h):
    t = jnp.tanh(GELU_A * h * (1.0 + GELU_B * (h * h)))
    return h * (0.5 * (1.0 + t))


def one_hot(column, width):
    lanes = lax.broadcasted_iota(jnp.int32, (column.shape[0], width), 1).astype(F32)
    return (lanes == column).astype(F32).astype(BF)


class Plan:
    def __init__(self, mesh):
        self.seq = mesh.shape["seq"]
        self.head = mesh.shape["head"]
        self.chips = self.seq // 2
        side = int(math.isqrt(self.chips))
        while self.chips % side:
            side -= 1
        self.Y, self.X = side, self.chips // side
        self.L = self.head // 2
        self.G = self.head
        self.hd = HEADS // self.G
        self.HW = self.hd * HEAD_DIM
        self.QW = -(-3 * self.HW // 128) * 128
        self.DR = D // self.seq
        self.FR = FF // self.seq
        self.VR = VOCAB // self.seq
        self.sizes = {"y": self.Y, "x": self.X, "core": 2, "zh": 2, "zl": self.L}
        self.names = ("y", "x", "core", "zh", "zl")

    def coords(self):
        for linear in range(self.seq * self.head):
            s, z = divmod(linear, self.head)
            yx, core = divmod(s, 2)
            y, x = divmod(yx, self.X)
            zh, zl = divmod(z, self.L)
            yield linear, {"y": y, "x": x, "core": core, "zh": zh, "zl": zl}

    def linear(self, c):
        s = (c["y"] * self.X + c["x"]) * 2 + c["core"]
        return s * self.head + c["zh"] * self.L + c["zl"]

    def permute(self, v, to):
        pairs = []
        for here, c in self.coords():
            there = to(c)
            if there is not None:
                pairs.append((here, self.linear(there)))
        return lax.ppermute(v, AXES, pairs)

    def shift(self, v, **steps):
        def to(c):
            return {k: (c[k] + steps.get(k, 0)) % self.sizes[k] for k in self.names}

        return self.permute(v, to)

    def place(self):
        s = lax.axis_index("seq")
        z = lax.axis_index("head")
        yx, core = s // 2, s % 2
        return {
            "y": yx // self.X,
            "x": yx % self.X,
            "core": core,
            "zh": z // self.L,
            "zl": z % self.L,
        }

    def tables(self):
        me = self.place()
        G, L, Y, X = self.G, self.L, self.Y, self.X

        def block(sign):
            return [
                ((me["core"] + sign * dc) % 2) * L + (me["zl"] + sign * dl) % L
                for dc in range(2)
                for dl in range(L)
            ]

        def chip(dy, dx):
            return ((me["y"] + dy) % Y) * X + (me["x"] + dx) % X

        chip_src = [chip(-dy, -dx) for dy in range(Y) for dx in range(X)]
        by_x = [chip(dy, dx) for dx in range(X) for dy in range(Y)]
        by_y = [chip(dy, dx) for dy in range(Y) for dx in range(X)]
        entries = [me["core"]] + block(1) + block(-1) + chip_src + by_x + by_y
        self.at_core = 0
        self.at_dst = 1
        self.at_src = 1 + G
        self.at_chip = 1 + 2 * G
        self.at_order = {"x": 1 + 2 * G + Y * X, "y": 1 + 2 * G + 2 * Y * X}
        return jnp.stack([jnp.asarray(e, jnp.int32) for e in entries])


def run(name, body, outs, smem, arrays, scratch=(), flops=0, trans=0, limit=48):
    nbytes = sum(a.size * a.dtype.itemsize for a in arrays)
    nbytes += sum(math.prod(o.shape) * jnp.dtype(o.dtype).itemsize for o in outs)
    return pl.pallas_call(
        body,
        out_shape=tuple(outs),
        in_specs=[SM] * len(smem) + [VM] * len(arrays),
        out_specs=tuple([VM] * len(outs)),
        scratch_shapes=list(scratch),
        compiler_params=pltpu.CompilerParams(vmem_limit_bytes=limit << 20),
        cost_estimate=pl.CostEstimate(
            flops=int(flops), bytes_accessed=int(nbytes), transcendentals=int(trans)
        ),
        name=name,
    )(*smem, *arrays)


def sds(shape, dtype):
    return jax.ShapeDtypeStruct(shape, dtype)


def prep_kernel(plan, idx, *refs):
    pieces = refs[: plan.chips]
    table_out, atab_out, gain_out, table_scr, gain_scr = refs[plan.chips :]
    VR, DR, QW = plan.VR, plan.DR, plan.QW
    for r in range(plan.chips):
        k = idx[plan.at_chip + r]
        for core in range(2):
            for half in range(2):
                rows = pieces[r][core * DR + half * VR : core * DR + (half + 1) * VR, QW : QW + 256]
                table_scr[
                    pl.ds(pl.multiple_of(k * 2 * VR, 2 * VR) + core * VR, VR),
                    half * 256 : half * 256 + 256,
                ] = rows.astype(F32)
        gain_scr[pl.ds(pl.multiple_of(k * 2 * DR, 2 * DR), 2 * DR), :] = pieces[r][
            :, QW + 256 : QW + 384
        ].astype(F32)
    gains = gain_scr[...].T[0:16, :]
    gain_out[...] = gains
    table = table_scr[...]
    table_out[...] = table.astype(BF)
    atab_out[...] = (table * root_of(table) * gains[0:1, :]).astype(BF)


def load_weight(plan, idx, pieces, lo, w_scr):
    width = 3 * plan.HW
    for r in range(plan.chips):
        k = idx[plan.at_chip + r]
        w_scr[pl.ds(pl.multiple_of(k * 2 * plan.DR, 2 * plan.DR), 2 * plan.DR), :] = pieces[r][
            :, lo : lo + width
        ]


def live_bias(lim, n, tile, j):
    per = tile // n
    row = lax.broadcasted_iota(jnp.int32, (tile, 1), 0)
    bias = jnp.full((tile, 1), MASKED, F32)
    for sub in range(per):
        inside = (row >= sub * n) & (row < sub * n + lim[j * per + sub])
        bias = jnp.where(inside, 0.0, bias)
    return bias


def head_pad(plan, part, h):
    if plan.hd == 1:
        return part
    blank = jnp.zeros_like(part)
    return jnp.concatenate([part if k == h else blank for k in range(plan.hd)], axis=0)


def rot_pair(a, b, cos, sin):
    return a * cos - b * sin, b * cos + a * sin


def attn_fwd_kernel(plan, n, lo, embed, masked, idx, lim, *refs):
    G, HW, hd = plan.G, plan.HW, plan.hd
    S = G * n
    refs = list(refs)
    cos_ref, sin_ref = refs[0], refs[1]
    refs = refs[2:]
    if embed:
        ints_ref, atab_ref = refs[0], refs[1]
        refs = refs[2:]
    else:
        a_refs = refs[:G]
        refs = refs[G:]
    w_refs = refs[: plan.chips]
    refs = refs[plan.chips :]
    c_outs = refs[:G]
    qkvt, ot, lse = refs[G : G + 3]
    w_scr, k_scr, c_scr = refs[G + 3 :]
    load_weight(plan, idx, w_refs, lo, w_scr)
    wt = w_scr[...].T
    if embed:
        base = split3(dot(wt, atab_ref[...], NT))
    for r in range(G):
        at = pl.ds(pl.multiple_of(idx[plan.at_src + r] * n, n), n)
        if embed:
            ids = ints_ref[8 * r : 8 * r + 1, :]
            hot = (lax.broadcasted_iota(jnp.int32, (VOCAB, n), 0) == ids).astype(F32).astype(BF)
            m = dot(base[0], hot) + (dot(base[1], hot) + dot(base[2], hot))
        else:
            m = dot(wt, a_refs[r][...], NT)
        cos, sin = cos_ref[:, at], sin_ref[:, at]
        for h in range(hd):
            for part, factor in ((0, SCALE), (1, 1.0)):
                top = part * HW + h * HEAD_DIM
                one, two = rot_pair(m[top : top + HALF], m[top + HALF : top + HEAD_DIM], cos, sin)
                qkvt[top : top + HALF, at] = (one * factor).astype(BF)
                qkvt[top + HALF : top + HEAD_DIM, at] = (two * factor).astype(BF)
        qkvt[2 * HW : 3 * HW, at] = m[2 * HW : 3 * HW].astype(BF)
        k_scr[at, :] = qkvt[HW : 2 * HW, at].T
    tile = min(512, S)

    def tile_scores(q_pads, keys, j, diagonal):
        out = []
        for h in range(hd):
            s = dot(keys, q_pads[h])
            if masked:
                s = s + live_bias(lim, n, tile, j)
            if diagonal:
                kk = lax.broadcasted_iota(jnp.int32, (tile, tile), 0)
                qq = lax.broadcasted_iota(jnp.int32, (tile, tile), 1)
                s = jnp.where(kk <= qq, s, MASKED)
            out.append(s)
        return out

    def one_query(i, _):
        cols = pl.ds(pl.multiple_of(i * tile, tile), tile)
        q_pads = [
            head_pad(plan, qkvt[h * HEAD_DIM : (h + 1) * HEAD_DIM, cols], h) for h in range(hd)
        ]

        def step(j, state, diagonal):
            rows = pl.ds(pl.multiple_of(j * tile, tile), tile)
            scores = tile_scores(q_pads, k_scr[rows, :], j, diagonal)
            new = []
            for h in range(hd):
                top, total, acc = state[3 * h : 3 * h + 3]
                s = scores[h]
                new_top = jnp.maximum(top, jnp.max(s, axis=0, keepdims=True))
                p = jnp.exp(s - new_top)
                keep = jnp.exp(top - new_top)
                total = total * keep + jnp.sum(p, axis=0, keepdims=True)
                vt = qkvt[2 * HW + h * HEAD_DIM : 2 * HW + (h + 1) * HEAD_DIM, rows]
                acc = acc * keep + dot(vt, p.astype(BF))
                new += [new_top, total, acc]
            return tuple(new)

        state = ()
        for h in range(hd):
            state += (
                jnp.full((1, tile), -1e30, F32),
                jnp.zeros((1, tile), F32),
                jnp.zeros((HEAD_DIM, tile), F32),
            )
        state = lax.fori_loop(0, i, lambda j, st: step(j, st, False), state)
        state = step(i, state, True)
        for h in range(hd):
            top, total, acc = state[3 * h : 3 * h + 3]
            ot[h * HEAD_DIM : (h + 1) * HEAD_DIM, cols] = acc / total
            lse[h : h + 1, cols] = top + jnp.log(total)
        c_scr[cols, :] = ot[:, cols].T.astype(BF)
        return 0

    lax.fori_loop(0, S // tile, one_query, 0)
    for r in range(G):
        c_outs[r][...] = c_scr[pl.ds(pl.multiple_of(idx[plan.at_dst + r] * n, n), n), :]


def attn_forward(plan, idx, lim, cos, sin, source, weights, lo, n, embed, masked):
    G, HW = plan.G, plan.HW
    S = G * n
    outs = [sds((n, HW), BF)] * G + [
        sds((3 * HW, S), BF),
        sds((HW, S), F32),
        sds((8, S), F32),
    ]
    res = run(
        "attention_forward",
        functools.partial(attn_fwd_kernel, plan, n, lo, embed, masked),
        outs,
        [idx, lim],
        [cos, sin, *source, *weights],
        [
            pltpu.VMEM((D, 3 * HW), BF),
            pltpu.VMEM((S, HW), BF),
            pltpu.VMEM((S, HW), BF),
        ],
        flops=2 * S * D * 3 * HW + 2 * plan.hd * S * S * 256,
        trans=plan.hd * S * S // 2,
    )
    return res[:G], res[G:]


def attn_bwd_kernel(plan, n, lo, embed, masked, idx, lim, *refs):
    G, HW, hd = plan.G, plan.HW, plan.hd
    S = G * n
    refs = list(refs)
    cos_ref, sin_ref = refs[0], refs[1]
    refs = refs[2:]
    if embed:
        ints_ref, atab_ref = refs[0], refs[1]
        refs = refs[2:]
    else:
        a_refs = refs[:G]
        refs = refs[G:]
    w_refs = refs[: plan.chips]
    refs = refs[plan.chips :]
    do_refs = refs[:G]
    qkvt, ot, lse = refs[G : G + 3]
    refs = refs[G + 3 :]
    dw_out = refs[0]
    refs = refs[1:]
    if embed:
        tab_out = refs[0]
        refs = refs[1:]
    else:
        da_outs = refs[:G]
        refs = refs[G:]
    w_scr, do_all, k_scr, v_scr, qz, qtz, doz, dotz, delta, dqt, dk, dv, dmt = refs
    load_weight(plan, idx, w_refs, lo, w_scr)
    wt = w_scr[...].T
    for r in range(G):
        at = pl.ds(pl.multiple_of(idx[plan.at_src + r] * n, n), n)
        do_all[at, :] = do_refs[r][...]
    tile = min(512, S)
    blocks = S // tile
    lane = lax.broadcasted_iota(jnp.int32, (tile, HW), 1) // HEAD_DIM
    for b in range(blocks):
        at = slice(b * tile, (b + 1) * tile)
        dob = do_all[at, :]
        dobt = dob.T
        kt = qkvt[HW : 2 * HW, at]
        k_scr[at, :] = kt.T
        v_scr[at, :] = qkvt[2 * HW : 3 * HW, at].T
        prod = dobt.astype(F32) * ot[:, at]
        dob32 = dob.astype(F32)
        for h in range(hd):
            rows = slice(h * HEAD_DIM, (h + 1) * HEAD_DIM)
            pad = head_pad(plan, qkvt[rows, at], h)
            qtz[h, :, at] = pad
            qz[h, at, :] = pad.T
            dotz[h, :, at] = head_pad(plan, dobt[rows, :], h)
            doz[h, at, :] = jnp.where(lane == h, dob32, 0.0).astype(BF)
            delta[h : h + 1, at] = jnp.sum(prod[rows, :], axis=0, keepdims=True)
    dqt[...] = jnp.zeros_like(dqt)

    def one_key(j, _):
        rows = pl.ds(pl.multiple_of(j * tile, tile), tile)
        keys, values = k_scr[rows, :], v_scr[rows, :]
        dk[...] = jnp.zeros_like(dk)
        dv[...] = jnp.zeros_like(dv)
        bias = live_bias(lim, n, tile, j) if masked else None

        def step(i, diagonal):
            cols = pl.ds(pl.multiple_of(i * tile, tile), tile)
            for h in range(hd):
                s = dot(keys, qtz[h, :, cols])
                if masked:
                    s = s + bias
                if diagonal:
                    kk = lax.broadcasted_iota(jnp.int32, (tile, tile), 0)
                    qq = lax.broadcasted_iota(jnp.int32, (tile, tile), 1)
                    s = jnp.where(kk <= qq, s, MASKED)
                p = jnp.exp(s - lse[h : h + 1, cols])
                dp = dot(values, dotz[h, :, cols])
                ds = (p * (dp - delta[h : h + 1, cols])).astype(BF)
                dv[...] += dot(p.astype(BF), doz[h, cols, :])
                dk[...] += dot(ds, qz[h, cols, :])
                kt = qkvt[HW + h * HEAD_DIM : HW + (h + 1) * HEAD_DIM, rows]
                dqt[h * HEAD_DIM : (h + 1) * HEAD_DIM, cols] += dot(kt, ds)

        step(j, True)

        def more(i, carry):
            step(i, False)
            return carry

        lax.fori_loop(j + 1, blocks, more, 0)
        dkt = dk[...].T
        cos, sin = cos_ref[:, rows], sin_ref[:, rows]
        for h in range(hd):
            top = h * HEAD_DIM
            one, two = rot_pair(
                dkt[top : top + HALF], dkt[top + HALF : top + HEAD_DIM], cos, -sin
            )
            dmt[HW + top : HW + top + HALF, rows] = one.astype(BF)
            dmt[HW + top + HALF : HW + top + HEAD_DIM, rows] = two.astype(BF)
        dmt[2 * HW : 3 * HW, rows] = dv[...].T.astype(BF)
        return 0

    lax.fori_loop(0, blocks, one_key, 0)
    cos, sin = cos_ref[:, 0:S], sin_ref[:, 0:S]
    for h in range(hd):
        top = h * HEAD_DIM
        one, two = rot_pair(
            dqt[top : top + HALF, :] * SCALE,
            dqt[top + HALF : top + HEAD_DIM, :] * SCALE,
            cos,
            -sin,
        )
        dmt[top : top + HALF, :] = one.astype(BF)
        dmt[top + HALF : top + HEAD_DIM, :] = two.astype(BF)
    grad = jnp.zeros((3 * HW, VOCAB if embed else D), F32)
    for r in range(G):
        at = pl.ds(pl.multiple_of(idx[plan.at_src + r] * n, n), n)
        if embed:
            ids = ints_ref[8 * r : 8 * r + 1, :]
            hot = (lax.broadcasted_iota(jnp.int32, (VOCAB, n), 0) == ids).astype(F32).astype(BF)
            grad += dot(dmt[:, at], hot, NT)
        else:
            grad += dot(dmt[:, at], a_refs[r][...])
    if embed:
        sums = grad
        high = sums.astype(BF)
        low = (sums - high.astype(F32)).astype(BF)
        grad = dot(high, atab_ref[...]) + dot(low, atab_ref[...])
        tab_out[...] = dot(high.T, wt) + dot(low.T, wt)
    else:
        for r in range(G):
            at = pl.ds(pl.multiple_of(idx[plan.at_dst + r] * n, n), n)
            da_outs[r][...] = dot(dmt[:, at].T, wt).astype(BF)
    w_scr[...] = grad.T.astype(BF)
    for r in range(plan.chips):
        k = idx[plan.at_order["x"] + r]
        dw_out[r] = w_scr[pl.ds(pl.multiple_of(k * 2 * plan.DR, 2 * plan.DR), 2 * plan.DR), :]


def attn_backward(plan, idx, lim, cos, sin, source, weights, lo, dos, saved, n, embed, masked):
    G, HW, hd = plan.G, plan.HW, plan.hd
    S = G * n
    tile = min(512, S)
    outs = [sds((plan.chips, 2 * plan.DR, 3 * HW), BF)]
    outs += [sds((VOCAB, D), F32)] if embed else [sds((n, D), BF)] * G
    res = run(
        "attention_backward",
        functools.partial(attn_bwd_kernel, plan, n, lo, embed, masked),
        outs,
        [idx, lim],
        [cos, sin, *source, *weights, *dos, *saved],
        [
            pltpu.VMEM((D, 3 * HW), BF),
            pltpu.VMEM((S, HW), BF),
            pltpu.VMEM((S, HW), BF),
            pltpu.VMEM((S, HW), BF),
            pltpu.VMEM((hd, S, HW), BF),
            pltpu.VMEM((hd, HW, S), BF),
            pltpu.VMEM((hd, S, HW), BF),
            pltpu.VMEM((hd, HW, S), BF),
            pltpu.VMEM((8, S), F32),
            pltpu.VMEM((HW, S), F32),
            pltpu.VMEM((tile, HW), F32),
            pltpu.VMEM((tile, HW), F32),
            pltpu.VMEM((3 * HW, S), BF),
        ],
        flops=4 * S * D * 3 * HW + 5 * hd * S * S * 256,
        trans=hd * S * S // 2,
    )
    return res[0], res[1:]


def up_chunk(plan, pack, j):
    rows = pl.ds(pl.multiple_of(j * plan.DR, plan.DR), plan.DR)
    return pack[:, rows, :].reshape(D, CHUNK)


def down_chunk(plan, pack, j):
    per = CHUNK // plan.FR
    top = 4 * plan.DR
    return pack[pl.ds(j * per, per), top : top + plan.FR, :].reshape(CHUNK, D)


def proj_rows(plan, pack):
    top = 4 * plan.DR + plan.FR
    return pack[:, top : top + plan.DR, :].reshape(D, D)


def ffn_fwd_kernel(plan, layer, idx, *refs):
    G, HW = plan.G, plan.HW
    c_refs = refs[:G]
    x_ref, pack, gains, y_out, x_out, proj_scr, acc, normed = refs[G:]
    proj_scr[...] = proj_rows(plan, pack)
    y = x_ref[...]
    for r in range(G):
        k = idx[plan.at_src + r]
        y += dot(c_refs[r][...], proj_scr[pl.ds(pl.multiple_of(k * HW, HW), HW), :])
    y_out[...] = y
    normed[...] = (y * root_of(y) * gains[2 * layer + 1 : 2 * layer + 2, :]).astype(BF)
    acc[...] = y

    def chunk(j, carry):
        h = dot(normed[...], up_chunk(plan, pack, j))
        acc[...] += dot(gelu_value(h).astype(BF), down_chunk(plan, pack, j))
        return carry

    lax.fori_loop(0, FF // CHUNK, chunk, 0)
    x_out[...] = acc[...]


def ffn_forward(plan, idx, layer, pieces, x, pack, gains):
    n = x.shape[0]
    return run(
        "ffn_forward",
        functools.partial(ffn_fwd_kernel, plan, layer),
        [sds((n, D), F32), sds((n, D), F32)],
        [idx],
        [*pieces, x, pack, gains],
        [pltpu.VMEM((D, D), BF), pltpu.VMEM((n, D), F32), pltpu.VMEM((n, D), BF)],
        flops=2 * n * D * (D + 2 * FF),
        trans=n * FF,
    )


def ffn_bwd_kernel(plan, layer, order, extra, idx, *refs):
    G, HW, C = plan.G, plan.HW, plan.chips
    c_refs = refs[:G]
    refs = refs[G:]
    gout, y_ref, pack, gains = refs[:4]
    refs = refs[4:]
    if extra:
        dp3, dtab = refs[:2]
        refs = refs[2:]
    gmid_out = refs[0]
    dc_outs = refs[1 : 1 + G]
    mine, theirs, dgain_out = refs[1 + G : 4 + G]
    proj_scr, unit, normed, normt, low, dn, dup, ddown, dproj = refs[4 + G :]
    proj_scr[...] = proj_rows(plan, pack)
    y = y_ref[...]
    root = root_of(y)
    gain = gains[2 * layer + 1 : 2 * layer + 2, :]
    unit[...] = y * root
    nrm = (y * root * gain).astype(BF)
    normed[...] = nrm
    normt[...] = nrm.T
    low[...] = gout[...].astype(BF)
    dn[...] = jnp.zeros_like(dn)

    def chunk(j, carry):
        up = up_chunk(plan, pack, j)
        h = dot(normed[...], up)
        value, slope = gelu_parts(h)
        ddown[pl.ds(pl.multiple_of(j * CHUNK, CHUNK), CHUNK), :] = dot(
            value.astype(BF).T, low[...]
        ).astype(BF)
        dact = dot(low[...], down_chunk(plan, pack, j), NT)
        dh = (dact * slope).astype(BF)
        dup[j] = dot(normt[...], dh).astype(BF)
        dn[...] += dot(dh, up, NT)
        return carry

    lax.fori_loop(0, FF // CHUNK, chunk, 0)
    dx, dgain = norm_back(unit[...], root, gain, dn[...])
    gmid = gout[...] + dx
    gmid_out[...] = gmid
    dgain_out[...] = jnp.broadcast_to(dgain, dgain_out.shape)
    low[...] = gmid.astype(BF)
    for r in range(G):
        k = idx[plan.at_src + r]
        at = pl.ds(pl.multiple_of(k * HW, HW), HW)
        dproj[at, :] = dot(c_refs[r][...].T, low[...]).astype(BF)
        k = idx[plan.at_dst + r]
        at = pl.ds(pl.multiple_of(k * HW, HW), HW)
        dc_outs[r][...] = dot(low[...], proj_scr[at, :], NT).astype(BF)
    DR, FR, VR = plan.DR, plan.FR, plan.VR
    core = idx[plan.at_core]
    for dc, out in ((0, mine), (1, theirs)):
        for r in range(C):
            s = idx[plan.at_order[order] + r] * 2 + lax.rem(core + dc, 2)
            at = pl.ds(pl.multiple_of(s * DR, DR), DR)
            for j in range(4):
                out[r, j * DR : (j + 1) * DR, :] = dup[j, at, :]
            top = 4 * DR
            out[r, top : top + FR, :] = ddown[pl.ds(pl.multiple_of(s * FR, FR), FR), :]
            top += FR
            out[r, top : top + DR, :] = dproj[at, :]
            if extra:
                top += DR
                out[r, top : top + DR, :] = dp3[at, :]
                top += DR
                out[r, top : top + VR, :] = dtab[
                    pl.ds(pl.multiple_of(s * VR, VR), VR), :
                ].astype(BF)


def ffn_backward(plan, idx, layer, order, pieces, gout, y, pack, gains, extra=()):
    n = y.shape[0]
    G, HW, C = plan.G, plan.HW, plan.chips
    rows = 5 * plan.DR + plan.FR
    if extra:
        rows += plan.DR + plan.VR
    res = run(
        "ffn_backward",
        functools.partial(ffn_bwd_kernel, plan, layer, order, bool(extra)),
        [sds((n, D), F32)]
        + [sds((n, HW), BF)] * G
        + [sds((C, rows, D), BF)] * 2
        + [sds((8, D), F32)],
        [idx],
        [*pieces, gout, y, pack, gains, *extra],
        [
            pltpu.VMEM((D, D), BF),
            pltpu.VMEM((n, D), F32),
            pltpu.VMEM((n, D), BF),
            pltpu.VMEM((D, n), BF),
            pltpu.VMEM((n, D), BF),
            pltpu.VMEM((n, D), F32),
            pltpu.VMEM((FF // CHUNK, D, CHUNK), BF),
            pltpu.VMEM((FF, D), BF),
            pltpu.VMEM((D, D), BF),
        ],
        flops=2 * n * D * (2 * D + 5 * FF),
        trans=n * FF,
    )
    return res[0], res[1 : 1 + G], res[1 + G], res[2 + G], res[3 + G]


VALID, TARGET, NEXT, SLOT, BYTE = range(5)


def square_of(cols, x):
    rows = jnp.sum(x * x, axis=-1, keepdims=True) * cols[:, VALID : VALID + 1]
    return jnp.sum(rows, axis=0, keepdims=True)


def pool_kernel(x_ref, cols, gains, pooled_out, a_out, stat):
    x = x_ref[...]
    member = one_hot(cols[:, SLOT : SLOT + 1], CAP)
    turned = member.T
    counts = jnp.sum(turned.astype(F32), axis=1, keepdims=True)
    pooled = exact_dot(turned, x) / jnp.maximum(counts, 1.0)
    pooled_out[...] = pooled
    a_out[...] = (pooled * root_of(pooled) * gains[2:3, :]).astype(BF)
    stat[...] = jnp.broadcast_to(square_of(cols, x), stat.shape)


def unpool_kernel(x_ref, mid_ref, cols, gains, x_out, a_out, stat):
    member = one_hot(cols[:, SLOT : SLOT + 1], CAP)
    x = x_ref[...] + exact_dot(member, mid_ref[...])
    x_out[...] = x
    a_out[...] = (x * root_of(x) * gains[4:5, :]).astype(BF)
    stat[...] = jnp.broadcast_to(square_of(cols, x), stat.shape)


def embed_kernel(cols, table, x_out):
    x_out[...] = dot(one_hot(cols[:, BYTE : BYTE + 1], VOCAB), table[...])


def loss_kernel(plan, x_ref, cols, pack, gains, grad_out, dtab_out, dgain_out, stat):
    top = 6 * plan.DR + plan.FR
    table = pack[:, top : top + plan.VR, :].reshape(VOCAB, D)
    x = x_ref[...]
    valid = cols[:, VALID : VALID + 1]
    root = root_of(x)
    unit = x * root
    gain = gains[6:7, :]
    rows = (unit * gain).astype(BF)
    logits = dot(rows, table, NT)
    top_row = jnp.max(logits, axis=-1, keepdims=True)
    total = jnp.sum(jnp.exp(logits - top_row), axis=-1, keepdims=True)
    log_norm = top_row + jnp.log(total)
    hot = one_hot(cols[:, NEXT : NEXT + 1], VOCAB).astype(F32)
    picked = jnp.sum(logits * hot, axis=-1, keepdims=True)
    ce = jnp.sum(valid * (log_norm - picked), axis=0, keepdims=True)
    glog = (valid * (jnp.exp(logits - log_norm) - hot)).astype(BF)
    dtab_out[...] = dot(glog.T, rows)
    dx, dgain = norm_back(unit, root, gain, dot(glog, table))
    grad_out[...] = dx
    dgain_out[...] = jnp.broadcast_to(dgain, dgain_out.shape)
    stat[0:8, :] = jnp.broadcast_to(ce, (8, 128))
    stat[8:16, :] = jnp.broadcast_to(square_of(cols, x), (8, 128))


def bound_kernel(plan, x_ref, cols, pack, gains, grad_out, dp_out, dgain_out, stat):
    top = 5 * plan.DR + plan.FR
    weight = pack[:, top : top + plan.DR, :].reshape(D, D)
    x = x_ref[...]
    valid = cols[:, VALID : VALID + 1]
    target = cols[:, TARGET : TARGET + 1]
    root = root_of(x)
    unit = x * root
    gain = gains[7:8, :]
    rows = (unit * gain).astype(BF)
    value, slope = gelu_parts(dot(rows, weight))
    out_gain = gains[8:9, :]
    z = jnp.sum(value * out_gain, axis=-1, keepdims=True) * D ** (-0.5)
    small = jnp.exp(-jnp.abs(z))
    soft = jnp.maximum(z, 0.0) + jnp.log(1.0 + small)
    bce = jnp.sum(valid * (soft - target * z), axis=0, keepdims=True)
    sig = jnp.where(z >= 0, 1.0, small) / (1.0 + small)
    dz = valid * (sig - target) * D ** (-0.5)
    dh = (dz * out_gain * slope).astype(BF)
    dp_out[...] = dot(rows.T, dh).astype(BF)
    dx, dgain = norm_back(unit, root, gain, dot(dh, weight, NT))
    grad_out[...] = dx
    dgain_out[0:8, :] = jnp.broadcast_to(dgain, (8, D))
    dgain_out[8:16, :] = jnp.broadcast_to(jnp.sum(dz * value, axis=0, keepdims=True), (8, D))
    stat[...] = jnp.broadcast_to(bce, stat.shape)


def joined(count, refs):
    total = refs[0][...].astype(F32)
    for ref in refs[1:count]:
        total += ref[...].astype(F32)
    return total


def join_last_kernel(count, *refs):
    gmid, x_ref, cols, gains, grad_out, pool_out, dgain_out = refs[count:]
    x = x_ref[...]
    root = root_of(x)
    dx, dgain = norm_back(x * root, root, gains[4:5, :], joined(count, refs))
    grad = gmid[...] + dx
    grad_out[...] = grad
    pool_out[...] = exact_dot(one_hot(cols[:, SLOT : SLOT + 1], CAP).T, grad)
    dgain_out[...] = jnp.broadcast_to(dgain, dgain_out.shape)


def join_middle_kernel(count, *refs):
    gmid, x_ref, cols, gains, second, bound, grad_out, dgain_out = refs[count:]
    x = x_ref[...]
    root = root_of(x)
    dx, dgain = norm_back(x * root, root, gains[2:3, :], joined(count, refs))
    member = one_hot(cols[:, SLOT : SLOT + 1], CAP)
    counts = jnp.sum(member.T.astype(F32), axis=1, keepdims=True)
    grad = (gmid[...] + dx) / jnp.maximum(counts, 1.0)
    grad_out[...] = second[...] + bound[...] + exact_dot(member, grad)
    dgain_out[...] = jnp.broadcast_to(dgain, dgain_out.shape)


def tail_kernel(plan, idx, gmid, dtab, table, cols, dw, gains, *refs):
    d1, d2, d3, d4, d5, d6, d78, pack_out, tab, gt, turned = refs
    t = table[...].astype(F32)
    root = root_of(t)
    dx, dgain = norm_back(t * root, root, gains[0:1, :], dtab[...])
    hot = one_hot(cols[:, BYTE : BYTE + 1], VOCAB).T
    g = gmid[...]
    high = g.astype(BF)
    tab[...] = dx + (dot(hot, high) + dot(hot, (g - high.astype(F32)).astype(BF)))
    gt[...] = jnp.zeros_like(gt)
    gt[0:1, :] = dgain
    for k, ref in ((1, d1), (2, d2), (3, d3), (4, d4), (5, d5), (6, d6), (7, d78)):
        gt[k : k + 1, :] = ref[0:1, :]
    gt[8:9, :] = d78[8:9, :]
    turned[...] = gt[...].T
    DR, VR, HW = plan.DR, plan.VR, plan.HW
    for r in range(plan.chips):
        k = idx[plan.at_order["x"] + r]
        if 3 * HW < D - 128:
            pack_out[r, 0 : 2 * DR, :] = jnp.zeros((2 * DR, D), BF)
        pack_out[r, 0 : 2 * DR, 0 : 3 * HW] = dw[r]
        rows = turned[pl.ds(pl.multiple_of(k * 2 * DR, 2 * DR), 2 * DR), :]
        pack_out[r, 0 : 2 * DR, D - 128 : D] = rows.astype(BF)
        rows = tab[pl.ds(pl.multiple_of(k * 2 * VR, 2 * VR), 2 * VR), :]
        pack_out[r, 2 * DR : 2 * DR + 2 * VR, :] = rows.astype(BF)


def adam_update(weight, first, second, grad, rate):
    mean = BETA_FIRST * first + (1.0 - BETA_FIRST) * grad
    meansq = BETA_SECOND * second + (1.0 - BETA_SECOND) * grad * grad
    mean_hat = mean / (1.0 - BETA_FIRST**STEP)
    meansq_hat = meansq / (1.0 - BETA_SECOND**STEP)
    master = weight - rate * (mean_hat / (jnp.sqrt(meansq_hat) + ADAM_EPS) + DECAY_RATE * weight)
    return (master, mean, meansq)


def add(a, b):
    return (a.astype(F32) + b.astype(F32)).astype(BF)


def sum_axis(plan, blocks, axis):
    total = blocks[0].astype(F32)
    for d in range(1, plan.sizes[axis]):
        total = total + plan.shift(blocks[d], **{axis: d}).astype(F32)
    return total.astype(BF)


def sum_head(plan, v):
    if plan.head != 4:
        return lax.psum(v, "head")
    z = lax.axis_index("head")

    def hop(v, pairs):
        def to(c):
            there = pairs.get(c["zh"] * 2 + c["zl"])
            return None if there is None else {**c, "zh": there // 2, "zl": there % 2}

        return plan.permute(v, to)

    part = add(v, hop(v, {0: 1, 3: 2}))
    total = add(part, hop(part, {1: 2, 2: 1}))
    back = hop(total, {1: 0, 2: 3})
    return jnp.where((z == 1) | (z == 2), total, back)


def reduce_pack(plan, mine, theirs, order):
    first, second = ("x", "y") if order == "x" else ("y", "x")
    s = add(mine, plan.shift(theirs, core=1))
    s = s.reshape((plan.sizes[first], plan.sizes[second]) + s.shape[1:])
    s = sum_axis(plan, s, first)
    s = sum_axis(plan, s, second)
    return sum_head(plan, s)


def reduce_heads(plan, t, qkv_rows, me):
    s = t.reshape((plan.X, plan.Y) + t.shape[1:])
    s = sum_axis(plan, s, "x")
    s = sum_axis(plan, s, "y")
    s = add(s, plan.shift(s, zh=1))
    core = me["core"]

    def halves(v):
        v = v.reshape((2, v.shape[0] // 2) + v.shape[1:])
        own = lax.dynamic_index_in_dim(v, core, 0, keepdims=False)
        other = lax.dynamic_index_in_dim(v, 1 - core, 0, keepdims=False)
        return own, other

    own_q, send_q = halves(s[:qkv_rows])
    extra = s.shape[0] > qkv_rows
    if extra:
        own_t, send_t = halves(s[qkv_rows:])
        got = plan.shift(jnp.concatenate([send_q, send_t]), core=1)
        got_q, got_t = got[: plan.DR], got[plan.DR :]
        tab = add(own_t, got_t)
        gain = add(own_q[:, D - 128 :], got_q[:, D - 128 :])
        own_q = jnp.concatenate([own_q[:, : D - 128], gain], axis=1)
        out = jnp.concatenate([own_q, got_q, tab])
    else:
        got_q = plan.shift(send_q, core=1)
        out = jnp.concatenate([own_q, got_q])
    parts = [out] + [plan.shift(out, zl=d) for d in range(1, plan.L)]
    rel = jnp.stack(
        [p[: plan.DR] for p in parts] + [p[plan.DR : 2 * plan.DR] for p in parts]
    )
    order = [
        ((core - c) % 2) * plan.L + (me["zl"] - l) % plan.L for c in range(2) for l in range(plan.L)
    ]
    blocks = jnp.stack([lax.dynamic_index_in_dim(rel, i, 0, keepdims=False) for i in order])
    if not extra:
        return blocks, None, None
    tab = sum(p[2 * plan.DR :].astype(F32) for p in parts)
    gain = sum(p[: plan.DR, D - 128 :].astype(F32) for p in parts)
    return blocks, tab, gain


def qkv_columns(plan, blocks):
    v = blocks.reshape(plan.G, plan.DR, 3, plan.HW)
    return jnp.transpose(v, (1, 2, 0, 3)).reshape(plan.DR, 3 * D)


def per_device(plan, *args):
    (
        byte_ids,
        next_bytes,
        loss_mask,
        pool_slots,
        qkv_weight,
        proj_weight,
        upward_weight,
        downward_weight,
        table_weight,
        gain_weight,
        qkv_first,
        qkv_second,
        proj_first,
        proj_second,
        upward_first,
        upward_second,
        downward_first,
        downward_second,
        table_first,
        table_second,
        gain_first,
        gain_second,
    ) = args
    G, L, HW, QW, DR, FR, VR = plan.G, plan.L, plan.HW, plan.QW, plan.DR, plan.FR, plan.VR
    n = byte_ids.shape[1]
    length = n * G
    me = plan.place()
    idx = plan.tables()
    core = me["core"]

    ints = jnp.concatenate([byte_ids, next_bytes, loss_mask, pool_slots], axis=0)
    ints = jnp.concatenate([ints, jnp.zeros_like(ints)], axis=0)
    pieces = []
    for dc in range(2):
        for dl in range(L):

            def to(c, dc=dc, dl=dl):
                return {
                    **c,
                    "core": (c["zh"] + dc) % 2,
                    "zh": c["core"],
                    "zl": (c["zl"] + dl) % L,
                }

            pieces.append(plan.permute(ints, to))
    own = pieces[0]
    ints_all = jnp.concatenate(pieces, axis=0)
    slots = own[3]
    previous = jnp.concatenate([slots[:1], slots[:-1]])
    opening = (jnp.arange(n) == 0) | (slots != previous)
    cols = jnp.stack(
        [
            own[2].astype(F32),
            opening.astype(F32),
            own[1].astype(F32),
            slots.astype(F32),
            own[0].astype(F32),
            jnp.zeros((n,), F32),
            jnp.zeros((n,), F32),
            jnp.zeros((n,), F32),
        ],
        axis=1,
    )
    at_src = idx[plan.at_src : plan.at_src + G]
    last = jnp.stack([p[3, -1] for p in pieces]) + 1
    lim = jnp.sum(
        jnp.where(at_src[:, None] == jnp.arange(G)[None, :], last[:, None], 0), axis=0
    ).astype(jnp.int32)

    qkv_low = qkv_weight.astype(BF).reshape(3, DR, 3, D)
    table_low = table_weight.astype(BF)
    gain_t = jnp.pad(gain_weight.astype(BF).T, ((0, 0), (0, 128 - gain_weight.shape[0])))
    table_part = jnp.concatenate([table_low[0][:, :256], table_low[0][:, 256:]], axis=0)

    def columns(which, at_core):
        at = (at_core * L + me["zl"]) * HW
        part = lax.dynamic_slice_in_dim(qkv_low[which], at, HW, axis=2).reshape(DR, 3 * HW)
        return jnp.pad(part, ((0, 0), (0, QW - 3 * HW)))

    def chip_rows(keep, send):
        got = plan.shift(send, core=1)
        return jnp.where(
            core == 0,
            jnp.concatenate([keep, got], axis=0),
            jnp.concatenate([got, keep], axis=0),
        )

    def gather_chips(v):
        by_x = [v] + [plan.shift(v, x=d) for d in range(1, plan.X)]
        out = list(by_x)
        for d in range(1, plan.Y):
            out += [plan.shift(p, y=d) for p in by_x]
        return out

    early = [
        jnp.concatenate([columns(0, k), table_part, gain_t], axis=1) for k in (core, 1 - core)
    ]
    early = gather_chips(chip_rows(*early))
    late = [jnp.concatenate([columns(1, k), columns(2, k)], axis=1) for k in (core, 1 - core)]
    late = gather_chips(chip_rows(*late))

    def pack_of(layer):
        up = upward_weight[layer].astype(BF)
        rows = [up[:, j * CHUNK : (j + 1) * CHUNK] for j in range(FF // CHUNK)]
        rows += [downward_weight[layer].astype(BF), proj_weight[layer].astype(BF)]
        if layer == 2:
            rows += [proj_weight[3].astype(BF), table_low[1]]
        return lax.all_gather(jnp.concatenate(rows, axis=0), "seq", axis=0, tiled=False)

    packs = [pack_of(layer) for layer in range(3)]

    table, atab, gains = run(
        "tables",
        functools.partial(prep_kernel, plan),
        [sds((VOCAB, D), BF), sds((VOCAB, D), BF), sds((16, D), F32)],
        [idx],
        early,
        [pltpu.VMEM((VOCAB, D), F32), pltpu.VMEM((D, 128), F32)],
    )
    half = np.arange(HALF, dtype=np.float32) / np.float32(HALF)
    frequency = np.float32(10000.0) ** (-half)
    angles = frequency[:, None] * np.arange(length, dtype=np.float32)[None, :]
    cos = jnp.asarray(np.cos(angles.astype(np.float64)).astype(np.float32))
    sin = jnp.asarray(np.sin(angles.astype(np.float64)).astype(np.float32))

    def exchange(parts):
        out = [parts[0]]
        for r in range(1, G):
            dc, dl = divmod(r, L)
            out.append(plan.shift(parts[r], core=dc, zl=dl))
        return out

    def gather_group(a):
        near = [a] + [plan.shift(a, zl=d) for d in range(1, L)]
        return near + [plan.shift(p, core=1) for p in near]

    def scatter_group(das):
        terms = [das[0], plan.shift(das[L], core=1)]
        for d in range(1, L):
            both = add(das[d], plan.shift(das[L + d], core=1))
            terms.append(plan.shift(both, zl=d))
        return terms

    (x0,) = run("embed", embed_kernel, [sds((n, D), F32)], [], [cols, table], flops=2 * n * VOCAB * D)
    source0 = [ints_all, atab]
    c0, saved0 = attn_forward(plan, idx, lim, cos, sin, source0, early, 0, n, True, False)
    c0 = exchange(c0)
    y0, x1 = ffn_forward(plan, idx, 0, c0, x0, packs[0], gains)
    pooled, a1, stat1 = run(
        "pool",
        pool_kernel,
        [sds((CAP, D), F32), sds((CAP, D), BF), sds((8, 128), F32)],
        [],
        [x1, cols, gains],
        flops=6 * n * CAP * D,
    )
    a1 = gather_group(a1)
    c1, saved1 = attn_forward(plan, idx, lim, cos, sin, a1, late, 0, CAP, False, True)
    c1 = exchange(c1)
    y1, mid = ffn_forward(plan, idx, 1, c1, pooled, packs[1], gains)
    x2, a2, stat2 = run(
        "unpool",
        unpool_kernel,
        [sds((n, D), F32), sds((n, D), BF), sds((8, 128), F32)],
        [],
        [x1, mid, cols, gains],
        flops=6 * n * CAP * D,
    )
    a2 = gather_group(a2)
    c2, saved2 = attn_forward(plan, idx, lim, cos, sin, a2, late, QW, n, False, False)
    c2 = exchange(c2)
    y2, x3 = ffn_forward(plan, idx, 2, c2, x2, packs[2], gains)
    bound_grad, dp3, dgain78, stat_b = run(
        "boundary",
        functools.partial(bound_kernel, plan),
        [sds((n, D), F32), sds((D, D), BF), sds((16, D), F32), sds((8, 128), F32)],
        [],
        [x1, cols, packs[2], gains],
        flops=6 * n * D * D,
        trans=n * D,
    )
    glast, dtab1, dgain6, stat3 = run(
        "loss",
        functools.partial(loss_kernel, plan),
        [sds((n, D), F32), sds((VOCAB, D), F32), sds((8, D), F32), sds((16, 128), F32)],
        [],
        [x3, cols, packs[2], gains],
        flops=6 * n * D * VOCAB,
        trans=2 * n * VOCAB,
    )
    locals_ = jnp.stack(
        [
            stat3[0, 0],
            stat_b[0, 0],
            stat1[0, 0],
            stat2[0, 0],
            stat3[8, 0],
            jnp.sum(own[2].astype(F32)),
        ]
    )
    totals = lax.psum(locals_, AXES)

    gmid2, dc2, mine2, theirs2, dgain5 = ffn_backward(
        plan, idx, 2, "x", c2, glast, y2, packs[2], gains, (dp3, dtab1)
    )
    dc2 = exchange(dc2)
    shard2 = reduce_pack(plan, mine2, theirs2, "x")
    dw2, das = attn_backward(
        plan, idx, lim, cos, sin, a2, late, QW, dc2, saved2, n, False, False
    )
    terms = scatter_group(das)
    gsecond, gpool_out, dgain4 = run(
        "join_last",
        functools.partial(join_last_kernel, len(terms)),
        [sds((n, D), F32), sds((CAP, D), F32), sds((8, D), F32)],
        [],
        [*terms, gmid2, x2, cols, gains],
        flops=6 * n * CAP * D,
    )
    gmid1, dc1, mine1, theirs1, dgain3 = ffn_backward(
        plan, idx, 1, "y", c1, gpool_out, y1, packs[1], gains
    )
    dc1 = exchange(dc1)
    shard1 = reduce_pack(plan, mine1, theirs1, "y")
    dw1, das = attn_backward(
        plan, idx, lim, cos, sin, a1, late, 0, dc1, saved1, CAP, False, True
    )
    terms = scatter_group(das)
    gfirst, dgain2 = run(
        "join_middle",
        functools.partial(join_middle_kernel, len(terms)),
        [sds((n, D), F32), sds((8, D), F32)],
        [],
        [*terms, gmid1, pooled, cols, gains, gsecond, bound_grad],
        flops=6 * n * CAP * D,
    )
    blocks21, _, _ = reduce_heads(plan, jnp.concatenate([dw1, dw2], axis=2), 2 * DR, me)
    gmid0, dc0, mine0, theirs0, dgain1 = ffn_backward(
        plan, idx, 0, "x", c0, gfirst, y0, packs[0], gains
    )
    dc0 = exchange(dc0)
    shard0 = reduce_pack(plan, mine0, theirs0, "x")
    dw0, (dtab0,) = attn_backward(
        plan, idx, lim, cos, sin, source0, early, 0, dc0, saved0, n, True, False
    )
    (tail,) = run(
        "tail",
        functools.partial(tail_kernel, plan),
        [sds((plan.chips, 2 * DR + 2 * VR, D), BF)],
        [idx],
        [gmid0, dtab0, table, cols, dw0, gains, dgain1, dgain2, dgain3, dgain4, dgain5, dgain6, dgain78],
        [pltpu.VMEM((VOCAB, D), F32), pltpu.VMEM((128, D), F32), pltpu.VMEM((D, 128), F32)],
        flops=4 * n * VOCAB * D,
    )
    blocks0, tab0, gain_t = reduce_heads(plan, tail, 2 * DR, me)

    shards = (shard0, shard1, shard2)
    top = 4 * DR
    grad_up = jnp.stack(
        [
            jnp.concatenate([s[j * DR : (j + 1) * DR] for j in range(4)], axis=1)
            for s in shards
        ]
    ).astype(F32)
    grad_down = jnp.stack([s[top : top + FR] for s in shards]).astype(F32)
    top += FR
    grad_proj = jnp.stack(
        [s[top : top + DR] for s in shards] + [shard2[top + DR : top + 2 * DR]]
    ).astype(F32)
    grad_table = jnp.stack([tab0, shard2[top + 2 * DR :].astype(F32)])
    grad_qkv = jnp.stack(
        [
            qkv_columns(plan, blocks0[:, :, : 3 * HW]),
            qkv_columns(plan, blocks21[:, :, : 3 * HW]),
            qkv_columns(plan, blocks21[:, :, 3 * HW :]),
        ]
    ).astype(F32)
    grad_gain = gain_t[:, : gain_weight.shape[0]].T
    grads = (grad_qkv, grad_proj, grad_up, grad_down, grad_table, grad_gain)

    valid_count = totals[5]
    inverse = 1.0 / valid_count
    local_square = sum((jnp.sum(grad * grad) for grad in grads))
    grad_norm = jnp.sqrt(lax.psum(local_square, "seq")) * inverse
    clip = jnp.minimum(1.0, CLIP_NORM / (grad_norm + 1e-06)) * inverse
    weights = (qkv_weight, proj_weight, upward_weight, downward_weight, table_weight, gain_weight)
    firsts = (qkv_first, proj_first, upward_first, downward_first, table_first, gain_first)
    seconds = (qkv_second, proj_second, upward_second, downward_second, table_second, gain_second)
    rates = (RATE_MATRIX,) * 4 + (RATE_VECTOR,) * 2
    new = [
        adam_update(w, a, b, g * clip, rate)
        for w, a, b, g, rate in zip(weights, firsts, seconds, grads, rates)
    ]
    residual_rms = jnp.sqrt(totals[2:5] / (valid_count * D))
    return (
        *[part for triple in new for part in triple],
        *[triple[0].astype(BF) for triple in new[:5]],
        totals[:2],
        valid_count,
        grad_norm,
        residual_rms,
    )


def solution(mesh):
    plan = Plan(mesh)
    tokens = P("seq", "head")
    matrix = P(None, "seq", None)
    vector = P(None, "seq")
    states = (matrix,) * 10 + (vector,) * 2
    return jax.shard_map(
        functools.partial(per_device, plan),
        mesh=mesh,
        in_specs=(tokens,) * 4 + (matrix,) * 5 + (vector,) + states,
        out_specs=(matrix,) * 15 + (vector,) * 3 + (matrix,) * 5 + (P(),) * 4,
        check_vma=False,
    )
```

```python
import functools
import math
from types import SimpleNamespace

import jax
import jax.numpy as jnp
import numpy as np
from jax import lax
from jax.experimental import pallas as pl
from jax.experimental.pallas import tpu as pltpu
from jax.sharding import PartitionSpec as P

D = 512
HEADS = 8
FF = 2048
VOCAB = 256
HEAD_DIM = 64
CAP = 256
STEP = 10
CHUNK = 512
HALF = HEAD_DIM // 2

NORM_EPS = 1e-06
BETA_FIRST = 0.9
BETA_SECOND = 0.95
ADAM_EPS = 1e-08
DECAY_RATE = 0.1
RATE_MATRIX = 0.05
RATE_VECTOR = 0.5
CLIP_NORM = 0.01
MASKED = -1000000000.0
SCALE = HEAD_DIM ** (-0.5)
GELU_A = math.sqrt(2.0 / math.pi)
GELU_B = 0.044715

BF = jnp.bfloat16
F32 = jnp.float32
NN = (((1,), (0,)), ((), ()))
NT = (((1,), (1,)), ((), ()))
AXES = ("seq", "head")
HB = pl.BlockSpec(memory_space=pltpu.HBM)
SM = pl.BlockSpec(memory_space=pltpu.SMEM)


def dot(a, b, dims=NN):
    return lax.dot_general(a, b, dims, preferred_element_type=F32)


def split3(v):
    high = v.astype(BF)
    rest = v - high.astype(F32)
    mid = rest.astype(BF)
    low = (rest - mid.astype(F32)).astype(BF)
    return (high, mid, low)


def exact_dot(ones, v):
    high, mid, low = split3(v)
    return dot(ones, high) + (dot(ones, mid) + dot(ones, low))


def root_of(v):
    return lax.rsqrt(jnp.mean(v * v, axis=-1, keepdims=True) + NORM_EPS)


def norm_back(unit, root, gain, grad):
    turned = grad * gain
    dx = root * (turned - unit * jnp.mean(turned * unit, axis=-1, keepdims=True))
    return dx, jnp.sum(grad * unit, axis=0, keepdims=True)


def gelu_parts(h):
    square = h * h
    t = jnp.tanh(GELU_A * h * (1.0 + GELU_B * square))
    half = 0.5 * (1.0 + t)
    value = h * half
    slope = half + 0.5 * h * (1.0 - t * t) * (GELU_A * (1.0 + 3.0 * GELU_B * square))
    return value, slope


def gelu_value(h):
    t = jnp.tanh(GELU_A * h * (1.0 + GELU_B * (h * h)))
    return h * (0.5 * (1.0 + t))


def one_hot(column, width):
    lanes = lax.broadcasted_iota(jnp.int32, (column.shape[0], width), 1).astype(F32)
    return (lanes == column).astype(F32).astype(BF)


class Plan:
    def __init__(self, mesh):
        self.seq = mesh.shape["seq"]
        self.head = mesh.shape["head"]
        self.chips = self.seq // 2
        side = int(math.isqrt(self.chips))
        while self.chips % side:
            side -= 1
        self.Y, self.X = side, self.chips // side
        self.L = self.head // 2
        self.G = self.head
        self.hd = HEADS // self.G
        self.HW = self.hd * HEAD_DIM
        self.QW = -(-3 * self.HW // 128) * 128
        self.DR = D // self.seq
        self.FR = FF // self.seq
        self.VR = VOCAB // self.seq
        self.sizes = {"y": self.Y, "x": self.X, "core": 2, "zh": 2, "zl": self.L}
        self.names = ("y", "x", "core", "zh", "zl")

    def coords(self):
        for linear in range(self.seq * self.head):
            s, z = divmod(linear, self.head)
            yx, core = divmod(s, 2)
            y, x = divmod(yx, self.X)
            zh, zl = divmod(z, self.L)
            yield linear, {"y": y, "x": x, "core": core, "zh": zh, "zl": zl}

    def linear(self, c):
        s = (c["y"] * self.X + c["x"]) * 2 + c["core"]
        return s * self.head + c["zh"] * self.L + c["zl"]

    def permute(self, v, to):
        pairs = []
        for here, c in self.coords():
            there = to(c)
            if there is not None:
                pairs.append((here, self.linear(there)))
        return lax.ppermute(v, AXES, pairs)

    def shift(self, v, **steps):
        def to(c):
            return {k: (c[k] + steps.get(k, 0)) % self.sizes[k] for k in self.names}

        return self.permute(v, to)

    def place(self):
        s = lax.axis_index("seq")
        z = lax.axis_index("head")
        yx, core = s // 2, s % 2
        return {
            "y": yx // self.X,
            "x": yx % self.X,
            "core": core,
            "zh": z // self.L,
            "zl": z % self.L,
        }

    def tables(self):
        me = self.place()
        G, L, Y, X = self.G, self.L, self.Y, self.X

        def block(sign):
            return [
                ((me["core"] + sign * dc) % 2) * L + (me["zl"] + sign * dl) % L
                for dc in range(2)
                for dl in range(L)
            ]

        def chip(dy, dx):
            return ((me["y"] + dy) % Y) * X + (me["x"] + dx) % X

        chip_src = [chip(-dy, -dx) for dy in range(Y) for dx in range(X)]
        by_x = [chip(dy, dx) for dx in range(X) for dy in range(Y)]
        by_y = [chip(dy, dx) for dy in range(Y) for dx in range(X)]
        entries = [me["core"], me["zl"]] + block(1) + block(-1) + chip_src + by_x + by_y
        self.at_core = 0
        self.at_zl = 1
        self.at_dst = 2
        self.at_src = 2 + G
        self.at_chip = 2 + 2 * G
        self.at_order = {"x": 2 + 2 * G + Y * X, "y": 2 + 2 * G + 2 * Y * X}
        return jnp.stack([jnp.asarray(e, jnp.int32) for e in entries])


def run(
    name,
    body,
    outs,
    smem,
    arrays,
    scratch=(),
    raw=(),
    raw_outs=(),
    sems=0,
    flops=0,
    trans=0,
    limit=60,
    after=(),
):
    operands = [*arrays, *raw]
    results = [*outs, *raw_outs]
    nbytes = sum(a.size * a.dtype.itemsize for a in operands)
    nbytes += sum(math.prod(o.shape) * jnp.dtype(o.dtype).itemsize for o in results)
    ns, ni, nr, na, no, nx = map(len, (smem, arrays, raw, after, outs, raw_outs))

    def wrapped(*refs):
        at = 0
        parts = []
        for count in (ns, ni, nr, na, no, nx, ni, no, len(scratch)):
            parts.append(refs[at : at + count])
            at += count
        s_refs, ins, raws, _, results_out, raws_out, bufs, out_bufs, own = parts
        sem = refs[at]
        copies = [
            pltpu.make_async_copy(src, dst, sem.at[k])
            for k, (src, dst) in enumerate(zip(ins, bufs))
        ]
        for copy in copies:
            copy.start()
        for copy in copies:
            copy.wait()
        extra = (refs[at + 1],) if sems else ()
        body(*s_refs, *bufs, *raws, *out_bufs, *raws_out, *own, *extra)
        copies = [
            pltpu.make_async_copy(src, dst, sem.at[k])
            for k, (src, dst) in enumerate(zip(out_bufs, results_out))
        ]
        for copy in copies:
            copy.start()
        for copy in copies:
            copy.wait()

    spaces = [pltpu.VMEM(v.shape, v.dtype) for v in (*arrays, *outs)]
    spaces += list(scratch) + [pltpu.SemaphoreType.DMA((max(ni, no, 1),))]
    if sems:
        spaces.append(pltpu.SemaphoreType.DMA((sems,)))
    return pl.pallas_call(
        wrapped,
        out_shape=tuple(results),
        in_specs=[SM] * ns + [HB] * (ni + nr) + [pl.BlockSpec(memory_space=pl.ANY)] * na,
        out_specs=tuple([HB] * len(results)),
        scratch_shapes=spaces,
        compiler_params=pltpu.CompilerParams(vmem_limit_bytes=limit << 20),
        cost_estimate=pl.CostEstimate(
            flops=int(flops), bytes_accessed=int(nbytes), transcendentals=int(trans)
        ),
        name=name,
    )(*smem, *operands, *after)


def run_named(name, body, outs, arrays, scratch, raw, raw_outs, idx, sems, flops, trans):
    def flat(group):
        out = []
        for value in group.values():
            out += list(value) if isinstance(value, (list, tuple)) else [value]
        return out

    def name_all(space, group, refs):
        for key, value in group.items():
            if isinstance(value, (list, tuple)):
                setattr(space, key, [refs.pop(0) for _ in value])
            else:
                setattr(space, key, refs.pop(0))

    def wrapped(idx_ref, *refs):
        space, refs = SimpleNamespace(idx=idx_ref), list(refs)
        for group in (arrays, raw, outs, raw_outs, scratch):
            name_all(space, group, refs)
        space.sem = refs.pop(0)
        body(space)

    res = list(
        run(
            name,
            wrapped,
            flat(outs),
            [idx],
            flat(arrays),
            flat(scratch),
            flat(raw),
            flat(raw_outs),
            sems,
            flops,
            trans,
        )
    )
    space = SimpleNamespace()
    for group in (outs, raw_outs):
        name_all(space, group, res)
    return space


def fence(*groups):
    return lax.optimization_barrier(groups)


class Copies:
    def __init__(self, sem):
        self.sem = sem
        self.count = 0
        self.open = []

    def start(self, src, dst):
        copy = pltpu.make_async_copy(src, dst, self.sem.at[self.count])
        self.count += 1
        copy.start()
        self.open.append(copy)
        return copy

    def finish(self):
        for copy in self.open:
            copy.wait()
        self.open = []


def rows_at(index, size):
    return pl.ds(pl.multiple_of(index * size, size), size)


def sds(shape, dtype):
    return jax.ShapeDtypeStruct(shape, dtype)


def first_kernel(plan, idx, qkv, table, gain, *refs):
    keep0, send0, keep1, send1, scr = refs
    DR, VR, HW, QW = plan.DR, plan.VR, plan.HW, plan.QW
    core, zl = idx[plan.at_core], idx[plan.at_zl]
    for which, outs in ((0, (keep0, keep1)), (1, (send0, send1))):
        block = lax.rem(core + which, 2) * plan.L + zl
        for layer in range(3):
            out, lo = ((outs[0], 0), (outs[1], 0), (outs[1], QW))[layer]
            for part in range(3):
                if HW % 128 == 0:
                    at = pl.ds(pl.multiple_of(part * D + block * HW, HW), HW)
                    piece = qkv[layer, :, at]
                else:
                    at = pl.ds(pl.multiple_of(part * D + block // 2 * 128, 128), 128)
                    both = qkv[layer, :, at]
                    piece = jnp.where(block % 2 == 0, both[:, :HW], both[:, HW:])
                out[:, lo + part * HW : lo + (part + 1) * HW] = piece.astype(BF)
    scr[...] = jnp.zeros_like(scr)
    scr[0 : gain.shape[0], 0:DR] = gain[...]
    turned = scr[...].T[0:DR, :].astype(BF)
    low = table[0].astype(BF)
    for out in (keep0, send0):
        out[:, QW : QW + 256] = jnp.concatenate([low[:, :256], low[:, 256:]], axis=0)
        out[:, QW + 256 : QW + 384] = turned


def pack_kernel(plan, layer, up, down, proj, table, out, up_scr, down_scr, proj_scr, tab_scr, sem):
    copies = Copies(sem)
    DR, FR, VR = plan.DR, plan.FR, plan.VR
    copies.start(up.at[layer], up_scr)
    copies.start(down.at[layer], down_scr)
    copies.start(proj.at[layer], proj_scr.at[0])
    if layer == 2:
        copies.start(proj.at[3], proj_scr.at[1])
        copies.start(table.at[1], tab_scr)
    copies.finish()
    for j in range(FF // CHUNK):
        out[j * DR : (j + 1) * DR, :] = up_scr[:, j * CHUNK : (j + 1) * CHUNK].astype(BF)
    top = 4 * DR
    out[top : top + FR, :] = down_scr[...].astype(BF)
    top += FR
    out[top : top + DR, :] = proj_scr[0].astype(BF)
    if layer == 2:
        top += DR
        out[top : top + DR, :] = proj_scr[1].astype(BF)
        top += DR
        out[top : top + VR, :] = tab_scr[...].astype(BF)


def pack_kernel(plan, layer, up, down, proj, table, out, up_scr, down_scr, proj_scr, tab_scr, sem):
    copies = Copies(sem)
    DR, FR, VR = plan.DR, plan.FR, plan.VR
    copies.start(up.at[layer], up_scr)
    copies.start(down.at[layer], down_scr)
    copies.start(proj.at[layer], proj_scr.at[0])
    if layer == 2:
        copies.start(proj.at[3], proj_scr.at[1])
        copies.start(table.at[1], tab_scr)
    copies.finish()
    for j in range(FF // CHUNK):
        out[j * DR : (j + 1) * DR, :] = up_scr[:, j * CHUNK : (j + 1) * CHUNK].astype(BF)
    top = 4 * DR
    out[top : top + FR, :] = down_scr[...].astype(BF)
    top += FR
    out[top : top + DR, :] = proj_scr[0].astype(BF)
    if layer == 2:
        top += DR
        out[top : top + DR, :] = proj_scr[1].astype(BF)
        top += DR
        out[top : top + VR, :] = tab_scr[...].astype(BF)


def chip_kernel(plan, idx, keep, got, ints, out, ints_out):
    DR = plan.DR
    core = idx[plan.at_core]
    out[pl.ds(pl.multiple_of(core * DR, DR), DR), :] = keep[...]
    out[pl.ds(pl.multiple_of((1 - core) * DR, DR), DR), :] = got[...]
    ints_out[...] = ints[...]


def gain_kernel(factor, gt, weight, first, second, master_out, mean_out, meansq_out):
    rows, width = weight.shape
    grad = gt[...].T[0:rows, 0:width] * factor[0]
    master, mean, meansq = adam_update(weight[...], first[...], second[...], grad, RATE_VECTOR)
    master_out[...] = master
    mean_out[...] = mean
    meansq_out[...] = meansq


def prep_kernel(plan, idx, ints, *refs):
    pieces = refs[: plan.chips]
    table_out, atab_out, gain_out, cols_out, table_scr, gain_scr, row_scr = refs[plan.chips :]
    slots = ints[3:4, :].astype(F32)
    n = slots.shape[1]
    lanes = lax.broadcasted_iota(jnp.int32, (1, n), 1)
    row_scr[...] = jnp.zeros_like(row_scr)
    row_scr[VALID : VALID + 1, :] = ints[2:3, :].astype(F32)
    changed = jnp.concatenate([slots[:, 0:1], slots[:, 0 : n - 1]], axis=1) != slots
    row_scr[TARGET : TARGET + 1, :] = jnp.where((lanes == 0) | changed, 1.0, 0.0)
    row_scr[NEXT : NEXT + 1, :] = ints[1:2, :].astype(F32)
    row_scr[SLOT : SLOT + 1, :] = slots
    row_scr[BYTE : BYTE + 1, :] = ints[0:1, :].astype(F32)
    cols_out[...] = row_scr[...].T
    VR, DR, QW = plan.VR, plan.DR, plan.QW
    for r in range(plan.chips):
        k = idx[plan.at_chip + r]
        for core in range(2):
            for half in range(2):
                rows = pieces[r][core * DR + half * VR : core * DR + (half + 1) * VR, QW : QW + 256]
                table_scr[
                    pl.ds(pl.multiple_of(k * 2 * VR, 2 * VR) + core * VR, VR),
                    half * 256 : half * 256 + 256,
                ] = rows.astype(F32)
        gain_scr[pl.ds(pl.multiple_of(k * 2 * DR, 2 * DR), 2 * DR), :] = pieces[r][
            :, QW + 256 : QW + 384
        ].astype(F32)
    gains = gain_scr[...].T[0:16, :]
    gain_out[...] = gains
    table = table_scr[...]
    table_out[...] = table.astype(BF)
    atab_out[...] = (table * root_of(table) * gains[0:1, :]).astype(BF)


def load_weight(plan, copies, idx, pieces, lo, w_scr):
    started = []
    for r in range(plan.chips):
        src = pieces[r].at[:, lo : lo + plan.QW]
        started.append(copies.start(src, w_scr.at[rows_at(idx[plan.at_chip + r], 2 * plan.DR), :]))
    return started


def live_bias(plan, idx, ints, n, bias_scr):
    row = lax.broadcasted_iota(jnp.int32, (n, 128), 0).astype(F32)
    for r in range(plan.G):
        slots = ints[8 * r + 3 : 8 * r + 4, :].astype(F32)
        last = jnp.max(slots, axis=1, keepdims=True)
        bias_scr[rows_at(idx[plan.at_src + r], n), :] = jnp.where(row <= last, 0.0, MASKED)


def head_pad(plan, part, h):
    if plan.hd == 1:
        return part
    blank = jnp.zeros_like(part)
    return jnp.concatenate([part if k == h else blank for k in range(plan.hd)], axis=0)


def rot_pair(a, b, cos, sin):
    return a * cos - b * sin, b * cos + a * sin


def attn_fwd_kernel(plan, n, lo, embed, masked, idx, *refs):
    G, HW, hd = plan.G, plan.HW, plan.hd
    S = G * n
    refs = list(refs)
    cos_ref, sin_ref = refs[0], refs[1]
    refs = refs[2:]
    if embed:
        ints_ref, atab_ref = refs[0], refs[1]
        refs = refs[2:]
    else:
        a_refs = refs[:G]
        refs = refs[G:]
    if masked:
        ints_ref = refs[0]
        refs = refs[1:]
    w_refs = refs[: plan.chips]
    refs = refs[plan.chips :]
    c_outs = refs[:G]
    qkvt_out, ot_out, lse_out = refs[G : G + 3]
    w_scr, cos_scr, sin_scr, src_scr, tab_scr, ints_scr, bias_scr = refs[G + 3 : G + 10]
    qkvt, ot, lse, k_scr, c_scr, sem = refs[G + 10 :]
    copies = Copies(sem)
    first = load_weight(plan, copies, idx, w_refs, lo, w_scr)
    first.append(copies.start(cos_ref.at[:, 0:S], cos_scr))
    first.append(copies.start(sin_ref.at[:, 0:S], sin_scr))
    sources = []
    if embed or masked:
        first.append(copies.start(ints_ref, ints_scr))
    if embed:
        first.append(copies.start(atab_ref, tab_scr))
    else:
        for r in range(G):
            dst = src_scr.at[rows_at(idx[plan.at_src + r], n), :]
            sources.append(copies.start(a_refs[r], dst))
    for copy in first:
        copy.wait()
    copies.open = []
    wt = w_scr[...].T[0 : 3 * HW, :]
    if embed:
        base = split3(dot(wt, tab_scr[...], NT))
    if masked:
        live_bias(plan, idx, ints_scr, n, bias_scr)
    for r in range(G):
        at = rows_at(idx[plan.at_src + r], n)
        if embed:
            ids = ints_scr[8 * r : 8 * r + 1, :]
            hot = (lax.broadcasted_iota(jnp.int32, (VOCAB, n), 0) == ids).astype(F32).astype(BF)
            m = dot(base[0], hot) + (dot(base[1], hot) + dot(base[2], hot))
        else:
            sources[r].wait()
            m = dot(wt, src_scr[at, :], NT)
        cos, sin = cos_scr[:, at], sin_scr[:, at]
        for h in range(hd):
            for part, factor in ((0, SCALE), (1, 1.0)):
                top = part * HW + h * HEAD_DIM
                one, two = rot_pair(m[top : top + HALF], m[top + HALF : top + HEAD_DIM], cos, sin)
                qkvt[top : top + HALF, at] = (one * factor).astype(BF)
                qkvt[top + HALF : top + HEAD_DIM, at] = (two * factor).astype(BF)
        qkvt[2 * HW : 3 * HW, at] = m[2 * HW : 3 * HW].astype(BF)
        k_scr[at, :] = qkvt[HW : 2 * HW, at].T
    copies.start(qkvt, qkvt_out)
    tile = min(512, S)

    def tile_scores(q_pads, keys, rows, diagonal):
        out = []
        for h in range(hd):
            s = dot(keys, q_pads[h])
            if masked:
                s = s + jnp.concatenate([bias_scr[rows, :]] * (tile // 128), axis=1)
            if diagonal:
                kk = lax.broadcasted_iota(jnp.int32, (tile, tile), 0)
                qq = lax.broadcasted_iota(jnp.int32, (tile, tile), 1)
                s = jnp.where(kk <= qq, s, MASKED)
            out.append(s)
        return out

    def one_query(i, _):
        cols = pl.ds(pl.multiple_of(i * tile, tile), tile)
        q_pads = [
            head_pad(plan, qkvt[h * HEAD_DIM : (h + 1) * HEAD_DIM, cols], h) for h in range(hd)
        ]

        def step(j, state, diagonal):
            rows = pl.ds(pl.multiple_of(j * tile, tile), tile)
            scores = tile_scores(q_pads, k_scr[rows, :], rows, diagonal)
            new = []
            for h in range(hd):
                top, total, acc = state[3 * h : 3 * h + 3]
                s = scores[h]
                new_top = jnp.maximum(top, jnp.max(s, axis=0, keepdims=True))
                p = jnp.exp(s - new_top)
                keep = jnp.exp(top - new_top)
                total = total * keep + jnp.sum(p, axis=0, keepdims=True)
                vt = qkvt[2 * HW + h * HEAD_DIM : 2 * HW + (h + 1) * HEAD_DIM, rows]
                acc = acc * keep + dot(vt, p.astype(BF))
                new += [new_top, total, acc]
            return tuple(new)

        state = ()
        for h in range(hd):
            state += (
                jnp.full((1, tile), -1e30, F32),
                jnp.zeros((1, tile), F32),
                jnp.zeros((HEAD_DIM, tile), F32),
            )
        state = lax.fori_loop(0, i, lambda j, st: step(j, st, False), state)
        state = step(i, state, True)
        for h in range(hd):
            top, total, acc = state[3 * h : 3 * h + 3]
            ot[h * HEAD_DIM : (h + 1) * HEAD_DIM, cols] = acc / total
            lse[h : h + 1, cols] = top + jnp.log(total)
        c_scr[cols, :] = ot[:, cols].T.astype(BF)
        return 0

    lax.fori_loop(0, S // tile, one_query, 0)
    for r in range(G):
        copies.start(c_scr.at[rows_at(idx[plan.at_dst + r], n), :], c_outs[r])
    copies.start(ot, ot_out)
    copies.start(lse, lse_out)
    copies.finish()


def source_scratch(embed, masked, S, G, source):
    none = pltpu.VMEM((16, 128), BF)
    return [
        none if embed else pltpu.VMEM((S, D), BF),
        pltpu.VMEM((VOCAB, D), BF) if embed else none,
        pltpu.VMEM(source[0 if embed else G].shape, jnp.int32) if embed or masked else none,
        pltpu.VMEM((S, 128), F32) if masked else none,
    ]


def attn_forward(plan, idx, cos, sin, source, weights, lo, n, embed, masked, after=()):
    G, HW = plan.G, plan.HW
    S = G * n
    outs = [sds((n, HW), BF)] * G + [
        sds((3 * HW, S), BF),
        sds((HW, S), F32),
        sds((8, S), F32),
    ]
    res = run(
        "attention_forward",
        functools.partial(attn_fwd_kernel, plan, n, lo, embed, masked),
        [],
        [idx],
        [],
        [
            pltpu.VMEM((D, plan.QW), BF),
            pltpu.VMEM((HALF, S), F32),
            pltpu.VMEM((HALF, S), F32),
            *source_scratch(embed, masked, S, G, source),
            pltpu.VMEM((3 * HW, S), BF),
            pltpu.VMEM((HW, S), F32),
            pltpu.VMEM((8, S), F32),
            pltpu.VMEM((S, HW), BF),
            pltpu.VMEM((S, HW), BF),
        ],
        raw=[cos, sin, *source, *weights],
        raw_outs=outs,
        sems=plan.chips + 2 * G + 8,
        flops=2 * S * D * 3 * HW + 2 * plan.hd * S * S * 256,
        trans=plan.hd * S * S // 2,
        after=after,
    )
    return res[:G], res[G:]


def attn_bwd_kernel(plan, n, lo, embed, masked, idx, *refs):
    G, HW, hd = plan.G, plan.HW, plan.hd
    S = G * n
    refs = list(refs)
    cos_ref, sin_ref = refs[0], refs[1]
    refs = refs[2:]
    if embed:
        ints_ref, atab_ref = refs[0], refs[1]
        refs = refs[2:]
    else:
        a_refs = refs[:G]
        refs = refs[G:]
    if masked:
        ints_ref = refs[0]
        refs = refs[1:]
    w_refs = refs[: plan.chips]
    refs = refs[plan.chips :]
    do_refs = refs[:G]
    qkvt_in, ot_in, lse_in = refs[G : G + 3]
    refs = refs[G + 3 :]
    dw_outs = refs[: plan.chips]
    refs = refs[plan.chips :]
    if embed:
        tab_out = refs[0]
        refs = refs[1:]
    else:
        da_outs = refs[:G]
        refs = refs[G:]
    w_scr, cos_scr, sin_scr, src_scr, tab_scr, ints_scr, bias_scr, qkvt, ot, lse = refs[:10]
    do_all, k_scr, v_scr, qz, qtz, doz, dotz, delta, dqt, dk, dv, dmt, res_scr, sem = refs[10:]
    copies = Copies(sem)
    if embed or masked:
        copies.start(ints_ref, ints_scr)
    copies.start(qkvt_in, qkvt)
    for r in range(G):
        copies.start(do_refs[r], do_all.at[rows_at(idx[plan.at_src + r], n), :])
    copies.start(ot_in, ot)
    copies.start(lse_in, lse)
    first, copies.open = copies.open, []
    copies.start(cos_ref.at[:, 0:S], cos_scr)
    copies.start(sin_ref.at[:, 0:S], sin_scr)
    angles, copies.open = copies.open, []
    load_weight(plan, copies, idx, w_refs, lo, w_scr)
    if embed:
        copies.start(atab_ref, tab_scr)
    else:
        for r in range(G):
            copies.start(a_refs[r], src_scr.at[rows_at(idx[plan.at_src + r], n), :])
    last, copies.open = copies.open, []
    for copy in first:
        copy.wait()
    tile = min(512, S)
    blocks = S // tile
    lane = lax.broadcasted_iota(jnp.int32, (tile, HW), 1) // HEAD_DIM
    for b in range(blocks):
        at = slice(b * tile, (b + 1) * tile)
        dob = do_all[at, :]
        dobt = dob.T
        kt = qkvt[HW : 2 * HW, at]
        k_scr[at, :] = kt.T
        v_scr[at, :] = qkvt[2 * HW : 3 * HW, at].T
        prod = dobt.astype(F32) * ot[:, at]
        dob32 = dob.astype(F32)
        for h in range(hd):
            rows = slice(h * HEAD_DIM, (h + 1) * HEAD_DIM)
            pad = head_pad(plan, qkvt[rows, at], h)
            qtz[h, :, at] = pad
            qz[h, at, :] = pad.T
            dotz[h, :, at] = head_pad(plan, dobt[rows, :], h)
            doz[h, at, :] = jnp.where(lane == h, dob32, 0.0).astype(BF)
            delta[h : h + 1, at] = jnp.sum(prod[rows, :], axis=0, keepdims=True)
    dqt[...] = jnp.zeros_like(dqt)
    if masked:
        live_bias(plan, idx, ints_scr, n, bias_scr)
    for copy in angles:
        copy.wait()

    def one_key(j, _):
        rows = pl.ds(pl.multiple_of(j * tile, tile), tile)
        keys, values = k_scr[rows, :], v_scr[rows, :]
        dk[...] = jnp.zeros_like(dk)
        dv[...] = jnp.zeros_like(dv)
        bias = jnp.concatenate([bias_scr[rows, :]] * (tile // 128), axis=1) if masked else None

        def step(i, diagonal):
            cols = pl.ds(pl.multiple_of(i * tile, tile), tile)
            for h in range(hd):
                s = dot(keys, qtz[h, :, cols])
                if masked:
                    s = s + bias
                if diagonal:
                    kk = lax.broadcasted_iota(jnp.int32, (tile, tile), 0)
                    qq = lax.broadcasted_iota(jnp.int32, (tile, tile), 1)
                    s = jnp.where(kk <= qq, s, MASKED)
                p = jnp.exp(s - lse[h : h + 1, cols])
                dp = dot(values, dotz[h, :, cols])
                ds = (p * (dp - delta[h : h + 1, cols])).astype(BF)
                dv[...] += dot(p.astype(BF), doz[h, cols, :])
                dk[...] += dot(ds, qz[h, cols, :])
                kt = qkvt[HW + h * HEAD_DIM : HW + (h + 1) * HEAD_DIM, rows]
                dqt[h * HEAD_DIM : (h + 1) * HEAD_DIM, cols] += dot(kt, ds)

        step(j, True)

        def more(i, carry):
            step(i, False)
            return carry

        lax.fori_loop(j + 1, blocks, more, 0)
        dkt = dk[...].T
        cos, sin = cos_scr[:, rows], sin_scr[:, rows]
        for h in range(hd):
            top = h * HEAD_DIM
            one, two = rot_pair(
                dkt[top : top + HALF], dkt[top + HALF : top + HEAD_DIM], cos, -sin
            )
            dmt[HW + top : HW + top + HALF, rows] = one.astype(BF)
            dmt[HW + top + HALF : HW + top + HEAD_DIM, rows] = two.astype(BF)
        dmt[2 * HW : 3 * HW, rows] = dv[...].T.astype(BF)
        return 0

    lax.fori_loop(0, blocks, one_key, 0)
    cos, sin = cos_scr[...], sin_scr[...]
    for h in range(hd):
        top = h * HEAD_DIM
        one, two = rot_pair(
            dqt[top : top + HALF, :] * SCALE,
            dqt[top + HALF : top + HEAD_DIM, :] * SCALE,
            cos,
            -sin,
        )
        dmt[top : top + HALF, :] = one.astype(BF)
        dmt[top + HALF : top + HEAD_DIM, :] = two.astype(BF)
    for copy in last:
        copy.wait()
    wt = w_scr[...].T[0 : 3 * HW, :]
    if embed:
        sums = jnp.zeros((3 * HW, VOCAB), F32)
        for r in range(G):
            at = rows_at(idx[plan.at_src + r], n)
            ids = ints_scr[8 * r : 8 * r + 1, :]
            hot = (lax.broadcasted_iota(jnp.int32, (VOCAB, n), 0) == ids).astype(F32).astype(BF)
            sums += dot(dmt[:, at], hot, NT)
        high = sums.astype(BF)
        low = (sums - high.astype(F32)).astype(BF)
        res_scr[...] = dot(high.T, wt) + dot(low.T, wt)
        copies.start(res_scr, tab_out)
        grad = dot(high, tab_scr[...]) + dot(low, tab_scr[...])
    else:
        for r in reversed(range(G)):
            at = rows_at(idx[plan.at_dst + r], n)
            res_scr[at, :] = dot(dmt[:, at].T, wt).astype(BF)
            copies.start(res_scr.at[at, :], da_outs[r])
        grad = dot(dmt[...], src_scr[...])
    w_scr[:, 0 : 3 * HW] = grad.T.astype(BF)
    for r in range(plan.chips):
        at = rows_at(idx[plan.at_order["x"] + r], 2 * plan.DR)
        copies.start(w_scr.at[at, :], dw_outs[r])
    copies.finish()


def attn_backward(
    plan, idx, cos, sin, source, weights, lo, dos, saved, n, embed, masked, after=()
):
    G, HW, hd = plan.G, plan.HW, plan.hd
    S = G * n
    tile = min(512, S)
    outs = [sds((2 * plan.DR, plan.QW), BF)] * plan.chips
    outs += [sds((VOCAB, D), F32)] if embed else [sds((n, D), BF)] * G
    res = run(
        "attention_backward",
        functools.partial(attn_bwd_kernel, plan, n, lo, embed, masked),
        [],
        [idx],
        [],
        [
            pltpu.VMEM((D, plan.QW), BF),
            pltpu.VMEM((HALF, S), F32),
            pltpu.VMEM((HALF, S), F32),
            *source_scratch(embed, masked, S, G, source),
            pltpu.VMEM((3 * HW, S), BF),
            pltpu.VMEM((HW, S), F32),
            pltpu.VMEM((8, S), F32),
            pltpu.VMEM((S, HW), BF),
            pltpu.VMEM((S, HW), BF),
            pltpu.VMEM((S, HW), BF),
            pltpu.VMEM((hd, S, HW), BF),
            pltpu.VMEM((hd, HW, S), BF),
            pltpu.VMEM((hd, S, HW), BF),
            pltpu.VMEM((hd, HW, S), BF),
            pltpu.VMEM((8, S), F32),
            pltpu.VMEM((HW, S), F32),
            pltpu.VMEM((tile, HW), F32),
            pltpu.VMEM((tile, HW), F32),
            pltpu.VMEM((3 * HW, S), BF),
            pltpu.VMEM((VOCAB, D), F32) if embed else pltpu.VMEM((S, D), BF),
        ],
        raw=[cos, sin, *source, *weights, *dos, *saved],
        raw_outs=outs,
        sems=2 * plan.chips + 3 * G + 8,
        flops=4 * S * D * 3 * HW + 5 * hd * S * S * 256,
        trans=hd * S * S // 2,
        after=after,
    )
    return res[: plan.chips], res[plan.chips :]


class Pack:
    def __init__(self, plan, copies, pack, scr):
        self.plan = plan
        self.up_scr, self.down_scr, self.proj_scr = scr
        DR, FR = plan.DR, plan.FR
        self.per = CHUNK // FR
        top = 4 * DR + FR
        self.proj_copy = copies.start(pack.at[:, top : top + DR, :], self.proj_scr)
        self.copies = []
        for j in range(FF // CHUNK):
            at = slice(j * self.per, (j + 1) * self.per)
            self.copies.append(
                (
                    copies.start(pack.at[:, j * DR : (j + 1) * DR, :], self.up_scr.at[j]),
                    copies.start(pack.at[at, 4 * DR : 4 * DR + FR, :], self.down_scr.at[j]),
                )
            )
        copies.open = []

    @staticmethod
    def scratch(plan):
        chunks = FF // CHUNK
        return [
            pltpu.VMEM((chunks, plan.seq, plan.DR, D), BF),
            pltpu.VMEM((chunks, CHUNK // plan.FR, plan.FR, D), BF),
            pltpu.VMEM((plan.seq, plan.DR, D), BF),
        ]

    def proj(self, k):
        per = self.plan.HW // self.plan.DR
        rows = self.proj_scr[pl.ds(k * per, per), :, :]
        return rows.reshape(self.plan.HW, D)

    def up(self, j):
        return self.up_scr[j].reshape(D, CHUNK)

    def down(self, j):
        return self.down_scr[j].reshape(CHUNK, D)


VALID, TARGET, NEXT, SLOT, BYTE = range(5)


def at_lane(lane, value):
    lanes = lax.broadcasted_iota(jnp.int32, (8, 128), 1)
    return jnp.where(lanes == lane, jnp.broadcast_to(value, (8, 128)), 0.0)


def square_of(cols, x):
    rows = jnp.sum(x * x, axis=-1, keepdims=True) * cols[:, VALID : VALID + 1]
    return jnp.sum(rows, axis=0, keepdims=True)


def attended(plan, k, x):
    k.pack.proj_copy.wait()
    y = x
    for r in range(plan.G):
        y += dot(k.c[r][...], k.pack.proj(k.idx[plan.at_src + r]))
    k.y[...] = y


def feed_forward(k, layer, y, keep=False):
    k.normed[...] = (y * root_of(y) * k.gains[2 * layer + 1 : 2 * layer + 2, :]).astype(BF)
    for j in range(FF // CHUNK):
        k.pack.copies[j][0].wait()
        h = dot(k.normed[...], k.pack.up(j))
        at = slice(j * CHUNK, (j + 1) * CHUNK)
        if keep:
            value, slope = gelu_parts(h)
            k.slope[j] = slope
        else:
            value = gelu_value(h)
        k.act[:, at] = value.astype(BF)
    for j in range(FF // CHUNK):
        k.pack.copies[j][1].wait()
    k.x_scr[...] = k.y[...] + dot(k.act[...], k.down_scr[...].reshape(FF, D))


def ffn_pool_kernel(plan, k):
    k.pack = Pack(plan, Copies(k.sem), k.pack_in, (k.up_scr, k.down_scr, k.proj_scr))
    x = dot(one_hot(k.cols[:, BYTE : BYTE + 1], VOCAB), k.table[...])
    attended(plan, k, x)
    feed_forward(k, 0, k.y[...])
    x = k.x_scr[...]
    k.x[...] = x
    turned = one_hot(k.cols[:, SLOT : SLOT + 1], CAP).T
    counts = jnp.sum(turned.astype(F32), axis=1, keepdims=True)
    pooled = exact_dot(turned, x) / jnp.maximum(counts, 1.0)
    k.pooled[...] = pooled
    k.a[...] = (pooled * root_of(pooled) * k.gains[2:3, :]).astype(BF)
    count = jnp.sum(k.cols[:, VALID : VALID + 1], axis=0, keepdims=True)
    k.stat[...] = at_lane(2, square_of(k.cols, x)) + at_lane(5, count)


def ffn_unpool_kernel(plan, k):
    k.pack = Pack(plan, Copies(k.sem), k.pack_in, (k.up_scr, k.down_scr, k.proj_scr))
    attended(plan, k, k.pooled[...])
    feed_forward(k, 1, k.y[...])
    x = k.x1[...] + exact_dot(one_hot(k.cols[:, SLOT : SLOT + 1], CAP), k.x_scr[...])
    k.x[...] = x
    k.a[...] = (x * root_of(x) * k.gains[4:5, :]).astype(BF)
    k.stat[...] = k.stat_in[...] + at_lane(3, square_of(k.cols, x))


def forward_scratch(plan, n):
    return {
        **dict(zip(("up_scr", "down_scr", "proj_scr"), Pack.scratch(plan))),
        "normed": pltpu.VMEM((n, D), BF),
        "act": pltpu.VMEM((n, FF), BF),
        "x_scr": pltpu.VMEM((n, D), F32),
    }


def loss_part(plan, k):
    k.tab_copy.wait()
    table = k.tab_scr[...].reshape(VOCAB, D)
    x = k.x_scr[...]
    valid = k.cols[:, VALID : VALID + 1]
    root = root_of(x)
    unit = x * root
    gain = k.gains[6:7, :]
    rows = (unit * gain).astype(BF)
    logits = dot(rows, table, NT)
    top_row = jnp.max(logits, axis=-1, keepdims=True)
    total = jnp.sum(jnp.exp(logits - top_row), axis=-1, keepdims=True)
    log_norm = top_row + jnp.log(total)
    hot = one_hot(k.cols[:, NEXT : NEXT + 1], VOCAB).astype(F32)
    picked = jnp.sum(logits * hot, axis=-1, keepdims=True)
    ce = jnp.sum(valid * (log_norm - picked), axis=0, keepdims=True)
    glog = (valid * (jnp.exp(logits - log_norm) - hot)).astype(BF)
    k.dtab[...] = dot(glog.T, rows).astype(BF)
    dx, dgain = norm_back(unit, root, gain, dot(glog, table))
    k.gout[...] = dx
    k.dgain6[...] = jnp.broadcast_to(dgain, k.dgain6.shape)
    k.stat[...] = (
        k.stat_a[...] + k.stat_b[...] + at_lane(0, ce) + at_lane(4, square_of(k.cols, x))
    )


def ffn_backward_part(plan, k, layer, y, kept=False):
    root = root_of(y)
    gain = k.gains[2 * layer + 1 : 2 * layer + 2, :]
    k.unit[...] = y * root
    if not kept:
        k.normed[...] = (y * root * gain).astype(BF)
    k.normt[...] = k.normed[...].T
    k.low[...] = k.gout[...].astype(BF)
    k.dn[...] = jnp.zeros_like(k.dn)
    for j in range(FF // CHUNK):
        if kept:
            value, slope = k.act[:, j * CHUNK : (j + 1) * CHUNK], k.slope[j]
            up = k.pack.up(j)
        else:
            for copy in k.pack.copies[j]:
                copy.wait()
            up = k.pack.up(j)
            value, slope = gelu_parts(dot(k.normed[...], up))
            value = value.astype(BF)
        k.ddown[j * CHUNK : (j + 1) * CHUNK, :] = dot(value.T, k.low[...]).astype(BF)
        dact = dot(k.low[...], k.pack.down(j), NT)
        dh = (dact * slope).astype(BF)
        k.dup[j] = dot(k.normt[...], dh).astype(BF)
        k.dn[...] += dot(dh, up, NT)
    dx, dgain = norm_back(k.unit[...], root, gain, k.dn[...])
    gmid = k.gout[...] + dx
    k.gmid[...] = gmid
    k.dgain[...] = jnp.broadcast_to(dgain, k.dgain.shape)
    k.low[...] = gmid.astype(BF)
    if not kept:
        k.pack.proj_copy.wait()
    HW = plan.HW
    for r in range(plan.G):
        at = rows_at(k.idx[plan.at_src + r], HW)
        k.dproj[at, :] = dot(k.c[r][...].T, k.low[...]).astype(BF)
        k.dc[r][...] = dot(k.low[...], k.pack.proj(k.idx[plan.at_dst + r]), NT).astype(BF)


def send_packs(plan, k, copies, extra=False):
    DR, FR, VR = plan.DR, plan.FR, plan.VR
    core = k.idx[plan.at_core]
    for dc in (1, 0):
        one, two = k.packs[2 * dc : 2 * dc + 2]
        for r in range(plan.chips):
            s = k.idx[plan.at_order["x"] + r] * 2 + lax.rem(core + dc, 2)
            for j in range(4):
                rows = slice(j * DR, (j + 1) * DR)
                copies.start(k.dup.at[j, rows_at(s, DR), :], one.at[r, rows, :])
            if extra:
                top = 4 * DR
                copies.start(k.dp3.at[rows_at(s, DR), :], one.at[r, top : top + DR, :])
                top += DR
                copies.start(k.dtab.at[rows_at(s, VR), :], one.at[r, top : top + VR, :])
            s = k.idx[plan.at_order["y"] + r] * 2 + lax.rem(core + dc, 2)
            copies.start(k.ddown.at[rows_at(s, FR), :], two.at[r, 0:FR, :])
            copies.start(k.dproj.at[rows_at(s, DR), :], two.at[r, FR : FR + DR, :])
    copies.finish()


def backward_scratch(plan, n):
    return {
        **forward_scratch(plan, n),
        "gout": pltpu.VMEM((n, D), F32),
        "unit": pltpu.VMEM((n, D), F32),
        "normt": pltpu.VMEM((D, n), BF),
        "low": pltpu.VMEM((n, D), BF),
        "dn": pltpu.VMEM((n, D), F32),
        "dup": pltpu.VMEM((FF // CHUNK, D, CHUNK), BF),
        "ddown": pltpu.VMEM((FF, D), BF),
        "dproj": pltpu.VMEM((D, D), BF),
    }


def backward_outs(plan, n, extra=False):
    C, DR, FR = plan.chips, plan.DR, plan.FR
    outs = {
        "gmid": sds((n, D), F32),
        "dc": [sds((n, plan.HW), BF)] * plan.G,
        "dgain": sds((8, D), F32),
    }
    rows = 4 * DR + (DR + plan.VR if extra else 0)
    return outs, {"packs": [sds((C, rows, D), BF), sds((C, FR + DR, D), BF)] * 2}


def ffn_loss_kernel(plan, k):
    copies = Copies(k.sem)
    k.pack = Pack(plan, copies, k.pack_in, (k.up_scr, k.down_scr, k.proj_scr))
    top = 6 * plan.DR + plan.FR
    k.tab_copy = copies.start(k.pack_in.at[:, top : top + plan.VR, :], k.tab_scr)
    copies.open = []
    attended(plan, k, k.x[...])
    feed_forward(k, 2, k.y[...], keep=True)
    loss_part(plan, k)
    ffn_backward_part(plan, k, 2, k.y[...], kept=True)
    send_packs(plan, k, copies, extra=True)


def joined(refs):
    total = refs[0][...].astype(F32)
    for ref in refs[1:]:
        total += ref[...].astype(F32)
    return total


def join_last_kernel(plan, k):
    copies = Copies(k.sem)
    k.pack = Pack(plan, copies, k.pack_in, (k.up_scr, k.down_scr, k.proj_scr))
    x = k.x[...]
    root = root_of(x)
    dx, dgain = norm_back(x * root, root, k.gains[4:5, :], joined(k.terms))
    grad = k.gnext[...] + dx
    k.second[...] = grad
    k.gout[...] = exact_dot(one_hot(k.cols[:, SLOT : SLOT + 1], CAP).T, grad)
    k.dgain_in[...] = jnp.broadcast_to(dgain, k.dgain_in.shape)
    ffn_backward_part(plan, k, 1, k.y[...])
    send_packs(plan, k, copies)


def join_middle_kernel(plan, k):
    copies = Copies(k.sem)
    k.pack = Pack(plan, copies, k.pack_in, (k.up_scr, k.down_scr, k.proj_scr))
    x = k.x[...]
    root = root_of(x)
    dx, dgain = norm_back(x * root, root, k.gains[2:3, :], joined(k.terms))
    member = one_hot(k.cols[:, SLOT : SLOT + 1], CAP)
    counts = jnp.sum(member.T.astype(F32), axis=1, keepdims=True)
    grad = (k.gnext[...] + dx) / jnp.maximum(counts, 1.0)
    k.gout[...] = k.second[...] + k.bound[...] + exact_dot(member, grad)
    k.dgain_in[...] = jnp.broadcast_to(dgain, k.dgain_in.shape)
    ffn_backward_part(plan, k, 0, k.y[...])
    send_packs(plan, k, copies)


def bound_kernel(plan, x_ref, cols, gains, pack, *refs):
    grad_out, dp_out, dgain_out, stat, weight_scr, sem = refs
    top = 5 * plan.DR + plan.FR
    copy = Copies(sem).start(pack.at[:, top : top + plan.DR, :], weight_scr)
    x = x_ref[...]
    valid = cols[:, VALID : VALID + 1]
    target = cols[:, TARGET : TARGET + 1]
    root = root_of(x)
    unit = x * root
    gain = gains[7:8, :]
    rows = (unit * gain).astype(BF)
    copy.wait()
    weight = weight_scr[...].reshape(D, D)
    value, slope = gelu_parts(dot(rows, weight))
    out_gain = gains[8:9, :]
    z = jnp.sum(value * out_gain, axis=-1, keepdims=True) * D ** (-0.5)
    small = jnp.exp(-jnp.abs(z))
    soft = jnp.maximum(z, 0.0) + jnp.log(1.0 + small)
    bce = jnp.sum(valid * (soft - target * z), axis=0, keepdims=True)
    sig = jnp.where(z >= 0, 1.0, small) / (1.0 + small)
    dz = valid * (sig - target) * D ** (-0.5)
    dh = (dz * out_gain * slope).astype(BF)
    dp_out[...] = dot(rows.T, dh).astype(BF)
    dx, dgain = norm_back(unit, root, gain, dot(dh, weight, NT))
    grad_out[...] = dx
    dgain_out[0:8, :] = jnp.broadcast_to(dgain, (8, D))
    dgain_out[8:16, :] = jnp.broadcast_to(jnp.sum(dz * value, axis=0, keepdims=True), (8, D))
    stat[...] = at_lane(1, bce)


def tail_kernel(plan, idx, gmid, dtab, table, cols, gains, *refs):
    d1, d2, d3, d4, d5, d6, d78 = refs[:7]
    dw = refs[7 : 7 + plan.chips]
    packs = refs[7 + plan.chips : 7 + 2 * plan.chips]
    tab, gt, turned = refs[7 + 2 * plan.chips :]
    t = table[...].astype(F32)
    root = root_of(t)
    dx, dgain = norm_back(t * root, root, gains[0:1, :], dtab[...])
    hot = one_hot(cols[:, BYTE : BYTE + 1], VOCAB).T
    g = gmid[...]
    high = g.astype(BF)
    tab[...] = dx + (dot(hot, high) + dot(hot, (g - high.astype(F32)).astype(BF)))
    gt[...] = jnp.zeros_like(gt)
    gt[0:1, :] = dgain
    for k, ref in ((1, d1), (2, d2), (3, d3), (4, d4), (5, d5), (6, d6), (7, d78)):
        gt[k : k + 1, :] = ref[0:1, :]
    gt[8:9, :] = d78[8:9, :]
    turned[...] = gt[...].T
    DR, VR, HW = plan.DR, plan.VR, plan.HW
    for r in range(plan.chips):
        k = idx[plan.at_order["x"] + r]
        if 3 * HW < D - 128:
            packs[r][0 : 2 * DR, :] = jnp.zeros((2 * DR, D), BF)
        packs[r][0 : 2 * DR, 0 : 3 * HW] = dw[r][:, 0 : 3 * HW]
        rows = turned[pl.ds(pl.multiple_of(k * 2 * DR, 2 * DR), 2 * DR), :]
        packs[r][0 : 2 * DR, D - 128 : D] = rows.astype(BF)
        rows = tab[pl.ds(pl.multiple_of(k * 2 * VR, 2 * VR), 2 * VR), :]
        packs[r][2 * DR : 2 * DR + 2 * VR, :] = rows.astype(BF)


def adam_update(weight, first, second, grad, rate):
    mean = BETA_FIRST * first + (1.0 - BETA_FIRST) * grad
    meansq = BETA_SECOND * second + (1.0 - BETA_SECOND) * grad * grad
    mean_hat = mean / (1.0 - BETA_FIRST**STEP)
    meansq_hat = meansq / (1.0 - BETA_SECOND**STEP)
    master = weight - rate * (mean_hat / (jnp.sqrt(meansq_hat) + ADAM_EPS) + DECAY_RATE * weight)
    return (master, mean, meansq)


def add(a, b):
    return (a.astype(F32) + b.astype(F32)).astype(BF)


def total_of(terms):
    total = terms[0].astype(F32)
    for term in terms[1:]:
        total = total + term.astype(F32)
    return total.astype(BF)


def sum_first(plan, blocks, axis):
    got = [plan.shift(blocks[d], **{axis: d}) for d in range(1, plan.sizes[axis])]
    return [total_of([b[e] for b in (blocks[0], *got)]) for e in range(blocks[0].shape[0])]


def sum_second(plan, blocks, axis):
    return total_of(
        [blocks[0]] + [plan.shift(blocks[d], **{axis: d}) for d in range(1, plan.sizes[axis])]
    )


def sum_chips(plan, blocks):
    terms = [blocks[0]]
    for r in range(1, plan.chips):
        dx, dy = divmod(r, plan.Y)
        terms.append(plan.shift(blocks[r], x=dx, y=dy))
    return total_of(terms)


def hop(plan, v, pairs):
    def to(c):
        there = pairs.get(c["zh"] * plan.L + c["zl"])
        return None if there is None else {**c, "zh": there // plan.L, "zl": there % plan.L}

    return plan.permute(v, to)


def head_in(plan, v):
    return add(v, hop(plan, v, {0: 1, 3: 2}))


def head_across(plan, v):
    return add(v, hop(plan, v, {1: 2, 2: 1}))


def head_out(plan, v):
    z = lax.axis_index("head")
    return jnp.where((z == 1) | (z == 2), v, hop(plan, v, {1: 0, 2: 3}))


def split_axes(plan, t, first, second):
    return t.reshape((plan.sizes[first], plan.sizes[second]) + t.shape[1:])


def exchange_blocks(plan, v, me):
    core = me["core"]
    own = lax.dynamic_index_in_dim(v, core, 0, keepdims=False)
    other = lax.dynamic_index_in_dim(v, 1 - core, 0, keepdims=False)
    parts = [own] + [plan.shift(own, zl=d) for d in range(1, plan.L)]
    parts += [plan.shift(other, core=1, zl=d) for d in range(plan.L)]
    rel = jnp.stack(parts)
    order = [
        ((core - c) % 2) * plan.L + (me["zl"] - l) % plan.L for c in range(2) for l in range(plan.L)
    ]
    return jnp.stack([lax.dynamic_index_in_dim(rel, i, 0, keepdims=False) for i in order])


def qkv_columns(plan, blocks):
    v = blocks.reshape(plan.G, plan.DR, 3, plan.HW)
    return jnp.transpose(v, (1, 2, 0, 3)).reshape(plan.DR, 3 * D)


def per_device(plan, *args):
    (
        byte_ids,
        next_bytes,
        loss_mask,
        pool_slots,
        qkv_weight,
        proj_weight,
        upward_weight,
        downward_weight,
        table_weight,
        gain_weight,
        qkv_first,
        qkv_second,
        proj_first,
        proj_second,
        upward_first,
        upward_second,
        downward_first,
        downward_second,
        table_first,
        table_second,
        gain_first,
        gain_second,
    ) = args
    G, L, HW, QW, DR, FR, VR = plan.G, plan.L, plan.HW, plan.QW, plan.DR, plan.FR, plan.VR
    n = byte_ids.shape[1]
    length = n * G
    me = plan.place()
    idx = plan.tables()
    core = me["core"]

    width0, width1 = QW + 384, 2 * QW
    keep0, send0, keep1, send1 = run(
        "first",
        functools.partial(first_kernel, plan),
        [sds((DR, width0), BF)] * 2 + [sds((DR, width1), BF)] * 2,
        [idx],
        [qkv_weight, table_weight, gain_weight],
        [pltpu.VMEM((128, 128), F32)],
    )
    ints = jnp.concatenate([byte_ids, next_bytes, loss_mask, pool_slots], axis=0)
    ints = jnp.concatenate([ints, jnp.zeros_like(ints)], axis=0)

    def chip_rows(keep, got):
        return jnp.where(
            core == 0,
            jnp.concatenate([keep, got], axis=0),
            jnp.concatenate([got, keep], axis=0),
        )

    def gather_first(v):
        by_x = [plan.shift(v, x=d) for d in range(1, plan.X)]
        by_y = [plan.shift(v, y=d) for d in range(1, plan.Y)]
        return by_x, by_y

    def gather_second(v, by_x, by_y):
        out = [v, *by_x]
        for d in range(1, plan.Y):
            out += [by_y[d - 1], *[plan.shift(p, y=d) for p in by_x]]
        return out

    def swap(c):
        return {**c, "core": c["zh"], "zh": c["core"]}

    got0, got1, own = fence(
        plan.shift(send0, core=1), plan.shift(send1, core=1), plan.permute(ints, swap)
    )
    chip0 = chip_rows(keep0, got0)
    chip1 = chip_rows(keep1, got1)
    (by_x, by_y), both, chip1 = fence(
        gather_first(chip0), jnp.concatenate([own, plan.shift(own, core=1)]), chip1
    )
    early = gather_second(chip0, by_x, by_y)
    pairs = [both] + [plan.shift(both, zl=d) for d in range(1, L)]
    ints_all = jnp.concatenate([p[:8] for p in pairs] + [p[8:] for p in pairs])

    def pack_of(layer):
        rows = 5 * DR + FR + (DR + VR if layer == 2 else 0)
        (pack,) = run(
            "pack",
            functools.partial(pack_kernel, plan, layer),
            [sds((rows, D), BF)],
            [],
            [],
            [
                pltpu.VMEM((DR, FF), F32),
                pltpu.VMEM((FR, D), F32),
                pltpu.VMEM((2, DR, D), F32),
                pltpu.VMEM((VR, D), F32),
            ],
            raw=[upward_weight, downward_weight, proj_weight, table_weight],
            sems=5,
            after=([keep0], [got0], [both])[layer],
        )
        return pack

    def gather_pack(pack):
        return lax.all_gather(pack, "seq", axis=0, tiled=False)

    shards = [pack_of(layer) for layer in range(3)]
    packs = [gather_pack(shards[0]), gather_pack(shards[1]), None]

    table, atab, gains, cols = run(
        "tables",
        functools.partial(prep_kernel, plan),
        [sds((VOCAB, D), BF), sds((VOCAB, D), BF), sds((16, D), F32), sds((n, 128), F32)],
        [idx],
        [own, *early],
        [pltpu.VMEM((VOCAB, D), F32), pltpu.VMEM((D, 128), F32), pltpu.VMEM((128, n), F32)],
    )
    half = np.arange(HALF, dtype=np.float32) / np.float32(HALF)
    frequency = np.float32(10000.0) ** (-half)
    angles = frequency[:, None] * np.arange(length, dtype=np.float32)[None, :]
    cos = jnp.asarray(np.cos(angles.astype(np.float64)).astype(np.float32))
    sin = jnp.asarray(np.sin(angles.astype(np.float64)).astype(np.float32))

    def exchange(parts):
        out = [parts[0]]
        for r in range(1, G):
            dc, dl = divmod(r, L)
            out.append(plan.shift(parts[r], core=dc, zl=dl))
        return out

    def gather_group(a):
        near = [a] + [plan.shift(a, zl=d) for d in range(1, L)]
        return near + [plan.shift(p, core=1) for p in near]

    def scatter_group(das):
        terms = [das[0], plan.shift(das[L], core=1)]
        for d in range(1, L):
            both = add(das[d], plan.shift(das[L + d], core=1))
            terms.append(plan.shift(both, zl=d))
        return terms

    early, table, atab, gains, cols, ints_all, chip1 = fence(
        early, table, atab, gains, cols, ints_all, chip1
    )
    late = gather_first(chip1)
    c0, saved0 = attn_forward(plan, idx, cos, sin, [ints_all, atab], early, 0, n, True, False)
    c0, saved0, late = fence(c0, saved0, late)
    c0, late = fence(exchange(c0), gather_second(chip1, *late))
    dense = 2 * D * (D + 2 * FF)
    res = run_named(
        "ffn_pool",
        functools.partial(ffn_pool_kernel, plan),
        {
            "y": sds((n, D), F32),
            "x": sds((n, D), F32),
            "pooled": sds((CAP, D), F32),
            "a": sds((CAP, D), BF),
            "stat": sds((8, 128), F32),
        },
        {"c": c0, "cols": cols, "table": table, "gains": gains},
        forward_scratch(plan, n),
        {"pack_in": packs[0]},
        {},
        idx,
        16,
        n * dense,
        n * FF,
    )
    y0, x1, pooled, a1, stat = res.y, res.x, res.pooled, res.a, res.stat
    a1 = gather_group(a1)
    c1, saved1 = attn_forward(plan, idx, cos, sin, [*a1, ints_all], late, 0, CAP, False, True)
    c1, saved1, last_shard = fence(c1, saved1, shards[2])
    packs[2] = gather_pack(last_shard)
    c1 = exchange(c1)
    res = run_named(
        "ffn_unpool",
        functools.partial(ffn_unpool_kernel, plan),
        {
            "y": sds((CAP, D), F32),
            "x": sds((n, D), F32),
            "a": sds((n, D), BF),
            "stat": sds((8, 128), F32),
        },
        {"c": c1, "pooled": pooled, "x1": x1, "cols": cols, "gains": gains, "stat_in": stat},
        forward_scratch(plan, CAP),
        {"pack_in": packs[1]},
        {},
        idx,
        16,
        CAP * dense,
        CAP * FF,
    )
    y1, x2, a2, stat = res.y, res.x, res.a, res.stat
    a2 = gather_group(a2)
    c2, saved2 = attn_forward(plan, idx, cos, sin, a2, late, QW, n, False, False)
    c2 = exchange(c2)
    bound_grad, dp3, dgain78, stat_b = run(
        "boundary",
        functools.partial(bound_kernel, plan),
        [sds((n, D), F32), sds((D, D), BF), sds((16, D), F32), sds((8, 128), F32)],
        [],
        [x1, cols, gains],
        [pltpu.VMEM((plan.seq, DR, D), BF)],
        raw=[packs[2]],
        sems=1,
        flops=6 * n * D * D,
        trans=n * D,
    )
    source0 = [ints_all, atab]
    line = plan.head == 4
    axes = (("x", "y"), ("y", "x"))

    def core_sums(packs):
        out = []
        for mine, theirs, ax in zip(packs[:2], packs[2:], axes):
            got = split_axes(plan, plan.shift(theirs, core=1), *ax)
            mine = split_axes(plan, mine, *ax)
            out.append([add(mine[d], got[d]) for d in range(mine.shape[0])])
        return out

    def first_sums(halves):
        return [sum_first(plan, half, ax[0]) for half, ax in zip(halves, axes)]

    def second_sums(halves):
        return [sum_second(plan, half, ax[1]) for half, ax in zip(halves, axes)]

    outs, raw_outs = backward_outs(plan, n, extra=True)
    res = run_named(
        "ffn_loss",
        functools.partial(ffn_loss_kernel, plan),
        {**outs, "dgain6": sds((8, D), F32), "stat": sds((8, 128), F32)},
        {
            "c": c2,
            "x": x2,
            "cols": cols,
            "gains": gains,
            "stat_a": stat,
            "stat_b": stat_b,
            "dp3": dp3,
        },
        {
            **backward_scratch(plan, n),
            "slope": pltpu.VMEM((FF // CHUNK, n, CHUNK), F32),
            "y": pltpu.VMEM((n, D), F32),
            "tab_scr": pltpu.VMEM((plan.seq, VR, D), BF),
            "dtab": pltpu.VMEM((VOCAB, D), BF),
        },
        {"pack_in": packs[2]},
        raw_outs,
        idx,
        20 + 8 * plan.seq,
        2 * n * D * (3 * D + 6 * FF),
        n * FF,
    )
    gmid2, dc2, packs2, dgain5, dgain6 = res.gmid, res.dc, res.packs, res.dgain, res.dgain6
    stat = res.stat
    dc2, half2, stat = fence(exchange(dc2), core_sums(packs2), stat)
    dw2, das = attn_backward(
        plan, idx, cos, sin, a2, late, QW, dc2, saved2, n, False, False
    )
    dw2, das, half2, stat = fence(dw2, das, first_sums(half2), stat + plan.shift(stat, zh=1))
    terms, shard2, stat = fence(
        scatter_group(das), jnp.concatenate(second_sums(half2), axis=0), stat
    )
    outs, raw_outs = backward_outs(plan, CAP)
    res = run_named(
        "join_last",
        functools.partial(join_last_kernel, plan),
        {**outs, "second": sds((n, D), F32), "dgain_in": sds((8, D), F32)},
        {
            "terms": terms,
            "gnext": gmid2,
            "x": x2,
            "cols": cols,
            "gains": gains,
            "y": y1,
            "c": c1,
        },
        backward_scratch(plan, CAP),
        {"pack_in": packs[1]},
        raw_outs,
        idx,
        16 + 8 * plan.seq,
        2 * CAP * D * (2 * D + 5 * FF),
        CAP * FF,
    )
    gmid1, dc1, packs1, dgain3, dgain4 = res.gmid, res.dc, res.packs, res.dgain, res.dgain_in
    gsecond = res.second
    if line:
        shard2 = head_in(plan, shard2)
    stat = stat + sum(plan.shift(stat, zl=d) for d in range(1, L))
    dc1, packs1, shard2, stat = fence(dc1, packs1, shard2, stat)
    dc1, half1, shard2 = fence(exchange(dc1), core_sums(packs1), shard2)
    dw1, das = attn_backward(
        plan, idx, cos, sin, [*a1, ints_all], late, 0, dc1, saved1, CAP, False, True
    )
    if line:
        shard2 = head_across(plan, shard2)
    dw1, das, half1, shard2 = fence(dw1, das, first_sums(half1), shard2)
    terms, shard1, shard2, dw1, dw2 = fence(
        scatter_group(das), jnp.concatenate(second_sums(half1), axis=0), shard2, dw1, dw2
    )
    outs, raw_outs = backward_outs(plan, n)
    res = run_named(
        "join_middle",
        functools.partial(join_middle_kernel, plan),
        {**outs, "dgain_in": sds((8, D), F32)},
        {
            "terms": terms,
            "gnext": gmid1,
            "x": pooled,
            "cols": cols,
            "gains": gains,
            "second": gsecond,
            "bound": bound_grad,
            "y": y0,
            "c": c0,
        },
        backward_scratch(plan, n),
        {"pack_in": packs[0]},
        raw_outs,
        idx,
        16 + 8 * plan.seq,
        2 * n * D * (2 * D + 5 * FF),
        n * FF,
    )
    gmid0, dc0, packs0, dgain1, dgain2 = res.gmid, res.dc, res.packs, res.dgain, res.dgain_in
    if line:
        shard2 = head_out(plan, shard2)
        shard1 = head_in(plan, shard1)
    dw21 = [sum_chips(plan, dw1), sum_chips(plan, dw2)]
    dc0, packs0, shard1, shard2, dw21 = fence(dc0, packs0, shard1, shard2, dw21)
    dc0, half0, dw21, shard1 = fence(exchange(dc0), core_sums(packs0), dw21, shard1)
    dw0, (dtab0,) = attn_backward(
        plan, idx, cos, sin, [ints_all, atab], early, 0, dc0, saved0, n, True, False
    )
    if line:
        shard1 = head_across(plan, shard1)
    dw21 = [add(v, plan.shift(v, zh=1)) for v in dw21]
    dw0, dtab0, half0, shard1, dw21 = fence(dw0, dtab0, first_sums(half0), shard1, dw21)
    tail = run(
        "tail",
        functools.partial(tail_kernel, plan),
        [sds((2 * DR + 2 * VR, D), BF)] * plan.chips,
        [idx],
        [
            *(gmid0, dtab0, table, cols, gains),
            *(dgain1, dgain2, dgain3, dgain4, dgain5, dgain6, dgain78),
            *dw0,
        ],
        [pltpu.VMEM((VOCAB, D), F32), pltpu.VMEM((128, D), F32), pltpu.VMEM((D, 128), F32)],
        flops=4 * n * VOCAB * D,
    )
    half0 = second_sums(half0)
    if line:
        shard1 = head_out(plan, shard1)
        half0 = [head_out(plan, head_across(plan, head_in(plan, v))) for v in half0]
    else:
        shard2, shard1, *half0 = [lax.psum(v, "head") for v in (shard2, shard1, *half0)]
    shard0 = jnp.concatenate(half0, axis=0)
    blocks21 = exchange_blocks(
        plan, jnp.concatenate([v.reshape(2, DR, QW) for v in dw21], axis=1), me
    )
    tail = sum_chips(plan, tail)
    tail = add(tail, plan.shift(tail, zh=1))
    tail = jnp.concatenate(
        [tail[: 2 * DR].reshape(2, DR, D), tail[2 * DR :].reshape(2, VR, D)], axis=1
    )
    blocks0 = exchange_blocks(plan, tail, me)
    tab0 = jnp.sum(blocks0[:, DR:].astype(F32), axis=0)
    gain_t = jnp.sum(blocks0[:, :DR, D - 128 :].astype(F32), axis=0)

    shards = (shard0, shard1, shard2)
    tops = [4 * DR] * 2 + [5 * DR + VR]
    grad_up = jnp.stack(
        [jnp.concatenate([s[j * DR : (j + 1) * DR] for j in range(4)], axis=1) for s in shards]
    ).astype(F32)
    grad_down = jnp.stack([s[t : t + FR] for s, t in zip(shards, tops)]).astype(F32)
    grad_proj = jnp.stack(
        [s[t + FR : t + FR + DR] for s, t in zip(shards, tops)] + [shard2[4 * DR : 5 * DR]]
    ).astype(F32)
    grad_table = jnp.stack([tab0, shard2[5 * DR : 5 * DR + VR].astype(F32)])
    grad_qkv = jnp.stack(
        [
            qkv_columns(plan, blocks0[:, :DR, : 3 * HW]),
            qkv_columns(plan, blocks21[:, :DR, : 3 * HW]),
            qkv_columns(plan, blocks21[:, DR:, : 3 * HW]),
        ]
    ).astype(F32)
    grads = (grad_qkv, grad_proj, grad_up, grad_down, grad_table)

    local_square = sum((jnp.sum(grad * grad) for grad in (*grads, gain_t)))
    lanes = lax.broadcasted_iota(jnp.int32, (8, 128), 1)
    totals = lax.psum(jnp.where(lanes == 6, local_square, stat), "seq")[0]
    valid_count = totals[5]
    inverse = 1.0 / valid_count
    grad_norm = jnp.sqrt(totals[6]) * inverse
    clip = jnp.minimum(1.0, CLIP_NORM / (grad_norm + 1e-06)) * inverse
    weights = (qkv_weight, proj_weight, upward_weight, downward_weight, table_weight)
    firsts = (qkv_first, proj_first, upward_first, downward_first, table_first)
    seconds = (qkv_second, proj_second, upward_second, downward_second, table_second)
    rates = (RATE_MATRIX,) * 4 + (RATE_VECTOR,)
    new = [
        adam_update(w, a, b, g * clip, rate)
        for w, a, b, g, rate in zip(weights, firsts, seconds, grads, rates)
    ]
    new.append(
        run(
            "gains",
            gain_kernel,
            [sds(gain_weight.shape, F32)] * 3,
            [clip.reshape(1)],
            [gain_t, gain_weight, gain_first, gain_second],
        )
    )
    residual_rms = jnp.sqrt(totals[2:5] / (valid_count * D))
    return (
        *[part for triple in new for part in triple],
        *[triple[0].astype(BF) for triple in new[:5]],
        totals[:2],
        valid_count,
        grad_norm,
        residual_rms,
    )


def solution(mesh):
    plan = Plan(mesh)
    tokens = P("seq", "head")
    matrix = P(None, "seq", None)
    vector = P(None, "seq")
    states = (matrix,) * 10 + (vector,) * 2
    return jax.shard_map(
        functools.partial(per_device, plan),
        mesh=mesh,
        in_specs=(tokens,) * 4 + (matrix,) * 5 + (vector,) + states,
        out_specs=(matrix,) * 15 + (vector,) * 3 + (matrix,) * 5 + (P(),) * 4,
        check_vma=False,
    )
```

```python
import functools
import math
from types import SimpleNamespace

import jax
import jax.numpy as jnp
import numpy as np
from jax import lax
from jax.experimental import pallas as pl
from jax.experimental.pallas import tpu as pltpu
from jax.sharding import PartitionSpec as P

D = 512
HEADS = 8
FF = 2048
VOCAB = 256
HEAD_DIM = 64
CAP = 256
STEP = 10
CHUNK = 512
HALF = HEAD_DIM // 2

NORM_EPS = 1e-06
BETA_FIRST = 0.9
BETA_SECOND = 0.95
ADAM_EPS = 1e-08
DECAY_RATE = 0.1
RATE_MATRIX = 0.05
RATE_VECTOR = 0.5
CLIP_NORM = 0.01
MASKED = -1000000000.0
SCALE = HEAD_DIM ** (-0.5)
GELU_A = math.sqrt(2.0 / math.pi)
GELU_B = 0.044715

BF = jnp.bfloat16
F32 = jnp.float32
NN = (((1,), (0,)), ((), ()))
NT = (((1,), (1,)), ((), ()))
AXES = ("seq", "head")
HB = pl.BlockSpec(memory_space=pltpu.HBM)
SM = pl.BlockSpec(memory_space=pltpu.SMEM)


def dot(a, b, dims=NN):
    return lax.dot_general(a, b, dims, preferred_element_type=F32)


def split3(v):
    high = v.astype(BF)
    rest = v - high.astype(F32)
    mid = rest.astype(BF)
    low = (rest - mid.astype(F32)).astype(BF)
    return (high, mid, low)


def exact_dot(ones, v):
    high, mid, low = split3(v)
    return dot(ones, high) + (dot(ones, mid) + dot(ones, low))


def root_of(v):
    return lax.rsqrt(jnp.mean(v * v, axis=-1, keepdims=True) + NORM_EPS)


def norm_back(unit, root, gain, grad):
    turned = grad * gain
    dx = root * (turned - unit * jnp.mean(turned * unit, axis=-1, keepdims=True))
    return dx, jnp.sum(grad * unit, axis=0, keepdims=True)


def gelu_parts(h):
    square = h * h
    t = jnp.tanh(GELU_A * h * (1.0 + GELU_B * square))
    half = 0.5 * (1.0 + t)
    value = h * half
    slope = half + 0.5 * h * (1.0 - t * t) * (GELU_A * (1.0 + 3.0 * GELU_B * square))
    return value, slope


def gelu_value(h):
    t = jnp.tanh(GELU_A * h * (1.0 + GELU_B * (h * h)))
    return h * (0.5 * (1.0 + t))


def one_hot(column, width):
    lanes = lax.broadcasted_iota(jnp.int32, (column.shape[0], width), 1).astype(F32)
    return (lanes == column).astype(F32).astype(BF)


class Plan:
    def __init__(self, mesh):
        self.seq = mesh.shape["seq"]
        self.head = mesh.shape["head"]
        self.chips = self.seq // 2
        side = int(math.isqrt(self.chips))
        while self.chips % side:
            side -= 1
        self.Y, self.X = side, self.chips // side
        self.L = self.head // 2
        self.G = self.head
        self.hd = HEADS // self.G
        self.HW = self.hd * HEAD_DIM
        self.QW = -(-3 * self.HW // 128) * 128
        self.DR = D // self.seq
        self.FR = FF // self.seq
        self.VR = VOCAB // self.seq
        self.sizes = {"y": self.Y, "x": self.X, "core": 2, "zh": 2, "zl": self.L}
        self.names = ("y", "x", "core", "zh", "zl")

    def coords(self):
        for linear in range(self.seq * self.head):
            s, z = divmod(linear, self.head)
            yx, core = divmod(s, 2)
            y, x = divmod(yx, self.X)
            zh, zl = divmod(z, self.L)
            yield linear, {"y": y, "x": x, "core": core, "zh": zh, "zl": zl}

    def linear(self, c):
        s = (c["y"] * self.X + c["x"]) * 2 + c["core"]
        return s * self.head + c["zh"] * self.L + c["zl"]

    def permute(self, v, to):
        pairs = []
        for here, c in self.coords():
            there = to(c)
            if there is not None:
                pairs.append((here, self.linear(there)))
        return lax.ppermute(v, AXES, pairs)

    def shift(self, v, **steps):
        def to(c):
            return {k: (c[k] + steps.get(k, 0)) % self.sizes[k] for k in self.names}

        return self.permute(v, to)

    def place(self):
        s = lax.axis_index("seq")
        z = lax.axis_index("head")
        yx, core = s // 2, s % 2
        return {
            "y": yx // self.X,
            "x": yx % self.X,
            "core": core,
            "zh": z // self.L,
            "zl": z % self.L,
        }

    def tables(self):
        me = self.place()
        G, L, Y, X = self.G, self.L, self.Y, self.X

        def block(sign):
            return [
                ((me["core"] + sign * dc) % 2) * L + (me["zl"] + sign * dl) % L
                for dc in range(2)
                for dl in range(L)
            ]

        def chip(dy, dx):
            return ((me["y"] + dy) % Y) * X + (me["x"] + dx) % X

        chip_src = [chip(-dy, -dx) for dy in range(Y) for dx in range(X)]
        by_x = [chip(dy, dx) for dx in range(X) for dy in range(Y)]
        by_y = [chip(dy, dx) for dy in range(Y) for dx in range(X)]
        entries = [me["core"], me["zl"]] + block(1) + block(-1) + chip_src + by_x + by_y
        self.at_core = 0
        self.at_zl = 1
        self.at_dst = 2
        self.at_src = 2 + G
        self.at_chip = 2 + 2 * G
        self.at_order = {"x": 2 + 2 * G + Y * X, "y": 2 + 2 * G + 2 * Y * X}
        return jnp.stack([jnp.asarray(e, jnp.int32) for e in entries])


def run(
    name,
    body,
    outs,
    smem,
    arrays,
    scratch=(),
    raw=(),
    raw_outs=(),
    sems=0,
    flops=0,
    trans=0,
    limit=60,
    after=(),
):
    operands = [*arrays, *raw]
    results = [*outs, *raw_outs]
    nbytes = sum(a.size * a.dtype.itemsize for a in operands)
    nbytes += sum(math.prod(o.shape) * jnp.dtype(o.dtype).itemsize for o in results)
    ns, ni, nr, na, no, nx = map(len, (smem, arrays, raw, after, outs, raw_outs))

    def wrapped(*refs):
        at = 0
        parts = []
        for count in (ns, ni, nr, na, no, nx, ni, no, len(scratch)):
            parts.append(refs[at : at + count])
            at += count
        s_refs, ins, raws, _, results_out, raws_out, bufs, out_bufs, own = parts
        sem = refs[at]
        copies = [
            pltpu.make_async_copy(src, dst, sem.at[k])
            for k, (src, dst) in enumerate(zip(ins, bufs))
        ]
        for copy in copies:
            copy.start()
        for copy in copies:
            copy.wait()
        extra = (refs[at + 1],) if sems else ()
        body(*s_refs, *bufs, *raws, *out_bufs, *raws_out, *own, *extra)
        copies = [
            pltpu.make_async_copy(src, dst, sem.at[k])
            for k, (src, dst) in enumerate(zip(out_bufs, results_out))
        ]
        for copy in copies:
            copy.start()
        for copy in copies:
            copy.wait()

    spaces = [pltpu.VMEM(v.shape, v.dtype) for v in (*arrays, *outs)]
    spaces += list(scratch) + [pltpu.SemaphoreType.DMA((max(ni, no, 1),))]
    if sems:
        spaces.append(pltpu.SemaphoreType.DMA((sems,)))
    return pl.pallas_call(
        wrapped,
        out_shape=tuple(results),
        in_specs=[SM] * ns + [HB] * (ni + nr) + [pl.BlockSpec(memory_space=pl.ANY)] * na,
        out_specs=tuple([HB] * len(results)),
        scratch_shapes=spaces,
        compiler_params=pltpu.CompilerParams(vmem_limit_bytes=limit << 20),
        cost_estimate=pl.CostEstimate(
            flops=int(flops), bytes_accessed=int(nbytes), transcendentals=int(trans)
        ),
        name=name,
    )(*smem, *operands, *after)


def run_named(name, body, outs, arrays, scratch, raw, raw_outs, idx, sems, flops, trans):
    def flat(group):
        out = []
        for value in group.values():
            out += list(value) if isinstance(value, (list, tuple)) else [value]
        return out

    def name_all(space, group, refs):
        for key, value in group.items():
            if isinstance(value, (list, tuple)):
                setattr(space, key, [refs.pop(0) for _ in value])
            else:
                setattr(space, key, refs.pop(0))

    def wrapped(idx_ref, *refs):
        space, refs = SimpleNamespace(idx=idx_ref), list(refs)
        for group in (arrays, raw, outs, raw_outs, scratch):
            name_all(space, group, refs)
        space.sem = refs.pop(0)
        body(space)

    res = list(
        run(
            name,
            wrapped,
            flat(outs),
            [idx],
            flat(arrays),
            flat(scratch),
            flat(raw),
            flat(raw_outs),
            sems,
            flops,
            trans,
        )
    )
    space = SimpleNamespace()
    for group in (outs, raw_outs):
        name_all(space, group, res)
    return space


def fence(*groups):
    return lax.optimization_barrier(groups)


class Copies:
    def __init__(self, sem):
        self.sem = sem
        self.count = 0
        self.open = []

    def start(self, src, dst):
        copy = pltpu.make_async_copy(src, dst, self.sem.at[self.count])
        self.count += 1
        copy.start()
        self.open.append(copy)
        return copy

    def finish(self):
        for copy in self.open:
            copy.wait()
        self.open = []


def rows_at(index, size):
    return pl.ds(pl.multiple_of(index * size, size), size)


def sds(shape, dtype):
    return jax.ShapeDtypeStruct(shape, dtype)


def first_kernel(plan, idx, qkv, table, gain, *refs):
    keep0, send0, keep1, send1, scr = refs
    DR, VR, HW, QW = plan.DR, plan.VR, plan.HW, plan.QW
    core, zl = idx[plan.at_core], idx[plan.at_zl]
    for which, outs in ((0, (keep0, keep1)), (1, (send0, send1))):
        block = lax.rem(core + which, 2) * plan.L + zl
        for layer in range(3):
            out, lo = ((outs[0], 0), (outs[1], 0), (outs[1], QW))[layer]
            for part in range(3):
                if HW % 128 == 0:
                    at = pl.ds(pl.multiple_of(part * D + block * HW, HW), HW)
                    piece = qkv[layer, :, at]
                else:
                    at = pl.ds(pl.multiple_of(part * D + block // 2 * 128, 128), 128)
                    both = qkv[layer, :, at]
                    piece = jnp.where(block % 2 == 0, both[:, :HW], both[:, HW:])
                out[:, lo + part * HW : lo + (part + 1) * HW] = piece.astype(BF)
    scr[...] = jnp.zeros_like(scr)
    scr[0 : gain.shape[0], 0:DR] = gain[...]
    turned = scr[...].T[0:DR, :].astype(BF)
    low = table[0].astype(BF)
    for out in (keep0, send0):
        out[:, QW : QW + 256] = jnp.concatenate([low[:, :256], low[:, 256:]], axis=0)
        out[:, QW + 256 : QW + 384] = turned


def pack_kernel(plan, layer, up, down, proj, table, out, up_scr, down_scr, proj_scr, tab_scr, sem):
    copies = Copies(sem)
    DR, FR, VR = plan.DR, plan.FR, plan.VR
    copies.start(up.at[layer], up_scr)
    copies.start(down.at[layer], down_scr)
    copies.start(proj.at[layer], proj_scr.at[0])
    if layer == 1:
        copies.start(proj.at[3], proj_scr.at[1])
    if layer == 2:
        copies.start(table.at[1], tab_scr)
    copies.finish()
    for j in range(FF // CHUNK):
        out[j * DR : (j + 1) * DR, :] = up_scr[:, j * CHUNK : (j + 1) * CHUNK].astype(BF)
    top = 4 * DR
    out[top : top + FR, :] = down_scr[...].astype(BF)
    top += FR
    out[top : top + DR, :] = proj_scr[0].astype(BF)
    top += DR
    if layer == 1:
        out[top : top + DR, :] = proj_scr[1].astype(BF)
    if layer == 2:
        out[top : top + VR, :] = tab_scr[...].astype(BF)


def gain_kernel(factor, gt, weight, first, second, master_out, mean_out, meansq_out):
    rows, width = weight.shape
    grad = gt[...].T[0:rows, 0:width] * factor[0]
    master, mean, meansq = adam_update(weight[...], first[...], second[...], grad, RATE_VECTOR)
    master_out[...] = master
    mean_out[...] = mean
    meansq_out[...] = meansq


def prep_kernel(plan, idx, ints, *refs):
    pieces = refs[: plan.chips]
    table_out, atab_out, gain_out, cols_out, table_scr, gain_scr, row_scr = refs[plan.chips :]
    slots = ints[3:4, :].astype(F32)
    n = slots.shape[1]
    lanes = lax.broadcasted_iota(jnp.int32, (1, n), 1)
    row_scr[...] = jnp.zeros_like(row_scr)
    row_scr[VALID : VALID + 1, :] = ints[2:3, :].astype(F32)
    changed = jnp.concatenate([slots[:, 0:1], slots[:, 0 : n - 1]], axis=1) != slots
    row_scr[TARGET : TARGET + 1, :] = jnp.where((lanes == 0) | changed, 1.0, 0.0)
    row_scr[NEXT : NEXT + 1, :] = ints[1:2, :].astype(F32)
    row_scr[SLOT : SLOT + 1, :] = slots
    row_scr[BYTE : BYTE + 1, :] = ints[0:1, :].astype(F32)
    cols_out[...] = row_scr[...].T
    VR, DR, QW = plan.VR, plan.DR, plan.QW
    for r in range(plan.chips):
        k = idx[plan.at_chip + r]
        for core in range(2):
            for half in range(2):
                rows = pieces[r][core * DR + half * VR : core * DR + (half + 1) * VR, QW : QW + 256]
                table_scr[
                    pl.ds(pl.multiple_of(k * 2 * VR, 2 * VR) + core * VR, VR),
                    half * 256 : half * 256 + 256,
                ] = rows.astype(F32)
        gain_scr[pl.ds(pl.multiple_of(k * 2 * DR, 2 * DR), 2 * DR), :] = pieces[r][
            :, QW + 256 : QW + 384
        ].astype(F32)
    gains = gain_scr[...].T[0:16, :]
    gain_out[...] = gains
    table = table_scr[...]
    table_out[...] = table.astype(BF)
    atab_out[...] = (table * root_of(table) * gains[0:1, :]).astype(BF)


def load_weight(plan, copies, idx, pieces, lo, w_scr):
    started = []
    for r in range(plan.chips):
        src = pieces[r].at[:, lo : lo + plan.QW]
        started.append(copies.start(src, w_scr.at[rows_at(idx[plan.at_chip + r], 2 * plan.DR), :]))
    return started


def live_bias(plan, idx, ints, n, bias_scr):
    row = lax.broadcasted_iota(jnp.int32, (n, 128), 0).astype(F32)
    for r in range(plan.G):
        slots = ints[8 * r + 3 : 8 * r + 4, :].astype(F32)
        last = jnp.max(slots, axis=1, keepdims=True)
        bias_scr[rows_at(idx[plan.at_src + r], n), :] = jnp.where(row <= last, 0.0, MASKED)


def head_pad(plan, part, h):
    if plan.hd == 1:
        return part
    blank = jnp.zeros_like(part)
    return jnp.concatenate([part if k == h else blank for k in range(plan.hd)], axis=0)


def rot_pair(a, b, cos, sin):
    return a * cos - b * sin, b * cos + a * sin


def attn_fwd_kernel(plan, n, lo, embed, masked, idx, *refs):
    G, HW, hd = plan.G, plan.HW, plan.hd
    S = G * n
    refs = list(refs)
    cos_ref, sin_ref = refs[0], refs[1]
    refs = refs[2:]
    if embed:
        ints_ref, atab_ref = refs[0], refs[1]
        refs = refs[2:]
    else:
        a_refs = refs[:G]
        refs = refs[G:]
    if masked:
        ints_ref = refs[0]
        refs = refs[1:]
    w_refs = refs[: plan.chips]
    refs = refs[plan.chips :]
    c_outs = refs[:G]
    qkvt_out, ot_out, lse_out = refs[G : G + 3]
    w_scr, cos_scr, sin_scr, src_scr, tab_scr, ints_scr, bias_scr = refs[G + 3 : G + 10]
    qkvt, ot, lse, k_scr, c_scr, sem = refs[G + 10 :]
    copies = Copies(sem)
    first = load_weight(plan, copies, idx, w_refs, lo, w_scr)
    first.append(copies.start(cos_ref, cos_scr))
    first.append(copies.start(sin_ref, sin_scr))
    sources = []
    if embed or masked:
        first.append(copies.start(ints_ref, ints_scr))
    if embed:
        first.append(copies.start(atab_ref, tab_scr))
    else:
        for r in range(G):
            dst = src_scr.at[rows_at(idx[plan.at_src + r], n), :]
            sources.append(copies.start(a_refs[r], dst))
    for copy in first:
        copy.wait()
    copies.open = []
    wt = w_scr[...].T[0 : 3 * HW, :]
    if embed:
        base = split3(dot(wt, tab_scr[...], NT))
    if masked:
        live_bias(plan, idx, ints_scr, n, bias_scr)
    for r in range(G):
        at = rows_at(idx[plan.at_src + r], n)
        if embed:
            ids = ints_scr[8 * r : 8 * r + 1, :]
            hot = (lax.broadcasted_iota(jnp.int32, (VOCAB, n), 0) == ids).astype(F32).astype(BF)
            m = dot(base[0], hot) + (dot(base[1], hot) + dot(base[2], hot))
        else:
            sources[r].wait()
            m = dot(wt, src_scr[at, :], NT)
        cos, sin = cos_scr[:, at], sin_scr[:, at]
        for h in range(hd):
            for part, factor in ((0, SCALE), (1, 1.0)):
                top = part * HW + h * HEAD_DIM
                one, two = rot_pair(m[top : top + HALF], m[top + HALF : top + HEAD_DIM], cos, sin)
                qkvt[top : top + HALF, at] = (one * factor).astype(BF)
                qkvt[top + HALF : top + HEAD_DIM, at] = (two * factor).astype(BF)
        qkvt[2 * HW : 3 * HW, at] = m[2 * HW : 3 * HW].astype(BF)
        k_scr[at, :] = qkvt[HW : 2 * HW, at].T
    copies.start(qkvt, qkvt_out)
    tile = min(512, S)

    def tile_scores(q_pads, keys, rows, diagonal):
        out = []
        for h in range(hd):
            s = dot(keys, q_pads[h])
            if masked:
                s = s + jnp.concatenate([bias_scr[rows, :]] * (tile // 128), axis=1)
            if diagonal:
                kk = lax.broadcasted_iota(jnp.int32, (tile, tile), 0)
                qq = lax.broadcasted_iota(jnp.int32, (tile, tile), 1)
                s = jnp.where(kk <= qq, s, MASKED)
            out.append(s)
        return out

    def one_query(i, _):
        cols = pl.ds(pl.multiple_of(i * tile, tile), tile)
        q_pads = [
            head_pad(plan, qkvt[h * HEAD_DIM : (h + 1) * HEAD_DIM, cols], h) for h in range(hd)
        ]

        def step(j, state, diagonal):
            rows = pl.ds(pl.multiple_of(j * tile, tile), tile)
            scores = tile_scores(q_pads, k_scr[rows, :], rows, diagonal)
            new = []
            for h in range(hd):
                top, total, acc = state[3 * h : 3 * h + 3]
                s = scores[h]
                new_top = jnp.maximum(top, jnp.max(s, axis=0, keepdims=True))
                p = jnp.exp(s - new_top)
                keep = jnp.exp(top - new_top)
                total = total * keep + jnp.sum(p, axis=0, keepdims=True)
                vt = qkvt[2 * HW + h * HEAD_DIM : 2 * HW + (h + 1) * HEAD_DIM, rows]
                acc = acc * keep + dot(vt, p.astype(BF))
                new += [new_top, total, acc]
            return tuple(new)

        state = ()
        for h in range(hd):
            state += (
                jnp.full((1, tile), -1e30, F32),
                jnp.zeros((1, tile), F32),
                jnp.zeros((HEAD_DIM, tile), F32),
            )
        state = lax.fori_loop(0, i, lambda j, st: step(j, st, False), state)
        state = step(i, state, True)
        for h in range(hd):
            top, total, acc = state[3 * h : 3 * h + 3]
            ot[h * HEAD_DIM : (h + 1) * HEAD_DIM, cols] = acc / total
            lse[h : h + 1, cols] = top + jnp.log(total)
        c_scr[cols, :] = ot[:, cols].T.astype(BF)
        return 0

    lax.fori_loop(0, S // tile, one_query, 0)
    for r in range(G):
        copies.start(c_scr.at[rows_at(idx[plan.at_dst + r], n), :], c_outs[r])
    copies.start(ot, ot_out)
    copies.start(lse, lse_out)
    copies.finish()


def source_scratch(embed, masked, S, G, source):
    none = pltpu.VMEM((16, 128), BF)
    return [
        none if embed else pltpu.VMEM((S, D), BF),
        pltpu.VMEM((VOCAB, D), BF) if embed else none,
        pltpu.VMEM(source[0 if embed else G].shape, jnp.int32) if embed or masked else none,
        pltpu.VMEM((S, 128), F32) if masked else none,
    ]


def attn_forward(plan, idx, cos, sin, source, weights, lo, n, embed, masked, after=()):
    G, HW = plan.G, plan.HW
    S = G * n
    outs = [sds((n, HW), BF)] * G + [
        sds((3 * HW, S), BF),
        sds((HW, S), F32),
        sds((8, S), F32),
    ]
    res = run(
        "attention_forward",
        functools.partial(attn_fwd_kernel, plan, n, lo, embed, masked),
        [],
        [idx],
        [],
        [
            pltpu.VMEM((D, plan.QW), BF),
            pltpu.VMEM(cos.shape, F32),
            pltpu.VMEM(cos.shape, F32),
            *source_scratch(embed, masked, S, G, source),
            pltpu.VMEM((3 * HW, S), BF),
            pltpu.VMEM((HW, S), F32),
            pltpu.VMEM((8, S), F32),
            pltpu.VMEM((S, HW), BF),
            pltpu.VMEM((S, HW), BF),
        ],
        raw=[cos, sin, *source, *weights],
        raw_outs=outs,
        sems=plan.chips + 2 * G + 8,
        flops=2 * S * D * 3 * HW + 2 * plan.hd * S * S * 256,
        trans=plan.hd * S * S // 2,
        after=after,
    )
    return res[:G], res[G:]


def attn_bwd_kernel(plan, n, lo, embed, masked, idx, *refs):
    G, HW, hd = plan.G, plan.HW, plan.hd
    S = G * n
    refs = list(refs)
    cos_ref, sin_ref = refs[0], refs[1]
    refs = refs[2:]
    if embed:
        ints_ref, atab_ref = refs[0], refs[1]
        refs = refs[2:]
    else:
        a_refs = refs[:G]
        refs = refs[G:]
    if masked:
        ints_ref = refs[0]
        refs = refs[1:]
    w_refs = refs[: plan.chips]
    refs = refs[plan.chips :]
    do_refs = refs[:G]
    qkvt_in, ot_in, lse_in = refs[G : G + 3]
    refs = refs[G + 3 :]
    dw_outs = refs[: plan.chips]
    refs = refs[plan.chips :]
    if embed:
        tab_out = refs[0]
        refs = refs[1:]
    else:
        da_outs = refs[:G]
        refs = refs[G:]
    w_scr, cos_scr, sin_scr, src_scr, tab_scr, ints_scr, bias_scr, qkvt, ot, lse = refs[:10]
    do_all, k_scr, v_scr, qz, qtz, doz, dotz, delta, dqt, dk, dv, dmt, res_scr, dw_scr, sem = refs[10:]
    copies = Copies(sem)
    if embed or masked:
        copies.start(ints_ref, ints_scr)
    copies.start(qkvt_in, qkvt)
    for r in range(G):
        copies.start(do_refs[r], do_all.at[rows_at(idx[plan.at_src + r], n), :])
    copies.start(ot_in, ot)
    copies.start(lse_in, lse)
    first, copies.open = copies.open, []
    copies.start(cos_ref, cos_scr)
    copies.start(sin_ref, sin_scr)
    angles, copies.open = copies.open, []
    load_weight(plan, copies, idx, w_refs, lo, w_scr)
    if embed:
        copies.start(atab_ref, tab_scr)
    else:
        for r in range(G):
            copies.start(a_refs[r], src_scr.at[rows_at(idx[plan.at_src + r], n), :])
    last, copies.open = copies.open, []
    for copy in first:
        copy.wait()
    tile = min(512, S)
    blocks = S // tile
    lane = lax.broadcasted_iota(jnp.int32, (tile, HW), 1) // HEAD_DIM
    for b in range(blocks):
        at = slice(b * tile, (b + 1) * tile)
        dob = do_all[at, :]
        dobt = dob.T
        kt = qkvt[HW : 2 * HW, at]
        k_scr[at, :] = kt.T
        v_scr[at, :] = qkvt[2 * HW : 3 * HW, at].T
        prod = dobt.astype(F32) * ot[:, at]
        dob32 = dob.astype(F32)
        for h in range(hd):
            rows = slice(h * HEAD_DIM, (h + 1) * HEAD_DIM)
            pad = head_pad(plan, qkvt[rows, at], h)
            qtz[h, :, at] = pad
            qz[h, at, :] = pad.T
            dotz[h, :, at] = head_pad(plan, dobt[rows, :], h)
            doz[h, at, :] = jnp.where(lane == h, dob32, 0.0).astype(BF)
            delta[h : h + 1, at] = jnp.sum(prod[rows, :], axis=0, keepdims=True)
    dqt[...] = jnp.zeros_like(dqt)
    if masked:
        live_bias(plan, idx, ints_scr, n, bias_scr)
    for copy in angles:
        copy.wait()

    def one_key(j, _):
        rows = pl.ds(pl.multiple_of(j * tile, tile), tile)
        keys, values = k_scr[rows, :], v_scr[rows, :]
        dk[...] = jnp.zeros_like(dk)
        dv[...] = jnp.zeros_like(dv)
        bias = jnp.concatenate([bias_scr[rows, :]] * (tile // 128), axis=1) if masked else None

        def step(i, diagonal):
            cols = pl.ds(pl.multiple_of(i * tile, tile), tile)
            for h in range(hd):
                s = dot(keys, qtz[h, :, cols])
                if masked:
                    s = s + bias
                if diagonal:
                    kk = lax.broadcasted_iota(jnp.int32, (tile, tile), 0)
                    qq = lax.broadcasted_iota(jnp.int32, (tile, tile), 1)
                    s = jnp.where(kk <= qq, s, MASKED)
                p = jnp.exp(s - lse[h : h + 1, cols])
                dp = dot(values, dotz[h, :, cols])
                ds = (p * (dp - delta[h : h + 1, cols])).astype(BF)
                dv[...] += dot(p.astype(BF), doz[h, cols, :])
                dk[...] += dot(ds, qz[h, cols, :])
                kt = qkvt[HW + h * HEAD_DIM : HW + (h + 1) * HEAD_DIM, rows]
                dqt[h * HEAD_DIM : (h + 1) * HEAD_DIM, cols] += dot(kt, ds)

        step(j, True)

        def more(i, carry):
            step(i, False)
            return carry

        lax.fori_loop(j + 1, blocks, more, 0)
        dkt = dk[...].T
        cos, sin = cos_scr[:, rows], sin_scr[:, rows]
        for h in range(hd):
            top = h * HEAD_DIM
            one, two = rot_pair(
                dkt[top : top + HALF], dkt[top + HALF : top + HEAD_DIM], cos, -sin
            )
            dmt[HW + top : HW + top + HALF, rows] = one.astype(BF)
            dmt[HW + top + HALF : HW + top + HEAD_DIM, rows] = two.astype(BF)
        dmt[2 * HW : 3 * HW, rows] = dv[...].T.astype(BF)
        return 0

    lax.fori_loop(0, blocks, one_key, 0)
    cos, sin = cos_scr[:, 0:S], sin_scr[:, 0:S]
    for h in range(hd):
        top = h * HEAD_DIM
        one, two = rot_pair(
            dqt[top : top + HALF, :] * SCALE,
            dqt[top + HALF : top + HEAD_DIM, :] * SCALE,
            cos,
            -sin,
        )
        dmt[top : top + HALF, :] = one.astype(BF)
        dmt[top + HALF : top + HEAD_DIM, :] = two.astype(BF)
    for copy in last:
        copy.wait()
    wt = w_scr[...].T[0 : 3 * HW, :]
    if embed:
        sums = jnp.zeros((3 * HW, VOCAB), F32)
        for r in range(G):
            at = rows_at(idx[plan.at_src + r], n)
            ids = ints_scr[8 * r : 8 * r + 1, :]
            hot = (lax.broadcasted_iota(jnp.int32, (VOCAB, n), 0) == ids).astype(F32).astype(BF)
            sums += dot(dmt[:, at], hot, NT)
        high = sums.astype(BF)
        low = (sums - high.astype(F32)).astype(BF)
        res_scr[...] = dot(high.T, wt) + dot(low.T, wt)
        copies.start(res_scr, tab_out)
        grad = dot(high, tab_scr[...]) + dot(low, tab_scr[...])
    else:
        for r in reversed(range(G)):
            at = rows_at(idx[plan.at_dst + r], n)
            res_scr[at, :] = dot(dmt[:, at].T, wt).astype(BF)
            copies.start(res_scr.at[at, :], da_outs[r])
        grad = dot(dmt[...], src_scr[...])
    dw_scr[:, 0 : 3 * HW] = grad.T.astype(BF)
    dw_scr[:, 3 * HW : D] = jnp.zeros((D, D - 3 * HW), BF)
    for r in range(plan.chips):
        at = rows_at(idx[plan.at_order["x"] + r], 2 * plan.DR)
        copies.start(dw_scr.at[at, :], dw_outs[r])
    copies.finish()


def attn_backward(
    plan, idx, cos, sin, source, weights, lo, dos, saved, n, embed, masked, after=()
):
    G, HW, hd = plan.G, plan.HW, plan.hd
    S = G * n
    tile = min(512, S)
    outs = [sds((2 * plan.DR, D), BF)] * plan.chips
    outs += [sds((VOCAB, D), F32)] if embed else [sds((n, D), BF)] * G
    res = run(
        "attention_backward",
        functools.partial(attn_bwd_kernel, plan, n, lo, embed, masked),
        [],
        [idx],
        [],
        [
            pltpu.VMEM((D, plan.QW), BF),
            pltpu.VMEM(cos.shape, F32),
            pltpu.VMEM(cos.shape, F32),
            *source_scratch(embed, masked, S, G, source),
            pltpu.VMEM((3 * HW, S), BF),
            pltpu.VMEM((HW, S), F32),
            pltpu.VMEM((8, S), F32),
            pltpu.VMEM((S, HW), BF),
            pltpu.VMEM((S, HW), BF),
            pltpu.VMEM((S, HW), BF),
            pltpu.VMEM((hd, S, HW), BF),
            pltpu.VMEM((hd, HW, S), BF),
            pltpu.VMEM((hd, S, HW), BF),
            pltpu.VMEM((hd, HW, S), BF),
            pltpu.VMEM((8, S), F32),
            pltpu.VMEM((HW, S), F32),
            pltpu.VMEM((tile, HW), F32),
            pltpu.VMEM((tile, HW), F32),
            pltpu.VMEM((3 * HW, S), BF),
            pltpu.VMEM((VOCAB, D), F32) if embed else pltpu.VMEM((S, D), BF),
            pltpu.VMEM((D, D), BF),
        ],
        raw=[cos, sin, *source, *weights, *dos, *saved],
        raw_outs=outs,
        sems=2 * plan.chips + 3 * G + 8,
        flops=4 * S * D * 3 * HW + 5 * hd * S * S * 256,
        trans=hd * S * S // 2,
        after=after,
    )
    return res[: plan.chips], res[plan.chips :]


class Pack:
    def __init__(self, plan, copies, pack, scr):
        self.plan = plan
        self.up_scr, self.down_scr, self.proj_scr = scr
        DR, FR = plan.DR, plan.FR
        self.per = CHUNK // FR
        top = 4 * DR + FR
        self.proj_copy = copies.start(pack.at[:, top : top + DR, :], self.proj_scr)
        self.copies = []
        for j in range(FF // CHUNK):
            at = slice(j * self.per, (j + 1) * self.per)
            self.copies.append(
                (
                    copies.start(pack.at[:, j * DR : (j + 1) * DR, :], self.up_scr.at[j]),
                    copies.start(pack.at[at, 4 * DR : 4 * DR + FR, :], self.down_scr.at[j]),
                )
            )
        copies.open = []

    @staticmethod
    def scratch(plan):
        chunks = FF // CHUNK
        return [
            pltpu.VMEM((chunks, plan.seq, plan.DR, D), BF),
            pltpu.VMEM((chunks, CHUNK // plan.FR, plan.FR, D), BF),
            pltpu.VMEM((plan.seq, plan.DR, D), BF),
        ]

    def proj(self, k):
        per = self.plan.HW // self.plan.DR
        rows = self.proj_scr[pl.ds(k * per, per), :, :]
        return rows.reshape(self.plan.HW, D)

    def up(self, j):
        return self.up_scr[j].reshape(D, CHUNK)

    def down(self, j):
        return self.down_scr[j].reshape(CHUNK, D)


VALID, TARGET, NEXT, SLOT, BYTE = range(5)


def at_lane(lane, value):
    lanes = lax.broadcasted_iota(jnp.int32, (8, 128), 1)
    return jnp.where(lanes == lane, jnp.broadcast_to(value, (8, 128)), 0.0)


def square_of(cols, x):
    rows = jnp.sum(x * x, axis=-1, keepdims=True) * cols[:, VALID : VALID + 1]
    return jnp.sum(rows, axis=0, keepdims=True)


def attended(plan, k, x):
    k.pack.proj_copy.wait()
    y = x
    for r in range(plan.G):
        y += dot(k.c[r][...], k.pack.proj(k.idx[plan.at_src + r]))
    k.y[...] = y


def feed_forward(k, layer, y, keep=False):
    k.normed[...] = (y * root_of(y) * k.gains[2 * layer + 1 : 2 * layer + 2, :]).astype(BF)
    for j in range(FF // CHUNK):
        k.pack.copies[j][0].wait()
        h = dot(k.normed[...], k.pack.up(j))
        at = slice(j * CHUNK, (j + 1) * CHUNK)
        if keep:
            value, slope = gelu_parts(h)
            k.slope[j] = slope
        else:
            value = gelu_value(h)
        k.act[:, at] = value.astype(BF)
    for j in range(FF // CHUNK):
        k.pack.copies[j][1].wait()
    k.x_scr[...] = k.y[...] + dot(k.act[...], k.down_scr[...].reshape(FF, D))


def ffn_pool_kernel(plan, k):
    k.pack = Pack(plan, Copies(k.sem), k.pack_in, (k.up_scr, k.down_scr, k.proj_scr))
    x = dot(one_hot(k.cols[:, BYTE : BYTE + 1], VOCAB), k.table[...])
    attended(plan, k, x)
    feed_forward(k, 0, k.y[...])
    x = k.x_scr[...]
    k.x[...] = x
    turned = one_hot(k.cols[:, SLOT : SLOT + 1], CAP).T
    counts = jnp.sum(turned.astype(F32), axis=1, keepdims=True)
    pooled = exact_dot(turned, x) / jnp.maximum(counts, 1.0)
    k.pooled[...] = pooled
    k.a[...] = (pooled * root_of(pooled) * k.gains[2:3, :]).astype(BF)
    count = jnp.sum(k.cols[:, VALID : VALID + 1], axis=0, keepdims=True)
    k.stat[...] = at_lane(2, square_of(k.cols, x)) + at_lane(5, count)


def ffn_unpool_kernel(plan, k):
    k.pack = Pack(plan, Copies(k.sem), k.pack_in, (k.up_scr, k.down_scr, k.proj_scr))
    attended(plan, k, k.pooled[...])
    feed_forward(k, 1, k.y[...])
    x = k.x1[...] + exact_dot(one_hot(k.cols[:, SLOT : SLOT + 1], CAP), k.x_scr[...])
    k.x[...] = x
    k.a[...] = (x * root_of(x) * k.gains[4:5, :]).astype(BF)
    k.stat[...] = k.stat_in[...] + at_lane(3, square_of(k.cols, x))


def forward_scratch(plan, n):
    return {
        **dict(zip(("up_scr", "down_scr", "proj_scr"), Pack.scratch(plan))),
        "normed": pltpu.VMEM((n, D), BF),
        "act": pltpu.VMEM((n, FF), BF),
        "x_scr": pltpu.VMEM((n, D), F32),
    }


def loss_part(plan, k):
    k.tab_copy.wait()
    table = k.tab_scr[...].reshape(VOCAB, D)
    x = k.x_scr[...]
    valid = k.cols[:, VALID : VALID + 1]
    root = root_of(x)
    unit = x * root
    gain = k.gains[6:7, :]
    rows = (unit * gain).astype(BF)
    logits = dot(rows, table, NT)
    top_row = jnp.max(logits, axis=-1, keepdims=True)
    total = jnp.sum(jnp.exp(logits - top_row), axis=-1, keepdims=True)
    log_norm = top_row + jnp.log(total)
    hot = one_hot(k.cols[:, NEXT : NEXT + 1], VOCAB).astype(F32)
    picked = jnp.sum(logits * hot, axis=-1, keepdims=True)
    ce = jnp.sum(valid * (log_norm - picked), axis=0, keepdims=True)
    glog = (valid * (jnp.exp(logits - log_norm) - hot)).astype(BF)
    k.dtab[...] = dot(glog.T, rows).astype(BF).reshape(plan.seq, plan.VR, D)
    dx, dgain = norm_back(unit, root, gain, dot(glog, table))
    k.gout[...] = dx
    k.dgain6[...] = jnp.broadcast_to(dgain, k.dgain6.shape)
    k.stat[...] = (
        k.stat_a[...] + k.stat_b[...] + at_lane(0, ce) + at_lane(4, square_of(k.cols, x))
    )


def ffn_backward_part(plan, k, layer, y, send, kept=False):
    root = root_of(y)
    gain = k.gains[2 * layer + 1 : 2 * layer + 2, :]
    k.unit[...] = y * root
    if not kept:
        k.normed[...] = (y * root * gain).astype(BF)
    k.normt[...] = k.normed[...].T
    k.low[...] = k.gout[...].astype(BF)
    k.dn[...] = jnp.zeros_like(k.dn)
    for j in range(FF // CHUNK):
        if kept:
            value, slope = k.act[:, j * CHUNK : (j + 1) * CHUNK], k.slope[j]
            up = k.pack.up(j)
        else:
            for copy in k.pack.copies[j]:
                copy.wait()
            up = k.pack.up(j)
            value, slope = gelu_parts(dot(k.normed[...], up))
            value = value.astype(BF)
        per = CHUNK // plan.FR
        grad = dot(value.T, k.low[...]).astype(BF)
        k.ddown[j * per : (j + 1) * per] = grad.reshape(per, plan.FR, D)
        dact = dot(k.low[...], k.pack.down(j), NT)
        dh = (dact * slope).astype(BF)
        k.dup[j] = dot(k.normt[...], dh).astype(BF).reshape(plan.seq, plan.DR, CHUNK)
        send(j)
        k.dn[...] += dot(dh, up, NT)
    dx, dgain = norm_back(k.unit[...], root, gain, k.dn[...])
    gmid = k.gout[...] + dx
    k.gmid[...] = gmid
    k.dgain[...] = jnp.broadcast_to(dgain, k.dgain.shape)
    k.low[...] = gmid.astype(BF)
    if not kept:
        k.pack.proj_copy.wait()
    HW = plan.HW
    for r in range(plan.G):
        per = HW // plan.DR
        grad = dot(k.c[r][...].T, k.low[...]).astype(BF)
        k.dproj[pl.ds(k.idx[plan.at_src + r] * per, per)] = grad.reshape(per, plan.DR, D)
        k.dc[r][...] = dot(k.low[...], k.pack.proj(k.idx[plan.at_dst + r]), NT).astype(BF)


def send_packs(plan, k, copies):
    DR, FR = plan.DR, plan.FR

    def shard(order, r, dc):
        core = lax.rem(k.idx[plan.at_core] + dc, 2)
        return k.idx[plan.at_order[order] + r] * 2 + core

    def upward(j):
        for dc in (1, 0):
            for r in range(plan.chips):
                out = k.packs[2 * dc].at[r, j * DR : (j + 1) * DR, :]
                copies.start(k.dup.at[j, shard("x", r, dc)], out)

    def rest():
        for dc in (1, 0):
            two = k.packs[2 * dc + 1]
            for r in range(plan.chips):
                s = shard("y", r, dc)
                copies.start(k.ddown.at[s], two.at[r, 0:FR, :])
                copies.start(k.dproj.at[s], two.at[r, FR : FR + DR, :])
        copies.finish()

    return upward, rest


def send_whole(plan, k, copies):
    DR, FR, VR = plan.DR, plan.FR, plan.VR
    (out,) = k.packs
    per = CHUNK // FR

    def upward(j):
        copies.start(k.dup.at[j], out.at[:, j * DR : (j + 1) * DR, :])
        at = slice(j * per, (j + 1) * per)
        top = 5 * DR + VR
        copies.start(k.ddown.at[at], out.at[at, top : top + FR, :])

    def rest():
        top = 4 * DR
        copies.start(k.dp3, out.at[:, top : top + DR, :])
        top += DR
        copies.start(k.dtab, out.at[:, top : top + VR, :])
        top += VR + FR
        copies.start(k.dproj, out.at[:, top : top + DR, :])
        copies.finish()

    return upward, rest


def backward_scratch(plan, n):
    return {
        **forward_scratch(plan, n),
        "gout": pltpu.VMEM((n, D), F32),
        "unit": pltpu.VMEM((n, D), F32),
        "normt": pltpu.VMEM((D, n), BF),
        "low": pltpu.VMEM((n, D), BF),
        "dn": pltpu.VMEM((n, D), F32),
        "dup": pltpu.VMEM((FF // CHUNK, plan.seq, plan.DR, CHUNK), BF),
        "ddown": pltpu.VMEM((plan.seq, plan.FR, D), BF),
        "dproj": pltpu.VMEM((plan.seq, plan.DR, D), BF),
    }


def backward_outs(plan, n, extra=False):
    C, DR, FR = plan.chips, plan.DR, plan.FR
    outs = {
        "gmid": sds((n, D), F32),
        "dc": [sds((n, plan.HW), BF)] * plan.G,
        "dgain": sds((8, D), F32),
    }
    if extra:
        return outs, {"packs": [sds((plan.seq, 6 * DR + plan.VR + FR, D), BF)]}
    return outs, {"packs": [sds((C, 4 * DR, D), BF), sds((C, FR + DR, D), BF)] * 2}


def ffn_loss_kernel(plan, k):
    copies = Copies(k.sem)
    k.pack = Pack(plan, copies, k.pack_in, (k.up_scr, k.down_scr, k.proj_scr))
    top = 5 * plan.DR + plan.FR
    k.tab_copy = copies.start(k.pack_in.at[:, top : top + plan.VR, :], k.tab_scr)
    copies.open = []
    attended(plan, k, k.x[...])
    feed_forward(k, 2, k.y[...], keep=True)
    loss_part(plan, k)
    upward, rest = send_whole(plan, k, copies)
    ffn_backward_part(plan, k, 2, k.y[...], upward, kept=True)
    rest()


def joined(refs):
    total = refs[0][...].astype(F32)
    for ref in refs[1:]:
        total += ref[...].astype(F32)
    return total


def join_last_kernel(plan, k):
    copies = Copies(k.sem)
    k.pack = Pack(plan, copies, k.pack_in, (k.up_scr, k.down_scr, k.proj_scr))
    x = k.x[...]
    root = root_of(x)
    dx, dgain = norm_back(x * root, root, k.gains[4:5, :], joined(k.terms))
    grad = k.gnext[...] + dx
    k.second[...] = grad
    k.gout[...] = exact_dot(one_hot(k.cols[:, SLOT : SLOT + 1], CAP).T, grad)
    k.dgain_in[...] = jnp.broadcast_to(dgain, k.dgain_in.shape)
    upward, rest = send_packs(plan, k, copies)
    ffn_backward_part(plan, k, 1, k.y[...], upward)
    rest()


def join_middle_kernel(plan, k):
    copies = Copies(k.sem)
    k.pack = Pack(plan, copies, k.pack_in, (k.up_scr, k.down_scr, k.proj_scr))
    x = k.x[...]
    root = root_of(x)
    dx, dgain = norm_back(x * root, root, k.gains[2:3, :], joined(k.terms))
    member = one_hot(k.cols[:, SLOT : SLOT + 1], CAP)
    counts = jnp.sum(member.T.astype(F32), axis=1, keepdims=True)
    grad = (k.gnext[...] + dx) / jnp.maximum(counts, 1.0)
    k.gout[...] = k.second[...] + k.bound[...] + exact_dot(member, grad)
    k.dgain_in[...] = jnp.broadcast_to(dgain, k.dgain_in.shape)
    upward, rest = send_packs(plan, k, copies)
    ffn_backward_part(plan, k, 0, k.y[...], upward)
    rest()


def bound_kernel(plan, x_ref, cols, gains, pack, *refs):
    grad_out, dp_out, dgain_out, stat, weight_scr, sem = refs
    top = 5 * plan.DR + plan.FR
    copy = Copies(sem).start(pack.at[:, top : top + plan.DR, :], weight_scr)
    x = x_ref[...]
    valid = cols[:, VALID : VALID + 1]
    target = cols[:, TARGET : TARGET + 1]
    root = root_of(x)
    unit = x * root
    gain = gains[7:8, :]
    rows = (unit * gain).astype(BF)
    copy.wait()
    weight = weight_scr[...].reshape(D, D)
    value, slope = gelu_parts(dot(rows, weight))
    out_gain = gains[8:9, :]
    z = jnp.sum(value * out_gain, axis=-1, keepdims=True) * D ** (-0.5)
    small = jnp.exp(-jnp.abs(z))
    soft = jnp.maximum(z, 0.0) + jnp.log(1.0 + small)
    bce = jnp.sum(valid * (soft - target * z), axis=0, keepdims=True)
    sig = jnp.where(z >= 0, 1.0, small) / (1.0 + small)
    dz = valid * (sig - target) * D ** (-0.5)
    dh = (dz * out_gain * slope).astype(BF)
    dp_out[...] = dot(rows.T, dh).astype(BF).reshape(dp_out.shape)
    dx, dgain = norm_back(unit, root, gain, dot(dh, weight, NT))
    grad_out[...] = dx
    dgain_out[0:8, :] = jnp.broadcast_to(dgain, (8, D))
    dgain_out[8:16, :] = jnp.broadcast_to(jnp.sum(dz * value, axis=0, keepdims=True), (8, D))
    stat[...] = at_lane(1, bce)


def tail_kernel(plan, idx, gmid, dtab, table, cols, gains, *refs):
    d1, d2, d3, d4, d5, d6, d78 = refs[:7]
    dw = refs[7 : 7 + plan.chips]
    packs = refs[7 + plan.chips : 7 + 2 * plan.chips]
    tab, gt, turned = refs[7 + 2 * plan.chips :]
    t = table[...].astype(F32)
    root = root_of(t)
    dx, dgain = norm_back(t * root, root, gains[0:1, :], dtab[...])
    hot = one_hot(cols[:, BYTE : BYTE + 1], VOCAB).T
    g = gmid[...]
    high = g.astype(BF)
    tab[...] = dx + (dot(hot, high) + dot(hot, (g - high.astype(F32)).astype(BF)))
    gt[...] = jnp.zeros_like(gt)
    gt[0:1, :] = dgain
    for k, ref in ((1, d1), (2, d2), (3, d3), (4, d4), (5, d5), (6, d6), (7, d78)):
        gt[k : k + 1, :] = ref[0:1, :]
    gt[8:9, :] = d78[8:9, :]
    turned[...] = gt[...].T
    DR, VR, HW = plan.DR, plan.VR, plan.HW
    for r in range(plan.chips):
        k = idx[plan.at_order["x"] + r]
        if 3 * HW < D - 128:
            packs[r][0 : 2 * DR, :] = jnp.zeros((2 * DR, D), BF)
        packs[r][0 : 2 * DR, 0 : 3 * HW] = dw[r][:, 0 : 3 * HW]
        rows = turned[pl.ds(pl.multiple_of(k * 2 * DR, 2 * DR), 2 * DR), :]
        packs[r][0 : 2 * DR, D - 128 : D] = rows.astype(BF)
        rows = tab[pl.ds(pl.multiple_of(k * 2 * VR, 2 * VR), 2 * VR), :]
        packs[r][2 * DR : 2 * DR + 2 * VR, :] = rows.astype(BF)


def adam_update(weight, first, second, grad, rate):
    mean = BETA_FIRST * first + (1.0 - BETA_FIRST) * grad
    meansq = BETA_SECOND * second + (1.0 - BETA_SECOND) * grad * grad
    mean_hat = mean / (1.0 - BETA_FIRST**STEP)
    meansq_hat = meansq / (1.0 - BETA_SECOND**STEP)
    master = weight - rate * (mean_hat / (jnp.sqrt(meansq_hat) + ADAM_EPS) + DECAY_RATE * weight)
    return (master, mean, meansq)


def add(a, b):
    return (a.astype(F32) + b.astype(F32)).astype(BF)


def total_of(terms):
    total = terms[0].astype(F32)
    for term in terms[1:]:
        total = total + term.astype(F32)
    return total.astype(BF)


def sum_first(plan, blocks, axis):
    got = [plan.shift(blocks[d], **{axis: d}) for d in range(1, plan.sizes[axis])]
    return [total_of([b[e] for b in (blocks[0], *got)]) for e in range(blocks[0].shape[0])]


def sum_second(plan, blocks, axis):
    return total_of(
        [blocks[0]] + [plan.shift(blocks[d], **{axis: d}) for d in range(1, plan.sizes[axis])]
    )


def sum_chips(plan, blocks):
    terms = [blocks[0]]
    for r in range(1, plan.chips):
        dx, dy = divmod(r, plan.Y)
        terms.append(plan.shift(blocks[r], x=dx, y=dy))
    return total_of(terms)


def head_sum(plan, v, axis):
    return add(v, plan.shift(v, **{axis: 1}))


def split_axes(plan, t, first, second):
    return t.reshape((plan.sizes[first], plan.sizes[second]) + t.shape[1:])


def by_core(first, second):
    halves = [v.reshape((2, v.shape[0] // 2) + v.shape[1:]) for v in (first, second)]
    return jnp.concatenate(halves, axis=1)


def exchange_columns(plan, v, me):
    own = lax.dynamic_index_in_dim(v, me["core"], 0, keepdims=False)
    other = lax.dynamic_index_in_dim(v, 1 - me["core"], 0, keepdims=False)
    parts = [own] + [plan.shift(own, zl=d) for d in range(1, plan.L)]
    return parts + [plan.shift(other, core=1, zl=d) for d in range(plan.L)]


def final_kernel(plan, idx, *refs):
    DR, FR, VR, HW, G = plan.DR, plan.FR, plan.VR, plan.HW, plan.G
    shards = [refs[2 * layer : 2 * layer + 2] for layer in range(3)]
    refs = refs[6:]
    columns0, columns12, stat_in = refs[:G], refs[G : 2 * G], refs[2 * G]
    qkv, proj, up, down, table, gain, stat, scr0, scr12 = refs[2 * G + 1 :]
    for r in range(G):
        b = idx[plan.at_src + r]
        scr0[b] = columns0[r][...]
        scr12[b] = columns12[r][...]
    for b in range(G):
        for part in range(3):
            src = slice(part * HW, (part + 1) * HW)
            dst = slice(part * D + b * HW, part * D + (b + 1) * HW)
            qkv[0, :, dst] = scr0[b, 0:DR, src]
            qkv[1, :, dst] = scr12[b, 0:DR, src]
            qkv[2, :, dst] = scr12[b, DR : 2 * DR, src]
    tab = scr0[0, DR : DR + VR, :].astype(F32)
    gains = scr0[0, 0:DR, D - 128 : D].astype(F32)
    for b in range(1, G):
        tab += scr0[b, DR : DR + VR, :].astype(F32)
        gains += scr0[b, 0:DR, D - 128 : D].astype(F32)
    gain[...] = gains
    table[0] = tab
    for layer in range(3):
        one, two = shards[layer]
        for j in range(4):
            up[layer, :, j * CHUNK : (j + 1) * CHUNK] = one[j * DR : (j + 1) * DR, :]
        top = 0
        if layer == 2:
            proj[3] = two[0:DR, :]
            table[1] = two[DR : DR + VR, :].astype(F32)
            top = DR + VR
        down[layer] = two[top : top + FR, :]
        proj[layer] = two[top + FR : top + FR + DR, :]
    total = jnp.zeros((1, 1), F32)
    for ref in (qkv, proj, up, down, table, gain):
        pieces = [ref[...]] if len(ref.shape) == 2 else [ref[l] for l in range(ref.shape[0])]
        for piece in pieces:
            v = piece.astype(F32)
            total += jnp.sum(jnp.sum(v * v, axis=0, keepdims=True), axis=1, keepdims=True)
    stat[...] = stat_in[...] + at_lane(6, total)


def per_device(plan, *args):
    (
        byte_ids,
        next_bytes,
        loss_mask,
        pool_slots,
        qkv_weight,
        proj_weight,
        upward_weight,
        downward_weight,
        table_weight,
        gain_weight,
        qkv_first,
        qkv_second,
        proj_first,
        proj_second,
        upward_first,
        upward_second,
        downward_first,
        downward_second,
        table_first,
        table_second,
        gain_first,
        gain_second,
    ) = args
    G, L, HW, QW, DR, FR, VR = plan.G, plan.L, plan.HW, plan.QW, plan.DR, plan.FR, plan.VR
    n = byte_ids.shape[1]
    length = n * G
    me = plan.place()
    idx = plan.tables()
    core = me["core"]

    width0, width1 = QW + 384, 2 * QW
    keep0, send0, keep1, send1 = run(
        "first",
        functools.partial(first_kernel, plan),
        [sds((DR, width0), BF)] * 2 + [sds((DR, width1), BF)] * 2,
        [idx],
        [qkv_weight, table_weight, gain_weight],
        [pltpu.VMEM((128, 128), F32)],
    )
    ints = jnp.concatenate([byte_ids, next_bytes, loss_mask, pool_slots], axis=0)
    ints = jnp.concatenate([ints, jnp.zeros_like(ints)], axis=0)

    def chip_rows(keep, got):
        return jnp.where(
            core == 0,
            jnp.concatenate([keep, got], axis=0),
            jnp.concatenate([got, keep], axis=0),
        )

    def gather_first(v):
        by_x = [plan.shift(v, x=d) for d in range(1, plan.X)]
        by_y = [plan.shift(v, y=d) for d in range(1, plan.Y)]
        return by_x, by_y

    def gather_second(v, by_x, by_y):
        out = [v, *by_x]
        for d in range(1, plan.Y):
            out += [by_y[d - 1], *[plan.shift(p, y=d) for p in by_x]]
        return out

    def swap(c):
        return {**c, "core": c["zh"], "zh": c["core"]}

    got0, got1, own = fence(
        plan.shift(send0, core=1), plan.shift(send1, core=1), plan.permute(ints, swap)
    )
    chip0 = chip_rows(keep0, got0)
    chip1 = chip_rows(keep1, got1)
    (by_x, by_y), both, chip1 = fence(
        gather_first(chip0), jnp.concatenate([own, plan.shift(own, core=1)]), chip1
    )
    early = gather_second(chip0, by_x, by_y)
    pairs = [both] + [plan.shift(both, zl=d) for d in range(1, L)]
    ints_all = jnp.concatenate([p[:8] for p in pairs] + [p[8:] for p in pairs])

    def pack_of(layer, after):
        rows = 5 * DR + FR + (0, DR, VR)[layer]
        (pack,) = run(
            "pack",
            functools.partial(pack_kernel, plan, layer),
            [sds((rows, D), BF)],
            [],
            [],
            [
                pltpu.VMEM((DR, FF), F32),
                pltpu.VMEM((FR, D), F32),
                pltpu.VMEM((2, DR, D), F32),
                pltpu.VMEM((VR, D), F32),
            ],
            raw=[upward_weight, downward_weight, proj_weight, table_weight],
            sems=5,
            after=after,
        )
        return pack

    def gather_pack(pack):
        return lax.all_gather(pack, "seq", axis=0, tiled=False)

    packs = [gather_pack(pack_of(0, [keep0]))]

    table, atab, gains, cols = run(
        "tables",
        functools.partial(prep_kernel, plan),
        [sds((VOCAB, D), BF), sds((VOCAB, D), BF), sds((16, D), F32), sds((n, 128), F32)],
        [idx],
        [own, *early],
        [pltpu.VMEM((VOCAB, D), F32), pltpu.VMEM((D, 128), F32), pltpu.VMEM((128, n), F32)],
    )
    half = np.arange(HALF, dtype=np.float32) / np.float32(HALF)
    frequency = np.float32(10000.0) ** (-half)
    angles = frequency[:, None] * np.arange(length, dtype=np.float32)[None, :]
    cos = jnp.asarray(np.cos(angles.astype(np.float64)).astype(np.float32))
    sin = jnp.asarray(np.sin(angles.astype(np.float64)).astype(np.float32))

    def exchange(parts):
        out = [parts[0]]
        for r in range(1, G):
            dc, dl = divmod(r, L)
            out.append(plan.shift(parts[r], core=dc, zl=dl))
        return out

    def gather_near(a):
        return [a] + [plan.shift(a, zl=d) for d in range(1, L)]

    def gather_far(near):
        return near + [plan.shift(p, core=1) for p in near]

    def scatter_group(das):
        terms = [das[0], plan.shift(das[L], core=1)]
        for d in range(1, L):
            both = add(das[d], plan.shift(das[L + d], core=1))
            terms.append(plan.shift(both, zl=d))
        return terms

    early, table, atab, gains, cols, ints_all, chip1 = fence(
        early, table, atab, gains, cols, ints_all, chip1
    )
    late = gather_first(chip1)
    c0, saved0 = attn_forward(plan, idx, cos, sin, [ints_all, atab], early, 0, n, True, False)
    c0, saved0, late = fence(c0, saved0, late)
    packs.append(gather_pack(pack_of(1, [c0[0]])))
    c0, late = fence(exchange(c0), gather_second(chip1, *late))
    dense = 2 * D * (D + 2 * FF)
    res = run_named(
        "ffn_pool",
        functools.partial(ffn_pool_kernel, plan),
        {
            "y": sds((n, D), F32),
            "x": sds((n, D), F32),
            "pooled": sds((CAP, D), F32),
            "a": sds((CAP, D), BF),
            "stat": sds((8, 128), F32),
        },
        {"c": c0, "cols": cols, "table": table, "gains": gains},
        forward_scratch(plan, n),
        {"pack_in": packs[0]},
        {},
        idx,
        16,
        n * dense,
        n * FF,
    )
    y0, x1, pooled, a1, stat = res.y, res.x, res.pooled, res.a, res.stat
    packs.append(gather_pack(pack_of(2, [a1])))
    a1 = gather_far(gather_near(a1))
    c1, saved1 = attn_forward(plan, idx, cos, sin, [*a1, ints_all], late, 0, CAP, False, True)
    c1, saved1 = fence(c1, saved1)
    c1 = exchange(c1)
    res = run_named(
        "ffn_unpool",
        functools.partial(ffn_unpool_kernel, plan),
        {
            "y": sds((CAP, D), F32),
            "x": sds((n, D), F32),
            "a": sds((n, D), BF),
            "stat": sds((8, 128), F32),
        },
        {"c": c1, "pooled": pooled, "x1": x1, "cols": cols, "gains": gains, "stat_in": stat},
        forward_scratch(plan, CAP),
        {"pack_in": packs[1]},
        {},
        idx,
        16,
        CAP * dense,
        CAP * FF,
    )
    y1, x2, a2, stat = res.y, res.x, res.a, res.stat
    bound_grad, dp3, dgain78, stat_b = run(
        "boundary",
        functools.partial(bound_kernel, plan),
        [sds((n, D), F32), sds((plan.seq, DR, D), BF), sds((16, D), F32), sds((8, 128), F32)],
        [],
        [x1, cols, gains],
        [pltpu.VMEM((plan.seq, DR, D), BF)],
        raw=[packs[1]],
        sems=1,
        flops=6 * n * D * D,
        trans=n * D,
    )
    a2, bound_grad, dp3, dgain78, stat_b = fence(
        gather_near(a2), bound_grad, dp3, dgain78, stat_b
    )
    a2 = gather_far(a2)
    c2, saved2 = attn_forward(plan, idx, cos, sin, a2, late, QW, n, False, False)
    c2 = exchange(c2)

    source0 = [ints_all, atab]
    swaps = plan.head == 4
    cut = 4 * DR

    def swap_first(v):
        if not swaps:
            return [lax.psum(v[:cut], "head"), lax.psum(v[cut:], "head")]
        return [head_sum(plan, v[:cut], "zl"), head_sum(plan, v[cut:], "zh")]

    def swap_second(parts):
        if not swaps:
            return parts
        return [head_sum(plan, parts[0], "zh"), head_sum(plan, parts[1], "zl")]

    axes = (("x", "y"), ("y", "x"))

    def core_sums(packs, rider=None):
        out = []
        for mine, theirs, ax in zip(packs[:2], packs[2:], axes):
            got = split_axes(plan, plan.shift(theirs, core=1), *ax)
            mine = split_axes(plan, mine, *ax)
            out.append([add(mine[d], got[d]) for d in range(mine.shape[0])])
        if rider is None:
            return out
        rider = split_axes(plan, jnp.stack(rider), *axes[0])
        out[0] = [jnp.concatenate([v, rider[d]], axis=1) for d, v in enumerate(out[0])]
        return out

    def first_sums(halves):
        return [sum_first(plan, half, ax[0]) for half, ax in zip(halves, axes)]

    def second_sums(halves):
        return [sum_second(plan, half, ax[1]) for half, ax in zip(halves, axes)]

    outs, raw_outs = backward_outs(plan, n, extra=True)
    res = run_named(
        "ffn_loss",
        functools.partial(ffn_loss_kernel, plan),
        {**outs, "dgain6": sds((8, D), F32), "stat": sds((8, 128), F32)},
        {
            "c": c2,
            "x": x2,
            "cols": cols,
            "gains": gains,
            "stat_a": stat,
            "stat_b": stat_b,
            "dp3": dp3,
        },
        {
            **backward_scratch(plan, n),
            "slope": pltpu.VMEM((FF // CHUNK, n, CHUNK), F32),
            "y": pltpu.VMEM((n, D), F32),
            "tab_scr": pltpu.VMEM((plan.seq, VR, D), BF),
            "dtab": pltpu.VMEM((plan.seq, VR, D), BF),
        },
        {"pack_in": packs[2]},
        raw_outs,
        idx,
        20 + 8 * plan.seq,
        2 * n * D * (3 * D + 6 * FF),
        n * FF,
    )
    gmid2, dc2, dgain5, dgain6, stat = res.gmid, res.dc, res.dgain, res.dgain6, res.stat
    shard2 = lax.psum_scatter(res.packs[0], "seq", scatter_dimension=0)
    dc2, stat = fence(exchange(dc2), stat)
    dw2, das = attn_backward(
        plan, idx, cos, sin, a2, late, QW, dc2, saved2, n, False, False
    )
    dw2, das, stat = fence(dw2, das, stat + plan.shift(stat, zh=1))
    terms, stat = fence(scatter_group(das), stat)
    outs, raw_outs = backward_outs(plan, CAP)
    res = run_named(
        "join_last",
        functools.partial(join_last_kernel, plan),
        {**outs, "second": sds((n, D), F32), "dgain_in": sds((8, D), F32)},
        {
            "terms": terms,
            "gnext": gmid2,
            "x": x2,
            "cols": cols,
            "gains": gains,
            "y": y1,
            "c": c1,
        },
        backward_scratch(plan, CAP),
        {"pack_in": packs[1]},
        raw_outs,
        idx,
        16 + 8 * plan.seq,
        2 * CAP * D * (2 * D + 5 * FF),
        CAP * FF,
    )
    gmid1, dc1, packs1, dgain3, dgain4 = res.gmid, res.dc, res.packs, res.dgain, res.dgain_in
    gsecond = res.second
    stat = stat + sum(plan.shift(stat, zl=d) for d in range(1, L))
    dc1, packs1, dw2, stat = fence(dc1, packs1, dw2, stat)
    dc1, half1, shard2 = fence(exchange(dc1), core_sums(packs1, dw2), shard2)
    dw1, das = attn_backward(
        plan, idx, cos, sin, [*a1, ints_all], late, 0, dc1, saved1, CAP, False, True
    )
    dw1, das, half1, shard2 = fence(dw1, das, first_sums(half1), swap_first(shard2))
    terms, half1, dw1, shard2 = fence(scatter_group(das), second_sums(half1), dw1, shard2)
    dw2 = half1[0][4 * DR :]
    shard1 = jnp.concatenate([half1[0][: 4 * DR], half1[1]], axis=0)
    outs, raw_outs = backward_outs(plan, n)
    res = run_named(
        "join_middle",
        functools.partial(join_middle_kernel, plan),
        {**outs, "dgain_in": sds((8, D), F32)},
        {
            "terms": terms,
            "gnext": gmid1,
            "x": pooled,
            "cols": cols,
            "gains": gains,
            "second": gsecond,
            "bound": bound_grad,
            "y": y0,
            "c": c0,
        },
        backward_scratch(plan, n),
        {"pack_in": packs[0]},
        raw_outs,
        idx,
        16 + 8 * plan.seq,
        2 * n * D * (2 * D + 5 * FF),
        n * FF,
    )
    gmid0, dc0, packs0, dgain1, dgain2 = res.gmid, res.dc, res.packs, res.dgain, res.dgain_in
    shard2 = swap_second(shard2)
    dw1 = sum_chips(plan, dw1)
    dc0, packs0, dw1, dw2, shard1, shard2 = fence(dc0, packs0, dw1, dw2, shard1, shard2)
    dc0, half0, dw12, shard1 = fence(
        exchange(dc0), core_sums(packs0), jnp.concatenate([dw1, dw2], axis=0), shard1
    )
    dw0, (dtab0,) = attn_backward(
        plan, idx, cos, sin, [ints_all, atab], early, 0, dc0, saved0, n, True, False
    )
    dw0, dtab0, half0, dw12, shard1 = fence(
        dw0, dtab0, first_sums(half0), head_sum(plan, dw12, "zh"), swap_first(shard1)
    )
    tail = run(
        "tail",
        functools.partial(tail_kernel, plan),
        [sds((2 * DR + 2 * VR, D), BF)] * plan.chips,
        [idx],
        [
            *(gmid0, dtab0, table, cols, gains),
            *(dgain1, dgain2, dgain3, dgain4, dgain5, dgain6, dgain78),
            *dw0,
        ],
        [pltpu.VMEM((VOCAB, D), F32), pltpu.VMEM((128, D), F32), pltpu.VMEM((D, 128), F32)],
        flops=4 * n * VOCAB * D,
    )
    tail, half0, shard1 = fence(tail, second_sums(half0), swap_second(shard1))
    shard0 = jnp.concatenate(half0, axis=0)
    columns12 = exchange_columns(plan, by_core(dw12[: 2 * DR], dw12[2 * DR :]), me)
    tail, shard0 = fence(sum_chips(plan, tail), swap_first(shard0))
    tail, shard0, columns12 = fence(
        head_sum(plan, tail, "zh"), swap_second(shard0), columns12
    )
    columns0 = exchange_columns(plan, by_core(tail[: 2 * DR], tail[2 * DR :]), me)
    matrix_grad = functools.partial(sds, dtype=BF)
    *grads, gain_t, stat = run(
        "gradients",
        functools.partial(final_kernel, plan),
        [
            matrix_grad(qkv_weight.shape),
            matrix_grad(proj_weight.shape),
            matrix_grad(upward_weight.shape),
            matrix_grad(downward_weight.shape),
            sds(table_weight.shape, F32),
            sds((DR, 128), F32),
            sds((8, 128), F32),
        ],
        [idx],
        [*shard0, *shard1, *shard2, *columns0, *columns12, stat],
        [pltpu.VMEM((G, DR + VR, D), BF), pltpu.VMEM((G, 2 * DR, D), BF)],
        limit=40,
    )
    totals = lax.psum(stat, "seq")[0]
    grads = [grad.astype(F32) for grad in grads]
    valid_count = totals[5]
    inverse = 1.0 / valid_count
    grad_norm = jnp.sqrt(totals[6]) * inverse
    clip = jnp.minimum(1.0, CLIP_NORM / (grad_norm + 1e-06)) * inverse
    weights = (qkv_weight, proj_weight, upward_weight, downward_weight, table_weight)
    firsts = (qkv_first, proj_first, upward_first, downward_first, table_first)
    seconds = (qkv_second, proj_second, upward_second, downward_second, table_second)
    rates = (RATE_MATRIX,) * 4 + (RATE_VECTOR,)
    new = [
        adam_update(w, a, b, g * clip, rate)
        for w, a, b, g, rate in zip(weights, firsts, seconds, grads, rates)
    ]
    new.append(
        run(
            "gains",
            gain_kernel,
            [sds(gain_weight.shape, F32)] * 3,
            [clip.reshape(1)],
            [gain_t, gain_weight, gain_first, gain_second],
        )
    )
    residual_rms = jnp.sqrt(totals[2:5] / (valid_count * D))
    return (
        *[part for triple in new for part in triple],
        *[triple[0].astype(BF) for triple in new[:5]],
        totals[:2],
        valid_count,
        grad_norm,
        residual_rms,
    )


def solution(mesh):
    plan = Plan(mesh)
    tokens = P("seq", "head")
    matrix = P(None, "seq", None)
    vector = P(None, "seq")
    states = (matrix,) * 10 + (vector,) * 2
    return jax.shard_map(
        functools.partial(per_device, plan),
        mesh=mesh,
        in_specs=(tokens,) * 4 + (matrix,) * 5 + (vector,) + states,
        out_specs=(matrix,) * 15 + (vector,) * 3 + (matrix,) * 5 + (P(),) * 4,
        check_vma=False,
    )
```

```python
import functools
import math
from types import SimpleNamespace

import jax
import jax.numpy as jnp
import numpy as np
from jax import lax
from jax.experimental import pallas as pl
from jax.experimental.pallas import tpu as pltpu
from jax.sharding import PartitionSpec as P

D = 512
HEADS = 8
FF = 2048
VOCAB = 256
HEAD_DIM = 64
CAP = 256
STEP = 10
CHUNK = 512
HALF = HEAD_DIM // 2

NORM_EPS = 1e-06
BETA_FIRST = 0.9
BETA_SECOND = 0.95
ADAM_EPS = 1e-08
DECAY_RATE = 0.1
RATE_MATRIX = 0.05
RATE_VECTOR = 0.5
CLIP_NORM = 0.01
MASKED = -1000000000.0
SCALE = HEAD_DIM ** (-0.5)
GELU_A = math.sqrt(2.0 / math.pi)
GELU_B = 0.044715

BF = jnp.bfloat16
F32 = jnp.float32
NN = (((1,), (0,)), ((), ()))
NT = (((1,), (1,)), ((), ()))
AXES = ("seq", "head")
HB = pl.BlockSpec(memory_space=pltpu.HBM)
SM = pl.BlockSpec(memory_space=pltpu.SMEM)


def dot(a, b, dims=NN):
    return lax.dot_general(a, b, dims, preferred_element_type=F32)


def split3(v):
    high = v.astype(BF)
    rest = v - high.astype(F32)
    mid = rest.astype(BF)
    low = (rest - mid.astype(F32)).astype(BF)
    return (high, mid, low)


def exact_dot(ones, v):
    high, mid, low = split3(v)
    return dot(ones, high) + (dot(ones, mid) + dot(ones, low))


def root_of(v):
    return lax.rsqrt(jnp.mean(v * v, axis=-1, keepdims=True) + NORM_EPS)


def norm_back(unit, root, gain, grad):
    turned = grad * gain
    dx = root * (turned - unit * jnp.mean(turned * unit, axis=-1, keepdims=True))
    return dx, jnp.sum(grad * unit, axis=0, keepdims=True)


def gelu_parts(h):
    square = h * h
    t = jnp.tanh(GELU_A * h * (1.0 + GELU_B * square))
    half = 0.5 * (1.0 + t)
    value = h * half
    slope = half + 0.5 * h * (1.0 - t * t) * (GELU_A * (1.0 + 3.0 * GELU_B * square))
    return value, slope


def gelu_value(h):
    t = jnp.tanh(GELU_A * h * (1.0 + GELU_B * (h * h)))
    return h * (0.5 * (1.0 + t))


def one_hot(column, width):
    lanes = lax.broadcasted_iota(jnp.int32, (column.shape[0], width), 1).astype(F32)
    return (lanes == column).astype(F32).astype(BF)


class Plan:
    def __init__(self, mesh):
        self.seq = mesh.shape["seq"]
        self.head = mesh.shape["head"]
        self.chips = self.seq // 2
        side = int(math.isqrt(self.chips))
        while self.chips % side:
            side -= 1
        self.Y, self.X = side, self.chips // side
        self.L = self.head // 2
        self.G = self.head
        self.hd = HEADS // self.G
        self.HW = self.hd * HEAD_DIM
        self.QW = -(-3 * self.HW // 128) * 128
        self.DR = D // self.seq
        self.FR = FF // self.seq
        self.VR = VOCAB // self.seq
        self.sizes = {"y": self.Y, "x": self.X, "core": 2, "zh": 2, "zl": self.L}
        self.names = ("y", "x", "core", "zh", "zl")

    def coords(self):
        for linear in range(self.seq * self.head):
            s, z = divmod(linear, self.head)
            yx, core = divmod(s, 2)
            y, x = divmod(yx, self.X)
            zh, zl = divmod(z, self.L)
            yield linear, {"y": y, "x": x, "core": core, "zh": zh, "zl": zl}

    def linear(self, c):
        s = (c["y"] * self.X + c["x"]) * 2 + c["core"]
        return s * self.head + c["zh"] * self.L + c["zl"]

    def permute(self, v, to):
        pairs = []
        for here, c in self.coords():
            there = to(c)
            if there is not None:
                pairs.append((here, self.linear(there)))
        return lax.ppermute(v, AXES, pairs)

    def shift(self, v, **steps):
        def to(c):
            return {k: (c[k] + steps.get(k, 0)) % self.sizes[k] for k in self.names}

        return self.permute(v, to)

    def place(self):
        s = lax.axis_index("seq")
        z = lax.axis_index("head")
        yx, core = s // 2, s % 2
        return {
            "y": yx // self.X,
            "x": yx % self.X,
            "core": core,
            "zh": z // self.L,
            "zl": z % self.L,
        }

    def tables(self):
        me = self.place()
        G, L, Y, X = self.G, self.L, self.Y, self.X

        def block(sign):
            return [
                ((me["core"] + sign * dc) % 2) * L + (me["zl"] + sign * dl) % L
                for dc in range(2)
                for dl in range(L)
            ]

        def chip(dy, dx):
            return ((me["y"] + dy) % Y) * X + (me["x"] + dx) % X

        chip_src = [chip(-dy, -dx) for dy in range(Y) for dx in range(X)]
        by_x = [chip(dy, dx) for dx in range(X) for dy in range(Y)]
        by_y = [chip(dy, dx) for dy in range(Y) for dx in range(X)]
        entries = [me["core"], me["zl"]] + block(1) + block(-1) + chip_src + by_x + by_y
        self.at_core = 0
        self.at_zl = 1
        self.at_dst = 2
        self.at_src = 2 + G
        self.at_chip = 2 + 2 * G
        self.at_order = {"x": 2 + 2 * G + Y * X, "y": 2 + 2 * G + 2 * Y * X}
        return jnp.stack([jnp.asarray(e, jnp.int32) for e in entries])


def run(
    name,
    body,
    outs,
    smem,
    arrays,
    scratch=(),
    raw=(),
    raw_outs=(),
    sems=0,
    flops=0,
    trans=0,
    limit=60,
    after=(),
):
    operands = [*arrays, *raw]
    results = [*outs, *raw_outs]
    nbytes = sum(a.size * a.dtype.itemsize for a in operands)
    nbytes += sum(math.prod(o.shape) * jnp.dtype(o.dtype).itemsize for o in results)
    ns, ni, nr, na, no, nx = map(len, (smem, arrays, raw, after, outs, raw_outs))

    def wrapped(*refs):
        at = 0
        parts = []
        for count in (ns, ni, nr, na, no, nx, ni, no, len(scratch)):
            parts.append(refs[at : at + count])
            at += count
        s_refs, ins, raws, _, results_out, raws_out, bufs, out_bufs, own = parts
        sem = refs[at]
        copies = [
            pltpu.make_async_copy(src, dst, sem.at[k])
            for k, (src, dst) in enumerate(zip(ins, bufs))
        ]
        for copy in copies:
            copy.start()
        for copy in copies:
            copy.wait()
        extra = (refs[at + 1],) if sems else ()
        body(*s_refs, *bufs, *raws, *out_bufs, *raws_out, *own, *extra)
        copies = [
            pltpu.make_async_copy(src, dst, sem.at[k])
            for k, (src, dst) in enumerate(zip(out_bufs, results_out))
        ]
        for copy in copies:
            copy.start()
        for copy in copies:
            copy.wait()

    spaces = [pltpu.VMEM(v.shape, v.dtype) for v in (*arrays, *outs)]
    spaces += list(scratch) + [pltpu.SemaphoreType.DMA((max(ni, no, 1),))]
    if sems:
        spaces.append(pltpu.SemaphoreType.DMA((sems,)))
    return pl.pallas_call(
        wrapped,
        out_shape=tuple(results),
        in_specs=[SM] * ns + [HB] * (ni + nr) + [pl.BlockSpec(memory_space=pl.ANY)] * na,
        out_specs=tuple([HB] * len(results)),
        scratch_shapes=spaces,
        compiler_params=pltpu.CompilerParams(vmem_limit_bytes=limit << 20),
        cost_estimate=pl.CostEstimate(
            flops=int(flops), bytes_accessed=int(nbytes), transcendentals=int(trans)
        ),
        name=name,
    )(*smem, *operands, *after)


def run_named(name, body, outs, arrays, scratch, raw, raw_outs, idx, sems, flops, trans):
    def flat(group):
        out = []
        for value in group.values():
            out += list(value) if isinstance(value, (list, tuple)) else [value]
        return out

    def name_all(space, group, refs):
        for key, value in group.items():
            if isinstance(value, (list, tuple)):
                setattr(space, key, [refs.pop(0) for _ in value])
            else:
                setattr(space, key, refs.pop(0))

    def wrapped(idx_ref, *refs):
        space, refs = SimpleNamespace(idx=idx_ref), list(refs)
        for group in (arrays, raw, outs, raw_outs, scratch):
            name_all(space, group, refs)
        space.sem = refs.pop(0)
        body(space)

    res = list(
        run(
            name,
            wrapped,
            flat(outs),
            [idx],
            flat(arrays),
            flat(scratch),
            flat(raw),
            flat(raw_outs),
            sems,
            flops,
            trans,
        )
    )
    space = SimpleNamespace()
    for group in (outs, raw_outs):
        name_all(space, group, res)
    return space


def fence(*groups):
    return lax.optimization_barrier(groups)


class Copies:
    def __init__(self, sem):
        self.sem = sem
        self.count = 0
        self.open = []

    def start(self, src, dst):
        copy = pltpu.make_async_copy(src, dst, self.sem.at[self.count])
        self.count += 1
        copy.start()
        self.open.append(copy)
        return copy

    def finish(self):
        for copy in self.open:
            copy.wait()
        self.open = []


def rows_at(index, size):
    return pl.ds(pl.multiple_of(index * size, size), size)


def sds(shape, dtype):
    return jax.ShapeDtypeStruct(shape, dtype)


def first_kernel(plan, idx, qkv, table, gain, *refs):
    keep0, send0, keep1, send1, scr = refs
    DR, VR, HW, QW = plan.DR, plan.VR, plan.HW, plan.QW
    core, zl = idx[plan.at_core], idx[plan.at_zl]
    for which, outs in ((0, (keep0, keep1)), (1, (send0, send1))):
        block = lax.rem(core + which, 2) * plan.L + zl
        for layer in range(3):
            out, lo = ((outs[0], 0), (outs[1], 0), (outs[1], QW))[layer]
            for part in range(3):
                if HW % 128 == 0:
                    at = pl.ds(pl.multiple_of(part * D + block * HW, HW), HW)
                    piece = qkv[layer, :, at]
                else:
                    at = pl.ds(pl.multiple_of(part * D + block // 2 * 128, 128), 128)
                    both = qkv[layer, :, at]
                    piece = jnp.where(block % 2 == 0, both[:, :HW], both[:, HW:])
                out[:, lo + part * HW : lo + (part + 1) * HW] = piece.astype(BF)
    scr[...] = jnp.zeros_like(scr)
    scr[0 : gain.shape[0], 0:DR] = gain[...]
    turned = scr[...].T[0:DR, :].astype(BF)
    low = table[0].astype(BF)
    for out in (keep0, send0):
        out[:, QW : QW + 256] = jnp.concatenate([low[:, :256], low[:, 256:]], axis=0)
        out[:, QW + 256 : QW + 384] = turned


class PackCast:
    def __init__(self, plan, layer, copies, sources, scr):
        self.plan, self.layer = plan, layer
        up, down, proj, table = sources
        self.up, self.down, self.proj, self.table = scr
        self.copies = [
            copies.start(up.at[layer], self.up),
            copies.start(down.at[layer], self.down),
            copies.start(proj.at[layer], self.proj.at[0]),
        ]
        if layer == 1:
            self.copies.append(copies.start(proj.at[3], self.proj.at[1]))
        if layer == 2:
            self.copies.append(copies.start(table.at[1], self.table))
        copies.open = []

    @staticmethod
    def rows(plan, layer):
        return 5 * plan.DR + plan.FR + (0, plan.DR, plan.VR)[layer]

    @staticmethod
    def scratch(plan):
        return [
            pltpu.VMEM((plan.DR, FF), F32),
            pltpu.VMEM((plan.FR, D), F32),
            pltpu.VMEM((2, plan.DR, D), F32),
            pltpu.VMEM((plan.VR, D), F32),
        ]

    def write(self, out):
        DR, FR, VR = self.plan.DR, self.plan.FR, self.plan.VR
        for copy in self.copies:
            copy.wait()
        for j in range(FF // CHUNK):
            at = slice(j * CHUNK, (j + 1) * CHUNK)
            out[j * DR : (j + 1) * DR, :] = self.up[:, at].astype(BF)
        top = 4 * DR
        out[top : top + FR, :] = self.down[...].astype(BF)
        top += FR
        out[top : top + DR, :] = self.proj[0].astype(BF)
        top += DR
        if self.layer == 1:
            out[top : top + DR, :] = self.proj[1].astype(BF)
        if self.layer == 2:
            out[top : top + VR, :] = self.table[...].astype(BF)


def pack_kernel(plan, layer, up, down, proj, table, out, *scr):
    *scr, sem = scr
    PackCast(plan, layer, Copies(sem), (up, down, proj, table), scr).write(out)


def gain_kernel(factor, gt, weight, first, second, master_out, mean_out, meansq_out):
    rows, width = weight.shape
    grad = gt[...].T[0:rows, 0:width] * factor[0]
    master, mean, meansq = adam_update(weight[...], first[...], second[...], grad, RATE_VECTOR)
    master_out[...] = master
    mean_out[...] = mean
    meansq_out[...] = meansq


def prep_kernel(plan, idx, ints, *refs):
    pieces = refs[: plan.chips]
    table_out, atab_out, gain_out, cols_out, table_scr, gain_scr, row_scr = refs[plan.chips :]
    slots = ints[3:4, :].astype(F32)
    n = slots.shape[1]
    lanes = lax.broadcasted_iota(jnp.int32, (1, n), 1)
    row_scr[...] = jnp.zeros_like(row_scr)
    row_scr[VALID : VALID + 1, :] = ints[2:3, :].astype(F32)
    changed = jnp.concatenate([slots[:, 0:1], slots[:, 0 : n - 1]], axis=1) != slots
    row_scr[TARGET : TARGET + 1, :] = jnp.where((lanes == 0) | changed, 1.0, 0.0)
    row_scr[NEXT : NEXT + 1, :] = ints[1:2, :].astype(F32)
    row_scr[SLOT : SLOT + 1, :] = slots
    row_scr[BYTE : BYTE + 1, :] = ints[0:1, :].astype(F32)
    cols_out[...] = row_scr[...].T
    VR, DR, QW = plan.VR, plan.DR, plan.QW
    for r in range(plan.chips):
        k = idx[plan.at_chip + r]
        for core in range(2):
            for half in range(2):
                rows = pieces[r][core * DR + half * VR : core * DR + (half + 1) * VR, QW : QW + 256]
                table_scr[
                    pl.ds(pl.multiple_of(k * 2 * VR, 2 * VR) + core * VR, VR),
                    half * 256 : half * 256 + 256,
                ] = rows.astype(F32)
        gain_scr[pl.ds(pl.multiple_of(k * 2 * DR, 2 * DR), 2 * DR), :] = pieces[r][
            :, QW + 256 : QW + 384
        ].astype(F32)
    gains = gain_scr[...].T[0:16, :]
    gain_out[...] = gains
    table = table_scr[...]
    table_out[...] = table.astype(BF)
    atab_out[...] = (table * root_of(table) * gains[0:1, :]).astype(BF)


def load_weight(plan, copies, idx, pieces, lo, w_scr):
    started = []
    for r in range(plan.chips):
        src = pieces[r].at[:, lo : lo + plan.QW]
        started.append(copies.start(src, w_scr.at[rows_at(idx[plan.at_chip + r], 2 * plan.DR), :]))
    return started


def live_bias(plan, idx, ints, n, bias_scr):
    row = lax.broadcasted_iota(jnp.int32, (n, 128), 0).astype(F32)
    for r in range(plan.G):
        slots = ints[8 * r + 3 : 8 * r + 4, :].astype(F32)
        last = jnp.max(slots, axis=1, keepdims=True)
        bias_scr[rows_at(idx[plan.at_src + r], n), :] = jnp.where(row <= last, 0.0, MASKED)


def head_pad(plan, part, h):
    if plan.hd == 1:
        return part
    blank = jnp.zeros_like(part)
    return jnp.concatenate([part if k == h else blank for k in range(plan.hd)], axis=0)


def rot_pair(a, b, cos, sin):
    return a * cos - b * sin, b * cos + a * sin


def attn_fwd_kernel(plan, n, lo, embed, masked, rider, idx, *refs):
    G, HW, hd = plan.G, plan.HW, plan.hd
    S = G * n
    refs = list(refs)
    cos_ref, sin_ref = refs[0], refs[1]
    refs = refs[2:]
    if embed:
        ints_ref, atab_ref = refs[0], refs[1]
        refs = refs[2:]
    else:
        a_refs = refs[:G]
        refs = refs[G:]
    if masked:
        ints_ref = refs[0]
        refs = refs[1:]
    w_refs = refs[: plan.chips]
    refs = refs[plan.chips :]
    if rider:
        rider_in, refs = refs[:4], refs[4:]
    c_outs = refs[:G]
    qkvt_out, ot_out, lse_out = refs[G : G + 3]
    refs = refs[G + 3 :]
    if rider:
        rider_out, refs = refs[0], refs[1:]
    w_scr, cos_scr, sin_scr, src_scr, tab_scr, ints_scr, bias_scr = refs[:7]
    qkvt, ot, lse, k_scr, c_scr = refs[7:12]
    *rider_scr, sem = refs[12:]
    copies = Copies(sem)
    first = load_weight(plan, copies, idx, w_refs, lo, w_scr)
    first.append(copies.start(cos_ref, cos_scr))
    first.append(copies.start(sin_ref, sin_scr))
    sources = []
    if embed or masked:
        first.append(copies.start(ints_ref, ints_scr))
    if embed:
        first.append(copies.start(atab_ref, tab_scr))
    else:
        for r in range(G):
            dst = src_scr.at[rows_at(idx[plan.at_src + r], n), :]
            sources.append(copies.start(a_refs[r], dst))
    copies.open = []
    if rider:
        cast = PackCast(plan, rider, copies, rider_in, rider_scr[1:])
    for copy in first:
        copy.wait()
    wt = w_scr[...].T[0 : 3 * HW, :]
    if embed:
        base = split3(dot(wt, tab_scr[...], NT))
    if masked:
        live_bias(plan, idx, ints_scr, n, bias_scr)
    for r in range(G):
        at = rows_at(idx[plan.at_src + r], n)
        if embed:
            ids = ints_scr[8 * r : 8 * r + 1, :]
            hot = (lax.broadcasted_iota(jnp.int32, (VOCAB, n), 0) == ids).astype(F32).astype(BF)
            m = dot(base[0], hot) + (dot(base[1], hot) + dot(base[2], hot))
        else:
            sources[r].wait()
            m = dot(wt, src_scr[at, :], NT)
        cos, sin = cos_scr[:, at], sin_scr[:, at]
        for h in range(hd):
            for part, factor in ((0, SCALE), (1, 1.0)):
                top = part * HW + h * HEAD_DIM
                one, two = rot_pair(m[top : top + HALF], m[top + HALF : top + HEAD_DIM], cos, sin)
                qkvt[top : top + HALF, at] = (one * factor).astype(BF)
                qkvt[top + HALF : top + HEAD_DIM, at] = (two * factor).astype(BF)
        qkvt[2 * HW : 3 * HW, at] = m[2 * HW : 3 * HW].astype(BF)
        k_scr[at, :] = qkvt[HW : 2 * HW, at].T
    copies.start(qkvt, qkvt_out)
    if rider:
        cast.write(rider_scr[0])
        copies.start(rider_scr[0], rider_out)
    tile = min(512, S)

    def tile_scores(q_pads, keys, rows, diagonal):
        out = []
        for h in range(hd):
            s = dot(keys, q_pads[h])
            if masked:
                s = s + jnp.concatenate([bias_scr[rows, :]] * (tile // 128), axis=1)
            if diagonal:
                kk = lax.broadcasted_iota(jnp.int32, (tile, tile), 0)
                qq = lax.broadcasted_iota(jnp.int32, (tile, tile), 1)
                s = jnp.where(kk <= qq, s, MASKED)
            out.append(s)
        return out

    def one_query(i, _):
        cols = pl.ds(pl.multiple_of(i * tile, tile), tile)
        q_pads = [
            head_pad(plan, qkvt[h * HEAD_DIM : (h + 1) * HEAD_DIM, cols], h) for h in range(hd)
        ]

        def step(j, state, diagonal):
            rows = pl.ds(pl.multiple_of(j * tile, tile), tile)
            scores = tile_scores(q_pads, k_scr[rows, :], rows, diagonal)
            new = []
            for h in range(hd):
                top, total, acc = state[3 * h : 3 * h + 3]
                s = scores[h]
                new_top = jnp.maximum(top, jnp.max(s, axis=0, keepdims=True))
                p = jnp.exp(s - new_top)
                keep = jnp.exp(top - new_top)
                total = total * keep + jnp.sum(p, axis=0, keepdims=True)
                vt = qkvt[2 * HW + h * HEAD_DIM : 2 * HW + (h + 1) * HEAD_DIM, rows]
                acc = acc * keep + dot(vt, p.astype(BF))
                new += [new_top, total, acc]
            return tuple(new)

        state = ()
        for h in range(hd):
            state += (
                jnp.full((1, tile), -1e30, F32),
                jnp.zeros((1, tile), F32),
                jnp.zeros((HEAD_DIM, tile), F32),
            )
        state = lax.fori_loop(0, i, lambda j, st: step(j, st, False), state)
        state = step(i, state, True)
        for h in range(hd):
            top, total, acc = state[3 * h : 3 * h + 3]
            ot[h * HEAD_DIM : (h + 1) * HEAD_DIM, cols] = acc / total
            lse[h : h + 1, cols] = top + jnp.log(total)
        c_scr[cols, :] = ot[:, cols].T.astype(BF)
        return 0

    lax.fori_loop(0, S // tile, one_query, 0)
    for r in range(G):
        copies.start(c_scr.at[rows_at(idx[plan.at_dst + r], n), :], c_outs[r])
    copies.start(ot, ot_out)
    copies.start(lse, lse_out)
    copies.finish()


def source_scratch(embed, masked, S, G, source):
    none = pltpu.VMEM((16, 128), BF)
    return [
        none if embed else pltpu.VMEM((S, D), BF),
        pltpu.VMEM((VOCAB, D), BF) if embed else none,
        pltpu.VMEM(source[0 if embed else G].shape, jnp.int32) if embed or masked else none,
        pltpu.VMEM((S, 128), F32) if masked else none,
    ]


def attn_forward(
    plan, idx, cos, sin, source, weights, lo, n, embed, masked, rider=0, rider_in=()
):
    G, HW = plan.G, plan.HW
    S = G * n
    outs = [sds((n, HW), BF)] * G + [
        sds((3 * HW, S), BF),
        sds((HW, S), F32),
        sds((8, S), F32),
    ]
    extra = []
    if rider:
        outs.append(sds((PackCast.rows(plan, rider), D), BF))
        extra = [pltpu.VMEM(outs[-1].shape, BF), *PackCast.scratch(plan)]
    res = run(
        "attention_forward",
        functools.partial(attn_fwd_kernel, plan, n, lo, embed, masked, rider),
        [],
        [idx],
        [],
        [
            pltpu.VMEM((D, plan.QW), BF),
            pltpu.VMEM(cos.shape, F32),
            pltpu.VMEM(cos.shape, F32),
            *source_scratch(embed, masked, S, G, source),
            pltpu.VMEM((3 * HW, S), BF),
            pltpu.VMEM((HW, S), F32),
            pltpu.VMEM((8, S), F32),
            pltpu.VMEM((S, HW), BF),
            pltpu.VMEM((S, HW), BF),
            *extra,
        ],
        raw=[cos, sin, *source, *weights, *rider_in],
        raw_outs=outs,
        sems=plan.chips + 2 * G + 16,
        flops=2 * S * D * 3 * HW + 2 * plan.hd * S * S * 256,
        trans=plan.hd * S * S // 2,
    )
    if rider:
        return res[:G], res[G : G + 3], res[G + 3]
    return res[:G], res[G:]


def attn_bwd_kernel(plan, n, lo, embed, masked, idx, *refs):
    G, HW, hd = plan.G, plan.HW, plan.hd
    S = G * n
    refs = list(refs)
    cos_ref, sin_ref = refs[0], refs[1]
    refs = refs[2:]
    if embed:
        ints_ref, atab_ref = refs[0], refs[1]
        refs = refs[2:]
    else:
        a_refs = refs[:G]
        refs = refs[G:]
    if masked:
        ints_ref = refs[0]
        refs = refs[1:]
    w_refs = refs[: plan.chips]
    refs = refs[plan.chips :]
    do_refs = refs[:G]
    qkvt_in, ot_in, lse_in = refs[G : G + 3]
    refs = refs[G + 3 :]
    dw_outs = refs[: plan.chips]
    refs = refs[plan.chips :]
    if embed:
        tab_out = refs[0]
        refs = refs[1:]
    else:
        da_outs = refs[:G]
        refs = refs[G:]
    w_scr, cos_scr, sin_scr, src_scr, tab_scr, ints_scr, bias_scr, qkvt, ot, lse = refs[:10]
    do_all, k_scr, v_scr, qz, qtz, doz, dotz, delta, dqt, dk, dv, dmt, res_scr, dw_scr, sem = refs[10:]
    copies = Copies(sem)
    if embed or masked:
        copies.start(ints_ref, ints_scr)
    copies.start(qkvt_in, qkvt)
    for r in range(G):
        copies.start(do_refs[r], do_all.at[rows_at(idx[plan.at_src + r], n), :])
    copies.start(ot_in, ot)
    copies.start(lse_in, lse)
    first, copies.open = copies.open, []
    copies.start(cos_ref, cos_scr)
    copies.start(sin_ref, sin_scr)
    angles, copies.open = copies.open, []
    load_weight(plan, copies, idx, w_refs, lo, w_scr)
    if embed:
        copies.start(atab_ref, tab_scr)
    else:
        for r in range(G):
            copies.start(a_refs[r], src_scr.at[rows_at(idx[plan.at_src + r], n), :])
    last, copies.open = copies.open, []
    for copy in first:
        copy.wait()
    tile = min(512, S)
    blocks = S // tile
    lane = lax.broadcasted_iota(jnp.int32, (tile, HW), 1) // HEAD_DIM
    for b in range(blocks):
        at = slice(b * tile, (b + 1) * tile)
        dob = do_all[at, :]
        dobt = dob.T
        kt = qkvt[HW : 2 * HW, at]
        k_scr[at, :] = kt.T
        v_scr[at, :] = qkvt[2 * HW : 3 * HW, at].T
        prod = dobt.astype(F32) * ot[:, at]
        dob32 = dob.astype(F32)
        for h in range(hd):
            rows = slice(h * HEAD_DIM, (h + 1) * HEAD_DIM)
            pad = head_pad(plan, qkvt[rows, at], h)
            qtz[h, :, at] = pad
            qz[h, at, :] = pad.T
            dotz[h, :, at] = head_pad(plan, dobt[rows, :], h)
            doz[h, at, :] = jnp.where(lane == h, dob32, 0.0).astype(BF)
            delta[h : h + 1, at] = jnp.sum(prod[rows, :], axis=0, keepdims=True)
    dqt[...] = jnp.zeros_like(dqt)
    if masked:
        live_bias(plan, idx, ints_scr, n, bias_scr)
    for copy in angles:
        copy.wait()

    def one_key(j, _):
        rows = pl.ds(pl.multiple_of(j * tile, tile), tile)
        keys, values = k_scr[rows, :], v_scr[rows, :]
        dk[...] = jnp.zeros_like(dk)
        dv[...] = jnp.zeros_like(dv)
        bias = jnp.concatenate([bias_scr[rows, :]] * (tile // 128), axis=1) if masked else None

        def step(i, diagonal):
            cols = pl.ds(pl.multiple_of(i * tile, tile), tile)
            for h in range(hd):
                s = dot(keys, qtz[h, :, cols])
                if masked:
                    s = s + bias
                if diagonal:
                    kk = lax.broadcasted_iota(jnp.int32, (tile, tile), 0)
                    qq = lax.broadcasted_iota(jnp.int32, (tile, tile), 1)
                    s = jnp.where(kk <= qq, s, MASKED)
                p = jnp.exp(s - lse[h : h + 1, cols])
                dp = dot(values, dotz[h, :, cols])
                ds = (p * (dp - delta[h : h + 1, cols])).astype(BF)
                dv[...] += dot(p.astype(BF), doz[h, cols, :])
                dk[...] += dot(ds, qz[h, cols, :])
                kt = qkvt[HW + h * HEAD_DIM : HW + (h + 1) * HEAD_DIM, rows]
                dqt[h * HEAD_DIM : (h + 1) * HEAD_DIM, cols] += dot(kt, ds)

        step(j, True)

        def more(i, carry):
            step(i, False)
            return carry

        lax.fori_loop(j + 1, blocks, more, 0)
        dkt = dk[...].T
        cos, sin = cos_scr[:, rows], sin_scr[:, rows]
        for h in range(hd):
            top = h * HEAD_DIM
            one, two = rot_pair(
                dkt[top : top + HALF], dkt[top + HALF : top + HEAD_DIM], cos, -sin
            )
            dmt[HW + top : HW + top + HALF, rows] = one.astype(BF)
            dmt[HW + top + HALF : HW + top + HEAD_DIM, rows] = two.astype(BF)
        dmt[2 * HW : 3 * HW, rows] = dv[...].T.astype(BF)
        return 0

    lax.fori_loop(0, blocks, one_key, 0)
    cos, sin = cos_scr[:, 0:S], sin_scr[:, 0:S]
    for h in range(hd):
        top = h * HEAD_DIM
        one, two = rot_pair(
            dqt[top : top + HALF, :] * SCALE,
            dqt[top + HALF : top + HEAD_DIM, :] * SCALE,
            cos,
            -sin,
        )
        dmt[top : top + HALF, :] = one.astype(BF)
        dmt[top + HALF : top + HEAD_DIM, :] = two.astype(BF)
    for copy in last:
        copy.wait()
    wt = w_scr[...].T[0 : 3 * HW, :]
    if embed:
        sums = jnp.zeros((3 * HW, VOCAB), F32)
        for r in range(G):
            at = rows_at(idx[plan.at_src + r], n)
            ids = ints_scr[8 * r : 8 * r + 1, :]
            hot = (lax.broadcasted_iota(jnp.int32, (VOCAB, n), 0) == ids).astype(F32).astype(BF)
            sums += dot(dmt[:, at], hot, NT)
        high = sums.astype(BF)
        low = (sums - high.astype(F32)).astype(BF)
        res_scr[...] = dot(high.T, wt) + dot(low.T, wt)
        copies.start(res_scr, tab_out)
        grad = dot(high, tab_scr[...]) + dot(low, tab_scr[...])
    else:
        for r in reversed(range(G)):
            at = rows_at(idx[plan.at_dst + r], n)
            res_scr[at, :] = dot(dmt[:, at].T, wt).astype(BF)
            copies.start(res_scr.at[at, :], da_outs[r])
        grad = dot(dmt[...], src_scr[...])
    dw_scr[:, 0 : 3 * HW] = grad.T.astype(BF)
    dw_scr[:, 3 * HW : D] = jnp.zeros((D, D - 3 * HW), BF)
    for r in range(plan.chips):
        at = rows_at(idx[plan.at_order["x"] + r], 2 * plan.DR)
        copies.start(dw_scr.at[at, :], dw_outs[r])
    copies.finish()


def attn_backward(
    plan, idx, cos, sin, source, weights, lo, dos, saved, n, embed, masked, after=()
):
    G, HW, hd = plan.G, plan.HW, plan.hd
    S = G * n
    tile = min(512, S)
    outs = [sds((2 * plan.DR, D), BF)] * plan.chips
    outs += [sds((VOCAB, D), F32)] if embed else [sds((n, D), BF)] * G
    res = run(
        "attention_backward",
        functools.partial(attn_bwd_kernel, plan, n, lo, embed, masked),
        [],
        [idx],
        [],
        [
            pltpu.VMEM((D, plan.QW), BF),
            pltpu.VMEM(cos.shape, F32),
            pltpu.VMEM(cos.shape, F32),
            *source_scratch(embed, masked, S, G, source),
            pltpu.VMEM((3 * HW, S), BF),
            pltpu.VMEM((HW, S), F32),
            pltpu.VMEM((8, S), F32),
            pltpu.VMEM((S, HW), BF),
            pltpu.VMEM((S, HW), BF),
            pltpu.VMEM((S, HW), BF),
            pltpu.VMEM((hd, S, HW), BF),
            pltpu.VMEM((hd, HW, S), BF),
            pltpu.VMEM((hd, S, HW), BF),
            pltpu.VMEM((hd, HW, S), BF),
            pltpu.VMEM((8, S), F32),
            pltpu.VMEM((HW, S), F32),
            pltpu.VMEM((tile, HW), F32),
            pltpu.VMEM((tile, HW), F32),
            pltpu.VMEM((3 * HW, S), BF),
            pltpu.VMEM((VOCAB, D), F32) if embed else pltpu.VMEM((S, D), BF),
            pltpu.VMEM((D, D), BF),
        ],
        raw=[cos, sin, *source, *weights, *dos, *saved],
        raw_outs=outs,
        sems=2 * plan.chips + 3 * G + 8,
        flops=4 * S * D * 3 * HW + 5 * hd * S * S * 256,
        trans=hd * S * S // 2,
        after=after,
    )
    return res[: plan.chips], res[plan.chips :]


class Pack:
    def __init__(self, plan, copies, pack, scr):
        self.plan = plan
        self.up_scr, self.down_scr, self.proj_scr = scr
        DR, FR = plan.DR, plan.FR
        self.per = CHUNK // FR
        top = 4 * DR + FR
        self.proj_copy = copies.start(pack.at[:, top : top + DR, :], self.proj_scr)
        self.copies = []
        for j in range(FF // CHUNK):
            at = slice(j * self.per, (j + 1) * self.per)
            self.copies.append(
                (
                    copies.start(pack.at[:, j * DR : (j + 1) * DR, :], self.up_scr.at[j]),
                    copies.start(pack.at[at, 4 * DR : 4 * DR + FR, :], self.down_scr.at[j]),
                )
            )
        copies.open = []

    @staticmethod
    def scratch(plan):
        chunks = FF // CHUNK
        return [
            pltpu.VMEM((chunks, plan.seq, plan.DR, D), BF),
            pltpu.VMEM((chunks, CHUNK // plan.FR, plan.FR, D), BF),
            pltpu.VMEM((plan.seq, plan.DR, D), BF),
        ]

    def proj(self, k):
        per = self.plan.HW // self.plan.DR
        rows = self.proj_scr[pl.ds(k * per, per), :, :]
        return rows.reshape(self.plan.HW, D)

    def up(self, j):
        return self.up_scr[j].reshape(D, CHUNK)

    def down(self, j):
        return self.down_scr[j].reshape(CHUNK, D)


VALID, TARGET, NEXT, SLOT, BYTE = range(5)


def at_lane(lane, value):
    lanes = lax.broadcasted_iota(jnp.int32, (8, 128), 1)
    return jnp.where(lanes == lane, jnp.broadcast_to(value, (8, 128)), 0.0)


def square_of(cols, x):
    rows = jnp.sum(x * x, axis=-1, keepdims=True) * cols[:, VALID : VALID + 1]
    return jnp.sum(rows, axis=0, keepdims=True)


def attended(plan, k, x):
    k.pack.proj_copy.wait()
    y = x
    for r in range(plan.G):
        y += dot(k.c[r][...], k.pack.proj(k.idx[plan.at_src + r]))
    k.y[...] = y


def feed_forward(k, layer, y, keep=False):
    k.normed[...] = (y * root_of(y) * k.gains[2 * layer + 1 : 2 * layer + 2, :]).astype(BF)
    for j in range(FF // CHUNK):
        k.pack.copies[j][0].wait()
        h = dot(k.normed[...], k.pack.up(j))
        at = slice(j * CHUNK, (j + 1) * CHUNK)
        if keep:
            value, slope = gelu_parts(h)
            k.slope[j] = slope
        else:
            value = gelu_value(h)
        k.act[:, at] = value.astype(BF)
    for j in range(FF // CHUNK):
        k.pack.copies[j][1].wait()
    k.x_scr[...] = k.y[...] + dot(k.act[...], k.down_scr[...].reshape(FF, D))


def ffn_pool_kernel(plan, k):
    k.pack = Pack(plan, Copies(k.sem), k.pack_in, (k.up_scr, k.down_scr, k.proj_scr))
    x = dot(one_hot(k.cols[:, BYTE : BYTE + 1], VOCAB), k.table[...])
    attended(plan, k, x)
    feed_forward(k, 0, k.y[...])
    x = k.x_scr[...]
    k.x[...] = x
    turned = one_hot(k.cols[:, SLOT : SLOT + 1], CAP).T
    counts = jnp.sum(turned.astype(F32), axis=1, keepdims=True)
    pooled = exact_dot(turned, x) / jnp.maximum(counts, 1.0)
    k.pooled[...] = pooled
    k.a[...] = (pooled * root_of(pooled) * k.gains[2:3, :]).astype(BF)
    count = jnp.sum(k.cols[:, VALID : VALID + 1], axis=0, keepdims=True)
    k.stat[...] = at_lane(2, square_of(k.cols, x)) + at_lane(5, count)


def ffn_unpool_kernel(plan, k):
    k.pack = Pack(plan, Copies(k.sem), k.pack_in, (k.up_scr, k.down_scr, k.proj_scr))
    attended(plan, k, k.pooled[...])
    feed_forward(k, 1, k.y[...])
    x = k.x1[...] + exact_dot(one_hot(k.cols[:, SLOT : SLOT + 1], CAP), k.x_scr[...])
    k.x[...] = x
    k.a[...] = (x * root_of(x) * k.gains[4:5, :]).astype(BF)
    k.stat[...] = k.stat_in[...] + at_lane(3, square_of(k.cols, x))


def forward_scratch(plan, n):
    return {
        **dict(zip(("up_scr", "down_scr", "proj_scr"), Pack.scratch(plan))),
        "normed": pltpu.VMEM((n, D), BF),
        "act": pltpu.VMEM((n, FF), BF),
        "x_scr": pltpu.VMEM((n, D), F32),
    }


def loss_part(plan, k):
    k.tab_copy.wait()
    table = k.tab_scr[...].reshape(VOCAB, D)
    x = k.x_scr[...]
    valid = k.cols[:, VALID : VALID + 1]
    root = root_of(x)
    unit = x * root
    gain = k.gains[6:7, :]
    rows = (unit * gain).astype(BF)
    logits = dot(rows, table, NT)
    top_row = jnp.max(logits, axis=-1, keepdims=True)
    total = jnp.sum(jnp.exp(logits - top_row), axis=-1, keepdims=True)
    log_norm = top_row + jnp.log(total)
    hot = one_hot(k.cols[:, NEXT : NEXT + 1], VOCAB).astype(F32)
    picked = jnp.sum(logits * hot, axis=-1, keepdims=True)
    ce = jnp.sum(valid * (log_norm - picked), axis=0, keepdims=True)
    glog = (valid * (jnp.exp(logits - log_norm) - hot)).astype(BF)
    k.dtab[...] = dot(glog.T, rows).astype(BF).reshape(plan.seq, plan.VR, D)
    dx, dgain = norm_back(unit, root, gain, dot(glog, table))
    k.gout[...] = dx
    k.dgain6[...] = jnp.broadcast_to(dgain, k.dgain6.shape)
    k.stat[...] = (
        k.stat_a[...] + k.stat_b[...] + at_lane(0, ce) + at_lane(4, square_of(k.cols, x))
    )


def ffn_backward_part(plan, k, layer, y, send, kept=False):
    root = root_of(y)
    gain = k.gains[2 * layer + 1 : 2 * layer + 2, :]
    k.unit[...] = y * root
    if not kept:
        k.normed[...] = (y * root * gain).astype(BF)
    k.normt[...] = k.normed[...].T
    k.low[...] = k.gout[...].astype(BF)
    k.dn[...] = jnp.zeros_like(k.dn)
    for j in range(FF // CHUNK):
        if kept:
            value, slope = k.act[:, j * CHUNK : (j + 1) * CHUNK], k.slope[j]
            up = k.pack.up(j)
        else:
            for copy in k.pack.copies[j]:
                copy.wait()
            up = k.pack.up(j)
            value, slope = gelu_parts(dot(k.normed[...], up))
            value = value.astype(BF)
        per = CHUNK // plan.FR
        grad = dot(value.T, k.low[...]).astype(BF)
        k.ddown[j * per : (j + 1) * per] = grad.reshape(per, plan.FR, D)
        dact = dot(k.low[...], k.pack.down(j), NT)
        dh = (dact * slope).astype(BF)
        k.dup[j] = dot(k.normt[...], dh).astype(BF).reshape(plan.seq, plan.DR, CHUNK)
        send(j)
        k.dn[...] += dot(dh, up, NT)
    dx, dgain = norm_back(k.unit[...], root, gain, k.dn[...])
    gmid = k.gout[...] + dx
    k.gmid[...] = gmid
    k.dgain[...] = jnp.broadcast_to(dgain, k.dgain.shape)
    k.low[...] = gmid.astype(BF)
    if not kept:
        k.pack.proj_copy.wait()
    HW = plan.HW
    for r in range(plan.G):
        per = HW // plan.DR
        grad = dot(k.c[r][...].T, k.low[...]).astype(BF)
        k.dproj[pl.ds(k.idx[plan.at_src + r] * per, per)] = grad.reshape(per, plan.DR, D)
        k.dc[r][...] = dot(k.low[...], k.pack.proj(k.idx[plan.at_dst + r]), NT).astype(BF)


def send_packs(plan, k, copies):
    DR, FR = plan.DR, plan.FR

    def shard(order, r, dc):
        core = lax.rem(k.idx[plan.at_core] + dc, 2)
        return k.idx[plan.at_order[order] + r] * 2 + core

    def upward(j):
        for dc in (1, 0):
            for r in range(plan.chips):
                out = k.packs[2 * dc].at[r, j * DR : (j + 1) * DR, :]
                copies.start(k.dup.at[j, shard("x", r, dc)], out)

    def rest():
        for dc in (1, 0):
            two = k.packs[2 * dc + 1]
            for r in range(plan.chips):
                s = shard("y", r, dc)
                copies.start(k.ddown.at[s], two.at[r, 0:FR, :])
                copies.start(k.dproj.at[s], two.at[r, FR : FR + DR, :])
        copies.finish()

    return upward, rest


def send_whole(plan, k, copies, extra=False):
    DR, FR, VR = plan.DR, plan.FR, plan.VR
    (out,) = k.packs
    per = CHUNK // FR
    down_at = 4 * DR + (DR + VR if extra else 0)

    def upward(j):
        copies.start(k.dup.at[j], out.at[:, j * DR : (j + 1) * DR, :])
        at = slice(j * per, (j + 1) * per)
        copies.start(k.ddown.at[at], out.at[at, down_at : down_at + FR, :])

    def rest():
        top = 4 * DR
        if extra:
            copies.start(k.dp3, out.at[:, top : top + DR, :])
            top += DR
            copies.start(k.dtab, out.at[:, top : top + VR, :])
        top = down_at + FR
        copies.start(k.dproj, out.at[:, top : top + DR, :])
        copies.finish()

    return upward, rest


def backward_scratch(plan, n):
    return {
        **forward_scratch(plan, n),
        "gout": pltpu.VMEM((n, D), F32),
        "unit": pltpu.VMEM((n, D), F32),
        "normt": pltpu.VMEM((D, n), BF),
        "low": pltpu.VMEM((n, D), BF),
        "dn": pltpu.VMEM((n, D), F32),
        "dup": pltpu.VMEM((FF // CHUNK, plan.seq, plan.DR, CHUNK), BF),
        "ddown": pltpu.VMEM((plan.seq, plan.FR, D), BF),
        "dproj": pltpu.VMEM((plan.seq, plan.DR, D), BF),
    }


def backward_outs(plan, n, whole=False, extra=False):
    C, DR, FR = plan.chips, plan.DR, plan.FR
    outs = {
        "gmid": sds((n, D), F32),
        "dc": [sds((n, plan.HW), BF)] * plan.G,
        "dgain": sds((8, D), F32),
    }
    if whole:
        rows = 5 * DR + FR + (DR + plan.VR if extra else 0)
        return outs, {"packs": [sds((plan.seq, rows, D), BF)]}
    return outs, {"packs": [sds((C, 4 * DR, D), BF), sds((C, FR + DR, D), BF)] * 2}


def ffn_loss_kernel(plan, k):
    copies = Copies(k.sem)
    k.pack = Pack(plan, copies, k.pack_in, (k.up_scr, k.down_scr, k.proj_scr))
    top = 5 * plan.DR + plan.FR
    k.tab_copy = copies.start(k.pack_in.at[:, top : top + plan.VR, :], k.tab_scr)
    copies.open = []
    attended(plan, k, k.x[...])
    feed_forward(k, 2, k.y[...], keep=True)
    loss_part(plan, k)
    upward, rest = send_whole(plan, k, copies, extra=True)
    ffn_backward_part(plan, k, 2, k.y[...], upward, kept=True)
    rest()


def joined(refs):
    total = refs[0][...].astype(F32)
    for ref in refs[1:]:
        total += ref[...].astype(F32)
    return total


def join_last_kernel(plan, k):
    copies = Copies(k.sem)
    k.pack = Pack(plan, copies, k.pack_in, (k.up_scr, k.down_scr, k.proj_scr))
    x = k.x[...]
    root = root_of(x)
    dx, dgain = norm_back(x * root, root, k.gains[4:5, :], joined(k.terms))
    grad = k.gnext[...] + dx
    k.second[...] = grad
    k.gout[...] = exact_dot(one_hot(k.cols[:, SLOT : SLOT + 1], CAP).T, grad)
    k.dgain_in[...] = jnp.broadcast_to(dgain, k.dgain_in.shape)
    upward, rest = send_whole(plan, k, copies)
    ffn_backward_part(plan, k, 1, k.y[...], upward)
    rest()


def join_middle_kernel(plan, k):
    copies = Copies(k.sem)
    k.pack = Pack(plan, copies, k.pack_in, (k.up_scr, k.down_scr, k.proj_scr))
    x = k.x[...]
    root = root_of(x)
    dx, dgain = norm_back(x * root, root, k.gains[2:3, :], joined(k.terms))
    member = one_hot(k.cols[:, SLOT : SLOT + 1], CAP)
    counts = jnp.sum(member.T.astype(F32), axis=1, keepdims=True)
    grad = (k.gnext[...] + dx) / jnp.maximum(counts, 1.0)
    k.gout[...] = k.second[...] + k.bound[...] + exact_dot(member, grad)
    k.dgain_in[...] = jnp.broadcast_to(dgain, k.dgain_in.shape)
    upward, rest = send_packs(plan, k, copies)
    ffn_backward_part(plan, k, 0, k.y[...], upward)
    rest()


def bound_kernel(plan, x_ref, cols, gains, pack, *refs):
    grad_out, dp_out, dgain_out, stat, weight_scr, sem = refs
    top = 5 * plan.DR + plan.FR
    copy = Copies(sem).start(pack.at[:, top : top + plan.DR, :], weight_scr)
    x = x_ref[...]
    valid = cols[:, VALID : VALID + 1]
    target = cols[:, TARGET : TARGET + 1]
    root = root_of(x)
    unit = x * root
    gain = gains[7:8, :]
    rows = (unit * gain).astype(BF)
    copy.wait()
    weight = weight_scr[...].reshape(D, D)
    value, slope = gelu_parts(dot(rows, weight))
    out_gain = gains[8:9, :]
    z = jnp.sum(value * out_gain, axis=-1, keepdims=True) * D ** (-0.5)
    small = jnp.exp(-jnp.abs(z))
    soft = jnp.maximum(z, 0.0) + jnp.log(1.0 + small)
    bce = jnp.sum(valid * (soft - target * z), axis=0, keepdims=True)
    sig = jnp.where(z >= 0, 1.0, small) / (1.0 + small)
    dz = valid * (sig - target) * D ** (-0.5)
    dh = (dz * out_gain * slope).astype(BF)
    dp_out[...] = dot(rows.T, dh).astype(BF).reshape(dp_out.shape)
    dx, dgain = norm_back(unit, root, gain, dot(dh, weight, NT))
    grad_out[...] = dx
    dgain_out[0:8, :] = jnp.broadcast_to(dgain, (8, D))
    dgain_out[8:16, :] = jnp.broadcast_to(jnp.sum(dz * value, axis=0, keepdims=True), (8, D))
    stat[...] = at_lane(1, bce)


def tail_kernel(plan, idx, gmid, dtab, table, cols, gains, *refs):
    d1, d2, d3, d4, d5, d6, d78 = refs[:7]
    dw = refs[7 : 7 + plan.chips]
    packs = refs[7 + plan.chips : 7 + 2 * plan.chips]
    tab, gt, turned = refs[7 + 2 * plan.chips :]
    t = table[...].astype(F32)
    root = root_of(t)
    dx, dgain = norm_back(t * root, root, gains[0:1, :], dtab[...])
    hot = one_hot(cols[:, BYTE : BYTE + 1], VOCAB).T
    g = gmid[...]
    high = g.astype(BF)
    tab[...] = dx + (dot(hot, high) + dot(hot, (g - high.astype(F32)).astype(BF)))
    gt[...] = jnp.zeros_like(gt)
    gt[0:1, :] = dgain
    for k, ref in ((1, d1), (2, d2), (3, d3), (4, d4), (5, d5), (6, d6), (7, d78)):
        gt[k : k + 1, :] = ref[0:1, :]
    gt[8:9, :] = d78[8:9, :]
    turned[...] = gt[...].T
    DR, VR, HW = plan.DR, plan.VR, plan.HW
    for r in range(plan.chips):
        k = idx[plan.at_order["x"] + r]
        if 3 * HW < D - 128:
            packs[r][0 : 2 * DR, :] = jnp.zeros((2 * DR, D), BF)
        packs[r][0 : 2 * DR, 0 : 3 * HW] = dw[r][:, 0 : 3 * HW]
        rows = turned[pl.ds(pl.multiple_of(k * 2 * DR, 2 * DR), 2 * DR), :]
        packs[r][0 : 2 * DR, D - 128 : D] = rows.astype(BF)
        rows = tab[pl.ds(pl.multiple_of(k * 2 * VR, 2 * VR), 2 * VR), :]
        packs[r][2 * DR : 2 * DR + 2 * VR, :] = rows.astype(BF)


def adam_update(weight, first, second, grad, rate):
    mean = BETA_FIRST * first + (1.0 - BETA_FIRST) * grad
    meansq = BETA_SECOND * second + (1.0 - BETA_SECOND) * grad * grad
    mean_hat = mean / (1.0 - BETA_FIRST**STEP)
    meansq_hat = meansq / (1.0 - BETA_SECOND**STEP)
    master = weight - rate * (mean_hat / (jnp.sqrt(meansq_hat) + ADAM_EPS) + DECAY_RATE * weight)
    return (master, mean, meansq)


def add(a, b):
    return (a.astype(F32) + b.astype(F32)).astype(BF)


def total_of(terms):
    total = terms[0].astype(F32)
    for term in terms[1:]:
        total = total + term.astype(F32)
    return total.astype(BF)


def sum_first(plan, blocks, axis):
    got = [plan.shift(blocks[d], **{axis: d}) for d in range(1, plan.sizes[axis])]
    return [total_of([b[e] for b in (blocks[0], *got)]) for e in range(blocks[0].shape[0])]


def sum_second(plan, blocks, axis):
    return total_of(
        [blocks[0]] + [plan.shift(blocks[d], **{axis: d}) for d in range(1, plan.sizes[axis])]
    )


def sum_chips(plan, blocks):
    terms = [blocks[0]]
    for r in range(1, plan.chips):
        dx, dy = divmod(r, plan.Y)
        terms.append(plan.shift(blocks[r], x=dx, y=dy))
    return total_of(terms)


def head_sum(plan, v, axis):
    return add(v, plan.shift(v, **{axis: 1}))


def split_axes(plan, t, first, second):
    return t.reshape((plan.sizes[first], plan.sizes[second]) + t.shape[1:])


def by_core(first, second):
    halves = [v.reshape((2, v.shape[0] // 2) + v.shape[1:]) for v in (first, second)]
    return jnp.concatenate(halves, axis=1)


def exchange_columns(plan, v, me):
    own = lax.dynamic_index_in_dim(v, me["core"], 0, keepdims=False)
    other = lax.dynamic_index_in_dim(v, 1 - me["core"], 0, keepdims=False)
    parts = [own] + [plan.shift(own, zl=d) for d in range(1, plan.L)]
    return parts + [plan.shift(other, core=1, zl=d) for d in range(plan.L)]


def final_kernel(plan, idx, *refs):
    DR, FR, VR, HW, G = plan.DR, plan.FR, plan.VR, plan.HW, plan.G
    shards = [refs[2 * layer : 2 * layer + 2] for layer in range(3)]
    refs = refs[6:]
    columns0, columns12, stat_in = refs[:G], refs[G : 2 * G], refs[2 * G]
    qkv, proj, up, down, table, gain, stat, scr0, scr12 = refs[2 * G + 1 :]
    for r in range(G):
        b = idx[plan.at_src + r]
        scr0[b] = columns0[r][...]
        scr12[b] = columns12[r][...]
    for b in range(G):
        for part in range(3):
            src = slice(part * HW, (part + 1) * HW)
            dst = slice(part * D + b * HW, part * D + (b + 1) * HW)
            qkv[0, :, dst] = scr0[b, 0:DR, src]
            qkv[1, :, dst] = scr12[b, 0:DR, src]
            qkv[2, :, dst] = scr12[b, DR : 2 * DR, src]
    tab = scr0[0, DR : DR + VR, :].astype(F32)
    gains = scr0[0, 0:DR, D - 128 : D].astype(F32)
    for b in range(1, G):
        tab += scr0[b, DR : DR + VR, :].astype(F32)
        gains += scr0[b, 0:DR, D - 128 : D].astype(F32)
    gain[...] = gains
    table[0] = tab
    for layer in range(3):
        one, two = shards[layer]
        for j in range(4):
            up[layer, :, j * CHUNK : (j + 1) * CHUNK] = one[j * DR : (j + 1) * DR, :]
        top = 0
        if layer == 2:
            proj[3] = two[0:DR, :]
            table[1] = two[DR : DR + VR, :].astype(F32)
            top = DR + VR
        down[layer] = two[top : top + FR, :]
        proj[layer] = two[top + FR : top + FR + DR, :]
    total = jnp.zeros((1, 1), F32)
    for ref in (qkv, proj, up, down, table, gain):
        pieces = [ref[...]] if len(ref.shape) == 2 else [ref[l] for l in range(ref.shape[0])]
        for piece in pieces:
            v = piece.astype(F32)
            total += jnp.sum(jnp.sum(v * v, axis=0, keepdims=True), axis=1, keepdims=True)
    stat[...] = stat_in[...] + at_lane(6, total)


def per_device(plan, *args):
    (
        byte_ids,
        next_bytes,
        loss_mask,
        pool_slots,
        qkv_weight,
        proj_weight,
        upward_weight,
        downward_weight,
        table_weight,
        gain_weight,
        qkv_first,
        qkv_second,
        proj_first,
        proj_second,
        upward_first,
        upward_second,
        downward_first,
        downward_second,
        table_first,
        table_second,
        gain_first,
        gain_second,
    ) = args
    G, L, HW, QW, DR, FR, VR = plan.G, plan.L, plan.HW, plan.QW, plan.DR, plan.FR, plan.VR
    n = byte_ids.shape[1]
    length = n * G
    me = plan.place()
    idx = plan.tables()
    core = me["core"]

    width0, width1 = QW + 384, 2 * QW
    keep0, send0, keep1, send1 = run(
        "first",
        functools.partial(first_kernel, plan),
        [sds((DR, width0), BF)] * 2 + [sds((DR, width1), BF)] * 2,
        [idx],
        [qkv_weight, table_weight, gain_weight],
        [pltpu.VMEM((128, 128), F32)],
    )
    ints = jnp.concatenate([byte_ids, next_bytes, loss_mask, pool_slots], axis=0)
    ints = jnp.concatenate([ints, jnp.zeros_like(ints)], axis=0)

    def chip_rows(keep, got):
        return jnp.where(
            core == 0,
            jnp.concatenate([keep, got], axis=0),
            jnp.concatenate([got, keep], axis=0),
        )

    def gather_chips(v, want=lambda dy, dx: True):
        out = [v]
        for r in range(1, plan.chips):
            dy, dx = divmod(r, plan.X)
            if want(dy, dx):
                out.append(plan.shift(v, y=dy, x=dx))
        return out

    def swap(c):
        return {**c, "core": c["zh"], "zh": c["core"]}

    got0, got1, own = fence(
        plan.shift(send0, core=1), plan.shift(send1, core=1), plan.permute(ints, swap)
    )
    chip0 = chip_rows(keep0, got0)
    chip1 = chip_rows(keep1, got1)
    early, both, chip1 = fence(
        gather_chips(chip0), jnp.concatenate([own, plan.shift(own, core=1)]), chip1
    )
    pairs = [both] + [plan.shift(both, zl=d) for d in range(1, L)]
    ints_all = jnp.concatenate([p[:8] for p in pairs] + [p[8:] for p in pairs])

    shard_inputs = [upward_weight, downward_weight, proj_weight, table_weight]

    def gather_pack(pack):
        return lax.all_gather(pack, "seq", axis=0, tiled=False)

    (pack0,) = run(
        "pack",
        functools.partial(pack_kernel, plan, 0),
        [sds((PackCast.rows(plan, 0), D), BF)],
        [],
        [],
        PackCast.scratch(plan),
        raw=shard_inputs,
        sems=5,
        after=[keep0],
    )
    packs = [gather_pack(pack0)]

    table, atab, gains, cols = run(
        "tables",
        functools.partial(prep_kernel, plan),
        [sds((VOCAB, D), BF), sds((VOCAB, D), BF), sds((16, D), F32), sds((n, 128), F32)],
        [idx],
        [own, *early],
        [pltpu.VMEM((VOCAB, D), F32), pltpu.VMEM((D, 128), F32), pltpu.VMEM((128, n), F32)],
    )
    half = np.arange(HALF, dtype=np.float32) / np.float32(HALF)
    frequency = np.float32(10000.0) ** (-half)
    angles = frequency[:, None] * np.arange(length, dtype=np.float32)[None, :]
    cos = jnp.asarray(np.cos(angles.astype(np.float64)).astype(np.float32))
    sin = jnp.asarray(np.sin(angles.astype(np.float64)).astype(np.float32))

    def exchange(parts):
        out = [parts[0]]
        for r in range(1, G):
            dc, dl = divmod(r, L)
            out.append(plan.shift(parts[r], core=dc, zl=dl))
        return out

    def gather_near(a):
        return [a] + [plan.shift(a, zl=d) for d in range(1, L)]

    def scatter_group(das):
        terms = [das[0], plan.shift(das[L], core=1)]
        for d in range(1, L):
            both = add(das[d], plan.shift(das[L + d], core=1))
            terms.append(plan.shift(both, zl=d))
        return terms

    early, table, atab, gains, cols, ints_all, chip1 = fence(
        early, table, atab, gains, cols, ints_all, chip1
    )
    straight = gather_chips(chip1, lambda dy, dx: not (dy and dx))
    c0, saved0, pack1 = attn_forward(
        plan, idx, cos, sin, [ints_all, atab], early, 0, n, True, False, 1, shard_inputs
    )
    packs.append(gather_pack(pack1))
    c0, saved0, straight = fence(c0, saved0, straight)
    c0, chip1 = fence(exchange(c0), chip1)
    dense = 2 * D * (D + 2 * FF)
    res = run_named(
        "ffn_pool",
        functools.partial(ffn_pool_kernel, plan),
        {
            "y": sds((n, D), F32),
            "x": sds((n, D), F32),
            "pooled": sds((CAP, D), F32),
            "a": sds((CAP, D), BF),
            "stat": sds((8, 128), F32),
        },
        {"c": c0, "cols": cols, "table": table, "gains": gains},
        forward_scratch(plan, n),
        {"pack_in": packs[0]},
        {},
        idx,
        16,
        n * dense,
        n * FF,
    )
    y0, x1, pooled, a1, stat = res.y, res.x, res.pooled, res.a, res.stat
    diagonal = gather_chips(chip1, lambda dy, dx: dy and dx)
    y0, x1, pooled, a1, stat, diagonal = fence(y0, x1, pooled, a1, stat, diagonal)
    late = [straight.pop(0)]
    diagonal.pop(0)
    for r in range(1, plan.chips):
        late.append((diagonal if all(divmod(r, plan.X)) else straight).pop(0))
    near, beside = gather_near(a1), plan.shift(a1, core=1)
    near, beside = fence(near, beside)
    a1 = [*near, beside, *[plan.shift(p, core=1) for p in near[1:]]]
    c1, saved1, pack2 = attn_forward(
        plan, idx, cos, sin, [*a1, ints_all], late, 0, CAP, False, True, 2, shard_inputs
    )
    packs.append(gather_pack(pack2))
    c1, saved1 = fence(c1, saved1)
    c1 = exchange(c1)
    res = run_named(
        "ffn_unpool",
        functools.partial(ffn_unpool_kernel, plan),
        {
            "y": sds((CAP, D), F32),
            "x": sds((n, D), F32),
            "a": sds((n, D), BF),
            "stat": sds((8, 128), F32),
        },
        {"c": c1, "pooled": pooled, "x1": x1, "cols": cols, "gains": gains, "stat_in": stat},
        forward_scratch(plan, CAP),
        {"pack_in": packs[1]},
        {},
        idx,
        16,
        CAP * dense,
        CAP * FF,
    )
    y1, x2, a2, stat = res.y, res.x, res.a, res.stat
    bound_grad, dp3, dgain78, stat_b = run(
        "boundary",
        functools.partial(bound_kernel, plan),
        [sds((n, D), F32), sds((plan.seq, DR, D), BF), sds((16, D), F32), sds((8, 128), F32)],
        [],
        [x1, cols, gains],
        [pltpu.VMEM((plan.seq, DR, D), BF)],
        raw=[packs[1]],
        sems=1,
        flops=6 * n * D * D,
        trans=n * D,
    )
    near, beside, bound_grad, dp3, dgain78, stat_b = fence(
        gather_near(a2), plan.shift(a2, core=1), bound_grad, dp3, dgain78, stat_b
    )
    a2 = [*near, beside, *[plan.shift(p, core=1) for p in near[1:]]]
    c2, saved2 = attn_forward(plan, idx, cos, sin, a2, late, QW, n, False, False)
    c2 = exchange(c2)

    source0 = [ints_all, atab]
    swaps = plan.head == 4
    cut = 4 * DR

    def swap_first(v, one="zl", two="zh"):
        if not swaps:
            return [lax.psum(v[:cut], "head"), lax.psum(v[cut:], "head")]
        return [head_sum(plan, v[:cut], one), head_sum(plan, v[cut:], two)]

    def swap_second(parts, one="zh", two="zl"):
        if not swaps:
            return parts
        return [head_sum(plan, parts[0], one), head_sum(plan, parts[1], two)]

    axes = (("x", "y"), ("y", "x"))

    def core_sums(packs):
        out = []
        for mine, theirs, ax in zip(packs[:2], packs[2:], axes):
            got = split_axes(plan, plan.shift(theirs, core=1), *ax)
            mine = split_axes(plan, mine, *ax)
            out.append([add(mine[d], got[d]) for d in range(mine.shape[0])])
        return out

    def first_sums(halves):
        return [sum_first(plan, half, ax[0]) for half, ax in zip(halves, axes)]

    def second_sums(halves):
        return [sum_second(plan, half, ax[1]) for half, ax in zip(halves, axes)]

    outs, raw_outs = backward_outs(plan, n, whole=True, extra=True)
    res = run_named(
        "ffn_loss",
        functools.partial(ffn_loss_kernel, plan),
        {**outs, "dgain6": sds((8, D), F32), "stat": sds((8, 128), F32)},
        {
            "c": c2,
            "x": x2,
            "cols": cols,
            "gains": gains,
            "stat_a": stat,
            "stat_b": stat_b,
            "dp3": dp3,
        },
        {
            **backward_scratch(plan, n),
            "slope": pltpu.VMEM((FF // CHUNK, n, CHUNK), F32),
            "y": pltpu.VMEM((n, D), F32),
            "tab_scr": pltpu.VMEM((plan.seq, VR, D), BF),
            "dtab": pltpu.VMEM((plan.seq, VR, D), BF),
        },
        {"pack_in": packs[2]},
        raw_outs,
        idx,
        20 + 8 * plan.seq,
        2 * n * D * (3 * D + 6 * FF),
        n * FF,
    )
    gmid2, dc2, dgain5, dgain6, stat = res.gmid, res.dc, res.dgain, res.dgain6, res.stat
    shard2 = lax.psum_scatter(res.packs[0], "seq", scatter_dimension=0)
    dc2, stat = fence(exchange(dc2), stat)
    dw2, das = attn_backward(
        plan, idx, cos, sin, a2, late, QW, dc2, saved2, n, False, False
    )
    dw2, das = fence(dw2, das)
    (terms,) = fence(scatter_group(das))
    outs, raw_outs = backward_outs(plan, CAP, whole=True)
    res = run_named(
        "join_last",
        functools.partial(join_last_kernel, plan),
        {**outs, "second": sds((n, D), F32), "dgain_in": sds((8, D), F32)},
        {
            "terms": terms,
            "gnext": gmid2,
            "x": x2,
            "cols": cols,
            "gains": gains,
            "y": y1,
            "c": c1,
        },
        backward_scratch(plan, CAP),
        {"pack_in": packs[1]},
        raw_outs,
        idx,
        16 + 8 * plan.seq,
        2 * CAP * D * (2 * D + 5 * FF),
        CAP * FF,
    )
    gmid1, dc1, dgain3, dgain4 = res.gmid, res.dc, res.dgain, res.dgain_in
    shard1 = lax.psum_scatter(res.packs[0], "seq", scatter_dimension=0)
    gsecond = res.second
    dc1, dw2 = fence(dc1, dw2)
    dc1, shard2 = fence(exchange(dc1), shard2)
    dw1, das = attn_backward(
        plan, idx, cos, sin, [*a1, ints_all], late, 0, dc1, saved1, CAP, False, True
    )
    dw1, das, shard2 = fence(dw1, das, swap_first(shard2, "zh", "zl"))
    terms, dw1, shard2 = fence(scatter_group(das), dw1, shard2)
    outs, raw_outs = backward_outs(plan, n)
    res = run_named(
        "join_middle",
        functools.partial(join_middle_kernel, plan),
        {**outs, "dgain_in": sds((8, D), F32)},
        {
            "terms": terms,
            "gnext": gmid1,
            "x": pooled,
            "cols": cols,
            "gains": gains,
            "second": gsecond,
            "bound": bound_grad,
            "y": y0,
            "c": c0,
        },
        backward_scratch(plan, n),
        {"pack_in": packs[0]},
        raw_outs,
        idx,
        16 + 8 * plan.seq,
        1,
        1,
    )
    gmid0, dc0, packs0, dgain1, dgain2 = res.gmid, res.dc, res.packs, res.dgain, res.dgain_in
    shard2 = swap_second(shard2, "zl", "zh")
    dw12 = sum_chips(plan, [jnp.concatenate(pair, axis=0) for pair in zip(dw1, dw2)])
    dc0, packs0, dw12, shard2, shard1 = fence(dc0, packs0, dw12, shard2, shard1)
    dc0, half0, dw12, shard1 = fence(
        exchange(dc0), core_sums(packs0), dw12, swap_first(shard1)
    )
    dw0, (dtab0,) = attn_backward(
        plan, idx, cos, sin, [ints_all, atab], early, 0, dc0, saved0, n, True, False
    )
    dw0, dtab0, half0, dw12, shard1 = fence(
        dw0, dtab0, first_sums(half0), head_sum(plan, dw12, "zh"), swap_second(shard1)
    )
    tail = run(
        "tail",
        functools.partial(tail_kernel, plan),
        [sds((2 * DR + 2 * VR, D), BF)] * plan.chips,
        [idx],
        [
            *(gmid0, dtab0, table, cols, gains),
            *(dgain1, dgain2, dgain3, dgain4, dgain5, dgain6, dgain78),
            *dw0,
        ],
        [pltpu.VMEM((VOCAB, D), F32), pltpu.VMEM((128, D), F32), pltpu.VMEM((D, 128), F32)],
        flops=4 * n * VOCAB * D,
    )
    columns12 = exchange_columns(plan, by_core(dw12[: 2 * DR], dw12[2 * DR :]), me)
    tail, half0, columns12 = fence(tail, second_sums(half0), columns12)
    shard0 = jnp.concatenate(half0, axis=0)
    tail, shard0, stat = fence(sum_chips(plan, tail), swap_first(shard0), stat)
    tail, shard0, stat = fence(
        head_sum(plan, tail, "zh"),
        swap_second(shard0),
        stat + sum(plan.shift(stat, zl=d) for d in range(1, L)),
    )
    stat = stat + plan.shift(stat, zh=1)
    columns0 = exchange_columns(plan, by_core(tail[: 2 * DR], tail[2 * DR :]), me)
    matrix_grad = functools.partial(sds, dtype=BF)
    *grads, gain_t, stat = run(
        "gradients",
        functools.partial(final_kernel, plan),
        [
            matrix_grad(qkv_weight.shape),
            matrix_grad(proj_weight.shape),
            matrix_grad(upward_weight.shape),
            matrix_grad(downward_weight.shape),
            sds(table_weight.shape, F32),
            sds((DR, 128), F32),
            sds((8, 128), F32),
        ],
        [idx],
        [*shard0, *shard1, *shard2, *columns0, *columns12, stat],
        [pltpu.VMEM((G, DR + VR, D), BF), pltpu.VMEM((G, 2 * DR, D), BF)],
        limit=40,
    )
    totals = lax.psum(stat, "seq")[0]
    grads = [grad.astype(F32) for grad in grads]
    valid_count = totals[5]
    inverse = 1.0 / valid_count
    grad_norm = jnp.sqrt(totals[6]) * inverse
    clip = jnp.minimum(1.0, CLIP_NORM / (grad_norm + 1e-06)) * inverse
    weights = (qkv_weight, proj_weight, upward_weight, downward_weight, table_weight)
    firsts = (qkv_first, proj_first, upward_first, downward_first, table_first)
    seconds = (qkv_second, proj_second, upward_second, downward_second, table_second)
    rates = (RATE_MATRIX,) * 4 + (RATE_VECTOR,)
    new = [
        adam_update(w, a, b, g * clip, rate)
        for w, a, b, g, rate in zip(weights, firsts, seconds, grads, rates)
    ]
    new.append(
        run(
            "gains",
            gain_kernel,
            [sds(gain_weight.shape, F32)] * 3,
            [clip.reshape(1)],
            [gain_t, gain_weight, gain_first, gain_second],
        )
    )
    residual_rms = jnp.sqrt(totals[2:5] / (valid_count * D))
    return (
        *[part for triple in new for part in triple],
        *[triple[0].astype(BF) for triple in new[:5]],
        totals[:2],
        valid_count,
        grad_norm,
        residual_rms,
    )


def solution(mesh):
    plan = Plan(mesh)
    tokens = P("seq", "head")
    matrix = P(None, "seq", None)
    vector = P(None, "seq")
    states = (matrix,) * 10 + (vector,) * 2
    return jax.shard_map(
        functools.partial(per_device, plan),
        mesh=mesh,
        in_specs=(tokens,) * 4 + (matrix,) * 5 + (vector,) + states,
        out_specs=(matrix,) * 15 + (vector,) * 3 + (matrix,) * 5 + (P(),) * 4,
        check_vma=False,
    )
```

```python
import functools
import math
from types import SimpleNamespace

import jax
import jax.numpy as jnp
import numpy as np
from jax import lax
from jax.experimental import pallas as pl
from jax.experimental.pallas import tpu as pltpu
from jax.sharding import PartitionSpec as P

D = 512
HEADS = 8
FF = 2048
VOCAB = 256
HEAD_DIM = 64
CAP = 256
STEP = 10
CHUNK = 512
HALF = HEAD_DIM // 2

NORM_EPS = 1e-06
BETA_FIRST = 0.9
BETA_SECOND = 0.95
ADAM_EPS = 1e-08
DECAY_RATE = 0.1
RATE_MATRIX = 0.05
RATE_VECTOR = 0.5
CLIP_NORM = 0.01
MASKED = -1000000000.0
SCALE = HEAD_DIM ** (-0.5)
GELU_A = math.sqrt(2.0 / math.pi)
GELU_B = 0.044715

BF = jnp.bfloat16
F32 = jnp.float32
NN = (((1,), (0,)), ((), ()))
NT = (((1,), (1,)), ((), ()))
AXES = ("seq", "head")
HB = pl.BlockSpec(memory_space=pltpu.HBM)
SM = pl.BlockSpec(memory_space=pltpu.SMEM)


def dot(a, b, dims=NN):
    return lax.dot_general(a, b, dims, preferred_element_type=F32)


def split3(v):
    high = v.astype(BF)
    rest = v - high.astype(F32)
    mid = rest.astype(BF)
    low = (rest - mid.astype(F32)).astype(BF)
    return (high, mid, low)


def exact_dot(ones, v):
    high, mid, low = split3(v)
    return dot(ones, high) + (dot(ones, mid) + dot(ones, low))


def root_of(v):
    return lax.rsqrt(jnp.mean(v * v, axis=-1, keepdims=True) + NORM_EPS)


def norm_back(unit, root, gain, grad):
    turned = grad * gain
    dx = root * (turned - unit * jnp.mean(turned * unit, axis=-1, keepdims=True))
    return dx, jnp.sum(grad * unit, axis=0, keepdims=True)


def gelu_parts(h):
    square = h * h
    t = jnp.tanh(GELU_A * h * (1.0 + GELU_B * square))
    half = 0.5 * (1.0 + t)
    value = h * half
    slope = half + 0.5 * h * (1.0 - t * t) * (GELU_A * (1.0 + 3.0 * GELU_B * square))
    return value, slope


def gelu_value(h):
    t = jnp.tanh(GELU_A * h * (1.0 + GELU_B * (h * h)))
    return h * (0.5 * (1.0 + t))


def one_hot(column, width):
    lanes = lax.broadcasted_iota(jnp.int32, (column.shape[0], width), 1).astype(F32)
    return (lanes == column).astype(F32).astype(BF)


class Plan:
    def __init__(self, mesh):
        self.seq = mesh.shape["seq"]
        self.head = mesh.shape["head"]
        self.chips = self.seq // 2
        side = int(math.isqrt(self.chips))
        while self.chips % side:
            side -= 1
        self.Y, self.X = side, self.chips // side
        self.L = self.head // 2
        self.G = self.head
        self.hd = HEADS // self.G
        self.HW = self.hd * HEAD_DIM
        self.QW = -(-3 * self.HW // 128) * 128
        self.DR = D // self.seq
        self.FR = FF // self.seq
        self.VR = VOCAB // self.seq
        self.sizes = {"y": self.Y, "x": self.X, "core": 2, "zh": 2, "zl": self.L}
        self.names = ("y", "x", "core", "zh", "zl")

    def coords(self):
        for linear in range(self.seq * self.head):
            s, z = divmod(linear, self.head)
            yx, core = divmod(s, 2)
            y, x = divmod(yx, self.X)
            zh, zl = divmod(z, self.L)
            yield linear, {"y": y, "x": x, "core": core, "zh": zh, "zl": zl}

    def linear(self, c):
        s = (c["y"] * self.X + c["x"]) * 2 + c["core"]
        return s * self.head + c["zh"] * self.L + c["zl"]

    def permute(self, v, to):
        pairs = []
        for here, c in self.coords():
            there = to(c)
            if there is not None:
                pairs.append((here, self.linear(there)))
        return lax.ppermute(v, AXES, pairs)

    def shift(self, v, **steps):
        def to(c):
            return {k: (c[k] + steps.get(k, 0)) % self.sizes[k] for k in self.names}

        return self.permute(v, to)

    def place(self):
        s = lax.axis_index("seq")
        z = lax.axis_index("head")
        yx, core = s // 2, s % 2
        return {
            "y": yx // self.X,
            "x": yx % self.X,
            "core": core,
            "zh": z // self.L,
            "zl": z % self.L,
        }

    def tables(self):
        me = self.place()
        G, L, Y, X = self.G, self.L, self.Y, self.X

        def block(sign):
            return [
                ((me["core"] + sign * dc) % 2) * L + (me["zl"] + sign * dl) % L
                for dc in range(2)
                for dl in range(L)
            ]

        def chip(dy, dx):
            return ((me["y"] + dy) % Y) * X + (me["x"] + dx) % X

        chip_src = [chip(-dy, -dx) for dy in range(Y) for dx in range(X)]
        by_x = [chip(dy, dx) for dx in range(X) for dy in range(Y)]
        by_y = [chip(dy, dx) for dy in range(Y) for dx in range(X)]
        head_src = [
            ((me["zh"] - dh) % 2) * L + (me["zl"] - dl) % L for dh in range(2) for dl in range(L)
        ]
        entries = [me["core"], me["zl"]] + block(1) + block(-1) + chip_src + by_x + by_y
        self.at_head = len(entries)
        entries += head_src
        self.at_core = 0
        self.at_zl = 1
        self.at_dst = 2
        self.at_src = 2 + G
        self.at_chip = 2 + 2 * G
        self.at_order = {"x": 2 + 2 * G + Y * X, "y": 2 + 2 * G + 2 * Y * X}
        return jnp.stack([jnp.asarray(e, jnp.int32) for e in entries])


def run(
    name,
    body,
    outs,
    smem,
    arrays,
    scratch=(),
    raw=(),
    raw_outs=(),
    sems=0,
    flops=0,
    trans=0,
    limit=60,
    after=(),
    before=None,
    scalars=(),
):
    operands = [*arrays, *raw]
    results = [*outs, *raw_outs]
    nbytes = sum(a.size * a.dtype.itemsize for a in operands)
    nbytes += sum(math.prod(o.shape) * jnp.dtype(o.dtype).itemsize for o in results)
    ns, ni, nr, na, no, nx = map(len, (smem, arrays, raw, after, outs, raw_outs))

    def wrapped(*refs):
        at = 0
        parts = []
        for count in (ns, ni, nr, na, no, nx, len(scalars), ni, no, len(scratch)):
            parts.append(refs[at : at + count])
            at += count
        s_refs, ins, raws, _, results_out, raws_out, small, bufs, out_bufs, own = parts
        sem = refs[at]
        copies = [
            pltpu.make_async_copy(src, dst, sem.at[k])
            for k, (src, dst) in enumerate(zip(ins, bufs))
        ]
        for copy in copies:
            copy.start()
        extra = (refs[at + 1],) if sems else ()
        if before is not None:
            before(*s_refs, *bufs, *raws, *out_bufs, *raws_out, *own, *extra)
        for copy in copies:
            copy.wait()
        body(*s_refs, *bufs, *raws, *out_bufs, *raws_out, *small, *own, *extra)
        copies = [
            pltpu.make_async_copy(src, dst, sem.at[k])
            for k, (src, dst) in enumerate(zip(out_bufs, results_out))
        ]
        for copy in copies:
            copy.start()
        for copy in copies:
            copy.wait()

    spaces = [pltpu.VMEM(v.shape, v.dtype) for v in (*arrays, *outs)]
    spaces += list(scratch) + [pltpu.SemaphoreType.DMA((max(ni, no, 1),))]
    if sems:
        spaces.append(pltpu.SemaphoreType.DMA((sems,)))
    return pl.pallas_call(
        wrapped,
        out_shape=tuple([*results, *[sds((count,), F32) for count in scalars]]),
        in_specs=[SM] * ns + [HB] * (ni + nr) + [pl.BlockSpec(memory_space=pl.ANY)] * na,
        out_specs=tuple([HB] * len(results) + [SM] * len(scalars)),
        scratch_shapes=spaces,
        compiler_params=pltpu.CompilerParams(vmem_limit_bytes=limit << 20),
        cost_estimate=pl.CostEstimate(
            flops=int(flops), bytes_accessed=int(nbytes), transcendentals=int(trans)
        ),
        name=name,
    )(*smem, *operands, *after)


def run_named(name, body, outs, arrays, scratch, raw, raw_outs, idx, sems, flops, trans, begin):
    def flat(group):
        out = []
        for value in group.values():
            out += list(value) if isinstance(value, (list, tuple)) else [value]
        return out

    def name_all(space, group, refs):
        for key, value in group.items():
            if isinstance(value, (list, tuple)):
                setattr(space, key, [refs.pop(0) for _ in value])
            else:
                setattr(space, key, refs.pop(0))

    space = SimpleNamespace()

    def before(idx_ref, *refs):
        space.idx, refs = idx_ref, list(refs)
        for group in (arrays, raw, outs, raw_outs, scratch):
            name_all(space, group, refs)
        space.sem = refs.pop(0)
        begin(space)

    def wrapped(*refs):
        body(space)

    res = list(
        run(
            name,
            wrapped,
            flat(outs),
            [idx],
            flat(arrays),
            flat(scratch),
            flat(raw),
            flat(raw_outs),
            sems,
            flops,
            trans,
            before=before,
        )
    )
    found = SimpleNamespace()
    for group in (outs, raw_outs):
        name_all(found, group, res)
    return found


def fence(*groups):
    return lax.optimization_barrier(groups)


class Copies:
    def __init__(self, sem):
        self.sem = sem
        self.count = 0
        self.open = []

    def start(self, src, dst):
        copy = pltpu.make_async_copy(src, dst, self.sem.at[self.count])
        self.count += 1
        copy.start()
        self.open.append(copy)
        return copy

    def finish(self):
        for copy in self.open:
            copy.wait()
        self.open = []


def rows_at(index, size):
    return pl.ds(pl.multiple_of(index * size, size), size)


def sds(shape, dtype):
    return jax.ShapeDtypeStruct(shape, dtype)


def first_kernel(plan, idx, qkv, table, gain, *refs):
    keep0, send0, keep1, send1, scr = refs
    DR, VR, HW, QW = plan.DR, plan.VR, plan.HW, plan.QW
    core, zl = idx[plan.at_core], idx[plan.at_zl]
    for which, outs in ((0, (keep0, keep1)), (1, (send0, send1))):
        block = lax.rem(core + which, 2) * plan.L + zl
        for layer in range(3):
            out, lo = ((outs[0], 0), (outs[1], 0), (outs[1], QW))[layer]
            for part in range(3):
                if HW % 128 == 0:
                    at = pl.ds(pl.multiple_of(part * D + block * HW, HW), HW)
                    piece = qkv[layer, :, at]
                else:
                    at = pl.ds(pl.multiple_of(part * D + block // 2 * 128, 128), 128)
                    both = qkv[layer, :, at]
                    piece = jnp.where(block % 2 == 0, both[:, :HW], both[:, HW:])
                out[:, lo + part * HW : lo + (part + 1) * HW] = piece.astype(BF)
    scr[...] = jnp.zeros_like(scr)
    scr[0 : gain.shape[0], 0:DR] = gain[...]
    turned = scr[...].T[0:DR, :].astype(BF)
    low = table[0].astype(BF)
    for out in (keep0, send0):
        out[:, QW : QW + 256] = jnp.concatenate([low[:, :256], low[:, 256:]], axis=0)
        out[:, QW + 256 : QW + 384] = turned


class PackCast:
    def __init__(self, plan, layer, copies, sources, scr):
        self.plan, self.layer = plan, layer
        up, down, proj, table = sources
        self.up, self.down, self.proj, self.table = scr
        self.copies = [
            copies.start(up.at[layer], self.up),
            copies.start(down.at[layer], self.down),
            copies.start(proj.at[layer], self.proj.at[0]),
        ]
        if layer == 1:
            self.copies.append(copies.start(proj.at[3], self.proj.at[1]))
        if layer == 2:
            self.copies.append(copies.start(table.at[1], self.table))
        copies.open = []

    @staticmethod
    def rows(plan, layer):
        return 5 * plan.DR + plan.FR + (0, plan.DR, plan.VR)[layer]

    @staticmethod
    def scratch(plan):
        return [
            pltpu.VMEM((plan.DR, FF), F32),
            pltpu.VMEM((plan.FR, D), F32),
            pltpu.VMEM((2, plan.DR, D), F32),
            pltpu.VMEM((plan.VR, D), F32),
        ]

    def write(self, out):
        DR, FR, VR = self.plan.DR, self.plan.FR, self.plan.VR
        for copy in self.copies:
            copy.wait()
        for j in range(FF // CHUNK):
            at = slice(j * CHUNK, (j + 1) * CHUNK)
            out[j * DR : (j + 1) * DR, :] = self.up[:, at].astype(BF)
        top = 4 * DR
        out[top : top + FR, :] = self.down[...].astype(BF)
        top += FR
        out[top : top + DR, :] = self.proj[0].astype(BF)
        top += DR
        if self.layer == 1:
            out[top : top + DR, :] = self.proj[1].astype(BF)
        if self.layer == 2:
            out[top : top + VR, :] = self.table[...].astype(BF)


def pack_kernel(plan, layer, up, down, proj, table, out, *scr):
    *scr, sem = scr
    PackCast(plan, layer, Copies(sem), (up, down, proj, table), scr).write(out)


def prep_kernel(plan, idx, ints, *refs):
    pieces = refs[: plan.chips]
    table_out, atab_out, gain_out, cols_out, table_scr, gain_scr, row_scr = refs[plan.chips :]
    slots = ints[3:4, :].astype(F32)
    n = slots.shape[1]
    lanes = lax.broadcasted_iota(jnp.int32, (1, n), 1)
    row_scr[...] = jnp.zeros_like(row_scr)
    row_scr[VALID : VALID + 1, :] = ints[2:3, :].astype(F32)
    changed = jnp.concatenate([slots[:, 0:1], slots[:, 0 : n - 1]], axis=1) != slots
    row_scr[TARGET : TARGET + 1, :] = jnp.where((lanes == 0) | changed, 1.0, 0.0)
    row_scr[NEXT : NEXT + 1, :] = ints[1:2, :].astype(F32)
    row_scr[SLOT : SLOT + 1, :] = slots
    row_scr[BYTE : BYTE + 1, :] = ints[0:1, :].astype(F32)
    cols_out[...] = row_scr[...].T
    VR, DR, QW = plan.VR, plan.DR, plan.QW
    for r in range(plan.chips):
        k = idx[plan.at_chip + r]
        for core in range(2):
            for half in range(2):
                rows = pieces[r][core * DR + half * VR : core * DR + (half + 1) * VR, QW : QW + 256]
                table_scr[
                    pl.ds(pl.multiple_of(k * 2 * VR, 2 * VR) + core * VR, VR),
                    half * 256 : half * 256 + 256,
                ] = rows.astype(F32)
        gain_scr[pl.ds(pl.multiple_of(k * 2 * DR, 2 * DR), 2 * DR), :] = pieces[r][
            :, QW + 256 : QW + 384
        ].astype(F32)
    gains = gain_scr[...].T[0:16, :]
    gain_out[...] = gains
    table = table_scr[...]
    table_out[...] = table.astype(BF)
    atab_out[...] = (table * root_of(table) * gains[0:1, :]).astype(BF)


def load_weight(plan, copies, idx, pieces, lo, w_scr):
    started = []
    for r in range(plan.chips):
        src = pieces[r].at[:, lo : lo + plan.QW]
        started.append(copies.start(src, w_scr.at[rows_at(idx[plan.at_chip + r], 2 * plan.DR), :]))
    return started


def live_bias(plan, idx, ints, n, bias_scr):
    row = lax.broadcasted_iota(jnp.int32, (n, 128), 0).astype(F32)
    for r in range(plan.G):
        slots = ints[8 * r + 3 : 8 * r + 4, :].astype(F32)
        last = jnp.max(slots, axis=1, keepdims=True)
        bias_scr[rows_at(idx[plan.at_src + r], n), :] = jnp.where(row <= last, 0.0, MASKED)


def head_pad(plan, part, h):
    if plan.hd == 1:
        return part
    blank = jnp.zeros_like(part)
    return jnp.concatenate([part if k == h else blank for k in range(plan.hd)], axis=0)


def rot_pair(a, b, cos, sin):
    return a * cos - b * sin, b * cos + a * sin


def attn_fwd_kernel(plan, n, lo, embed, masked, rider, idx, *refs):
    G, HW, hd = plan.G, plan.HW, plan.hd
    S = G * n
    refs = list(refs)
    cos_ref, sin_ref = refs[0], refs[1]
    refs = refs[2:]
    if embed:
        ints_ref, atab_ref = refs[0], refs[1]
        refs = refs[2:]
    else:
        a_refs = refs[:G]
        refs = refs[G:]
    if masked:
        ints_ref = refs[0]
        refs = refs[1:]
    w_refs = refs[: plan.chips]
    refs = refs[plan.chips :]
    if rider:
        rider_in, refs = refs[:4], refs[4:]
    c_outs = refs[:G]
    qkvt_out, ot_out, lse_out = refs[G : G + 3]
    refs = refs[G + 3 :]
    if rider:
        rider_out, refs = refs[0], refs[1:]
    w_scr, cos_scr, sin_scr, src_scr, tab_scr, ints_scr, bias_scr = refs[:7]
    qkvt, ot, lse, k_scr, c_scr = refs[7:12]
    *rider_scr, sem = refs[12:]
    copies = Copies(sem)
    first = load_weight(plan, copies, idx, w_refs, lo, w_scr)
    first.append(copies.start(cos_ref, cos_scr))
    first.append(copies.start(sin_ref, sin_scr))
    sources = []
    if embed or masked:
        first.append(copies.start(ints_ref, ints_scr))
    if embed:
        first.append(copies.start(atab_ref, tab_scr))
    else:
        for r in range(G):
            dst = src_scr.at[rows_at(idx[plan.at_src + r], n), :]
            sources.append(copies.start(a_refs[r], dst))
    copies.open = []
    if rider:
        cast = PackCast(plan, rider, copies, rider_in, rider_scr[1:])
    for copy in first:
        copy.wait()
    wt = w_scr[...].T[0 : 3 * HW, :]
    if embed:
        base = split3(dot(wt, tab_scr[...], NT))
    if masked:
        live_bias(plan, idx, ints_scr, n, bias_scr)
    for r in range(G):
        at = rows_at(idx[plan.at_src + r], n)
        if embed:
            ids = ints_scr[8 * r : 8 * r + 1, :]
            hot = (lax.broadcasted_iota(jnp.int32, (VOCAB, n), 0) == ids).astype(F32).astype(BF)
            m = dot(base[0], hot) + (dot(base[1], hot) + dot(base[2], hot))
        else:
            sources[r].wait()
            m = dot(wt, src_scr[at, :], NT)
        cos, sin = cos_scr[:, at], sin_scr[:, at]
        for h in range(hd):
            for part, factor in ((0, SCALE), (1, 1.0)):
                top = part * HW + h * HEAD_DIM
                one, two = rot_pair(m[top : top + HALF], m[top + HALF : top + HEAD_DIM], cos, sin)
                qkvt[top : top + HALF, at] = (one * factor).astype(BF)
                qkvt[top + HALF : top + HEAD_DIM, at] = (two * factor).astype(BF)
        qkvt[2 * HW : 3 * HW, at] = m[2 * HW : 3 * HW].astype(BF)
        k_scr[at, :] = qkvt[HW : 2 * HW, at].T
    copies.start(qkvt, qkvt_out)
    if rider:
        cast.write(rider_scr[0])
        copies.start(rider_scr[0], rider_out)
    tile = min(512, S)

    def tile_scores(q_pads, keys, rows, diagonal):
        out = []
        for h in range(hd):
            s = dot(keys, q_pads[h])
            if masked:
                s = s + jnp.concatenate([bias_scr[rows, :]] * (tile // 128), axis=1)
            if diagonal:
                kk = lax.broadcasted_iota(jnp.int32, (tile, tile), 0)
                qq = lax.broadcasted_iota(jnp.int32, (tile, tile), 1)
                s = jnp.where(kk <= qq, s, MASKED)
            out.append(s)
        return out

    def one_query(i, _):
        cols = pl.ds(pl.multiple_of(i * tile, tile), tile)
        q_pads = [
            head_pad(plan, qkvt[h * HEAD_DIM : (h + 1) * HEAD_DIM, cols], h) for h in range(hd)
        ]

        def step(j, state, diagonal):
            rows = pl.ds(pl.multiple_of(j * tile, tile), tile)
            scores = tile_scores(q_pads, k_scr[rows, :], rows, diagonal)
            new = []
            for h in range(hd):
                top, total, acc = state[3 * h : 3 * h + 3]
                s = scores[h]
                new_top = jnp.maximum(top, jnp.max(s, axis=0, keepdims=True))
                p = jnp.exp(s - new_top)
                keep = jnp.exp(top - new_top)
                total = total * keep + jnp.sum(p, axis=0, keepdims=True)
                vt = qkvt[2 * HW + h * HEAD_DIM : 2 * HW + (h + 1) * HEAD_DIM, rows]
                acc = acc * keep + dot(vt, p.astype(BF))
                new += [new_top, total, acc]
            return tuple(new)

        state = ()
        for h in range(hd):
            state += (
                jnp.full((1, tile), -1e30, F32),
                jnp.zeros((1, tile), F32),
                jnp.zeros((HEAD_DIM, tile), F32),
            )
        state = lax.fori_loop(0, i, lambda j, st: step(j, st, False), state)
        state = step(i, state, True)
        for h in range(hd):
            top, total, acc = state[3 * h : 3 * h + 3]
            ot[h * HEAD_DIM : (h + 1) * HEAD_DIM, cols] = acc / total
            lse[h : h + 1, cols] = top + jnp.log(total)
        c_scr[cols, :] = ot[:, cols].T.astype(BF)
        return 0

    lax.fori_loop(0, S // tile, one_query, 0)
    for r in range(G):
        copies.start(c_scr.at[rows_at(idx[plan.at_dst + r], n), :], c_outs[r])
    copies.start(ot, ot_out)
    copies.start(lse, lse_out)
    copies.finish()


def source_scratch(embed, masked, S, G, source):
    none = pltpu.VMEM((16, 128), BF)
    return [
        none if embed else pltpu.VMEM((S, D), BF),
        pltpu.VMEM((VOCAB, D), BF) if embed else none,
        pltpu.VMEM(source[0 if embed else G].shape, jnp.int32) if embed or masked else none,
        pltpu.VMEM((S, 128), F32) if masked else none,
    ]


def attn_forward(
    plan, idx, cos, sin, source, weights, lo, n, embed, masked, rider=0, rider_in=()
):
    G, HW = plan.G, plan.HW
    S = G * n
    outs = [sds((n, HW), BF)] * G + [
        sds((3 * HW, S), BF),
        sds((HW, S), F32),
        sds((8, S), F32),
    ]
    extra = []
    if rider:
        outs.append(sds((PackCast.rows(plan, rider), D), BF))
        extra = [pltpu.VMEM(outs[-1].shape, BF), *PackCast.scratch(plan)]
    res = run(
        "attention_forward",
        functools.partial(attn_fwd_kernel, plan, n, lo, embed, masked, rider),
        [],
        [idx],
        [],
        [
            pltpu.VMEM((D, plan.QW), BF),
            pltpu.VMEM(cos.shape, F32),
            pltpu.VMEM(cos.shape, F32),
            *source_scratch(embed, masked, S, G, source),
            pltpu.VMEM((3 * HW, S), BF),
            pltpu.VMEM((HW, S), F32),
            pltpu.VMEM((8, S), F32),
            pltpu.VMEM((S, HW), BF),
            pltpu.VMEM((S, HW), BF),
            *extra,
        ],
        raw=[cos, sin, *source, *weights, *rider_in],
        raw_outs=outs,
        sems=plan.chips + 2 * G + 16,
        flops=2 * S * D * 3 * HW + 2 * plan.hd * S * S * 256,
        trans=plan.hd * S * S // 2,
    )
    if rider:
        return res[:G], res[G : G + 3], res[G + 3]
    return res[:G], res[G:]


def attn_bwd_kernel(plan, n, lo, embed, masked, idx, *refs):
    G, HW, hd = plan.G, plan.HW, plan.hd
    S = G * n
    refs = list(refs)
    cos_ref, sin_ref = refs[0], refs[1]
    refs = refs[2:]
    if embed:
        ints_ref, atab_ref = refs[0], refs[1]
        refs = refs[2:]
    else:
        a_refs = refs[:G]
        refs = refs[G:]
    if masked:
        ints_ref = refs[0]
        refs = refs[1:]
    w_refs = refs[: plan.chips]
    refs = refs[plan.chips :]
    do_refs = refs[:G]
    qkvt_in, ot_in, lse_in = refs[G : G + 3]
    refs = refs[G + 3 :]
    dw_outs = refs[: plan.chips]
    refs = refs[plan.chips :]
    if embed:
        tab_out = refs[0]
        refs = refs[1:]
    else:
        da_outs = refs[:G]
        refs = refs[G:]
    w_scr, cos_scr, sin_scr, src_scr, tab_scr, ints_scr, bias_scr, qkvt, ot, lse = refs[:10]
    do_all, k_scr, v_scr, qz, qtz, doz, dotz, delta, dqt, dk, dv, dmt, res_scr, dw_scr, sem = refs[10:]
    copies = Copies(sem)
    if embed or masked:
        copies.start(ints_ref, ints_scr)
    copies.start(qkvt_in, qkvt)
    for r in range(G):
        copies.start(do_refs[r], do_all.at[rows_at(idx[plan.at_src + r], n), :])
    copies.start(ot_in, ot)
    copies.start(lse_in, lse)
    first, copies.open = copies.open, []
    copies.start(cos_ref, cos_scr)
    copies.start(sin_ref, sin_scr)
    angles, copies.open = copies.open, []
    load_weight(plan, copies, idx, w_refs, lo, w_scr)
    if embed:
        copies.start(atab_ref, tab_scr)
    else:
        for r in range(G):
            copies.start(a_refs[r], src_scr.at[rows_at(idx[plan.at_src + r], n), :])
    last, copies.open = copies.open, []
    for copy in first:
        copy.wait()
    tile = min(512, S)
    blocks = S // tile
    lane = lax.broadcasted_iota(jnp.int32, (tile, HW), 1) // HEAD_DIM
    for b in range(blocks):
        at = slice(b * tile, (b + 1) * tile)
        dob = do_all[at, :]
        dobt = dob.T
        kt = qkvt[HW : 2 * HW, at]
        k_scr[at, :] = kt.T
        v_scr[at, :] = qkvt[2 * HW : 3 * HW, at].T
        prod = dobt.astype(F32) * ot[:, at]
        dob32 = dob.astype(F32)
        for h in range(hd):
            rows = slice(h * HEAD_DIM, (h + 1) * HEAD_DIM)
            pad = head_pad(plan, qkvt[rows, at], h)
            qtz[h, :, at] = pad
            qz[h, at, :] = pad.T
            dotz[h, :, at] = head_pad(plan, dobt[rows, :], h)
            doz[h, at, :] = jnp.where(lane == h, dob32, 0.0).astype(BF)
            delta[h : h + 1, at] = jnp.sum(prod[rows, :], axis=0, keepdims=True)
    dqt[...] = jnp.zeros_like(dqt)
    if masked:
        live_bias(plan, idx, ints_scr, n, bias_scr)
    for copy in angles:
        copy.wait()

    def one_key(j, _):
        rows = pl.ds(pl.multiple_of(j * tile, tile), tile)
        keys, values = k_scr[rows, :], v_scr[rows, :]
        dk[...] = jnp.zeros_like(dk)
        dv[...] = jnp.zeros_like(dv)
        bias = jnp.concatenate([bias_scr[rows, :]] * (tile // 128), axis=1) if masked else None

        def step(i, diagonal):
            cols = pl.ds(pl.multiple_of(i * tile, tile), tile)
            for h in range(hd):
                s = dot(keys, qtz[h, :, cols])
                if masked:
                    s = s + bias
                if diagonal:
                    kk = lax.broadcasted_iota(jnp.int32, (tile, tile), 0)
                    qq = lax.broadcasted_iota(jnp.int32, (tile, tile), 1)
                    s = jnp.where(kk <= qq, s, MASKED)
                p = jnp.exp(s - lse[h : h + 1, cols])
                dp = dot(values, dotz[h, :, cols])
                ds = (p * (dp - delta[h : h + 1, cols])).astype(BF)
                dv[...] += dot(p.astype(BF), doz[h, cols, :])
                dk[...] += dot(ds, qz[h, cols, :])
                kt = qkvt[HW + h * HEAD_DIM : HW + (h + 1) * HEAD_DIM, rows]
                dqt[h * HEAD_DIM : (h + 1) * HEAD_DIM, cols] += dot(kt, ds)

        step(j, True)

        def more(i, carry):
            step(i, False)
            return carry

        lax.fori_loop(j + 1, blocks, more, 0)
        dkt = dk[...].T
        cos, sin = cos_scr[:, rows], sin_scr[:, rows]
        for h in range(hd):
            top = h * HEAD_DIM
            one, two = rot_pair(
                dkt[top : top + HALF], dkt[top + HALF : top + HEAD_DIM], cos, -sin
            )
            dmt[HW + top : HW + top + HALF, rows] = one.astype(BF)
            dmt[HW + top + HALF : HW + top + HEAD_DIM, rows] = two.astype(BF)
        dmt[2 * HW : 3 * HW, rows] = dv[...].T.astype(BF)
        return 0

    lax.fori_loop(0, blocks, one_key, 0)
    cos, sin = cos_scr[:, 0:S], sin_scr[:, 0:S]
    for h in range(hd):
        top = h * HEAD_DIM
        one, two = rot_pair(
            dqt[top : top + HALF, :] * SCALE,
            dqt[top + HALF : top + HEAD_DIM, :] * SCALE,
            cos,
            -sin,
        )
        dmt[top : top + HALF, :] = one.astype(BF)
        dmt[top + HALF : top + HEAD_DIM, :] = two.astype(BF)
    for copy in last:
        copy.wait()
    wt = w_scr[...].T[0 : 3 * HW, :]
    if embed:
        sums = jnp.zeros((3 * HW, VOCAB), F32)
        for r in range(G):
            at = rows_at(idx[plan.at_src + r], n)
            ids = ints_scr[8 * r : 8 * r + 1, :]
            hot = (lax.broadcasted_iota(jnp.int32, (VOCAB, n), 0) == ids).astype(F32).astype(BF)
            sums += dot(dmt[:, at], hot, NT)
        high = sums.astype(BF)
        low = (sums - high.astype(F32)).astype(BF)
        res_scr[...] = dot(high.T, wt) + dot(low.T, wt)
        copies.start(res_scr, tab_out)
        grad = dot(high, tab_scr[...]) + dot(low, tab_scr[...])
    else:
        for r in reversed(range(G)):
            at = rows_at(idx[plan.at_dst + r], n)
            res_scr[at, :] = dot(dmt[:, at].T, wt).astype(BF)
            copies.start(res_scr.at[at, :], da_outs[r])
        grad = dot(dmt[...], src_scr[...])
    dw_scr[:, 0 : 3 * HW] = grad.T.astype(BF)
    dw_scr[:, 3 * HW : D] = jnp.zeros((D, D - 3 * HW), BF)
    for r in range(plan.chips):
        at = rows_at(idx[plan.at_order["x"] + r], 2 * plan.DR)
        copies.start(dw_scr.at[at, :], dw_outs[r])
    copies.finish()


def attn_backward(
    plan, idx, cos, sin, source, weights, lo, dos, saved, n, embed, masked, after=()
):
    G, HW, hd = plan.G, plan.HW, plan.hd
    S = G * n
    tile = min(512, S)
    outs = [sds((2 * plan.DR, D), BF)] * plan.chips
    outs += [sds((VOCAB, D), F32)] if embed else [sds((n, D), BF)] * G
    res = run(
        "attention_backward",
        functools.partial(attn_bwd_kernel, plan, n, lo, embed, masked),
        [],
        [idx],
        [],
        [
            pltpu.VMEM((D, plan.QW), BF),
            pltpu.VMEM(cos.shape, F32),
            pltpu.VMEM(cos.shape, F32),
            *source_scratch(embed, masked, S, G, source),
            pltpu.VMEM((3 * HW, S), BF),
            pltpu.VMEM((HW, S), F32),
            pltpu.VMEM((8, S), F32),
            pltpu.VMEM((S, HW), BF),
            pltpu.VMEM((S, HW), BF),
            pltpu.VMEM((S, HW), BF),
            pltpu.VMEM((hd, S, HW), BF),
            pltpu.VMEM((hd, HW, S), BF),
            pltpu.VMEM((hd, S, HW), BF),
            pltpu.VMEM((hd, HW, S), BF),
            pltpu.VMEM((8, S), F32),
            pltpu.VMEM((HW, S), F32),
            pltpu.VMEM((tile, HW), F32),
            pltpu.VMEM((tile, HW), F32),
            pltpu.VMEM((3 * HW, S), BF),
            pltpu.VMEM((VOCAB, D), F32) if embed else pltpu.VMEM((S, D), BF),
            pltpu.VMEM((D, D), BF),
        ],
        raw=[cos, sin, *source, *weights, *dos, *saved],
        raw_outs=outs,
        sems=2 * plan.chips + 3 * G + 8,
        flops=4 * S * D * 3 * HW + 5 * hd * S * S * 256,
        trans=hd * S * S // 2,
        after=after,
    )
    return res[: plan.chips], res[plan.chips :]


class Pack:
    def __init__(self, plan, copies, pack, scr):
        self.plan = plan
        self.up_scr, self.down_scr, self.proj_scr = scr
        DR, FR = plan.DR, plan.FR
        self.per = CHUNK // FR
        top = 4 * DR + FR
        self.proj_copy = copies.start(pack.at[:, top : top + DR, :], self.proj_scr)
        self.copies = []
        for j in range(FF // CHUNK):
            at = slice(j * self.per, (j + 1) * self.per)
            self.copies.append(
                (
                    copies.start(pack.at[:, j * DR : (j + 1) * DR, :], self.up_scr.at[j]),
                    copies.start(pack.at[at, 4 * DR : 4 * DR + FR, :], self.down_scr.at[j]),
                )
            )
        copies.open = []

    @staticmethod
    def scratch(plan):
        chunks = FF // CHUNK
        return [
            pltpu.VMEM((chunks, plan.seq, plan.DR, D), BF),
            pltpu.VMEM((chunks, CHUNK // plan.FR, plan.FR, D), BF),
            pltpu.VMEM((plan.seq, plan.DR, D), BF),
        ]

    def proj(self, k):
        per = self.plan.HW // self.plan.DR
        rows = self.proj_scr[pl.ds(k * per, per), :, :]
        return rows.reshape(self.plan.HW, D)

    def up(self, j):
        return self.up_scr[j].reshape(D, CHUNK)

    def down(self, j):
        return self.down_scr[j].reshape(CHUNK, D)


VALID, TARGET, NEXT, SLOT, BYTE = range(5)


def at_lane(lane, value):
    lanes = lax.broadcasted_iota(jnp.int32, (8, 128), 1)
    return jnp.where(lanes == lane, jnp.broadcast_to(value, (8, 128)), 0.0)


def square_of(cols, x):
    rows = jnp.sum(x * x, axis=-1, keepdims=True) * cols[:, VALID : VALID + 1]
    return jnp.sum(rows, axis=0, keepdims=True)


def attended(plan, k, x):
    k.pack.proj_copy.wait()
    y = x
    for r in range(plan.G):
        y += dot(k.c[r][...], k.pack.proj(k.idx[plan.at_src + r]))
    k.y[...] = y


def feed_forward(k, layer, y, keep=False):
    k.normed[...] = (y * root_of(y) * k.gains[2 * layer + 1 : 2 * layer + 2, :]).astype(BF)
    for j in range(FF // CHUNK):
        k.pack.copies[j][0].wait()
        h = dot(k.normed[...], k.pack.up(j))
        at = slice(j * CHUNK, (j + 1) * CHUNK)
        if keep:
            value, slope = gelu_parts(h)
            k.slope[j] = slope
        else:
            value = gelu_value(h)
        k.act[:, at] = value.astype(BF)
    for j in range(FF // CHUNK):
        k.pack.copies[j][1].wait()
    k.x_scr[...] = k.y[...] + dot(k.act[...], k.down_scr[...].reshape(FF, D))


def begin_pack(plan, table, k):
    k.copies = Copies(k.sem)
    k.pack = Pack(plan, k.copies, k.pack_in, (k.up_scr, k.down_scr, k.proj_scr))
    if table:
        top = 5 * plan.DR + plan.FR
        k.tab_copy = k.copies.start(k.pack_in.at[:, top : top + plan.VR, :], k.tab_scr)
        k.copies.open = []


def ffn_pool_kernel(plan, k):
    x = dot(one_hot(k.cols[:, BYTE : BYTE + 1], VOCAB), k.table[...])
    attended(plan, k, x)
    feed_forward(k, 0, k.y[...])
    x = k.x_scr[...]
    k.x[...] = x
    turned = one_hot(k.cols[:, SLOT : SLOT + 1], CAP).T
    counts = jnp.sum(turned.astype(F32), axis=1, keepdims=True)
    pooled = exact_dot(turned, x) / jnp.maximum(counts, 1.0)
    k.pooled[...] = pooled
    k.a[...] = (pooled * root_of(pooled) * k.gains[2:3, :]).astype(BF)
    count = jnp.sum(k.cols[:, VALID : VALID + 1], axis=0, keepdims=True)
    k.stat[...] = at_lane(2, square_of(k.cols, x)) + at_lane(5, count)


def ffn_unpool_kernel(plan, k):
    attended(plan, k, k.pooled[...])
    feed_forward(k, 1, k.y[...])
    x = k.x1[...] + exact_dot(one_hot(k.cols[:, SLOT : SLOT + 1], CAP), k.x_scr[...])
    k.x[...] = x
    k.a[...] = (x * root_of(x) * k.gains[4:5, :]).astype(BF)
    k.stat[...] = k.stat_in[...] + at_lane(3, square_of(k.cols, x))


def forward_scratch(plan, n):
    return {
        **dict(zip(("up_scr", "down_scr", "proj_scr"), Pack.scratch(plan))),
        "normed": pltpu.VMEM((n, D), BF),
        "act": pltpu.VMEM((n, FF), BF),
        "x_scr": pltpu.VMEM((n, D), F32),
    }


def loss_part(plan, k):
    k.tab_copy.wait()
    table = k.tab_scr[...].reshape(VOCAB, D)
    x = k.x_scr[...]
    valid = k.cols[:, VALID : VALID + 1]
    root = root_of(x)
    unit = x * root
    gain = k.gains[6:7, :]
    rows = (unit * gain).astype(BF)
    logits = dot(rows, table, NT)
    top_row = jnp.max(logits, axis=-1, keepdims=True)
    total = jnp.sum(jnp.exp(logits - top_row), axis=-1, keepdims=True)
    log_norm = top_row + jnp.log(total)
    hot = one_hot(k.cols[:, NEXT : NEXT + 1], VOCAB).astype(F32)
    picked = jnp.sum(logits * hot, axis=-1, keepdims=True)
    ce = jnp.sum(valid * (log_norm - picked), axis=0, keepdims=True)
    glog = (valid * (jnp.exp(logits - log_norm) - hot)).astype(BF)
    k.dtab[...] = dot(glog.T, rows).astype(BF).reshape(plan.seq, plan.VR, D)
    dx, dgain = norm_back(unit, root, gain, dot(glog, table))
    k.gout[...] = dx
    k.dgain6[...] = jnp.broadcast_to(dgain, k.dgain6.shape)
    k.stat[...] = (
        k.stat_a[...] + k.stat_b[...] + at_lane(0, ce) + at_lane(4, square_of(k.cols, x))
    )


def ffn_backward_part(plan, k, layer, y, send, kept=False):
    root = root_of(y)
    gain = k.gains[2 * layer + 1 : 2 * layer + 2, :]
    k.unit[...] = y * root
    if not kept:
        k.normed[...] = (y * root * gain).astype(BF)
    k.normt[...] = k.normed[...].T
    k.low[...] = k.gout[...].astype(BF)
    k.dn[...] = jnp.zeros_like(k.dn)
    for j in range(FF // CHUNK):
        if kept:
            value, slope = k.act[:, j * CHUNK : (j + 1) * CHUNK], k.slope[j]
            up = k.pack.up(j)
        else:
            for copy in k.pack.copies[j]:
                copy.wait()
            up = k.pack.up(j)
            value, slope = gelu_parts(dot(k.normed[...], up))
            value = value.astype(BF)
        per = CHUNK // plan.FR
        grad = dot(value.T, k.low[...]).astype(BF)
        k.ddown[j * per : (j + 1) * per] = grad.reshape(per, plan.FR, D)
        dact = dot(k.low[...], k.pack.down(j), NT)
        dh = (dact * slope).astype(BF)
        k.dup[j] = dot(k.normt[...], dh).astype(BF).reshape(plan.seq, plan.DR, CHUNK)
        send(j)
        k.dn[...] += dot(dh, up, NT)
    dx, dgain = norm_back(k.unit[...], root, gain, k.dn[...])
    gmid = k.gout[...] + dx
    k.gmid[...] = gmid
    k.dgain[...] = jnp.broadcast_to(dgain, k.dgain.shape)
    k.low[...] = gmid.astype(BF)
    if not kept:
        k.pack.proj_copy.wait()
    HW = plan.HW
    for r in range(plan.G):
        per = HW // plan.DR
        grad = dot(k.c[r][...].T, k.low[...]).astype(BF)
        k.dproj[pl.ds(k.idx[plan.at_src + r] * per, per)] = grad.reshape(per, plan.DR, D)
        k.dc[r][...] = dot(k.low[...], k.pack.proj(k.idx[plan.at_dst + r]), NT).astype(BF)


def send_packs(plan, k, copies):
    DR, FR = plan.DR, plan.FR

    def shard(order, r, dc):
        core = lax.rem(k.idx[plan.at_core] + dc, 2)
        return k.idx[plan.at_order[order] + r] * 2 + core

    def upward(j):
        for dc in (1, 0):
            for r in range(plan.chips):
                out = k.packs[2 * dc].at[r, j * DR : (j + 1) * DR, :]
                copies.start(k.dup.at[j, shard("x", r, dc)], out)

    def rest():
        for dc in (1, 0):
            two = k.packs[2 * dc + 1]
            for r in range(plan.chips):
                s = shard("y", r, dc)
                copies.start(k.ddown.at[s], two.at[r, 0:FR, :])
                copies.start(k.dproj.at[s], two.at[r, FR : FR + DR, :])
        copies.finish()

    return upward, rest


def send_whole(plan, k, copies, extra=False):
    DR, FR, VR = plan.DR, plan.FR, plan.VR
    (out,) = k.packs
    per = CHUNK // FR
    down_at = 4 * DR + (DR + VR if extra else 0)

    def upward(j):
        copies.start(k.dup.at[j], out.at[:, j * DR : (j + 1) * DR, :])
        at = slice(j * per, (j + 1) * per)
        copies.start(k.ddown.at[at], out.at[at, down_at : down_at + FR, :])

    def rest():
        top = 4 * DR
        if extra:
            copies.start(k.dp3, out.at[:, top : top + DR, :])
            top += DR
            copies.start(k.dtab, out.at[:, top : top + VR, :])
        top = down_at + FR
        copies.start(k.dproj, out.at[:, top : top + DR, :])
        copies.finish()

    return upward, rest


def backward_scratch(plan, n):
    return {
        **forward_scratch(plan, n),
        "gout": pltpu.VMEM((n, D), F32),
        "unit": pltpu.VMEM((n, D), F32),
        "normt": pltpu.VMEM((D, n), BF),
        "low": pltpu.VMEM((n, D), BF),
        "dn": pltpu.VMEM((n, D), F32),
        "dup": pltpu.VMEM((FF // CHUNK, plan.seq, plan.DR, CHUNK), BF),
        "ddown": pltpu.VMEM((plan.seq, plan.FR, D), BF),
        "dproj": pltpu.VMEM((plan.seq, plan.DR, D), BF),
    }


def backward_outs(plan, n, whole=False, extra=False):
    C, DR, FR = plan.chips, plan.DR, plan.FR
    outs = {
        "gmid": sds((n, D), F32),
        "dc": [sds((n, plan.HW), BF)] * plan.G,
        "dgain": sds((8, D), F32),
    }
    if whole:
        rows = 5 * DR + FR + (DR + plan.VR if extra else 0)
        return outs, {"packs": [sds((plan.seq, rows, D), BF)]}
    return outs, {"packs": [sds((C, 4 * DR, D), BF), sds((C, FR + DR, D), BF)] * 2}


def ffn_loss_kernel(plan, k):
    copies = k.copies
    attended(plan, k, k.x[...])
    feed_forward(k, 2, k.y[...], keep=True)
    loss_part(plan, k)
    upward, rest = send_whole(plan, k, copies, extra=True)
    ffn_backward_part(plan, k, 2, k.y[...], upward, kept=True)
    rest()


def joined(refs):
    total = refs[0][...].astype(F32)
    for ref in refs[1:]:
        total += ref[...].astype(F32)
    return total


def join_last_kernel(plan, k):
    copies = k.copies
    x = k.x[...]
    root = root_of(x)
    dx, dgain = norm_back(x * root, root, k.gains[4:5, :], joined(k.terms))
    grad = k.gnext[...] + dx
    k.second[...] = grad
    k.gout[...] = exact_dot(one_hot(k.cols[:, SLOT : SLOT + 1], CAP).T, grad)
    k.dgain_in[...] = jnp.broadcast_to(dgain, k.dgain_in.shape)
    upward, rest = send_whole(plan, k, copies)
    ffn_backward_part(plan, k, 1, k.y[...], upward)
    rest()


def join_middle_kernel(plan, k):
    copies = k.copies
    x = k.x[...]
    root = root_of(x)
    dx, dgain = norm_back(x * root, root, k.gains[2:3, :], joined(k.terms))
    member = one_hot(k.cols[:, SLOT : SLOT + 1], CAP)
    counts = jnp.sum(member.T.astype(F32), axis=1, keepdims=True)
    grad = (k.gnext[...] + dx) / jnp.maximum(counts, 1.0)
    k.gout[...] = k.second[...] + k.bound[...] + exact_dot(member, grad)
    k.dgain_in[...] = jnp.broadcast_to(dgain, k.dgain_in.shape)
    upward, rest = send_packs(plan, k, copies)
    ffn_backward_part(plan, k, 0, k.y[...], upward)
    rest()


def bound_kernel(plan, x_ref, cols, gains, pack, *refs):
    grad_out, dp_out, dgain_out, stat, weight_scr, sem = refs
    top = 5 * plan.DR + plan.FR
    copy = Copies(sem).start(pack.at[:, top : top + plan.DR, :], weight_scr)
    x = x_ref[...]
    valid = cols[:, VALID : VALID + 1]
    target = cols[:, TARGET : TARGET + 1]
    root = root_of(x)
    unit = x * root
    gain = gains[7:8, :]
    rows = (unit * gain).astype(BF)
    copy.wait()
    weight = weight_scr[...].reshape(D, D)
    value, slope = gelu_parts(dot(rows, weight))
    out_gain = gains[8:9, :]
    z = jnp.sum(value * out_gain, axis=-1, keepdims=True) * D ** (-0.5)
    small = jnp.exp(-jnp.abs(z))
    soft = jnp.maximum(z, 0.0) + jnp.log(1.0 + small)
    bce = jnp.sum(valid * (soft - target * z), axis=0, keepdims=True)
    sig = jnp.where(z >= 0, 1.0, small) / (1.0 + small)
    dz = valid * (sig - target) * D ** (-0.5)
    dh = (dz * out_gain * slope).astype(BF)
    dp_out[...] = dot(rows.T, dh).astype(BF).reshape(dp_out.shape)
    dx, dgain = norm_back(unit, root, gain, dot(dh, weight, NT))
    grad_out[...] = dx
    dgain_out[0:8, :] = jnp.broadcast_to(dgain, (8, D))
    dgain_out[8:16, :] = jnp.broadcast_to(jnp.sum(dz * value, axis=0, keepdims=True), (8, D))
    stat[...] = at_lane(1, bce)


def tail_kernel(plan, idx, gmid, dtab, table, cols, gains, *refs):
    d1, d2, d3, d4, d5, d6, d78 = refs[:7]
    dw = refs[7 : 7 + plan.chips]
    packs = refs[7 + plan.chips : 7 + 2 * plan.chips]
    tab, gt, turned = refs[7 + 2 * plan.chips :]
    t = table[...].astype(F32)
    root = root_of(t)
    dx, dgain = norm_back(t * root, root, gains[0:1, :], dtab[...])
    hot = one_hot(cols[:, BYTE : BYTE + 1], VOCAB).T
    g = gmid[...]
    high = g.astype(BF)
    tab[...] = dx + (dot(hot, high) + dot(hot, (g - high.astype(F32)).astype(BF)))
    gt[...] = jnp.zeros_like(gt)
    gt[0:1, :] = dgain
    for k, ref in ((1, d1), (2, d2), (3, d3), (4, d4), (5, d5), (6, d6), (7, d78)):
        gt[k : k + 1, :] = ref[0:1, :]
    gt[8:9, :] = d78[8:9, :]
    turned[...] = gt[...].T
    DR, VR, HW = plan.DR, plan.VR, plan.HW
    for r in range(plan.chips):
        k = idx[plan.at_order["x"] + r]
        if 3 * HW < D - 128:
            packs[r][0 : 2 * DR, :] = jnp.zeros((2 * DR, D), BF)
        packs[r][0 : 2 * DR, 0 : 3 * HW] = dw[r][:, 0 : 3 * HW]
        rows = turned[pl.ds(pl.multiple_of(k * 2 * DR, 2 * DR), 2 * DR), :]
        packs[r][0 : 2 * DR, D - 128 : D] = rows.astype(BF)
        rows = tab[pl.ds(pl.multiple_of(k * 2 * VR, 2 * VR), 2 * VR), :]
        packs[r][2 * DR : 2 * DR + 2 * VR, :] = rows.astype(BF)


def adam_update(weight, first, second, grad, rate):
    mean = BETA_FIRST * first + (1.0 - BETA_FIRST) * grad
    meansq = BETA_SECOND * second + (1.0 - BETA_SECOND) * grad * grad
    mean_hat = mean / (1.0 - BETA_FIRST**STEP)
    meansq_hat = meansq / (1.0 - BETA_SECOND**STEP)
    master = weight - rate * (mean_hat / (jnp.sqrt(meansq_hat) + ADAM_EPS) + DECAY_RATE * weight)
    return (master, mean, meansq)


def update_kernel(shapes, totals, gain, *refs):
    count = len(shapes)
    refs = list(refs)

    def take(n):
        taken = refs[:n]
        del refs[:n]
        return taken

    gain_in = take(3)
    ins = [take(count) for _ in range(4)]
    gain_out = take(3)
    outs = [take(count) for _ in range(4)]
    losses, counted, norm_out, rms = take(4)
    in_scr = [take(count) for _ in range(4)]
    out_scr = [take(count) for _ in range(4)]
    sem = refs[0]
    copies = Copies(sem)
    started = {}
    for t, shape in enumerate(shapes):
        for layer in range(shape[0]):
            started[t, layer] = [
                copies.start(src[t].at[layer], dst[t].at[layer]) for src, dst in zip(ins, in_scr)
            ]
    copies.open = []
    lanes = lax.broadcasted_iota(jnp.int32, (8, 128), 1)
    sums = totals[...]

    def lane(k):
        picked = jnp.where(lanes == k, sums, 0.0)[0:1, :]
        return jnp.sum(picked, axis=1, keepdims=True)

    inverse = 1.0 / lane(5)
    norm = jnp.sqrt(lane(6)) * inverse
    factor = jnp.minimum(1.0, CLIP_NORM / (norm + 1e-06)) * inverse
    losses[0] = lane(0)[0, 0]
    losses[1] = lane(1)[0, 0]
    counted[0] = lane(5)[0, 0]
    norm_out[0] = norm[0, 0]
    for k in range(3):
        rms[k] = jnp.sqrt(lane(2 + k) * inverse * (1.0 / D))[0, 0]
    rows, width = gain_in[0].shape
    grad = gain[...].T[0:rows, 0:width] * factor
    new = adam_update(*[v[...] for v in gain_in], grad, RATE_VECTOR)
    for ref, value in zip(gain_out, new):
        ref[...] = value
    for t, shape in enumerate(shapes):
        rate = RATE_VECTOR if t == count - 1 else RATE_MATRIX
        size = min(16, shape[1])
        for layer in range(shape[0]):
            for copy in started[t, layer]:
                copy.wait()

            def block(r, carry, t=t, layer=layer, rate=rate, size=size):
                at = rows_at(r, size)
                w, a, b, g = [scr[t][layer, at, :].astype(F32) for scr in in_scr]
                new = adam_update(w, a, b, g * factor, rate)
                for scr, value in zip(out_scr, (*new, new[0])):
                    scr[t][layer, at, :] = value.astype(scr[t].dtype)
                return carry

            lax.fori_loop(0, shape[1] // size, block, 0)
            for src, dst in zip(out_scr, outs):
                copies.start(src[t].at[layer], dst[t].at[layer])
    copies.finish()


def add(a, b):
    return (a.astype(F32) + b.astype(F32)).astype(BF)


def total_of(terms):
    total = terms[0].astype(F32)
    for term in terms[1:]:
        total = total + term.astype(F32)
    return total.astype(BF)


def sum_first(plan, blocks, axis):
    got = [plan.shift(blocks[d], **{axis: d}) for d in range(1, plan.sizes[axis])]
    return [total_of([b[e] for b in (blocks[0], *got)]) for e in range(blocks[0].shape[0])]


def sum_second(plan, blocks, axis):
    return total_of(
        [blocks[0]] + [plan.shift(blocks[d], **{axis: d}) for d in range(1, plan.sizes[axis])]
    )


def sum_chips(plan, blocks):
    terms = [blocks[0]]
    for r in range(1, plan.chips):
        dx, dy = divmod(r, plan.Y)
        terms.append(plan.shift(blocks[r], x=dx, y=dy))
    return total_of(terms)


def head_sum(plan, v, axis):
    return add(v, plan.shift(v, **{axis: 1}))


def split_axes(plan, t, first, second):
    return t.reshape((plan.sizes[first], plan.sizes[second]) + t.shape[1:])


def by_core(first, second):
    halves = [v.reshape((2, v.shape[0] // 2) + v.shape[1:]) for v in (first, second)]
    return jnp.concatenate(halves, axis=1)


def exchange_columns(plan, v, me):
    own = lax.dynamic_index_in_dim(v, me["core"], 0, keepdims=False)
    other = lax.dynamic_index_in_dim(v, 1 - me["core"], 0, keepdims=False)
    parts = [own] + [plan.shift(own, zl=d) for d in range(1, plan.L)]
    return parts + [plan.shift(other, core=1, zl=d) for d in range(plan.L)]


def final_kernel(plan, idx, *refs):
    DR, FR, VR, HW, G = plan.DR, plan.FR, plan.VR, plan.HW, plan.G
    cut = 4 * DR
    shard0, shard2, refs = refs[0:2], refs[2:4], refs[4:]
    columns0, columns12, stat_in = refs[:G], refs[G : 2 * G], refs[2 * G]
    parts, refs = refs[2 * G + 1 : -10], refs[-10:]
    qkv, proj, up, down, table, gain, stat, scr0, scr12, scr1 = refs
    for r, part in enumerate(parts):
        place = idx[plan.at_head + r] if len(parts) > 1 else 0
        scr1[place] = part[...]
    whole = scr1[...].reshape(scr1.shape[0] * scr1.shape[1], D)
    shards = [shard0, (whole[0:cut], whole[cut:]), shard2]
    for r in range(G):
        b = idx[plan.at_src + r]
        scr0[b] = columns0[r][...]
        scr12[b] = columns12[r][...]
    for b in range(G):
        for part in range(3):
            src = slice(part * HW, (part + 1) * HW)
            dst = slice(part * D + b * HW, part * D + (b + 1) * HW)
            qkv[0, :, dst] = scr0[b, 0:DR, src]
            qkv[1, :, dst] = scr12[b, 0:DR, src]
            qkv[2, :, dst] = scr12[b, DR : 2 * DR, src]
    tab = scr0[0, DR : DR + VR, :].astype(F32)
    gains = scr0[0, 0:DR, D - 128 : D].astype(F32)
    for b in range(1, G):
        tab += scr0[b, DR : DR + VR, :].astype(F32)
        gains += scr0[b, 0:DR, D - 128 : D].astype(F32)
    gain[...] = gains
    table[0] = tab
    for layer in range(3):
        one, two = shards[layer]
        for j in range(4):
            up[layer, :, j * CHUNK : (j + 1) * CHUNK] = one[j * DR : (j + 1) * DR, :]
        top = 0
        if layer == 2:
            proj[3] = two[0:DR, :]
            table[1] = two[DR : DR + VR, :].astype(F32)
            top = DR + VR
        down[layer] = two[top : top + FR, :]
        proj[layer] = two[top + FR : top + FR + DR, :]
    total = jnp.zeros((1, 1), F32)
    for ref in (qkv, proj, up, down, table, gain):
        pieces = [ref[...]] if len(ref.shape) == 2 else [ref[l] for l in range(ref.shape[0])]
        for piece in pieces:
            v = piece.astype(F32)
            total += jnp.sum(jnp.sum(v * v, axis=0, keepdims=True), axis=1, keepdims=True)
    stat[...] = stat_in[...] + at_lane(6, total)


def per_device(plan, *args):
    (
        byte_ids,
        next_bytes,
        loss_mask,
        pool_slots,
        qkv_weight,
        proj_weight,
        upward_weight,
        downward_weight,
        table_weight,
        gain_weight,
        qkv_first,
        qkv_second,
        proj_first,
        proj_second,
        upward_first,
        upward_second,
        downward_first,
        downward_second,
        table_first,
        table_second,
        gain_first,
        gain_second,
    ) = args
    G, L, HW, QW, DR, FR, VR = plan.G, plan.L, plan.HW, plan.QW, plan.DR, plan.FR, plan.VR
    n = byte_ids.shape[1]
    length = n * G
    me = plan.place()
    idx = plan.tables()
    core = me["core"]

    width0, width1 = QW + 384, 2 * QW
    keep0, send0, keep1, send1 = run(
        "first",
        functools.partial(first_kernel, plan),
        [sds((DR, width0), BF)] * 2 + [sds((DR, width1), BF)] * 2,
        [idx],
        [qkv_weight, table_weight, gain_weight],
        [pltpu.VMEM((128, 128), F32)],
    )
    ints = jnp.concatenate([byte_ids, next_bytes, loss_mask, pool_slots], axis=0)
    ints = jnp.concatenate([ints, jnp.zeros_like(ints)], axis=0)

    def chip_rows(keep, got):
        return jnp.where(
            core == 0,
            jnp.concatenate([keep, got], axis=0),
            jnp.concatenate([got, keep], axis=0),
        )

    def gather_chips(v, want=lambda dy, dx: True):
        out = [v]
        for r in range(1, plan.chips):
            dy, dx = divmod(r, plan.X)
            if want(dy, dx):
                out.append(plan.shift(v, y=dy, x=dx))
        return out

    def swap(c):
        return {**c, "core": c["zh"], "zh": c["core"]}

    got0, got1, own = fence(
        plan.shift(send0, core=1), plan.shift(send1, core=1), plan.permute(ints, swap)
    )
    chip0 = chip_rows(keep0, got0)
    chip1 = chip_rows(keep1, got1)
    early, both, chip1 = fence(
        gather_chips(chip0), jnp.concatenate([own, plan.shift(own, core=1)]), chip1
    )
    pairs = [both] + [plan.shift(both, zl=d) for d in range(1, L)]
    ints_all = jnp.concatenate([p[:8] for p in pairs] + [p[8:] for p in pairs])

    shard_inputs = [upward_weight, downward_weight, proj_weight, table_weight]

    def gather_pack(pack):
        return lax.all_gather(pack, "seq", axis=0, tiled=False)

    (pack0,) = run(
        "pack",
        functools.partial(pack_kernel, plan, 0),
        [sds((PackCast.rows(plan, 0), D), BF)],
        [],
        [],
        PackCast.scratch(plan),
        raw=shard_inputs,
        sems=5,
        after=[keep0],
    )
    packs = [gather_pack(pack0)]

    table, atab, gains, cols = run(
        "tables",
        functools.partial(prep_kernel, plan),
        [sds((VOCAB, D), BF), sds((VOCAB, D), BF), sds((16, D), F32), sds((n, 128), F32)],
        [idx],
        [own, *early],
        [pltpu.VMEM((VOCAB, D), F32), pltpu.VMEM((D, 128), F32), pltpu.VMEM((128, n), F32)],
    )
    half = np.arange(HALF, dtype=np.float32) / np.float32(HALF)
    frequency = np.float32(10000.0) ** (-half)
    angles = frequency[:, None] * np.arange(length, dtype=np.float32)[None, :]
    cos = jnp.asarray(np.cos(angles.astype(np.float64)).astype(np.float32))
    sin = jnp.asarray(np.sin(angles.astype(np.float64)).astype(np.float32))

    def exchange(parts):
        out = [parts[0]]
        for r in range(1, G):
            dc, dl = divmod(r, L)
            out.append(plan.shift(parts[r], core=dc, zl=dl))
        return out

    def gather_near(a):
        return [a] + [plan.shift(a, zl=d) for d in range(1, L)]

    def scatter_group(das):
        terms = [das[0], plan.shift(das[L], core=1)]
        for d in range(1, L):
            both = add(das[d], plan.shift(das[L + d], core=1))
            terms.append(plan.shift(both, zl=d))
        return terms

    early, table, atab, gains, cols, ints_all, chip1 = fence(
        early, table, atab, gains, cols, ints_all, chip1
    )
    c0, saved0, pack1 = attn_forward(
        plan, idx, cos, sin, [ints_all, atab], early, 0, n, True, False, 1, shard_inputs
    )
    packs.append(gather_pack(pack1))
    c0, saved0 = fence(c0, saved0)
    c0, chip1 = fence(exchange(c0), chip1)
    dense = 2 * D * (D + 2 * FF)
    res = run_named(
        "ffn_pool",
        functools.partial(ffn_pool_kernel, plan),
        {
            "y": sds((n, D), F32),
            "x": sds((n, D), F32),
            "pooled": sds((CAP, D), F32),
            "a": sds((CAP, D), BF),
            "stat": sds((8, 128), F32),
        },
        {"c": c0, "cols": cols, "table": table, "gains": gains},
        forward_scratch(plan, n),
        {"pack_in": packs[0]},
        {},
        idx,
        16,
        n * dense,
        n * FF,
        functools.partial(begin_pack, plan, False),
    )
    y0, x1, pooled, a1, stat = res.y, res.x, res.pooled, res.a, res.stat
    straight = gather_chips(chip1, lambda dy, dx: not (dy and dx))
    y0, x1, pooled, a1, stat, straight, chip1 = fence(
        y0, x1, pooled, a1, stat, straight, chip1
    )
    near, beside, diagonal = fence(
        gather_near(a1),
        plan.shift(a1, core=1),
        gather_chips(chip1, lambda dy, dx: dy and dx),
    )
    late = [straight.pop(0)]
    diagonal.pop(0)
    for r in range(1, plan.chips):
        late.append((diagonal if all(divmod(r, plan.X)) else straight).pop(0))
    a1 = [*near, beside, *[plan.shift(p, core=1) for p in near[1:]]]
    c1, saved1, pack2 = attn_forward(
        plan, idx, cos, sin, [*a1, ints_all], late, 0, CAP, False, True, 2, shard_inputs
    )
    packs.append(gather_pack(pack2))
    c1, saved1 = fence(c1, saved1)
    c1 = exchange(c1)
    res = run_named(
        "ffn_unpool",
        functools.partial(ffn_unpool_kernel, plan),
        {
            "y": sds((CAP, D), F32),
            "x": sds((n, D), F32),
            "a": sds((n, D), BF),
            "stat": sds((8, 128), F32),
        },
        {"c": c1, "pooled": pooled, "x1": x1, "cols": cols, "gains": gains, "stat_in": stat},
        forward_scratch(plan, CAP),
        {"pack_in": packs[1]},
        {},
        idx,
        16,
        CAP * dense,
        CAP * FF,
        functools.partial(begin_pack, plan, False),
    )
    y1, x2, a2, stat = res.y, res.x, res.a, res.stat
    bound_grad, dp3, dgain78, stat_b = run(
        "boundary",
        functools.partial(bound_kernel, plan),
        [sds((n, D), F32), sds((plan.seq, DR, D), BF), sds((16, D), F32), sds((8, 128), F32)],
        [],
        [x1, cols, gains],
        [pltpu.VMEM((plan.seq, DR, D), BF)],
        raw=[packs[1]],
        sems=1,
        flops=6 * n * D * D,
        trans=n * D,
    )
    near, beside, bound_grad, dp3, dgain78, stat_b = fence(
        gather_near(a2), plan.shift(a2, core=1), bound_grad, dp3, dgain78, stat_b
    )
    a2 = [*near, beside, *[plan.shift(p, core=1) for p in near[1:]]]
    c2, saved2 = attn_forward(plan, idx, cos, sin, a2, late, QW, n, False, False)
    c2 = exchange(c2)

    source0 = [ints_all, atab]
    swaps = plan.head == 4
    cut = 4 * DR

    def swap_first(v, one="zl", two="zh"):
        if not swaps:
            return [lax.psum(v[:cut], "head"), lax.psum(v[cut:], "head")]
        return [head_sum(plan, v[:cut], one), head_sum(plan, v[cut:], two)]

    def swap_second(parts, one="zh", two="zl"):
        if not swaps:
            return parts
        return [head_sum(plan, parts[0], one), head_sum(plan, parts[1], two)]

    axes = (("x", "y"), ("y", "x"))

    def core_sums(packs):
        out = []
        for mine, theirs, ax in zip(packs[:2], packs[2:], axes):
            got = split_axes(plan, plan.shift(theirs, core=1), *ax)
            mine = split_axes(plan, mine, *ax)
            out.append([add(mine[d], got[d]) for d in range(mine.shape[0])])
        return out

    def first_sums(halves):
        return [sum_first(plan, half, ax[0]) for half, ax in zip(halves, axes)]

    def second_sums(halves):
        return [sum_second(plan, half, ax[1]) for half, ax in zip(halves, axes)]

    outs, raw_outs = backward_outs(plan, n, whole=True, extra=True)
    res = run_named(
        "ffn_loss",
        functools.partial(ffn_loss_kernel, plan),
        {**outs, "dgain6": sds((8, D), F32), "stat": sds((8, 128), F32)},
        {
            "c": c2,
            "x": x2,
            "cols": cols,
            "gains": gains,
            "stat_a": stat,
            "stat_b": stat_b,
            "dp3": dp3,
        },
        {
            **backward_scratch(plan, n),
            "slope": pltpu.VMEM((FF // CHUNK, n, CHUNK), F32),
            "y": pltpu.VMEM((n, D), F32),
            "tab_scr": pltpu.VMEM((plan.seq, VR, D), BF),
            "dtab": pltpu.VMEM((plan.seq, VR, D), BF),
        },
        {"pack_in": packs[2]},
        raw_outs,
        idx,
        20 + 8 * plan.seq,
        2 * n * D * (3 * D + 6 * FF),
        n * FF,
        functools.partial(begin_pack, plan, True),
    )
    gmid2, dc2, dgain5, dgain6, stat = res.gmid, res.dc, res.dgain, res.dgain6, res.stat
    shard2 = lax.psum_scatter(res.packs[0], "seq", scatter_dimension=0)
    dc2, stat = fence(exchange(dc2), stat)
    dw2, das = attn_backward(
        plan, idx, cos, sin, a2, late, QW, dc2, saved2, n, False, False
    )
    dw2, das = fence(dw2, das)
    (terms,) = fence(scatter_group(das))
    outs, raw_outs = backward_outs(plan, CAP, whole=True)
    res = run_named(
        "join_last",
        functools.partial(join_last_kernel, plan),
        {**outs, "second": sds((n, D), F32), "dgain_in": sds((8, D), F32)},
        {
            "terms": terms,
            "gnext": gmid2,
            "x": x2,
            "cols": cols,
            "gains": gains,
            "y": y1,
            "c": c1,
        },
        backward_scratch(plan, CAP),
        {"pack_in": packs[1]},
        raw_outs,
        idx,
        16 + 8 * plan.seq,
        2 * CAP * D * (2 * D + 5 * FF),
        CAP * FF,
        functools.partial(begin_pack, plan, False),
    )
    gmid1, dc1, dgain3, dgain4 = res.gmid, res.dc, res.dgain, res.dgain_in
    shard1 = lax.psum_scatter(res.packs[0], "seq", scatter_dimension=0)
    gsecond = res.second
    dc1, dw2 = fence(dc1, dw2)
    dc1, shard2 = fence(exchange(dc1), shard2)
    dw1, das = attn_backward(
        plan, idx, cos, sin, [*a1, ints_all], late, 0, dc1, saved1, CAP, False, True
    )
    dw1, das, shard2 = fence(dw1, das, swap_first(shard2, "zh", "zl"))
    terms, dw1, shard2 = fence(scatter_group(das), dw1, shard2)
    outs, raw_outs = backward_outs(plan, n)
    res = run_named(
        "join_middle",
        functools.partial(join_middle_kernel, plan),
        {**outs, "dgain_in": sds((8, D), F32)},
        {
            "terms": terms,
            "gnext": gmid1,
            "x": pooled,
            "cols": cols,
            "gains": gains,
            "second": gsecond,
            "bound": bound_grad,
            "y": y0,
            "c": c0,
        },
        backward_scratch(plan, n),
        {"pack_in": packs[0]},
        raw_outs,
        idx,
        16 + 8 * plan.seq,
        1,
        1,
        functools.partial(begin_pack, plan, False),
    )
    gmid0, dc0, packs0, dgain1, dgain2 = res.gmid, res.dc, res.packs, res.dgain, res.dgain_in
    shard2 = swap_second(shard2, "zl", "zh")
    dw12 = sum_chips(plan, [jnp.concatenate(pair, axis=0) for pair in zip(dw1, dw2)])
    dc0, packs0, dw12, shard2, shard1 = fence(dc0, packs0, dw12, shard2, shard1)
    in_parts = shard1.shape[0] % (16 * plan.head) == 0
    if in_parts:
        shard1 = shard1.reshape(plan.head, shard1.shape[0] // plan.head, D)
        shard1 = lax.psum_scatter(shard1, "head", scatter_dimension=0)
    else:
        shard1 = lax.psum(shard1, "head")
    dc0, half0, dw12 = fence(exchange(dc0), core_sums(packs0), dw12)
    dw0, (dtab0,) = attn_backward(
        plan, idx, cos, sin, [ints_all, atab], early, 0, dc0, saved0, n, True, False
    )
    dw0, dtab0, half0, dw12, shard1 = fence(
        dw0, dtab0, first_sums(half0), head_sum(plan, dw12, "zh"), shard1
    )
    tail = run(
        "tail",
        functools.partial(tail_kernel, plan),
        [sds((2 * DR + 2 * VR, D), BF)] * plan.chips,
        [idx],
        [
            *(gmid0, dtab0, table, cols, gains),
            *(dgain1, dgain2, dgain3, dgain4, dgain5, dgain6, dgain78),
            *dw0,
        ],
        [pltpu.VMEM((VOCAB, D), F32), pltpu.VMEM((128, D), F32), pltpu.VMEM((D, 128), F32)],
        flops=4 * n * VOCAB * D,
    )
    if in_parts:
        shard1 = [
            plan.shift(shard1, zh=dh, zl=dl) if dh or dl else shard1
            for dh in range(2)
            for dl in range(L)
        ]
    else:
        shard1 = [shard1]
    tail, half0, shard1 = fence(tail, second_sums(half0), shard1)
    columns12 = exchange_columns(plan, by_core(dw12[: 2 * DR], dw12[2 * DR :]), me)
    shard0 = jnp.concatenate(half0, axis=0)
    tail, shard0, stat = fence(sum_chips(plan, tail), swap_first(shard0), stat)
    tail, shard0, stat, columns12 = fence(
        head_sum(plan, tail, "zh"),
        swap_second(shard0),
        stat + sum(plan.shift(stat, zl=d) for d in range(1, L)),
        columns12,
    )
    stat = stat + plan.shift(stat, zh=1)
    columns0 = exchange_columns(plan, by_core(tail[: 2 * DR], tail[2 * DR :]), me)
    matrix_grad = functools.partial(sds, dtype=BF)
    *grads, gain_t, stat = run(
        "gradients",
        functools.partial(final_kernel, plan),
        [
            matrix_grad(qkv_weight.shape),
            matrix_grad(proj_weight.shape),
            matrix_grad(upward_weight.shape),
            matrix_grad(downward_weight.shape),
            sds(table_weight.shape, F32),
            sds((DR, 128), F32),
            sds((8, 128), F32),
        ],
        [idx],
        [*shard0, *shard2, *columns0, *columns12, stat, *shard1],
        [
            pltpu.VMEM((G, DR + VR, D), BF),
            pltpu.VMEM((G, 2 * DR, D), BF),
            pltpu.VMEM((len(shard1), *shard1[0].shape), BF),
        ],
    )
    totals = lax.psum(stat, "seq")
    weights = (qkv_weight, proj_weight, upward_weight, downward_weight, table_weight)
    firsts = (qkv_first, proj_first, upward_first, downward_first, table_first)
    seconds = (qkv_second, proj_second, upward_second, downward_second, table_second)
    shapes = [w.shape for w in weights]
    matrices = [sds(shape, F32) for shape in shapes] * 3 + [sds(shape, BF) for shape in shapes]
    res = run(
        "update",
        functools.partial(update_kernel, shapes),
        [sds(gain_weight.shape, F32)] * 3,
        [],
        [totals, gain_t, gain_weight, gain_first, gain_second],
        [pltpu.VMEM(v.shape, v.dtype) for v in (*weights, *firsts, *seconds, *grads)]
        + [pltpu.VMEM(v.shape, v.dtype) for v in matrices],
        raw=[*weights, *firsts, *seconds, *grads],
        raw_outs=matrices,
        sems=8 * sum(shape[0] for shape in shapes),
        scalars=(2, 1, 1, 3),
    )
    gains_new, masters, means, meansqs, low, (losses, valid_count, grad_norm, rms) = [
        res[a:b] for a, b in ((0, 3), (3, 8), (8, 13), (13, 18), (18, 23), (23, 27))
    ]
    return (
        *[part for triple in zip(masters, means, meansqs) for part in triple],
        *gains_new,
        *low,
        losses,
        valid_count.reshape(()),
        grad_norm.reshape(()),
        rms,
    )


def solution(mesh):
    plan = Plan(mesh)
    tokens = P("seq", "head")
    matrix = P(None, "seq", None)
    vector = P(None, "seq")
    states = (matrix,) * 10 + (vector,) * 2
    return jax.shard_map(
        functools.partial(per_device, plan),
        mesh=mesh,
        in_specs=(tokens,) * 4 + (matrix,) * 5 + (vector,) + states,
        out_specs=(matrix,) * 15 + (vector,) * 3 + (matrix,) * 5 + (P(),) * 4,
        check_vma=False,
    )
```

```python
import functools
import math
from types import SimpleNamespace

import jax
import jax.numpy as jnp
import numpy as np
from jax import lax
from jax.experimental import pallas as pl
from jax.experimental.pallas import tpu as pltpu
from jax.sharding import PartitionSpec as P

D = 512
HEADS = 8
FF = 2048
VOCAB = 256
HEAD_DIM = 64
CAP = 256
STEP = 10
CHUNK = 512
HALF = HEAD_DIM // 2

NORM_EPS = 1e-06
BETA_FIRST = 0.9
BETA_SECOND = 0.95
ADAM_EPS = 1e-08
DECAY_RATE = 0.1
RATE_MATRIX = 0.05
RATE_VECTOR = 0.5
CLIP_NORM = 0.01
MASKED = -1000000000.0
SCALE = HEAD_DIM ** (-0.5)
GELU_A = math.sqrt(2.0 / math.pi)
GELU_B = 0.044715

BF = jnp.bfloat16
F32 = jnp.float32
NN = (((1,), (0,)), ((), ()))
NT = (((1,), (1,)), ((), ()))
AXES = ("seq", "head")
HB = pl.BlockSpec(memory_space=pltpu.HBM)
SM = pl.BlockSpec(memory_space=pltpu.SMEM)


def dot(a, b, dims=NN):
    return lax.dot_general(a, b, dims, preferred_element_type=F32)


def split3(v):
    high = v.astype(BF)
    rest = v - high.astype(F32)
    mid = rest.astype(BF)
    low = (rest - mid.astype(F32)).astype(BF)
    return (high, mid, low)


def exact_dot(ones, v):
    high, mid, low = split3(v)
    return dot(ones, high) + (dot(ones, mid) + dot(ones, low))


def root_of(v):
    return lax.rsqrt(jnp.mean(v * v, axis=-1, keepdims=True) + NORM_EPS)


def norm_back(unit, root, gain, grad):
    turned = grad * gain
    dx = root * (turned - unit * jnp.mean(turned * unit, axis=-1, keepdims=True))
    return dx, jnp.sum(grad * unit, axis=0, keepdims=True)


def gelu_parts(h):
    square = h * h
    t = jnp.tanh(GELU_A * h * (1.0 + GELU_B * square))
    half = 0.5 * (1.0 + t)
    value = h * half
    slope = half + 0.5 * h * (1.0 - t * t) * (GELU_A * (1.0 + 3.0 * GELU_B * square))
    return value, slope


def gelu_value(h):
    t = jnp.tanh(GELU_A * h * (1.0 + GELU_B * (h * h)))
    return h * (0.5 * (1.0 + t))


def one_hot(column, width):
    lanes = lax.broadcasted_iota(jnp.int32, (column.shape[0], width), 1).astype(F32)
    return (lanes == column).astype(F32).astype(BF)


class Plan:
    def __init__(self, mesh):
        self.seq = mesh.shape["seq"]
        self.head = mesh.shape["head"]
        self.chips = self.seq // 2
        side = int(math.isqrt(self.chips))
        while self.chips % side:
            side -= 1
        self.Y, self.X = side, self.chips // side
        self.L = self.head // 2
        self.G = self.head
        self.hd = HEADS // self.G
        self.HW = self.hd * HEAD_DIM
        self.QW = -(-3 * self.HW // 128) * 128
        self.DR = D // self.seq
        self.FR = FF // self.seq
        self.VR = VOCAB // self.seq
        self.sizes = {"y": self.Y, "x": self.X, "core": 2, "zh": 2, "zl": self.L}
        self.names = ("y", "x", "core", "zh", "zl")

    def coords(self):
        for linear in range(self.seq * self.head):
            s, z = divmod(linear, self.head)
            yx, core = divmod(s, 2)
            y, x = divmod(yx, self.X)
            zh, zl = divmod(z, self.L)
            yield linear, {"y": y, "x": x, "core": core, "zh": zh, "zl": zl}

    def linear(self, c):
        s = (c["y"] * self.X + c["x"]) * 2 + c["core"]
        return s * self.head + c["zh"] * self.L + c["zl"]

    def permute(self, v, to):
        pairs = []
        for here, c in self.coords():
            there = to(c)
            if there is not None:
                pairs.append((here, self.linear(there)))
        return lax.ppermute(v, AXES, pairs)

    def shift(self, v, **steps):
        def to(c):
            return {k: (c[k] + steps.get(k, 0)) % self.sizes[k] for k in self.names}

        return self.permute(v, to)

    def place(self):
        s = lax.axis_index("seq")
        z = lax.axis_index("head")
        yx, core = s // 2, s % 2
        return {
            "y": yx // self.X,
            "x": yx % self.X,
            "core": core,
            "zh": z // self.L,
            "zl": z % self.L,
        }

    def tables(self):
        me = self.place()
        G, L, Y, X = self.G, self.L, self.Y, self.X

        def block(sign):
            return [
                ((me["core"] + sign * dc) % 2) * L + (me["zl"] + sign * dl) % L
                for dc in range(2)
                for dl in range(L)
            ]

        def chip(dy, dx):
            return ((me["y"] + dy) % Y) * X + (me["x"] + dx) % X

        chip_src = [chip(-dy, -dx) for dy in range(Y) for dx in range(X)]
        by_x = [chip(dy, dx) for dx in range(X) for dy in range(Y)]
        by_y = [chip(dy, dx) for dy in range(Y) for dx in range(X)]
        head_src = [
            ((me["zh"] - dh) % 2) * L + (me["zl"] - dl) % L for dh in range(2) for dl in range(L)
        ]
        entries = [me["core"], me["zl"]] + block(1) + block(-1) + chip_src + by_x + by_y
        self.at_head = len(entries)
        entries += head_src
        self.at_core = 0
        self.at_zl = 1
        self.at_dst = 2
        self.at_src = 2 + G
        self.at_chip = 2 + 2 * G
        self.at_order = {"x": 2 + 2 * G + Y * X, "y": 2 + 2 * G + 2 * Y * X}
        return jnp.stack([jnp.asarray(e, jnp.int32) for e in entries])


def run(
    name,
    body,
    outs,
    smem,
    arrays,
    scratch=(),
    raw=(),
    raw_outs=(),
    sems=0,
    flops=0,
    trans=0,
    limit=60,
    after=(),
    before=None,
    scalars=(),
):
    operands = [*arrays, *raw]
    results = [*outs, *raw_outs]
    nbytes = sum(a.size * a.dtype.itemsize for a in operands)
    nbytes += sum(math.prod(o.shape) * jnp.dtype(o.dtype).itemsize for o in results)
    ns, ni, nr, na, no, nx = map(len, (smem, arrays, raw, after, outs, raw_outs))

    def wrapped(*refs):
        at = 0
        parts = []
        for count in (ns, ni, nr, na, no, nx, len(scalars), ni, no, len(scratch)):
            parts.append(refs[at : at + count])
            at += count
        s_refs, ins, raws, _, results_out, raws_out, small, bufs, out_bufs, own = parts
        sem = refs[at]
        copies = [
            pltpu.make_async_copy(src, dst, sem.at[k])
            for k, (src, dst) in enumerate(zip(ins, bufs))
        ]
        for copy in copies:
            copy.start()
        extra = (refs[at + 1],) if sems else ()
        if before is not None:
            before(*s_refs, *bufs, *raws, *out_bufs, *raws_out, *own, *extra)
        for copy in copies:
            copy.wait()
        body(*s_refs, *bufs, *raws, *out_bufs, *raws_out, *small, *own, *extra)
        copies = [
            pltpu.make_async_copy(src, dst, sem.at[k])
            for k, (src, dst) in enumerate(zip(out_bufs, results_out))
        ]
        for copy in copies:
            copy.start()
        for copy in copies:
            copy.wait()

    spaces = [pltpu.VMEM(v.shape, v.dtype) for v in (*arrays, *outs)]
    spaces += list(scratch) + [pltpu.SemaphoreType.DMA((max(ni, no, 1),))]
    if sems:
        spaces.append(pltpu.SemaphoreType.DMA((sems,)))
    return pl.pallas_call(
        wrapped,
        out_shape=tuple([*results, *[sds((count,), F32) for count in scalars]]),
        in_specs=[SM] * ns + [HB] * (ni + nr) + [pl.BlockSpec(memory_space=pl.ANY)] * na,
        out_specs=tuple([HB] * len(results) + [SM] * len(scalars)),
        scratch_shapes=spaces,
        compiler_params=pltpu.CompilerParams(vmem_limit_bytes=limit << 20),
        cost_estimate=pl.CostEstimate(
            flops=int(flops), bytes_accessed=int(nbytes), transcendentals=int(trans)
        ),
        name=name,
    )(*smem, *operands, *after)


def run_named(name, body, outs, arrays, scratch, raw, raw_outs, idx, sems, flops, trans, begin):
    def flat(group):
        out = []
        for value in group.values():
            out += list(value) if isinstance(value, (list, tuple)) else [value]
        return out

    def name_all(space, group, refs):
        for key, value in group.items():
            if isinstance(value, (list, tuple)):
                setattr(space, key, [refs.pop(0) for _ in value])
            else:
                setattr(space, key, refs.pop(0))

    space = SimpleNamespace()

    def before(idx_ref, *refs):
        space.idx, refs = idx_ref, list(refs)
        for group in (arrays, raw, outs, raw_outs, scratch):
            name_all(space, group, refs)
        space.sem = refs.pop(0)
        begin(space)

    def wrapped(*refs):
        body(space)

    res = list(
        run(
            name,
            wrapped,
            flat(outs),
            [idx],
            flat(arrays),
            flat(scratch),
            flat(raw),
            flat(raw_outs),
            sems,
            flops,
            trans,
            before=before,
        )
    )
    found = SimpleNamespace()
    for group in (outs, raw_outs):
        name_all(found, group, res)
    return found


def fence(*groups):
    return lax.optimization_barrier(groups)


class Copies:
    def __init__(self, sem):
        self.sem = sem
        self.count = 0
        self.open = []

    def start(self, src, dst):
        copy = pltpu.make_async_copy(src, dst, self.sem.at[self.count])
        self.count += 1
        copy.start()
        self.open.append(copy)
        return copy

    def finish(self):
        for copy in self.open:
            copy.wait()
        self.open = []


def rows_at(index, size):
    return pl.ds(pl.multiple_of(index * size, size), size)


def sds(shape, dtype):
    return jax.ShapeDtypeStruct(shape, dtype)


def first_kernel(plan, idx, qkv, table, gain, *refs):
    keep0, send0, keep1, send1, scr = refs
    DR, VR, HW, QW = plan.DR, plan.VR, plan.HW, plan.QW
    core, zl = idx[plan.at_core], idx[plan.at_zl]
    for which, outs in ((0, (keep0, keep1)), (1, (send0, send1))):
        block = lax.rem(core + which, 2) * plan.L + zl
        for layer in range(3):
            out, lo = ((outs[0], 0), (outs[1], 0), (outs[1], QW))[layer]
            for part in range(3):
                if HW % 128 == 0:
                    at = pl.ds(pl.multiple_of(part * D + block * HW, HW), HW)
                    piece = qkv[layer, :, at]
                else:
                    at = pl.ds(pl.multiple_of(part * D + block // 2 * 128, 128), 128)
                    both = qkv[layer, :, at]
                    piece = jnp.where(block % 2 == 0, both[:, :HW], both[:, HW:])
                out[:, lo + part * HW : lo + (part + 1) * HW] = piece.astype(BF)
    scr[...] = jnp.zeros_like(scr)
    scr[0 : gain.shape[0], 0:DR] = gain[...]
    turned = scr[...].T[0:DR, :].astype(BF)
    low = table[0].astype(BF)
    for out in (keep0, send0):
        out[:, QW : QW + 256] = jnp.concatenate([low[:, :256], low[:, 256:]], axis=0)
        out[:, QW + 256 : QW + 384] = turned


class PackCast:
    def __init__(self, plan, layer, copies, sources, scr):
        self.plan, self.layer = plan, layer
        up, down, proj, table = sources
        self.up, self.down, self.proj, self.table = scr
        self.copies = [
            copies.start(up.at[layer], self.up),
            copies.start(down.at[layer], self.down),
            copies.start(proj.at[layer], self.proj.at[0]),
        ]
        if layer == 2:
            self.copies.append(copies.start(proj.at[3], self.proj.at[1]))
            self.copies.append(copies.start(table.at[1], self.table))
        copies.open = []

    @staticmethod
    def rows(plan, layer):
        return 5 * plan.DR + plan.FR + (0, 0, plan.DR + plan.VR)[layer]

    @staticmethod
    def scratch(plan):
        return [
            pltpu.VMEM((plan.DR, FF), F32),
            pltpu.VMEM((plan.FR, D), F32),
            pltpu.VMEM((2, plan.DR, D), F32),
            pltpu.VMEM((plan.VR, D), F32),
        ]

    def write(self, out):
        DR, FR, VR = self.plan.DR, self.plan.FR, self.plan.VR
        for copy in self.copies:
            copy.wait()
        for j in range(FF // CHUNK):
            at = slice(j * CHUNK, (j + 1) * CHUNK)
            out[j * DR : (j + 1) * DR, :] = self.up[:, at].astype(BF)
        top = 4 * DR
        out[top : top + FR, :] = self.down[...].astype(BF)
        top += FR
        out[top : top + DR, :] = self.proj[0].astype(BF)
        top += DR
        if self.layer == 2:
            out[top : top + DR, :] = self.proj[1].astype(BF)
            top += DR
            out[top : top + VR, :] = self.table[...].astype(BF)


def pack_kernel(plan, layer, up, down, proj, table, out, *scr):
    *scr, sem = scr
    PackCast(plan, layer, Copies(sem), (up, down, proj, table), scr).write(out)


def prep_kernel(plan, idx, ints, *refs):
    pieces = refs[: plan.chips]
    table_out, atab_out, gain_out, cols_out, table_scr, gain_scr, row_scr = refs[plan.chips :]
    slots = ints[3:4, :].astype(F32)
    n = slots.shape[1]
    lanes = lax.broadcasted_iota(jnp.int32, (1, n), 1)
    row_scr[...] = jnp.zeros_like(row_scr)
    row_scr[VALID : VALID + 1, :] = ints[2:3, :].astype(F32)
    changed = jnp.concatenate([slots[:, 0:1], slots[:, 0 : n - 1]], axis=1) != slots
    row_scr[TARGET : TARGET + 1, :] = jnp.where((lanes == 0) | changed, 1.0, 0.0)
    row_scr[NEXT : NEXT + 1, :] = ints[1:2, :].astype(F32)
    row_scr[SLOT : SLOT + 1, :] = slots
    row_scr[BYTE : BYTE + 1, :] = ints[0:1, :].astype(F32)
    cols_out[...] = row_scr[...].T
    VR, DR, QW = plan.VR, plan.DR, plan.QW
    for r in range(plan.chips):
        k = idx[plan.at_chip + r]
        for core in range(2):
            for half in range(2):
                rows = pieces[r][core * DR + half * VR : core * DR + (half + 1) * VR, QW : QW + 256]
                table_scr[
                    pl.ds(pl.multiple_of(k * 2 * VR, 2 * VR) + core * VR, VR),
                    half * 256 : half * 256 + 256,
                ] = rows.astype(F32)
        gain_scr[pl.ds(pl.multiple_of(k * 2 * DR, 2 * DR), 2 * DR), :] = pieces[r][
            :, QW + 256 : QW + 384
        ].astype(F32)
    gains = gain_scr[...].T[0:16, :]
    gain_out[...] = gains
    table = table_scr[...]
    table_out[...] = table.astype(BF)
    atab_out[...] = (table * root_of(table) * gains[0:1, :]).astype(BF)


def load_weight(plan, copies, idx, pieces, lo, w_scr):
    started = []
    for r in range(plan.chips):
        src = pieces[r].at[:, lo : lo + plan.QW]
        started.append(copies.start(src, w_scr.at[rows_at(idx[plan.at_chip + r], 2 * plan.DR), :]))
    return started


def live_bias(plan, idx, ints, n, bias_scr):
    row = lax.broadcasted_iota(jnp.int32, (n, 128), 0).astype(F32)
    for r in range(plan.G):
        slots = ints[8 * r + 3 : 8 * r + 4, :].astype(F32)
        last = jnp.max(slots, axis=1, keepdims=True)
        bias_scr[rows_at(idx[plan.at_src + r], n), :] = jnp.where(row <= last, 0.0, MASKED)


def head_pad(plan, part, h):
    if plan.hd == 1:
        return part
    blank = jnp.zeros_like(part)
    return jnp.concatenate([part if k == h else blank for k in range(plan.hd)], axis=0)


def rot_pair(a, b, cos, sin):
    return a * cos - b * sin, b * cos + a * sin


def attn_fwd_kernel(plan, n, lo, embed, masked, rider, idx, *refs):
    G, HW, hd = plan.G, plan.HW, plan.hd
    S = G * n
    refs = list(refs)
    cos_ref, sin_ref = refs[0], refs[1]
    refs = refs[2:]
    if embed:
        ints_ref, atab_ref = refs[0], refs[1]
        refs = refs[2:]
    else:
        a_refs = refs[:G]
        refs = refs[G:]
    if masked:
        ints_ref = refs[0]
        refs = refs[1:]
    w_refs = refs[: plan.chips]
    refs = refs[plan.chips :]
    if rider:
        rider_in, refs = refs[:4], refs[4:]
    c_outs = refs[:G]
    qkvt_out, ot_out, lse_out = refs[G : G + 3]
    refs = refs[G + 3 :]
    if rider:
        rider_out, refs = refs[0], refs[1:]
    w_scr, cos_scr, sin_scr, src_scr, tab_scr, ints_scr, bias_scr = refs[:7]
    qkvt, ot, lse, k_scr, c_scr = refs[7:12]
    *rider_scr, sem = refs[12:]
    copies = Copies(sem)
    first = load_weight(plan, copies, idx, w_refs, lo, w_scr)
    first.append(copies.start(cos_ref, cos_scr))
    first.append(copies.start(sin_ref, sin_scr))
    sources = []
    if embed or masked:
        first.append(copies.start(ints_ref, ints_scr))
    if embed:
        first.append(copies.start(atab_ref, tab_scr))
    else:
        for r in range(G):
            dst = src_scr.at[rows_at(idx[plan.at_src + r], n), :]
            sources.append(copies.start(a_refs[r], dst))
    copies.open = []
    if rider:
        cast = PackCast(plan, rider, copies, rider_in, rider_scr[1:])
    for copy in first:
        copy.wait()
    wt = w_scr[...].T[0 : 3 * HW, :]
    if embed:
        base = split3(dot(wt, tab_scr[...], NT))
    if masked:
        live_bias(plan, idx, ints_scr, n, bias_scr)
    for r in range(G):
        at = rows_at(idx[plan.at_src + r], n)
        if embed:
            ids = ints_scr[8 * r : 8 * r + 1, :]
            hot = (lax.broadcasted_iota(jnp.int32, (VOCAB, n), 0) == ids).astype(F32).astype(BF)
            m = dot(base[0], hot) + (dot(base[1], hot) + dot(base[2], hot))
        else:
            sources[r].wait()
            m = dot(wt, src_scr[at, :], NT)
        cos, sin = cos_scr[:, at], sin_scr[:, at]
        for h in range(hd):
            for part, factor in ((0, SCALE), (1, 1.0)):
                top = part * HW + h * HEAD_DIM
                one, two = rot_pair(m[top : top + HALF], m[top + HALF : top + HEAD_DIM], cos, sin)
                qkvt[top : top + HALF, at] = (one * factor).astype(BF)
                qkvt[top + HALF : top + HEAD_DIM, at] = (two * factor).astype(BF)
        qkvt[2 * HW : 3 * HW, at] = m[2 * HW : 3 * HW].astype(BF)
        k_scr[at, :] = qkvt[HW : 2 * HW, at].T
    copies.start(qkvt, qkvt_out)
    if rider:
        cast.write(rider_scr[0])
        copies.start(rider_scr[0], rider_out)
    tile = min(512, S)

    def tile_scores(q_pads, keys, rows, diagonal):
        out = []
        for h in range(hd):
            s = dot(keys, q_pads[h])
            if masked:
                s = s + jnp.concatenate([bias_scr[rows, :]] * (tile // 128), axis=1)
            if diagonal:
                kk = lax.broadcasted_iota(jnp.int32, (tile, tile), 0)
                qq = lax.broadcasted_iota(jnp.int32, (tile, tile), 1)
                s = jnp.where(kk <= qq, s, MASKED)
            out.append(s)
        return out

    def one_query(i, _):
        cols = pl.ds(pl.multiple_of(i * tile, tile), tile)
        q_pads = [
            head_pad(plan, qkvt[h * HEAD_DIM : (h + 1) * HEAD_DIM, cols], h) for h in range(hd)
        ]

        def step(j, state, diagonal):
            rows = pl.ds(pl.multiple_of(j * tile, tile), tile)
            scores = tile_scores(q_pads, k_scr[rows, :], rows, diagonal)
            new = []
            for h in range(hd):
                top, total, acc = state[3 * h : 3 * h + 3]
                s = scores[h]
                new_top = jnp.maximum(top, jnp.max(s, axis=0, keepdims=True))
                p = jnp.exp(s - new_top)
                keep = jnp.exp(top - new_top)
                total = total * keep + jnp.sum(p, axis=0, keepdims=True)
                vt = qkvt[2 * HW + h * HEAD_DIM : 2 * HW + (h + 1) * HEAD_DIM, rows]
                acc = acc * keep + dot(vt, p.astype(BF))
                new += [new_top, total, acc]
            return tuple(new)

        state = ()
        for h in range(hd):
            state += (
                jnp.full((1, tile), -1e30, F32),
                jnp.zeros((1, tile), F32),
                jnp.zeros((HEAD_DIM, tile), F32),
            )
        state = lax.fori_loop(0, i, lambda j, st: step(j, st, False), state)
        state = step(i, state, True)
        for h in range(hd):
            top, total, acc = state[3 * h : 3 * h + 3]
            ot[h * HEAD_DIM : (h + 1) * HEAD_DIM, cols] = acc / total
            lse[h : h + 1, cols] = top + jnp.log(total)
        c_scr[cols, :] = ot[:, cols].T.astype(BF)
        return 0

    lax.fori_loop(0, S // tile, one_query, 0)
    for r in range(G):
        copies.start(c_scr.at[rows_at(idx[plan.at_dst + r], n), :], c_outs[r])
    copies.start(ot, ot_out)
    copies.start(lse, lse_out)
    copies.finish()


def source_scratch(embed, masked, S, G, source):
    none = pltpu.VMEM((16, 128), BF)
    return [
        none if embed else pltpu.VMEM((S, D), BF),
        pltpu.VMEM((VOCAB, D), BF) if embed else none,
        pltpu.VMEM(source[0 if embed else G].shape, jnp.int32) if embed or masked else none,
        pltpu.VMEM((S, 128), F32) if masked else none,
    ]


def attn_forward(
    plan, idx, cos, sin, source, weights, lo, n, embed, masked, rider=0, rider_in=()
):
    G, HW = plan.G, plan.HW
    S = G * n
    outs = [sds((n, HW), BF)] * G + [
        sds((3 * HW, S), BF),
        sds((HW, S), F32),
        sds((8, S), F32),
    ]
    extra = []
    if rider:
        outs.append(sds((PackCast.rows(plan, rider), D), BF))
        extra = [pltpu.VMEM(outs[-1].shape, BF), *PackCast.scratch(plan)]
    res = run(
        "attention_forward",
        functools.partial(attn_fwd_kernel, plan, n, lo, embed, masked, rider),
        [],
        [idx],
        [],
        [
            pltpu.VMEM((D, plan.QW), BF),
            pltpu.VMEM(cos.shape, F32),
            pltpu.VMEM(cos.shape, F32),
            *source_scratch(embed, masked, S, G, source),
            pltpu.VMEM((3 * HW, S), BF),
            pltpu.VMEM((HW, S), F32),
            pltpu.VMEM((8, S), F32),
            pltpu.VMEM((S, HW), BF),
            pltpu.VMEM((S, HW), BF),
            *extra,
        ],
        raw=[cos, sin, *source, *weights, *rider_in],
        raw_outs=outs,
        sems=plan.chips + 2 * G + 16,
        flops=2 * S * D * 3 * HW + 2 * plan.hd * S * S * 256,
        trans=plan.hd * S * S // 2,
    )
    if rider:
        return res[:G], res[G : G + 3], res[G + 3]
    return res[:G], res[G:]


def attn_bwd_kernel(plan, n, lo, embed, masked, idx, *refs):
    G, HW, hd = plan.G, plan.HW, plan.hd
    S = G * n
    refs = list(refs)
    cos_ref, sin_ref = refs[0], refs[1]
    refs = refs[2:]
    if embed:
        ints_ref, atab_ref = refs[0], refs[1]
        refs = refs[2:]
    else:
        a_refs = refs[:G]
        refs = refs[G:]
    if masked:
        ints_ref = refs[0]
        refs = refs[1:]
    w_refs = refs[: plan.chips]
    refs = refs[plan.chips :]
    do_refs = refs[:G]
    qkvt_in, ot_in, lse_in = refs[G : G + 3]
    refs = refs[G + 3 :]
    dw_outs = refs[: plan.chips]
    refs = refs[plan.chips :]
    if embed:
        tab_out = refs[0]
        refs = refs[1:]
    else:
        da_outs = refs[:G]
        refs = refs[G:]
    w_scr, cos_scr, sin_scr, src_scr, tab_scr, ints_scr, bias_scr, qkvt, ot, lse = refs[:10]
    do_all, k_scr, v_scr, qz, qtz, doz, dotz, delta, dqt, dk, dv, dmt, res_scr, dw_scr, sem = refs[10:]
    copies = Copies(sem)
    if embed or masked:
        copies.start(ints_ref, ints_scr)
    copies.start(qkvt_in, qkvt)
    for r in range(G):
        copies.start(do_refs[r], do_all.at[rows_at(idx[plan.at_src + r], n), :])
    copies.start(ot_in, ot)
    copies.start(lse_in, lse)
    first, copies.open = copies.open, []
    copies.start(cos_ref, cos_scr)
    copies.start(sin_ref, sin_scr)
    angles, copies.open = copies.open, []
    load_weight(plan, copies, idx, w_refs, lo, w_scr)
    if embed:
        copies.start(atab_ref, tab_scr)
    else:
        for r in range(G):
            copies.start(a_refs[r], src_scr.at[rows_at(idx[plan.at_src + r], n), :])
    last, copies.open = copies.open, []
    for copy in first:
        copy.wait()
    tile = min(512, S)
    blocks = S // tile
    lane = lax.broadcasted_iota(jnp.int32, (tile, HW), 1) // HEAD_DIM
    for b in range(blocks):
        at = slice(b * tile, (b + 1) * tile)
        dob = do_all[at, :]
        dobt = dob.T
        kt = qkvt[HW : 2 * HW, at]
        k_scr[at, :] = kt.T
        v_scr[at, :] = qkvt[2 * HW : 3 * HW, at].T
        prod = dobt.astype(F32) * ot[:, at]
        dob32 = dob.astype(F32)
        for h in range(hd):
            rows = slice(h * HEAD_DIM, (h + 1) * HEAD_DIM)
            pad = head_pad(plan, qkvt[rows, at], h)
            qtz[h, :, at] = pad
            qz[h, at, :] = pad.T
            dotz[h, :, at] = head_pad(plan, dobt[rows, :], h)
            doz[h, at, :] = jnp.where(lane == h, dob32, 0.0).astype(BF)
            delta[h : h + 1, at] = jnp.sum(prod[rows, :], axis=0, keepdims=True)
    dqt[...] = jnp.zeros_like(dqt)
    if masked:
        live_bias(plan, idx, ints_scr, n, bias_scr)
    for copy in angles:
        copy.wait()

    def one_key(j, _):
        rows = pl.ds(pl.multiple_of(j * tile, tile), tile)
        keys, values = k_scr[rows, :], v_scr[rows, :]
        dk[...] = jnp.zeros_like(dk)
        dv[...] = jnp.zeros_like(dv)
        bias = jnp.concatenate([bias_scr[rows, :]] * (tile // 128), axis=1) if masked else None

        def step(i, diagonal):
            cols = pl.ds(pl.multiple_of(i * tile, tile), tile)
            for h in range(hd):
                s = dot(keys, qtz[h, :, cols])
                if masked:
                    s = s + bias
                if diagonal:
                    kk = lax.broadcasted_iota(jnp.int32, (tile, tile), 0)
                    qq = lax.broadcasted_iota(jnp.int32, (tile, tile), 1)
                    s = jnp.where(kk <= qq, s, MASKED)
                p = jnp.exp(s - lse[h : h + 1, cols])
                dp = dot(values, dotz[h, :, cols])
                ds = (p * (dp - delta[h : h + 1, cols])).astype(BF)
                dv[...] += dot(p.astype(BF), doz[h, cols, :])
                dk[...] += dot(ds, qz[h, cols, :])
                kt = qkvt[HW + h * HEAD_DIM : HW + (h + 1) * HEAD_DIM, rows]
                dqt[h * HEAD_DIM : (h + 1) * HEAD_DIM, cols] += dot(kt, ds)

        step(j, True)

        def more(i, carry):
            step(i, False)
            return carry

        lax.fori_loop(j + 1, blocks, more, 0)
        dkt = dk[...].T
        cos, sin = cos_scr[:, rows], sin_scr[:, rows]
        for h in range(hd):
            top = h * HEAD_DIM
            one, two = rot_pair(
                dkt[top : top + HALF], dkt[top + HALF : top + HEAD_DIM], cos, -sin
            )
            dmt[HW + top : HW + top + HALF, rows] = one.astype(BF)
            dmt[HW + top + HALF : HW + top + HEAD_DIM, rows] = two.astype(BF)
        dmt[2 * HW : 3 * HW, rows] = dv[...].T.astype(BF)
        return 0

    lax.fori_loop(0, blocks, one_key, 0)
    cos, sin = cos_scr[:, 0:S], sin_scr[:, 0:S]
    for h in range(hd):
        top = h * HEAD_DIM
        one, two = rot_pair(
            dqt[top : top + HALF, :] * SCALE,
            dqt[top + HALF : top + HEAD_DIM, :] * SCALE,
            cos,
            -sin,
        )
        dmt[top : top + HALF, :] = one.astype(BF)
        dmt[top + HALF : top + HEAD_DIM, :] = two.astype(BF)
    for copy in last:
        copy.wait()
    wt = w_scr[...].T[0 : 3 * HW, :]
    if embed:
        sums = jnp.zeros((3 * HW, VOCAB), F32)
        for r in range(G):
            at = rows_at(idx[plan.at_src + r], n)
            ids = ints_scr[8 * r : 8 * r + 1, :]
            hot = (lax.broadcasted_iota(jnp.int32, (VOCAB, n), 0) == ids).astype(F32).astype(BF)
            sums += dot(dmt[:, at], hot, NT)
        high = sums.astype(BF)
        low = (sums - high.astype(F32)).astype(BF)
        res_scr[...] = dot(high.T, wt) + dot(low.T, wt)
        copies.start(res_scr, tab_out)
        grad = dot(high, tab_scr[...]) + dot(low, tab_scr[...])
    else:
        for r in reversed(range(G)):
            at = rows_at(idx[plan.at_dst + r], n)
            res_scr[at, :] = dot(dmt[:, at].T, wt).astype(BF)
            copies.start(res_scr.at[at, :], da_outs[r])
        grad = dot(dmt[...], src_scr[...])
    dw_scr[:, 0 : 3 * HW] = grad.T.astype(BF)
    dw_scr[:, 3 * HW : D] = jnp.zeros((D, D - 3 * HW), BF)
    for r in range(plan.chips):
        at = rows_at(idx[plan.at_order["x"] + r], 2 * plan.DR)
        copies.start(dw_scr.at[at, :], dw_outs[r])
    copies.finish()


def attn_backward(
    plan, idx, cos, sin, source, weights, lo, dos, saved, n, embed, masked, after=()
):
    G, HW, hd = plan.G, plan.HW, plan.hd
    S = G * n
    tile = min(512, S)
    outs = [sds((2 * plan.DR, D), BF)] * plan.chips
    outs += [sds((VOCAB, D), F32)] if embed else [sds((n, D), BF)] * G
    res = run(
        "attention_backward",
        functools.partial(attn_bwd_kernel, plan, n, lo, embed, masked),
        [],
        [idx],
        [],
        [
            pltpu.VMEM((D, plan.QW), BF),
            pltpu.VMEM(cos.shape, F32),
            pltpu.VMEM(cos.shape, F32),
            *source_scratch(embed, masked, S, G, source),
            pltpu.VMEM((3 * HW, S), BF),
            pltpu.VMEM((HW, S), F32),
            pltpu.VMEM((8, S), F32),
            pltpu.VMEM((S, HW), BF),
            pltpu.VMEM((S, HW), BF),
            pltpu.VMEM((S, HW), BF),
            pltpu.VMEM((hd, S, HW), BF),
            pltpu.VMEM((hd, HW, S), BF),
            pltpu.VMEM((hd, S, HW), BF),
            pltpu.VMEM((hd, HW, S), BF),
            pltpu.VMEM((8, S), F32),
            pltpu.VMEM((HW, S), F32),
            pltpu.VMEM((tile, HW), F32),
            pltpu.VMEM((tile, HW), F32),
            pltpu.VMEM((3 * HW, S), BF),
            pltpu.VMEM((VOCAB, D), F32) if embed else pltpu.VMEM((S, D), BF),
            pltpu.VMEM((D, D), BF),
        ],
        raw=[cos, sin, *source, *weights, *dos, *saved],
        raw_outs=outs,
        sems=2 * plan.chips + 3 * G + 8,
        flops=4 * S * D * 3 * HW + 5 * hd * S * S * 256,
        trans=hd * S * S // 2,
        after=after,
    )
    return res[: plan.chips], res[plan.chips :]


class Pack:
    def __init__(self, plan, copies, pack, scr):
        self.plan = plan
        self.up_scr, self.down_scr, self.proj_scr = scr
        DR, FR = plan.DR, plan.FR
        self.per = CHUNK // FR
        top = 4 * DR + FR
        self.proj_copy = copies.start(pack.at[:, top : top + DR, :], self.proj_scr)
        self.copies = []
        for j in range(FF // CHUNK):
            at = slice(j * self.per, (j + 1) * self.per)
            self.copies.append(
                (
                    copies.start(pack.at[:, j * DR : (j + 1) * DR, :], self.up_scr.at[j]),
                    copies.start(pack.at[at, 4 * DR : 4 * DR + FR, :], self.down_scr.at[j]),
                )
            )
        copies.open = []

    @staticmethod
    def scratch(plan):
        chunks = FF // CHUNK
        return [
            pltpu.VMEM((chunks, plan.seq, plan.DR, D), BF),
            pltpu.VMEM((chunks, CHUNK // plan.FR, plan.FR, D), BF),
            pltpu.VMEM((plan.seq, plan.DR, D), BF),
        ]

    def proj(self, k):
        per = self.plan.HW // self.plan.DR
        rows = self.proj_scr[pl.ds(k * per, per), :, :]
        return rows.reshape(self.plan.HW, D)

    def up(self, j):
        return self.up_scr[j].reshape(D, CHUNK)

    def down(self, j):
        return self.down_scr[j].reshape(CHUNK, D)


VALID, TARGET, NEXT, SLOT, BYTE = range(5)


def at_lane(lane, value):
    lanes = lax.broadcasted_iota(jnp.int32, (8, 128), 1)
    return jnp.where(lanes == lane, jnp.broadcast_to(value, (8, 128)), 0.0)


def square_of(cols, x):
    rows = jnp.sum(x * x, axis=-1, keepdims=True) * cols[:, VALID : VALID + 1]
    return jnp.sum(rows, axis=0, keepdims=True)


def attended(plan, k, x):
    k.pack.proj_copy.wait()
    y = x
    for r in range(plan.G):
        y += dot(k.c[r][...], k.pack.proj(k.idx[plan.at_src + r]))
    k.y[...] = y


def feed_forward(k, layer, y, keep=False):
    k.normed[...] = (y * root_of(y) * k.gains[2 * layer + 1 : 2 * layer + 2, :]).astype(BF)
    for j in range(FF // CHUNK):
        k.pack.copies[j][0].wait()
        h = dot(k.normed[...], k.pack.up(j))
        at = slice(j * CHUNK, (j + 1) * CHUNK)
        if keep:
            value, slope = gelu_parts(h)
            k.slope[j] = slope
        else:
            value = gelu_value(h)
        k.act[:, at] = value.astype(BF)
    for j in range(FF // CHUNK):
        k.pack.copies[j][1].wait()
    k.x_scr[...] = k.y[...] + dot(k.act[...], k.down_scr[...].reshape(FF, D))


def begin_pack(plan, table, k):
    k.copies = Copies(k.sem)
    k.pack = Pack(plan, k.copies, k.pack_in, (k.up_scr, k.down_scr, k.proj_scr))
    if table:
        top = 6 * plan.DR + plan.FR
        k.tab_copy = k.copies.start(k.pack_in.at[:, top : top + plan.VR, :], k.tab_scr)
        k.copies.open = []


def ffn_pool_kernel(plan, k):
    x = dot(one_hot(k.cols[:, BYTE : BYTE + 1], VOCAB), k.table[...])
    attended(plan, k, x)
    feed_forward(k, 0, k.y[...])
    x = k.x_scr[...]
    k.x[...] = x
    turned = one_hot(k.cols[:, SLOT : SLOT + 1], CAP).T
    counts = jnp.sum(turned.astype(F32), axis=1, keepdims=True)
    pooled = exact_dot(turned, x) / jnp.maximum(counts, 1.0)
    k.pooled[...] = pooled
    k.a[...] = (pooled * root_of(pooled) * k.gains[2:3, :]).astype(BF)
    count = jnp.sum(k.cols[:, VALID : VALID + 1], axis=0, keepdims=True)
    k.stat[...] = at_lane(2, square_of(k.cols, x)) + at_lane(5, count)


def ffn_unpool_kernel(plan, k):
    attended(plan, k, k.pooled[...])
    feed_forward(k, 1, k.y[...])
    x = k.x1[...] + exact_dot(one_hot(k.cols[:, SLOT : SLOT + 1], CAP), k.x_scr[...])
    k.x[...] = x
    k.a[...] = (x * root_of(x) * k.gains[4:5, :]).astype(BF)
    k.stat[...] = k.stat_in[...] + at_lane(3, square_of(k.cols, x))


def forward_scratch(plan, n):
    return {
        **dict(zip(("up_scr", "down_scr", "proj_scr"), Pack.scratch(plan))),
        "normed": pltpu.VMEM((n, D), BF),
        "act": pltpu.VMEM((n, FF), BF),
        "x_scr": pltpu.VMEM((n, D), F32),
    }


def loss_part(plan, k):
    k.tab_copy.wait()
    table = k.tab_scr[...].reshape(VOCAB, D)
    x = k.x_scr[...]
    valid = k.cols[:, VALID : VALID + 1]
    root = root_of(x)
    unit = x * root
    gain = k.gains[6:7, :]
    rows = (unit * gain).astype(BF)
    logits = dot(rows, table, NT)
    top_row = jnp.max(logits, axis=-1, keepdims=True)
    total = jnp.sum(jnp.exp(logits - top_row), axis=-1, keepdims=True)
    log_norm = top_row + jnp.log(total)
    hot = one_hot(k.cols[:, NEXT : NEXT + 1], VOCAB).astype(F32)
    picked = jnp.sum(logits * hot, axis=-1, keepdims=True)
    ce = jnp.sum(valid * (log_norm - picked), axis=0, keepdims=True)
    glog = (valid * (jnp.exp(logits - log_norm) - hot)).astype(BF)
    k.dtab[...] = dot(glog.T, rows).astype(BF).reshape(plan.seq, plan.VR, D)
    dx, dgain = norm_back(unit, root, gain, dot(glog, table))
    k.gout[...] = dx
    k.dgain6[...] = jnp.broadcast_to(dgain, k.dgain6.shape)
    k.stat[...] = (
        k.stat_a[...] + k.stat_b[...] + at_lane(0, ce) + at_lane(4, square_of(k.cols, x))
    )


def ffn_backward_part(plan, k, layer, y, send, kept=False):
    root = root_of(y)
    gain = k.gains[2 * layer + 1 : 2 * layer + 2, :]
    k.unit[...] = y * root
    if not kept:
        k.normed[...] = (y * root * gain).astype(BF)
    k.normt[...] = k.normed[...].T
    k.low[...] = k.gout[...].astype(BF)
    k.dn[...] = jnp.zeros_like(k.dn)
    for j in range(FF // CHUNK):
        if kept:
            value, slope = k.act[:, j * CHUNK : (j + 1) * CHUNK], k.slope[j]
            up = k.pack.up(j)
        else:
            for copy in k.pack.copies[j]:
                copy.wait()
            up = k.pack.up(j)
            value, slope = gelu_parts(dot(k.normed[...], up))
            value = value.astype(BF)
        per = CHUNK // plan.FR
        grad = dot(value.T, k.low[...]).astype(BF)
        k.ddown[j * per : (j + 1) * per] = grad.reshape(per, plan.FR, D)
        dact = dot(k.low[...], k.pack.down(j), NT)
        dh = (dact * slope).astype(BF)
        k.dup[j] = dot(k.normt[...], dh).astype(BF).reshape(plan.seq, plan.DR, CHUNK)
        send(j)
        k.dn[...] += dot(dh, up, NT)
    dx, dgain = norm_back(k.unit[...], root, gain, k.dn[...])
    gmid = k.gout[...] + dx
    k.gmid[...] = gmid
    k.dgain[...] = jnp.broadcast_to(dgain, k.dgain.shape)
    k.low[...] = gmid.astype(BF)
    if not kept:
        k.pack.proj_copy.wait()
    HW = plan.HW
    for r in range(plan.G):
        per = HW // plan.DR
        grad = dot(k.c[r][...].T, k.low[...]).astype(BF)
        k.dproj[pl.ds(k.idx[plan.at_src + r] * per, per)] = grad.reshape(per, plan.DR, D)
        k.dc[r][...] = dot(k.low[...], k.pack.proj(k.idx[plan.at_dst + r]), NT).astype(BF)


def send_packs(plan, k, copies):
    DR, FR = plan.DR, plan.FR

    def shard(order, r, dc):
        core = lax.rem(k.idx[plan.at_core] + dc, 2)
        return k.idx[plan.at_order[order] + r] * 2 + core

    def upward(j):
        for dc in (1, 0):
            for r in range(plan.chips):
                out = k.packs[2 * dc].at[r, j * DR : (j + 1) * DR, :]
                copies.start(k.dup.at[j, shard("x", r, dc)], out)

    def rest():
        for dc in (1, 0):
            two = k.packs[2 * dc + 1]
            for r in range(plan.chips):
                s = shard("y", r, dc)
                copies.start(k.ddown.at[s], two.at[r, 0:FR, :])
                copies.start(k.dproj.at[s], two.at[r, FR : FR + DR, :])
        copies.finish()

    return upward, rest


def send_whole(plan, k, copies, extra=False):
    DR, FR, VR = plan.DR, plan.FR, plan.VR
    (out,) = k.packs
    per = CHUNK // FR
    down_at = 4 * DR + (DR + VR if extra else 0)

    def upward(j):
        copies.start(k.dup.at[j], out.at[:, j * DR : (j + 1) * DR, :])
        at = slice(j * per, (j + 1) * per)
        copies.start(k.ddown.at[at], out.at[at, down_at : down_at + FR, :])

    def rest():
        top = 4 * DR
        if extra:
            copies.start(k.dp3, out.at[:, top : top + DR, :])
            top += DR
            copies.start(k.dtab, out.at[:, top : top + VR, :])
        top = down_at + FR
        copies.start(k.dproj, out.at[:, top : top + DR, :])
        copies.finish()

    return upward, rest


def backward_scratch(plan, n):
    return {
        **forward_scratch(plan, n),
        "gout": pltpu.VMEM((n, D), F32),
        "unit": pltpu.VMEM((n, D), F32),
        "normt": pltpu.VMEM((D, n), BF),
        "low": pltpu.VMEM((n, D), BF),
        "dn": pltpu.VMEM((n, D), F32),
        "dup": pltpu.VMEM((FF // CHUNK, plan.seq, plan.DR, CHUNK), BF),
        "ddown": pltpu.VMEM((plan.seq, plan.FR, D), BF),
        "dproj": pltpu.VMEM((plan.seq, plan.DR, D), BF),
    }


def backward_outs(plan, n, whole=False, extra=False):
    C, DR, FR = plan.chips, plan.DR, plan.FR
    outs = {
        "gmid": sds((n, D), F32),
        "dc": [sds((n, plan.HW), BF)] * plan.G,
        "dgain": sds((8, D), F32),
    }
    if whole:
        rows = 5 * DR + FR + (DR + plan.VR if extra else 0)
        return outs, {"packs": [sds((plan.seq, rows, D), BF)]}
    return outs, {"packs": [sds((C, 4 * DR, D), BF), sds((C, FR + DR, D), BF)] * 2}


def ffn_loss_kernel(plan, k):
    copies = k.copies
    attended(plan, k, k.x[...])
    feed_forward(k, 2, k.y[...], keep=True)
    loss_part(plan, k)
    upward, rest = send_whole(plan, k, copies, extra=True)
    ffn_backward_part(plan, k, 2, k.y[...], upward, kept=True)
    rest()


def joined(refs):
    total = refs[0][...].astype(F32)
    for ref in refs[1:]:
        total += ref[...].astype(F32)
    return total


def join_last_kernel(plan, k):
    copies = k.copies
    x = k.x[...]
    root = root_of(x)
    dx, dgain = norm_back(x * root, root, k.gains[4:5, :], joined(k.terms))
    grad = k.gnext[...] + dx
    k.second[...] = grad
    k.gout[...] = exact_dot(one_hot(k.cols[:, SLOT : SLOT + 1], CAP).T, grad)
    k.dgain_in[...] = jnp.broadcast_to(dgain, k.dgain_in.shape)
    upward, rest = send_whole(plan, k, copies)
    ffn_backward_part(plan, k, 1, k.y[...], upward)
    rest()


def join_middle_kernel(plan, k):
    copies = k.copies
    x = k.x[...]
    root = root_of(x)
    dx, dgain = norm_back(x * root, root, k.gains[2:3, :], joined(k.terms))
    member = one_hot(k.cols[:, SLOT : SLOT + 1], CAP)
    counts = jnp.sum(member.T.astype(F32), axis=1, keepdims=True)
    grad = (k.gnext[...] + dx) / jnp.maximum(counts, 1.0)
    k.gout[...] = k.second[...] + k.bound[...] + exact_dot(member, grad)
    k.dgain_in[...] = jnp.broadcast_to(dgain, k.dgain_in.shape)
    upward, rest = send_packs(plan, k, copies)
    ffn_backward_part(plan, k, 0, k.y[...], upward)
    rest()


def bound_kernel(plan, x_ref, cols, gains, pack, *refs):
    grad_out, dp_out, dgain_out, stat, weight_scr, sem = refs
    top = 5 * plan.DR + plan.FR
    copy = Copies(sem).start(pack.at[:, top : top + plan.DR, :], weight_scr)
    x = x_ref[...]
    valid = cols[:, VALID : VALID + 1]
    target = cols[:, TARGET : TARGET + 1]
    root = root_of(x)
    unit = x * root
    gain = gains[7:8, :]
    rows = (unit * gain).astype(BF)
    copy.wait()
    weight = weight_scr[...].reshape(D, D)
    value, slope = gelu_parts(dot(rows, weight))
    out_gain = gains[8:9, :]
    z = jnp.sum(value * out_gain, axis=-1, keepdims=True) * D ** (-0.5)
    small = jnp.exp(-jnp.abs(z))
    soft = jnp.maximum(z, 0.0) + jnp.log(1.0 + small)
    bce = jnp.sum(valid * (soft - target * z), axis=0, keepdims=True)
    sig = jnp.where(z >= 0, 1.0, small) / (1.0 + small)
    dz = valid * (sig - target) * D ** (-0.5)
    dh = (dz * out_gain * slope).astype(BF)
    dp_out[...] = dot(rows.T, dh).astype(BF).reshape(dp_out.shape)
    dx, dgain = norm_back(unit, root, gain, dot(dh, weight, NT))
    grad_out[...] = dx
    dgain_out[0:8, :] = jnp.broadcast_to(dgain, (8, D))
    dgain_out[8:16, :] = jnp.broadcast_to(jnp.sum(dz * value, axis=0, keepdims=True), (8, D))
    stat[...] = at_lane(1, bce)


def tail_kernel(plan, idx, gmid, dtab, table, cols, gains, *refs):
    d1, d2, d3, d4, d5, d6, d78 = refs[:7]
    dw = refs[7 : 7 + plan.chips]
    packs = refs[7 + plan.chips : 7 + 2 * plan.chips]
    tab, gt, turned = refs[7 + 2 * plan.chips :]
    t = table[...].astype(F32)
    root = root_of(t)
    dx, dgain = norm_back(t * root, root, gains[0:1, :], dtab[...])
    hot = one_hot(cols[:, BYTE : BYTE + 1], VOCAB).T
    g = gmid[...]
    high = g.astype(BF)
    tab[...] = dx + (dot(hot, high) + dot(hot, (g - high.astype(F32)).astype(BF)))
    gt[...] = jnp.zeros_like(gt)
    gt[0:1, :] = dgain
    for k, ref in ((1, d1), (2, d2), (3, d3), (4, d4), (5, d5), (6, d6), (7, d78)):
        gt[k : k + 1, :] = ref[0:1, :]
    gt[8:9, :] = d78[8:9, :]
    turned[...] = gt[...].T
    DR, VR, HW = plan.DR, plan.VR, plan.HW
    for r in range(plan.chips):
        k = idx[plan.at_order["x"] + r]
        if 3 * HW < D - 128:
            packs[r][0 : 2 * DR, :] = jnp.zeros((2 * DR, D), BF)
        packs[r][0 : 2 * DR, 0 : 3 * HW] = dw[r][:, 0 : 3 * HW]
        rows = turned[pl.ds(pl.multiple_of(k * 2 * DR, 2 * DR), 2 * DR), :]
        packs[r][0 : 2 * DR, D - 128 : D] = rows.astype(BF)
        rows = tab[pl.ds(pl.multiple_of(k * 2 * VR, 2 * VR), 2 * VR), :]
        packs[r][2 * DR : 2 * DR + 2 * VR, :] = rows.astype(BF)


def adam_update(weight, first, second, grad, rate):
    mean = BETA_FIRST * first + (1.0 - BETA_FIRST) * grad
    meansq = BETA_SECOND * second + (1.0 - BETA_SECOND) * grad * grad
    mean_hat = mean / (1.0 - BETA_FIRST**STEP)
    meansq_hat = meansq / (1.0 - BETA_SECOND**STEP)
    master = weight - rate * (mean_hat / (jnp.sqrt(meansq_hat) + ADAM_EPS) + DECAY_RATE * weight)
    return (master, mean, meansq)


def update_kernel(shapes, totals, gain, *refs):
    count = len(shapes)
    refs = list(refs)

    def take(n):
        taken = refs[:n]
        del refs[:n]
        return taken

    gain_in = take(3)
    ins = [take(count) for _ in range(4)]
    gain_out = take(3)
    outs = [take(count) for _ in range(4)]
    losses, counted, norm_out, rms = take(4)
    in_scr = [take(count) for _ in range(4)]
    out_scr = [take(count) for _ in range(4)]
    sem = refs[0]
    copies = Copies(sem)
    started = {}
    for t, shape in enumerate(shapes):
        for layer in range(shape[0]):
            started[t, layer] = [
                copies.start(src[t].at[layer], dst[t].at[layer]) for src, dst in zip(ins, in_scr)
            ]
    copies.open = []
    lanes = lax.broadcasted_iota(jnp.int32, (8, 128), 1)
    sums = totals[...]

    def lane(k):
        picked = jnp.where(lanes == k, sums, 0.0)[0:1, :]
        return jnp.sum(picked, axis=1, keepdims=True)

    inverse = 1.0 / lane(5)
    norm = jnp.sqrt(lane(6)) * inverse
    factor = jnp.minimum(1.0, CLIP_NORM / (norm + 1e-06)) * inverse
    losses[0] = lane(0)[0, 0]
    losses[1] = lane(1)[0, 0]
    counted[0] = lane(5)[0, 0]
    norm_out[0] = norm[0, 0]
    for k in range(3):
        rms[k] = jnp.sqrt(lane(2 + k) * inverse * (1.0 / D))[0, 0]
    rows, width = gain_in[0].shape
    grad = gain[...].T[0:rows, 0:width] * factor
    new = adam_update(*[v[...] for v in gain_in], grad, RATE_VECTOR)
    for ref, value in zip(gain_out, new):
        ref[...] = value
    for t, shape in enumerate(shapes):
        rate = RATE_VECTOR if t == count - 1 else RATE_MATRIX
        size = min(16, shape[1])
        for layer in range(shape[0]):
            for copy in started[t, layer]:
                copy.wait()

            def block(r, carry, t=t, layer=layer, rate=rate, size=size):
                at = rows_at(r, size)
                w, a, b, g = [scr[t][layer, at, :].astype(F32) for scr in in_scr]
                new = adam_update(w, a, b, g * factor, rate)
                for scr, value in zip(out_scr, (*new, new[0])):
                    scr[t][layer, at, :] = value.astype(scr[t].dtype)
                return carry

            lax.fori_loop(0, shape[1] // size, block, 0)
            for src, dst in zip(out_scr, outs):
                copies.start(src[t].at[layer], dst[t].at[layer])
    copies.finish()


def add(a, b):
    return (a.astype(F32) + b.astype(F32)).astype(BF)


def total_of(terms):
    total = terms[0].astype(F32)
    for term in terms[1:]:
        total = total + term.astype(F32)
    return total.astype(BF)


def sum_first(plan, blocks, axis):
    got = [plan.shift(blocks[d], **{axis: d}) for d in range(1, plan.sizes[axis])]
    return [total_of([b[e] for b in (blocks[0], *got)]) for e in range(blocks[0].shape[0])]


def sum_second(plan, blocks, axis):
    return total_of(
        [blocks[0]] + [plan.shift(blocks[d], **{axis: d}) for d in range(1, plan.sizes[axis])]
    )


def sum_chips(plan, blocks):
    terms = [blocks[0]]
    for r in range(1, plan.chips):
        dx, dy = divmod(r, plan.Y)
        terms.append(plan.shift(blocks[r], x=dx, y=dy))
    return total_of(terms)


def head_sum(plan, v, axis):
    return add(v, plan.shift(v, **{axis: 1}))


def split_axes(plan, t, first, second):
    return t.reshape((plan.sizes[first], plan.sizes[second]) + t.shape[1:])


def by_core(first, second):
    halves = [v.reshape((2, v.shape[0] // 2) + v.shape[1:]) for v in (first, second)]
    return jnp.concatenate(halves, axis=1)


def exchange_columns(plan, v, me):
    own = lax.dynamic_index_in_dim(v, me["core"], 0, keepdims=False)
    other = lax.dynamic_index_in_dim(v, 1 - me["core"], 0, keepdims=False)
    parts = [own] + [plan.shift(own, zl=d) for d in range(1, plan.L)]
    return parts + [plan.shift(other, core=1, zl=d) for d in range(plan.L)]


def final_kernel(plan, idx, *refs):
    DR, FR, VR, HW, G = plan.DR, plan.FR, plan.VR, plan.HW, plan.G
    cut = 4 * DR
    shard0, shard2, refs = refs[0:2], refs[2:4], refs[4:]
    columns0, columns12, stat_in = refs[:G], refs[G : 2 * G], refs[2 * G]
    parts, refs = refs[2 * G + 1 : -10], refs[-10:]
    qkv, proj, up, down, table, gain, stat, scr0, scr12, scr1 = refs
    for r, part in enumerate(parts):
        place = idx[plan.at_head + r] if len(parts) > 1 else 0
        scr1[place] = part[...]
    whole = scr1[...].reshape(scr1.shape[0] * scr1.shape[1], D)
    shards = [shard0, (whole[0:cut], whole[cut:]), shard2]
    for r in range(G):
        b = idx[plan.at_src + r]
        scr0[b] = columns0[r][...]
        scr12[b] = columns12[r][...]
    for b in range(G):
        for part in range(3):
            src = slice(part * HW, (part + 1) * HW)
            dst = slice(part * D + b * HW, part * D + (b + 1) * HW)
            qkv[0, :, dst] = scr0[b, 0:DR, src]
            qkv[1, :, dst] = scr12[b, 0:DR, src]
            qkv[2, :, dst] = scr12[b, DR : 2 * DR, src]
    tab = scr0[0, DR : DR + VR, :].astype(F32)
    gains = scr0[0, 0:DR, D - 128 : D].astype(F32)
    for b in range(1, G):
        tab += scr0[b, DR : DR + VR, :].astype(F32)
        gains += scr0[b, 0:DR, D - 128 : D].astype(F32)
    gain[...] = gains
    table[0] = tab
    for layer in range(3):
        one, two = shards[layer]
        for j in range(4):
            up[layer, :, j * CHUNK : (j + 1) * CHUNK] = one[j * DR : (j + 1) * DR, :]
        top = 0
        if layer == 2:
            proj[3] = two[0:DR, :]
            table[1] = two[DR : DR + VR, :].astype(F32)
            top = DR + VR
        down[layer] = two[top : top + FR, :]
        proj[layer] = two[top + FR : top + FR + DR, :]
    total = jnp.zeros((1, 1), F32)
    for ref in (qkv, proj, up, down, table, gain):
        pieces = [ref[...]] if len(ref.shape) == 2 else [ref[l] for l in range(ref.shape[0])]
        for piece in pieces:
            v = piece.astype(F32)
            total += jnp.sum(jnp.sum(v * v, axis=0, keepdims=True), axis=1, keepdims=True)
    stat[...] = stat_in[...] + at_lane(6, total)


def per_device(plan, *args):
    (
        byte_ids,
        next_bytes,
        loss_mask,
        pool_slots,
        qkv_weight,
        proj_weight,
        upward_weight,
        downward_weight,
        table_weight,
        gain_weight,
        qkv_first,
        qkv_second,
        proj_first,
        proj_second,
        upward_first,
        upward_second,
        downward_first,
        downward_second,
        table_first,
        table_second,
        gain_first,
        gain_second,
    ) = args
    G, L, HW, QW, DR, FR, VR = plan.G, plan.L, plan.HW, plan.QW, plan.DR, plan.FR, plan.VR
    n = byte_ids.shape[1]
    length = n * G
    me = plan.place()
    idx = plan.tables()
    core = me["core"]

    width0, width1 = QW + 384, 2 * QW
    keep0, send0, keep1, send1 = run(
        "first",
        functools.partial(first_kernel, plan),
        [sds((DR, width0), BF)] * 2 + [sds((DR, width1), BF)] * 2,
        [idx],
        [qkv_weight, table_weight, gain_weight],
        [pltpu.VMEM((128, 128), F32)],
    )
    ints = jnp.concatenate([byte_ids, next_bytes, loss_mask, pool_slots], axis=0)
    ints = jnp.concatenate([ints, jnp.zeros_like(ints)], axis=0)

    def chip_rows(keep, got):
        return jnp.where(
            core == 0,
            jnp.concatenate([keep, got], axis=0),
            jnp.concatenate([got, keep], axis=0),
        )

    def gather_chips(v, want=lambda dy, dx: True):
        out = [v]
        for r in range(1, plan.chips):
            dy, dx = divmod(r, plan.X)
            if want(dy, dx):
                out.append(plan.shift(v, y=dy, x=dx))
        return out

    def swap(c):
        return {**c, "core": c["zh"], "zh": c["core"]}

    got0, got1, own = fence(
        plan.shift(send0, core=1), plan.shift(send1, core=1), plan.permute(ints, swap)
    )
    chip0 = chip_rows(keep0, got0)
    chip1 = chip_rows(keep1, got1)
    early, both, chip1 = fence(
        gather_chips(chip0), jnp.concatenate([own, plan.shift(own, core=1)]), chip1
    )
    pairs = [both] + [plan.shift(both, zl=d) for d in range(1, L)]
    ints_all = jnp.concatenate([p[:8] for p in pairs] + [p[8:] for p in pairs])

    shard_inputs = [upward_weight, downward_weight, proj_weight, table_weight]

    def gather_pack(pack):
        return lax.all_gather(pack, "seq", axis=0, tiled=False)

    (pack0,) = run(
        "pack",
        functools.partial(pack_kernel, plan, 0),
        [sds((PackCast.rows(plan, 0), D), BF)],
        [],
        [],
        PackCast.scratch(plan),
        raw=shard_inputs,
        sems=5,
        after=[keep0],
    )
    packs = [gather_pack(pack0)]

    table, atab, gains, cols = run(
        "tables",
        functools.partial(prep_kernel, plan),
        [sds((VOCAB, D), BF), sds((VOCAB, D), BF), sds((16, D), F32), sds((n, 128), F32)],
        [idx],
        [own, *early],
        [pltpu.VMEM((VOCAB, D), F32), pltpu.VMEM((D, 128), F32), pltpu.VMEM((128, n), F32)],
    )
    half = np.arange(HALF, dtype=np.float32) / np.float32(HALF)
    frequency = np.float32(10000.0) ** (-half)
    angles = frequency[:, None] * np.arange(length, dtype=np.float32)[None, :]
    cos = jnp.asarray(np.cos(angles.astype(np.float64)).astype(np.float32))
    sin = jnp.asarray(np.sin(angles.astype(np.float64)).astype(np.float32))

    def exchange(parts):
        out = [parts[0]]
        for r in range(1, G):
            dc, dl = divmod(r, L)
            out.append(plan.shift(parts[r], core=dc, zl=dl))
        return out

    def gather_near(a):
        return [a] + [plan.shift(a, zl=d) for d in range(1, L)]

    def scatter_group(das):
        terms = [das[0], plan.shift(das[L], core=1)]
        for d in range(1, L):
            both = add(das[d], plan.shift(das[L + d], core=1))
            terms.append(plan.shift(both, zl=d))
        return terms

    early, table, atab, gains, cols, ints_all, chip1 = fence(
        early, table, atab, gains, cols, ints_all, chip1
    )
    c0, saved0, pack1 = attn_forward(
        plan, idx, cos, sin, [ints_all, atab], early, 0, n, True, False, 1, shard_inputs
    )
    packs.append(gather_pack(pack1))
    c0, saved0 = fence(c0, saved0)
    c0, chip1 = fence(exchange(c0), chip1)
    dense = 2 * D * (D + 2 * FF)
    res = run_named(
        "ffn_pool",
        functools.partial(ffn_pool_kernel, plan),
        {
            "y": sds((n, D), F32),
            "x": sds((n, D), F32),
            "pooled": sds((CAP, D), F32),
            "a": sds((CAP, D), BF),
            "stat": sds((8, 128), F32),
        },
        {"c": c0, "cols": cols, "table": table, "gains": gains},
        forward_scratch(plan, n),
        {"pack_in": packs[0]},
        {},
        idx,
        16,
        n * dense,
        n * FF,
        functools.partial(begin_pack, plan, False),
    )
    y0, x1, pooled, a1, stat = res.y, res.x, res.pooled, res.a, res.stat
    straight = gather_chips(chip1, lambda dy, dx: not (dy and dx))
    y0, x1, pooled, a1, stat, straight, chip1 = fence(
        y0, x1, pooled, a1, stat, straight, chip1
    )
    near, beside, diagonal = fence(
        gather_near(a1),
        plan.shift(a1, core=1),
        gather_chips(chip1, lambda dy, dx: dy and dx),
    )
    late = [straight.pop(0)]
    diagonal.pop(0)
    for r in range(1, plan.chips):
        late.append((diagonal if all(divmod(r, plan.X)) else straight).pop(0))
    a1 = [*near, beside, *[plan.shift(p, core=1) for p in near[1:]]]
    c1, saved1, pack2 = attn_forward(
        plan, idx, cos, sin, [*a1, ints_all], late, 0, CAP, False, True, 2, shard_inputs
    )
    packs.append(gather_pack(pack2))
    c1, saved1 = fence(c1, saved1)
    c1 = exchange(c1)
    res = run_named(
        "ffn_unpool",
        functools.partial(ffn_unpool_kernel, plan),
        {
            "y": sds((CAP, D), F32),
            "x": sds((n, D), F32),
            "a": sds((n, D), BF),
            "stat": sds((8, 128), F32),
        },
        {"c": c1, "pooled": pooled, "x1": x1, "cols": cols, "gains": gains, "stat_in": stat},
        forward_scratch(plan, CAP),
        {"pack_in": packs[1]},
        {},
        idx,
        16,
        CAP * dense,
        CAP * FF,
        functools.partial(begin_pack, plan, False),
    )
    y1, x2, a2, stat = res.y, res.x, res.a, res.stat
    near, beside = fence(gather_near(a2), plan.shift(a2, core=1))
    a2 = [*near, beside, *[plan.shift(p, core=1) for p in near[1:]]]
    c2, saved2 = attn_forward(plan, idx, cos, sin, a2, late, QW, n, False, False)
    bound_grad, dp3, dgain78, stat_b = run(
        "boundary",
        functools.partial(bound_kernel, plan),
        [sds((n, D), F32), sds((plan.seq, DR, D), BF), sds((16, D), F32), sds((8, 128), F32)],
        [],
        [x1, cols, gains],
        [pltpu.VMEM((plan.seq, DR, D), BF)],
        raw=[packs[2]],
        sems=1,
        flops=6 * n * D * D,
        trans=n * D,
    )
    c2, bound_grad, dp3, dgain78, stat_b = fence(
        exchange(c2), bound_grad, dp3, dgain78, stat_b
    )

    source0 = [ints_all, atab]
    swaps = plan.head == 4
    cut = 4 * DR

    def swap_first(v, one="zl", two="zh"):
        if not swaps:
            return [lax.psum(v[:cut], "head"), lax.psum(v[cut:], "head")]
        return [head_sum(plan, v[:cut], one), head_sum(plan, v[cut:], two)]

    def swap_second(parts, one="zh", two="zl"):
        if not swaps:
            return parts
        return [head_sum(plan, parts[0], one), head_sum(plan, parts[1], two)]

    axes = (("x", "y"), ("y", "x"))

    def core_sums(packs):
        out = []
        for mine, theirs, ax in zip(packs[:2], packs[2:], axes):
            got = split_axes(plan, plan.shift(theirs, core=1), *ax)
            mine = split_axes(plan, mine, *ax)
            out.append([add(mine[d], got[d]) for d in range(mine.shape[0])])
        return out

    def first_sums(halves):
        return [sum_first(plan, half, ax[0]) for half, ax in zip(halves, axes)]

    def second_sums(halves):
        return [sum_second(plan, half, ax[1]) for half, ax in zip(halves, axes)]

    outs, raw_outs = backward_outs(plan, n, whole=True, extra=True)
    res = run_named(
        "ffn_loss",
        functools.partial(ffn_loss_kernel, plan),
        {**outs, "dgain6": sds((8, D), F32), "stat": sds((8, 128), F32)},
        {
            "c": c2,
            "x": x2,
            "cols": cols,
            "gains": gains,
            "stat_a": stat,
            "stat_b": stat_b,
            "dp3": dp3,
        },
        {
            **backward_scratch(plan, n),
            "slope": pltpu.VMEM((FF // CHUNK, n, CHUNK), F32),
            "y": pltpu.VMEM((n, D), F32),
            "tab_scr": pltpu.VMEM((plan.seq, VR, D), BF),
            "dtab": pltpu.VMEM((plan.seq, VR, D), BF),
        },
        {"pack_in": packs[2]},
        raw_outs,
        idx,
        20 + 8 * plan.seq,
        2 * n * D * (3 * D + 6 * FF),
        n * FF,
        functools.partial(begin_pack, plan, True),
    )
    gmid2, dc2, dgain5, dgain6, stat = res.gmid, res.dc, res.dgain, res.dgain6, res.stat
    shard2 = lax.psum_scatter(res.packs[0], "seq", scatter_dimension=0)
    dc2, stat = fence(exchange(dc2), stat)
    dw2, das = attn_backward(
        plan, idx, cos, sin, a2, late, QW, dc2, saved2, n, False, False
    )
    dw2, das = fence(dw2, das)
    (terms,) = fence(scatter_group(das))
    outs, raw_outs = backward_outs(plan, CAP, whole=True)
    res = run_named(
        "join_last",
        functools.partial(join_last_kernel, plan),
        {**outs, "second": sds((n, D), F32), "dgain_in": sds((8, D), F32)},
        {
            "terms": terms,
            "gnext": gmid2,
            "x": x2,
            "cols": cols,
            "gains": gains,
            "y": y1,
            "c": c1,
        },
        backward_scratch(plan, CAP),
        {"pack_in": packs[1]},
        raw_outs,
        idx,
        16 + 8 * plan.seq,
        2 * CAP * D * (2 * D + 5 * FF),
        CAP * FF,
        functools.partial(begin_pack, plan, False),
    )
    gmid1, dc1, dgain3, dgain4 = res.gmid, res.dc, res.dgain, res.dgain_in
    shard1 = lax.psum_scatter(res.packs[0], "seq", scatter_dimension=0)
    gsecond = res.second
    dc1, dw2 = fence(dc1, dw2)
    dc1, shard2 = fence(exchange(dc1), shard2)
    dw1, das = attn_backward(
        plan, idx, cos, sin, [*a1, ints_all], late, 0, dc1, saved1, CAP, False, True
    )
    dw1, das, shard2 = fence(dw1, das, swap_first(shard2, "zh", "zl"))
    terms, dw1, shard2 = fence(scatter_group(das), dw1, shard2)
    outs, raw_outs = backward_outs(plan, n)
    res = run_named(
        "join_middle",
        functools.partial(join_middle_kernel, plan),
        {**outs, "dgain_in": sds((8, D), F32)},
        {
            "terms": terms,
            "gnext": gmid1,
            "x": pooled,
            "cols": cols,
            "gains": gains,
            "second": gsecond,
            "bound": bound_grad,
            "y": y0,
            "c": c0,
        },
        backward_scratch(plan, n),
        {"pack_in": packs[0]},
        raw_outs,
        idx,
        16 + 8 * plan.seq,
        1,
        1,
        functools.partial(begin_pack, plan, False),
    )
    gmid0, dc0, packs0, dgain1, dgain2 = res.gmid, res.dc, res.packs, res.dgain, res.dgain_in
    shard2 = swap_second(shard2, "zl", "zh")
    dw12 = sum_chips(plan, [jnp.concatenate(pair, axis=0) for pair in zip(dw1, dw2)])
    dc0, packs0, dw12, shard2, shard1 = fence(dc0, packs0, dw12, shard2, shard1)
    in_parts = shard1.shape[0] % (16 * plan.head) == 0
    if in_parts:
        shard1 = shard1.reshape(plan.head, shard1.shape[0] // plan.head, D)
        shard1 = lax.psum_scatter(shard1, "head", scatter_dimension=0)
    else:
        shard1 = lax.psum(shard1, "head")
    dc0, half0, dw12 = fence(exchange(dc0), core_sums(packs0), dw12)
    dw0, (dtab0,) = attn_backward(
        plan, idx, cos, sin, [ints_all, atab], early, 0, dc0, saved0, n, True, False
    )
    dw0, dtab0, half0, dw12, shard1 = fence(
        dw0, dtab0, first_sums(half0), head_sum(plan, dw12, "zh"), shard1
    )
    columns12 = exchange_columns(plan, by_core(dw12[: 2 * DR], dw12[2 * DR :]), me)
    tail = run(
        "tail",
        functools.partial(tail_kernel, plan),
        [sds((2 * DR + 2 * VR, D), BF)] * plan.chips,
        [idx],
        [
            *(gmid0, dtab0, table, cols, gains),
            *(dgain1, dgain2, dgain3, dgain4, dgain5, dgain6, dgain78),
            *dw0,
        ],
        [pltpu.VMEM((VOCAB, D), F32), pltpu.VMEM((128, D), F32), pltpu.VMEM((D, 128), F32)],
        flops=4 * n * VOCAB * D,
    )
    if in_parts:
        shard1 = [
            plan.shift(shard1, zh=dh, zl=dl) if dh or dl else shard1
            for dh in range(2)
            for dl in range(L)
        ]
    else:
        shard1 = [shard1]
    tail, half0, shard1, columns12 = fence(tail, second_sums(half0), shard1, columns12)
    shard0 = jnp.concatenate(half0, axis=0)
    tail, shard0, stat = fence(sum_chips(plan, tail), swap_first(shard0), stat)
    tail, shard0, stat = fence(
        head_sum(plan, tail, "zh"),
        swap_second(shard0),
        stat + sum(plan.shift(stat, zl=d) for d in range(1, L)),
    )
    stat = stat + plan.shift(stat, zh=1)
    columns0 = exchange_columns(plan, by_core(tail[: 2 * DR], tail[2 * DR :]), me)
    matrix_grad = functools.partial(sds, dtype=BF)
    *grads, gain_t, stat = run(
        "gradients",
        functools.partial(final_kernel, plan),
        [
            matrix_grad(qkv_weight.shape),
            matrix_grad(proj_weight.shape),
            matrix_grad(upward_weight.shape),
            matrix_grad(downward_weight.shape),
            sds(table_weight.shape, F32),
            sds((DR, 128), F32),
            sds((8, 128), F32),
        ],
        [idx],
        [*shard0, *shard2, *columns0, *columns12, stat, *shard1],
        [
            pltpu.VMEM((G, DR + VR, D), BF),
            pltpu.VMEM((G, 2 * DR, D), BF),
            pltpu.VMEM((len(shard1), *shard1[0].shape), BF),
        ],
    )
    totals = lax.psum(stat, "seq")
    weights = (qkv_weight, proj_weight, upward_weight, downward_weight, table_weight)
    firsts = (qkv_first, proj_first, upward_first, downward_first, table_first)
    seconds = (qkv_second, proj_second, upward_second, downward_second, table_second)
    shapes = [w.shape for w in weights]
    matrices = [sds(shape, F32) for shape in shapes] * 3 + [sds(shape, BF) for shape in shapes]
    res = run(
        "update",
        functools.partial(update_kernel, shapes),
        [sds(gain_weight.shape, F32)] * 3,
        [],
        [totals, gain_t, gain_weight, gain_first, gain_second],
        [pltpu.VMEM(v.shape, v.dtype) for v in (*weights, *firsts, *seconds, *grads)]
        + [pltpu.VMEM(v.shape, v.dtype) for v in matrices],
        raw=[*weights, *firsts, *seconds, *grads],
        raw_outs=matrices,
        sems=8 * sum(shape[0] for shape in shapes),
        scalars=(2, 1, 1, 3),
    )
    gains_new, masters, means, meansqs, low, (losses, valid_count, grad_norm, rms) = [
        res[a:b] for a, b in ((0, 3), (3, 8), (8, 13), (13, 18), (18, 23), (23, 27))
    ]
    return (
        *[part for triple in zip(masters, means, meansqs) for part in triple],
        *gains_new,
        *low,
        losses,
        valid_count.reshape(()),
        grad_norm.reshape(()),
        rms,
    )


def solution(mesh):
    plan = Plan(mesh)
    tokens = P("seq", "head")
    matrix = P(None, "seq", None)
    vector = P(None, "seq")
    states = (matrix,) * 10 + (vector,) * 2
    return jax.shard_map(
        functools.partial(per_device, plan),
        mesh=mesh,
        in_specs=(tokens,) * 4 + (matrix,) * 5 + (vector,) + states,
        out_specs=(matrix,) * 15 + (vector,) * 3 + (matrix,) * 5 + (P(),) * 4,
        check_vma=False,
    )
```
